128 devices in a mesh: dp: 16 (over x, y), expert: 8 (over z, core).
Axes of the slice: x: 4, y: 4, z: 4, core: 2. Of those that a mesh axis runs over, the one named last changes fastest.
Arguments:
- inputs: bfloat16 [49152, 512], P(('dp', 'expert')), may hold values from -6 to 6
- cotangent: bfloat16 [49152, 512], P(('dp', 'expert')), may hold values from -6 to 6
- norm_gain: float32 [512], replicated, may hold values from 0.5 to 1.5
- ffn_gain: float32 [512], replicated, may hold values from 0.5 to 1.5
- kv_weight: bfloat16 [512, 128], replicated, may hold values from -0.25 to 0.25
- router_weight: bfloat16 [512, 24], replicated, may hold values from -0.125 to 0.125
- query_weight: bfloat16 [24, 512, 64], P('expert'), may hold values from -0.25 to 0.25
- output_weight: bfloat16 [24, 64, 512], P('expert'), may hold values from -6 to 6
- up_weight: bfloat16 [512, 2048], replicated, may hold values from -0.25 to 0.25
- down_weight: bfloat16 [2048, 512], replicated, may hold values from -0.125 to 0.125
- routes: int32 [49152, 8], P(('dp', 'expert')), may hold values from 0 to 23, all different within a row; in each aligned block of 384 rows (0 to 383, 384 to 767, ...) at most 160 rows name the same one
- segment_ids: int32 [49152], P(('dp', 'expert')), may hold values from 0 to 2, as said below
Outputs:
- block_output: bfloat16 [49152, 512], P(('dp', 'expert'))
- input_grad: bfloat16 [49152, 512], P(('dp', 'expert'))
- norm_gain_grad: float32 [512], replicated
- ffn_gain_grad: float32 [512], replicated
- kv_weight_grad: float32 [512, 128], replicated
- router_weight_grad: float32 [512, 24], replicated
- query_weight_grad: float32 [24, 512, 64], P('expert')
- output_weight_grad: float32 [24, 64, 512], P('expert')
- up_weight_grad: float32 [512, 2048], replicated
- down_weight_grad: float32 [2048, 512], replicated
The draws below stay inside these ranges and needn't reach their ends.
Inputs may be any that keep to these rules, and one draw needn't show every extreme that they name: `routes`: each token names 8 different experts; the 384 rows of one device name any expert at most 160 times. `segment_ids`: within each group of 3072 consecutive tokens the ids start at 0 and never fall; three sequences, of which sequence 1 begins at a place from 1 to 383 of its group and ends at a place from 2688 to 3070.
All inputs are finite; a program needn't handle non-finite values.
Results may differ from the reference program's by a relative error of at most 0.019.
Values may be sent and summed in bfloat16 or wider, within the bound.
A program may use at most 320 MiB of HBM per device.

```python
import math
import jax
import jax.numpy as jnp
import numpy as np
from jax import lax

D = 512
HEAD = 64
FF = 2048
TOPK = 8
TOK_DEV = 384
EXPERTS = 24
GROUP = 3072
TOKENS = 49152
MOST = 160


def draw_segment_ids(key, part):
    key = jax.random.fold_in(key, 7)
    first_key, last_key, pick_key = jax.random.split(key, 3)
    group_count = TOKENS // GROUP
    starts = jax.random.randint(first_key, (group_count, 1), 1, TOK_DEV)
    last_starts = jax.random.randint(last_key, (group_count, 1), GROUP - TOK_DEV + 1, GROUP)
    chosen = jax.random.randint(pick_key, (), 0, group_count)
    group_index = jnp.arange(group_count)[:, None]
    starts = jnp.where(group_index == chosen, TOK_DEV - 1, starts)
    last_starts = jnp.where(group_index == chosen, GROUP - TOK_DEV + 1, last_starts)
    position = jnp.arange(GROUP)[None, :]
    segment = (position >= starts).astype(jnp.int32) + (position >= last_starts).astype(jnp.int32)
    return segment.reshape(-1)


def shard_levels(stream_key, extent, pieces, low, high):
    def one(dim, parts):
        draws = jax.random.uniform(jax.random.fold_in(jax.random.fold_in(stream_key, 6), dim), (parts,), jnp.float32, low / len(pieces), high / len(pieces))
        return jnp.repeat(jnp.exp(draws), extent[dim] // parts).reshape((-1,) + (1,) * (len(extent) - dim - 1))

    gain = one(*pieces[0])
    for cut in pieces[1:]:
        gain = gain * one(*cut)
    return gain


def shared_out(rng, own, number, rows, number_of, top, reach, lean):
    sequence = jax.random.permutation(rng, number_of)
    packed, ordinary = load_shares(number_of, rows * top, reach, lean, True), load_shares(number_of, rows * top, reach, lean, False)
    places = jnp.arange(number_of)

    def named(sizes, rotation):
        used = int((sizes > 0).sum())
        fixed = max(1, used // 4)
        shifted = fixed + (places - fixed + rotation * (used - fixed)) % max(1, number_of - fixed)
        return jnp.zeros((number_of,), jnp.int32).at[sequence[jnp.where(places < fixed, places, shifted)]].set(jnp.asarray(sizes, jnp.int32))

    sizes = jnp.where(number % 4 == 0, named(packed, number // 4), named(ordinary, number - number // 4 - 1))
    mixed = jax.random.permutation(jax.random.fold_in(own, 3), number_of)
    source_of, receiver = mixed[0:number_of // 2 * 2:2], mixed[1:number_of // 2 * 2:2]
    slack = jnp.minimum(sizes[source_of] - 1, reach - sizes[receiver]) // 2
    slack = jnp.where((source_of == sequence[0]) | (receiver == sequence[0]) | (sizes[receiver] == 0), 0, jnp.maximum(slack, 0))
    shifted = jax.random.randint(jax.random.fold_in(own, 4), (number_of // 2,), 0, 1 << 20) % (slack + 1)
    sizes = sizes.at[source_of].add(-shifted).at[receiver].add(shifted)
    labels = jnp.searchsorted(jnp.cumsum(sizes), jnp.arange(rows * top), side="right").astype(jnp.int32)
    grid = labels.reshape(top, rows).T
    grid = grid[jax.random.permutation(jax.random.fold_in(own, 1), rows)]
    rotation = jax.random.randint(jax.random.fold_in(own, 2), (rows, 1), 0, top)
    return jnp.take_along_axis(grid, (jnp.arange(top)[None, :] + rotation) % top, axis=1)


def load_shares(amount, total, reach, skew, full):
    loads = [(1 << 20) // math.isqrt(grade ** skew) + 1 for grade in range(1, amount + 1)]
    largest = reach if full else min(reach, max(-(-total // amount), total * loads[0] // sum(loads)))
    least = 1 if total - largest >= amount - 1 else 0
    holding, surplus = [largest] + [least] * (amount - 1), total - largest - least * (amount - 1)
    while surplus > 0:
        free = [i for i in range(1, amount) if holding[i] < largest] or [i for i in range(1, amount) if holding[i] < reach]
        pool, remaining = sum([loads[i] for i in free]), surplus
        for i in free:
            extra = min(reach - holding[i], max(1, remaining * loads[i] // pool), surplus)
            holding[i] = holding[i] + extra
            surplus = surplus - extra
    return np.array(holding)


def normal_values(stream_key, dims, spread, most, shards=(), dtype=jnp.bfloat16):
    array = spread * jax.random.normal(stream_key, dims, jnp.float32)
    if shards:
        array = array * shard_levels(stream_key, dims, shards, -0.22, 0.18)
    return jnp.clip(array, -most, most).astype(dtype)


def setup_inputs(seed: int = 0) -> dict:
    arg_keys = jax.random.split(jax.random.key(seed), 13)
    inputs = normal_values(arg_keys[0], (TOKENS, D), 1.0, 6.0, ((0, 128),))
    cotangent = normal_values(arg_keys[1], (TOKENS, D), 1.0, 6.0, ((0, 128),))
    norm_gain = jnp.clip(1.0 + 0.1 * jax.random.normal(arg_keys[2], (D,), jnp.float32), 0.5, 1.5)
    ffn_gain = jnp.clip(1.0 + 0.1 * jax.random.normal(arg_keys[3], (D,), jnp.float32), 0.5, 1.5)
    kv_weight = normal_values(arg_keys[4], (D, 2 * HEAD), D ** -0.5, 0.25)
    router_weight = normal_values(arg_keys[5], (D, EXPERTS), (4 * D) ** -0.5, 0.125)
    query_weight = normal_values(arg_keys[6], (EXPERTS, D, HEAD), D ** -0.5, 0.25, ((0, 8),))
    output_weight = normal_values(arg_keys[7], (EXPERTS, HEAD, D), 1 ** -0.5, 6.0, ((0, 8),))
    up_weight = normal_values(arg_keys[8], (D, FF), D ** -0.5, 0.25)
    down_weight = normal_values(arg_keys[9], (FF, D), FF ** -0.5, 0.125)
    routes_keys = jax.random.split(jax.random.fold_in(arg_keys[10], 1), TOKENS // TOK_DEV)
    routes_turns = jax.random.permutation(jax.random.fold_in(arg_keys[10], 3), TOKENS // TOK_DEV)
    routes = jax.vmap(lambda own, number: shared_out(jax.random.fold_in(arg_keys[10], 2), own, number, TOK_DEV, EXPERTS, TOPK, MOST, 2))(routes_keys, routes_turns).reshape((TOKENS, TOPK))
    segment_ids = draw_segment_ids(jax.random.fold_in(arg_keys[12], 71), 0)
    return {"inputs": inputs, "cotangent": cotangent, "norm_gain": norm_gain, "ffn_gain": ffn_gain, "kv_weight": kv_weight, "router_weight": router_weight, "query_weight": query_weight, "output_weight": output_weight, "up_weight": up_weight, "down_weight": down_weight, "routes": routes, "segment_ids": segment_ids}


@jax.custom_vjp
def low(v):
    return lax.optimization_barrier(v.astype(jnp.bfloat16)).astype(jnp.float32)

@jax.custom_vjp
def low_back(v):
    return v

def low_keep(v):
    return (low(v), None)

def low_pass(kept, grad):
    return (grad,)

def back_keep(v):
    return (v, None)

def back_low(kept, grad):
    return (low(grad),)
low.defvjp(low_keep, low_pass)
low_back.defvjp(back_keep, back_low)
epsilon = 1e-06
masked_score = -1e+30
highest_precision = lax.Precision.HIGHEST

def matmul_high(left_side, right_side):
    return jnp.dot(left_side, right_side, precision=highest_precision, preferred_element_type=jnp.float32)

def rms_scale(values, gain_vector):
    inverse = lax.rsqrt(lax.optimization_barrier(jnp.mean(values * values, axis=-1, keepdims=True)) + epsilon)
    return values * inverse * gain_vector

def gelu_curve(values):
    return 0.5 * values * (1.0 + jnp.tanh(0.7978845608028654 * (values + 0.044715 * values * values * values)))

def soft_rows(scores):
    exp_terms = jnp.exp(scores - lax.optimization_barrier(jnp.max(scores, axis=-1, keepdims=True)))
    return exp_terms / lax.optimization_barrier(jnp.sum(exp_terms, axis=-1, keepdims=True))

def group_forward(weight_set, group_inputs, group_segment, group_routes):
    norm_gain, ffn_gain, kv_weight, router_weight, query_weight, output_weight, up_weight, down_weight = weight_set
    normed = low(rms_scale(group_inputs, norm_gain))
    keys_values = low_back(low(matmul_high(normed, kv_weight)))
    key_part = keys_values[:, :HEAD]
    value_part = keys_values[:, HEAD:]
    logits = matmul_high(normed, router_weight)
    gate_weights = soft_rows(jnp.take_along_axis(logits, group_routes, axis=1))
    copies = low_back(jnp.broadcast_to(normed[None], (EXPERTS, GROUP, D)))
    queries = low_back(low(jnp.einsum('etd,edk->etk', copies, query_weight, precision=highest_precision) * 0.125))
    onehot = (group_routes[:, :, None] == jnp.arange(EXPERTS)[None, None, :]).astype(jnp.float32)
    picked = jnp.einsum('tje,etk->tjk', onehot, queries, precision=highest_precision)
    position = jnp.arange(GROUP)
    allowed = (group_segment[:, None] == group_segment[None, :]) & (position[None, :] <= position[:, None])
    scores = low_back(jnp.einsum('tjk,sk->tjs', picked, key_part, precision=highest_precision))
    scores = jnp.where(allowed[:, None, :], scores, masked_score)
    weights_soft = low(soft_rows(scores))
    attended = low_back(low(jnp.einsum('tjs,sk->tjk', weights_soft, value_part, precision=highest_precision)))
    spread_rows = jnp.einsum('tje,tjk->etk', onehot, attended, precision=highest_precision)
    projected = jnp.einsum('etk,ekd->etd', spread_rows, output_weight, precision=highest_precision)
    returned = low_back(low(jnp.einsum('tje,etd->tjd', onehot, projected, precision=highest_precision)))
    mixed_sum = group_inputs + lax.optimization_barrier(jnp.sum(gate_weights[:, :, None] * returned, axis=1))
    second = low(rms_scale(mixed_sum, ffn_gain))
    hidden = low_back(matmul_high(second, up_weight))
    active = low(gelu_curve(hidden))
    return mixed_sum + matmul_high(active, down_weight)

def reference(inputs, cotangent, norm_gain, ffn_gain, kv_weight, router_weight, query_weight, output_weight, up_weight, down_weight, routes, segment_ids):
    group_count = TOKENS // GROUP
    weight_set = tuple((item.astype(jnp.float32) for item in (norm_gain, ffn_gain, kv_weight, router_weight, query_weight, output_weight, up_weight, down_weight)))
    grouped_inputs = inputs.astype(jnp.float32).reshape(group_count, GROUP, D)
    grouped_cot = cotangent.astype(jnp.float32).reshape(group_count, GROUP, D)
    grouped_segments = segment_ids.reshape(group_count, GROUP)
    grouped_routes = routes.reshape(group_count, GROUP, TOPK)

    def forward(weight_values, input_values):

        def one_group(item):
            return group_forward(weight_values, item[0], item[1], item[2])
        return lax.map(jax.checkpoint(one_group), (input_values, grouped_segments, grouped_routes))
    result, pullback = jax.vjp(forward, weight_set, grouped_inputs)
    weight_grads, input_values_grad = pullback(grouped_cot)
    return (result.reshape(TOKENS, D).astype(jnp.bfloat16), input_values_grad.reshape(TOKENS, D).astype(jnp.bfloat16), weight_grads[0], weight_grads[1], weight_grads[2], weight_grads[3], weight_grads[4], weight_grads[5], weight_grads[6], weight_grads[7])
```

```python
import functools
import jax
import jax.numpy as jnp
from jax import lax
from jax.experimental import pallas as pl
from jax.experimental.pallas import tpu as pltpu
from jax.sharding import PartitionSpec as P

f32, bf16, i32 = jnp.float32, jnp.bfloat16, jnp.int32
T, D, H, J, E, FF, NB = 384, 512, 64, 8, 24, 2048, 8
EW = E * H
PAIRS = E // 2
HALF_J = 4
ROWS = HALF_J * T
eps = 1e-06
NEG = -1e30
VM = pltpu.VMEM


def nn(a, b):
    return lax.dot_general(a, b, (((1,), (0,)), ((), ())), preferred_element_type=f32)


def nt(a, b):
    return lax.dot_general(a, b, (((1,), (1,)), ((), ())), preferred_element_type=f32)


def tn(a, b):
    return lax.dot_general(a, b, (((0,), (0,)), ((), ())), preferred_element_type=f32)


def lanes(rows):
    return lax.broadcasted_iota(i32, (rows, 128), 1)


def split3(v):
    a = v.astype(bf16).astype(f32)
    b = (v - a).astype(bf16).astype(f32)
    c = (v - a - b).astype(bf16).astype(f32)
    return a, b, c


def causal(rows, cols):
    return lax.broadcasted_iota(i32, (rows, cols), 1) <= lax.broadcasted_iota(i32, (rows, cols), 0)


def segment_of(pos, bnd_ref):
    b0 = bnd_ref[0:1, :]
    b1 = bnd_ref[1:2, :]
    return (pos >= b0).astype(i32) + (pos >= b1).astype(i32)


def pick_rows(route_cols, row0, rows, j):
    return jnp.broadcast_to(route_cols[row0 : row0 + rows, j : j + 1], (rows, 128))


def expert_lane(rows):
    return (lanes(rows) >= H).astype(i32)


def kernel_a(x_ref, gain_ref, kvw_ref, rw_ref, routes_ref, normed_ref, kv_ref, gate_ref):
    x = x_ref[...].astype(f32)
    inv = lax.rsqrt(jnp.mean(x * x, axis=-1, keepdims=True) + eps)
    normed = (x * inv * gain_ref[...]).astype(bf16)
    normed_ref[...] = normed
    kv_ref[...] = nn(normed, kvw_ref[...]).astype(bf16)
    logits = nt(normed, rw_ref[...])
    cols = jnp.transpose(routes_ref[...])
    eid = lax.broadcasted_iota(i32, (T, E), 1)
    chosen = cols[:, 0:1] == eid
    for j in range(1, J):
        chosen = chosen | (cols[:, j : j + 1] == eid)
    logits = jnp.where(chosen, logits, NEG)
    top = jnp.max(logits, axis=-1, keepdims=True)
    e = jnp.where(chosen, jnp.exp(logits - top), 0.0)
    gate_ref[...] = e / jnp.sum(e, axis=-1, keepdims=True)


def prepare_keys(kv_ref, bnd_ref, kaug, vaug):
    ln = lanes(T)
    for b in range(NB):
        kv = kv_ref[b].astype(f32)
        pos = lax.broadcasted_iota(i32, (T, 128), 0) + b * T
        seg = segment_of(pos, bnd_ref)
        feat = jnp.where((ln < H + 3) & (seg != ln - H), NEG, 0.0)
        feat = jnp.where((ln >= H + 3) & (ln < H + 6), 1.0, feat)
        kaug[b] = jnp.where(ln < H, kv, feat).astype(bf16)
        one = jnp.where(ln < H + 3, 1.0, 0.0)
        vaug[b] = jnp.where(ln < H, pltpu.roll(kv, H, 1), one).astype(bf16)


def pick_queries(normed_ref, wq_ref, routes_ref, bnd_ref, me, qall, cols_ref, qa):
    cols_ref[...] = jnp.transpose(routes_ref[...])
    normed = normed_ref[...]
    for c in range(6):
        qall[:, c * 256 : (c + 1) * 256] = nt(normed, wq_ref[c * 256 : (c + 1) * 256, :]) * 0.125
    R = 128
    ln = lanes(R)
    half = expert_lane(R)

    def chunk(i, _):
        r0 = pl.multiple_of(i * R, R)
        pos = lax.broadcasted_iota(i32, (R, 128), 0) + me * T + r0
        seg = segment_of(pos, bnd_ref)
        feat = jnp.where((ln >= H) & (seg == ln - H), 1.0, 0.0)
        for j in range(J):
            rj = jnp.broadcast_to(cols_ref[pl.ds(r0, R), j : j + 1], (R, 128)) - half
            acc = jnp.zeros((R, 128), f32)
            for p in range(PAIRS):
                acc = jnp.where(rj == 2 * p, qall[pl.ds(r0, R), p * 128 : (p + 1) * 128], acc)
            acc = acc + pltpu.roll(acc, H, 1)
            qa[j, pl.ds(r0, R), :] = jnp.where(ln < H, acc, feat).astype(bf16)
        return 0

    lax.fori_loop(0, T // R, chunk, 0)


def attend_set(me, s, qa, kaug, vaug, att_ref, sbuf, mbuf, acc):
    mbuf[...] = jnp.full(mbuf.shape, NEG, f32)
    acc[...] = jnp.zeros(acc.shape, f32)

    def score(kb, masked):
        for j in range(HALF_J):
            sc = nt(qa[s * HALF_J + j], kaug[kb])
            if masked:
                sc = jnp.where(causal(T, T), sc, NEG)
            sbuf[kb, j] = sc
            m = jnp.maximum(sc[:, 0:128], jnp.maximum(sc[:, 128:256], sc[:, 256:384]))
            mbuf[j] = jnp.maximum(mbuf[j], m)

    lax.fori_loop(0, me, lambda kb, c: (score(kb, False), c)[1], 0)
    score(me, True)
    for j in range(HALF_J):
        mbuf[j] = jnp.broadcast_to(jnp.max(mbuf[j], axis=-1, keepdims=True), (T, 128))

    def weigh(kb, c):
        for j in range(HALF_J):
            m = mbuf[j]
            p = jnp.exp(sbuf[kb, j] - jnp.concatenate([m, m, m], axis=1)).astype(bf16)
            acc[j] += nn(p, vaug[kb])
        return c

    lax.fori_loop(0, me + 1, weigh, 0)
    ln = lanes(T)
    for j in range(HALF_J):
        a = acc[j]
        tot = jnp.broadcast_to(a[:, H : H + 1], (T, 128))
        att_ref[s * HALF_J + j] = (a / tot).astype(bf16)
        l1, l2, l3 = split3(-(mbuf[j] + jnp.log(tot)))
        lse = jnp.where(ln == H + 3, l1, jnp.where(ln == H + 4, l2, l3))
        old = qa[s * HALF_J + j].astype(f32)
        qa[s * HALF_J + j] = jnp.where((ln >= H + 3) & (ln < H + 6), lse, old).astype(bf16)


def kernel_b(normed_ref, wq_ref, routes_ref, bnd_ref, kv_ref, att_ref, qa_ref, qall, cols_ref, kaug, vaug, sbuf, mbuf, acc):
    me = lax.axis_index("expert")
    prepare_keys(kv_ref, bnd_ref, kaug, vaug)
    pick_queries(normed_ref, wq_ref, routes_ref, bnd_ref, me, qall, cols_ref, qa_ref)
    lax.fori_loop(0, 2, lambda s, c: (attend_set(me, s, qa_ref, kaug, vaug, att_ref, sbuf, mbuf, acc), c)[1], 0)


SCRATCH_B = [VM((T, EW), f32), VM((T, J), i32), VM((NB, T, 128), bf16), VM((NB, T, 128), bf16),
             VM((NB, HALF_J, T, T), f32), VM((HALF_J, T, 128), f32), VM((HALF_J, T, 128), f32)]


def kernel_c(x_ref, cot_ref, gate_ref, routes_ref, att_ref, wo_ref, up_ref, down_ref, fgain_ref, normed_ref, rw_ref,
             out_ref, da_ref, gm_ref, gn_ref, dwo_ref, dup_ref, ddown_ref, drw_ref, dfg_ref,
             cols_ref, gcol, ga, gall, hid, act, gmlow, gg):
    cols_ref[...] = jnp.transpose(routes_ref[...])
    R = 128
    ln = lanes(R)
    half = expert_lane(R)
    eidr = lax.broadcasted_iota(i32, (R, E), 1)

    def spread(i, _):
        r0 = pl.multiple_of(i * R, R)
        g = gate_ref[pl.ds(r0, R), :]
        tiles = []
        for j in range(J):
            rj = cols_ref[pl.ds(r0, R), j : j + 1]
            gj = jnp.sum(jnp.where(rj == eidr, g, 0.0), axis=-1, keepdims=True)
            gcol[j, pl.ds(r0, R), :] = jnp.broadcast_to(gj, (R, 128))
            a = att_ref[j, pl.ds(r0, R), :].astype(f32)
            a = jnp.where(ln < H, a, pltpu.roll(a, H, 1)) * gj
            tiles.append((jnp.broadcast_to(rj, (R, 128)) - half, a))
        for p in range(PAIRS):
            acc = jnp.zeros((R, 128), f32)
            for rj, a in tiles:
                acc = jnp.where(rj == 2 * p, a, acc)
            ga[pl.ds(r0, R), p * 128 : (p + 1) * 128] = acc.astype(bf16)
        return 0

    lax.fori_loop(0, T // R, spread, 0)
    x = x_ref[...].astype(f32)
    mixed = x + nn(ga[...], wo_ref[...])
    inv = lax.rsqrt(jnp.mean(mixed * mixed, axis=-1, keepdims=True) + eps)
    n = mixed * inv
    fgain = fgain_ref[...]
    second = (n * fgain).astype(bf16)
    cot = cot_ref[...]
    C = 512
    out = mixed
    gsec = jnp.zeros((T, D), f32)
    for c in range(FF // C):
        cs = slice(c * C, (c + 1) * C)
        v = nn(second, up_ref[:, cs])
        v2 = v * v
        th = jnp.tanh(0.7978845608028654 * (v + 0.044715 * v * v2))
        a = (0.5 * v * (1.0 + th)).astype(bf16)
        act[:, cs] = a
        dth = 0.5 * (1.0 + th) + 0.5 * v * (1.0 - th * th) * (0.7978845608028654 * (1.0 + 0.134145 * v2))
        gh = (nt(cot, down_ref[cs, :]) * dth).astype(bf16)
        out = out + nn(a, down_ref[cs, :])
        gsec = gsec + nt(gh, up_ref[:, cs])
        ddown_ref[cs, :] = tn(a, cot).astype(bf16)
        dup_ref[:, cs] = tn(second, gh).astype(bf16)
    out_ref[...] = out.astype(bf16)
    dfg_ref[...] = jnp.sum(gsec * n, axis=0, keepdims=True)
    hh = gsec * fgain
    gm = cot.astype(f32) + inv * (hh - n * jnp.mean(hh * n, axis=-1, keepdims=True))
    gm_ref[...] = gm
    gml = gm.astype(bf16)
    gmlow[...] = gml
    for c in range(3):
        gall[:, c * 512 : (c + 1) * 512] = nt(gml, wo_ref[c * 512 : (c + 1) * 512, :])

    def grads(i, _):
        r0 = pl.multiple_of(i * R, R)
        inner = jnp.zeros((R, 1), f32)
        ggs = []
        for j in range(J):
            rj = cols_ref[pl.ds(r0, R), j : j + 1]
            rb = jnp.broadcast_to(rj, (R, 128)) - half
            acc = jnp.zeros((R, 128), f32)
            for p in range(PAIRS):
                acc = jnp.where(rb == 2 * p, gall[pl.ds(r0, R), p * 128 : (p + 1) * 128], acc)
            acc = acc + pltpu.roll(acc, H, 1)
            a = att_ref[j, pl.ds(r0, R), :].astype(f32)
            dot = jnp.sum(jnp.where(ln < H, acc * a, 0.0), axis=-1, keepdims=True)
            gj = gcol[j, pl.ds(r0, R), :]
            g1 = gj[:, 0:1]
            inner = inner + g1 * dot
            ggs.append((rj, g1, dot))
            da = acc * gj
            d1, d2, d3 = split3(-jnp.broadcast_to(dot * g1, (R, 128)))
            ft = jnp.where(ln == H, d1, jnp.where(ln == H + 1, d2, jnp.where(ln == H + 2, d3, 0.0)))
            da_ref[j, pl.ds(r0, R), :] = jnp.where(ln < H, da, ft).astype(bf16)
        gl = jnp.zeros((R, E), f32)
        for rj, g1, dot in ggs:
            gl = jnp.where(rj == eidr, g1 * (dot - inner), gl)
        gg[pl.ds(r0, R), :] = gl
        return 0

    lax.fori_loop(0, T // R, grads, 0)
    gl = gg[...]
    hi = gl.astype(bf16)
    lo = (gl - hi.astype(f32)).astype(bf16)
    rw = rw_ref[...]
    gn_ref[...] = nn(hi, rw) + nn(lo, rw)
    nm = normed_ref[...]
    drw_ref[...] = tn(hi, nm) + tn(lo, nm)
    for c in range(3):
        dwo_ref[c * 512 : (c + 1) * 512, :] = tn(ga[:, c * 512 : (c + 1) * 512], gmlow[...]).astype(bf16)


SCRATCH_C = [VM((T, J), i32), VM((J, T, 128), f32), VM((T, EW), bf16), VM((T, EW), f32), VM((8, 128), f32),
             VM((T, FF), bf16), VM((T, D), bf16), VM((T, E), f32)]


def kernel_d(kv_ref, bnd_ref, qa_ref, da_ref, dq_ref, gkv_ref, kaug, vaug, qt, dat, dqacc):
    me = lax.axis_index("expert")
    prepare_keys(kv_ref, bnd_ref, kaug, vaug)
    for j in range(J):
        qt[j] = jnp.transpose(qa_ref[j].astype(f32))[:H].astype(bf16)
        dat[j] = jnp.transpose(da_ref[j].astype(f32))[:H].astype(bf16)
    dqacc[...] = jnp.zeros(dqacc.shape, f32)
    gkv_ref[...] = jnp.zeros(gkv_ref.shape, bf16)

    def block(kb, masked):
        def rows(j, tot):
            p = jnp.exp(nt(qa_ref[j], kaug[kb]))
            if masked:
                p = jnp.where(causal(T, T), p, 0.0)
            ds = (p * nt(da_ref[j], vaug[kb])).astype(bf16)
            dqacc[j] += nn(ds, kv_ref[kb])
            dk = nn(qt[j], ds)
            dv = nn(dat[j], p.astype(bf16))
            return tot + jnp.concatenate([dk, dv], axis=0)

        tot = lax.fori_loop(0, J, rows, jnp.zeros((128, T), f32))
        gkv_ref[kb] = jnp.transpose(tot).astype(bf16)

    lax.fori_loop(0, me, lambda kb, c: (block(kb, False), c)[1], 0)
    block(me, True)
    for j in range(J):
        dq_ref[j] = dqacc[j].astype(bf16)


SCRATCH_D = [VM((NB, T, 128), bf16), VM((NB, T, 128), bf16), VM((J, H, T), bf16), VM((J, H, T), bf16), VM((J, T, 128), f32)]


def kernel_e(dq_ref, routes_ref, wq_ref, normed_ref, gkv_ref, kvw_ref, gn_ref, x_ref, gain_ref, gm_ref,
             dwq_ref, ing_ref, dkvw_ref, dgain_ref, cols_ref, dqs):
    cols_ref[...] = jnp.transpose(routes_ref[...])
    R = 128
    ln = lanes(R)
    half = expert_lane(R)

    def spread(i, _):
        r0 = pl.multiple_of(i * R, R)
        tiles = []
        for j in range(J):
            a = dq_ref[j, pl.ds(r0, R), :].astype(f32)
            a = jnp.where(ln < H, a, pltpu.roll(a, H, 1)) * 0.125
            tiles.append((jnp.broadcast_to(cols_ref[pl.ds(r0, R), j : j + 1], (R, 128)) - half, a))
        for p in range(PAIRS):
            acc = jnp.zeros((R, 128), f32)
            for rj, a in tiles:
                acc = jnp.where(rj == 2 * p, a, acc)
            dqs[pl.ds(r0, R), p * 128 : (p + 1) * 128] = acc.astype(bf16)
        return 0

    lax.fori_loop(0, T // R, spread, 0)
    nm = normed_ref[...]
    for c in range(3):
        dwq_ref[c * 512 : (c + 1) * 512, :] = tn(dqs[:, c * 512 : (c + 1) * 512], nm).astype(bf16)
    gkv = gkv_ref[...]
    dkvw_ref[...] = tn(nm, gkv)
    gn = gn_ref[...] + nn(dqs[...], wq_ref[...]) + nt(gkv, kvw_ref[...])
    x = x_ref[...].astype(f32)
    inv = lax.rsqrt(jnp.mean(x * x, axis=-1, keepdims=True) + eps)
    n = x * inv
    dgain_ref[...] = jnp.sum(gn * n, axis=0, keepdims=True)
    hh = gn * gain_ref[...]
    ing_ref[...] = (gm_ref[...] + inv * (hh - n * jnp.mean(hh * n, axis=-1, keepdims=True))).astype(bf16)


SCRATCH_E = [VM((T, J), i32), VM((T, EW), bf16)]


def call(body, outs, scratch, vmem=56 << 20, flops=0, **kw):
    n = 0
    def run(*args):
        return pl.pallas_call(
            body,
            out_shape=[jax.ShapeDtypeStruct(s, t) for s, t in outs],
            in_specs=[pl.BlockSpec(memory_space=VM)] * len(args),
            out_specs=[pl.BlockSpec(memory_space=VM)] * len(outs),
            scratch_shapes=scratch,
            compiler_params=pltpu.CompilerParams(vmem_limit_bytes=vmem, **kw),
            cost_estimate=pl.CostEstimate(flops=flops, bytes_accessed=1 << 22, transcendentals=0),
        )(*args)
    return run


def per_device(inputs, cotangent, norm_gain, ffn_gain, kv_weight, router_weight, query_weight, output_weight, up_weight,
               down_weight, routes, segment_ids):
    wq = jnp.swapaxes(query_weight, 1, 2).reshape(3 * H, D)
    wo = output_weight.reshape(3 * H, D)
    rw = router_weight.T
    rt = routes.T
    gain = norm_gain.reshape(1, D)
    fgain = ffn_gain.reshape(1, D)
    wq_all = lax.all_gather(wq, "expert", axis=0, tiled=True)
    wo_all = lax.all_gather(wo, "expert", axis=0, tiled=True)
    seg = lax.all_gather(jnp.stack([jnp.sum(segment_ids == 0), jnp.sum(segment_ids <= 1)]), "expert", axis=0)
    seg = jnp.sum(seg, axis=0)
    bnd = jnp.broadcast_to(jnp.concatenate([seg, jnp.zeros((6,), i32)])[:, None], (8, 128))
    normed, kv, gate = call(kernel_a, [((T, D), bf16), ((T, 128), bf16), ((T, E), f32)], [])(
        inputs, gain, kv_weight, rw, rt)
    kv_all = lax.all_gather(kv, "expert", axis=0)
    att, qa = call(kernel_b, [((J, T, 128), bf16), ((J, T, 128), bf16)], SCRATCH_B, flops=1 << 33)(normed, wq_all, rt, bnd, kv_all)
    out, da, gm, gn, dwo, dup, ddown, drw, dfg = call(
        kernel_c,
        [((T, D), bf16), ((J, T, 128), bf16), ((T, D), f32), ((T, D), f32), ((EW, D), bf16), ((D, FF), bf16), ((FF, D), bf16),
         ((E, D), f32), ((1, D), f32)],
        SCRATCH_C, flops=1 << 33)(inputs, cotangent, gate, rt, att, wo_all, up_weight, down_weight, fgain, normed, rw)
    both = ("dp", "expert")
    dup, ddown = lax.psum((dup, ddown), both)
    dwo = lax.psum(lax.psum_scatter(dwo, "expert", scatter_dimension=0, tiled=True), "dp")
    dq, gkv = call(kernel_d, [((J, T, 128), bf16), ((NB, T, 128), bf16)], SCRATCH_D, flops=1 << 35)(kv_all, bnd, qa, da)
    gkv = lax.psum_scatter(gkv, "expert", scatter_dimension=0, tiled=False)
    dwq, ing, dkvw, dgain = call(
        kernel_e, [((EW, D), bf16), ((T, D), bf16), ((D, 128), f32), ((1, D), f32)], SCRATCH_E)(
        dq, rt, wq_all, normed, gkv, kv_weight, gn, inputs, gain, gm)
    dwq = lax.psum(lax.psum_scatter(dwq, "expert", scatter_dimension=0, tiled=True), "dp")
    dkvw, drw, dgain, dfg = lax.psum((dkvw, drw, dgain, dfg), both)
    return (out, ing, dgain.reshape(D), dfg.reshape(D), dkvw, drw.T,
            jnp.swapaxes(dwq.astype(f32).reshape(3, H, D), 1, 2), dwo.astype(f32).reshape(3, H, D),
            dup.astype(f32), ddown.astype(f32))


def solution(mesh):
    both = P(("dp", "expert"), None)
    ex = P("expert", None, None)
    return jax.shard_map(
        per_device, mesh=mesh,
        in_specs=(both, both, P(), P(), P(), P(), ex, ex, P(), P(), both, P(("dp", "expert"))),
        out_specs=(both, both, P(), P(), P(), P(), ex, ex, P(), P()),
        check_vma=False)
```

```python
import functools
import jax
import jax.numpy as jnp
from jax import lax
from jax.experimental import pallas as pl
from jax.experimental.pallas import tpu as pltpu
from jax.sharding import PartitionSpec as P

f32, bf16, i32 = jnp.float32, jnp.bfloat16, jnp.int32
T, D, H, J, E, FF, NB = 384, 512, 64, 8, 24, 2048, 8
EW = E * H
PAIRS = E // 2
HALF_J = 4
ROWS = HALF_J * T
eps = 1e-06
NEG = -1e30
VM = pltpu.VMEM


def nn(a, b):
    return lax.dot_general(a, b, (((1,), (0,)), ((), ())), preferred_element_type=f32)


def nt(a, b):
    return lax.dot_general(a, b, (((1,), (1,)), ((), ())), preferred_element_type=f32)


def tn(a, b):
    return lax.dot_general(a, b, (((0,), (0,)), ((), ())), preferred_element_type=f32)


def lanes(rows):
    return lax.broadcasted_iota(i32, (rows, 128), 1)


def split3(v):
    a = v.astype(bf16).astype(f32)
    b = (v - a).astype(bf16).astype(f32)
    c = (v - a - b).astype(bf16).astype(f32)
    return a, b, c


def causal(rows, cols):
    return lax.broadcasted_iota(i32, (rows, cols), 1) <= lax.broadcasted_iota(i32, (rows, cols), 0)


def segment_of(pos, bounds):
    return (pos >= bounds[0]).astype(i32) + (pos >= bounds[1]).astype(i32)


def expert_lane(rows):
    return (lanes(rows) >= H).astype(i32)


MESH = pl.DeviceIdType.MESH
LINES = [(a, k) for a in "xyz" for k in (1, 2, 3)]
ALL_PEERS = [("c", 0)] + LINES


class Place:
    def __init__(self):
        dp, ex = lax.axis_index("dp"), lax.axis_index("expert")
        self.ex = ex
        self.at = {"x": dp // 4, "y": dp % 4, "z": ex // 2, "c": ex % 2}
        self.peers = {("c", 0): self.device(c=1 - self.at["c"])}
        for axis, k in LINES:
            self.peers[axis, k] = self.device(**{axis: (self.at[axis] + k) % 4})

    def device(self, **moved):
        at = {**self.at, **moved}
        return (at["x"] * 4 + at["y"], at["z"] * 2 + at["c"])

    def enter(self, peers):
        bar = pltpu.get_barrier_semaphore()
        for p in peers:
            pl.semaphore_signal(bar, inc=1, device_id=self.peers[p], device_id_type=MESH)
        pl.semaphore_wait(bar, len(peers))


class Copies:
    def __init__(self, place, send, recv):
        self.place, self.send, self.recv, self.made = place, send, recv, []

    def add(self, src, dst, peer):
        self.made.append((src, dst, peer))
        return len(self.made) - 1

    def get(self, i):
        src, dst, peer = self.made[i]
        return pltpu.make_async_remote_copy(src_ref=src(), dst_ref=dst(), send_sem=self.send.at[i], recv_sem=self.recv.at[i],
                                            device_id=self.place.peers[peer], device_id_type=MESH)

    def start(self, ids):
        for i in ids:
            self.get(i).start()

    def arrived(self, ids):
        for i in ids:
            self.get(i).wait_recv()

    def sent(self, ids):
        for i in ids:
            self.get(i).wait_send()

    def drain(self):
        self.sent(range(len(self.made)))


class Scatter:
    def __init__(self, copies, src, total, r, u0, u1, order):
        self.cp, self.src, self.total, self.r = copies, src, total, r
        self.u0, self.u1 = u0, u1
        at = copies.place.at
        self.c, self.m = at["c"], [at[a] for a in order]
        us = pl.ds(u0, u1 - u0)
        self.ids = [[copies.add(lambda: src.at[us, 1 - self.c], lambda: r[0].at[us], ("c", 0))]]
        for level in (1, 2, 3):
            def piece(k, level=level):
                pre = tuple(self.m[: level - 1])
                return total.at[(us,) + pre + ((self.m[level - 1] + k) % 4,)]
            self.ids.append([
                copies.add(functools.partial(piece, k), lambda k=k, level=level: r[level].at[us, k - 1], (order[level - 1], k))
                for k in (1, 2, 3)])

    def start(self, level):
        self.cp.start(self.ids[level])

    def finish(self, level):
        self.cp.arrived(self.ids[level])
        for u in range(self.u0, self.u1):
            if level == 0:
                for a in range(4):
                    v = self.src[u, self.c, a].astype(f32) + self.r[0][u, a].astype(f32)
                    self.total[u, a] = v.astype(bf16)
                continue
            at = (u,) + tuple(self.m[:level])
            v = self.total[at].astype(f32)
            for k in range(3):
                v = v + self.r[level][u, k].astype(f32)
            self.total[at] = v.astype(bf16)

    def result(self, u):
        return self.total[(u,) + tuple(self.m)]


class Spread:
    def __init__(self, copies, out, u0, u1, order):
        self.cp, self.out = copies, out
        at = copies.place.at
        self.c, self.m = at["c"], [at[a] for a in order]
        us = pl.ds(u0, u1 - u0)
        self.ids = []
        for level in range(4):
            ref = lambda level=level: out.at[(us, self.c) + tuple(self.m[:level])]
            peers = [("c", 0)] if level == 0 else [(order[level - 1], k) for k in (1, 2, 3)]
            self.ids.append([copies.add(ref, ref, p) for p in peers])

    def put(self, u, value):
        self.out[(u, self.c) + tuple(self.m)] = value

    def start(self, level):
        self.cp.start(self.ids[level])

    def finish(self, level):
        self.cp.arrived(self.ids[level])


class SpreadPlane:
    def __init__(self, copies, out, u0, u1):
        self.cp, self.out = copies, out
        self.x, self.y = copies.place.at["x"], copies.place.at["y"]
        us = pl.ds(u0, u1 - u0)
        one = lambda: out.at[us, self.x, self.y]
        row = lambda: out.at[us, self.x]
        self.ids = {"y": [copies.add(one, one, ("y", k)) for k in (1, 2, 3)],
                    "x": [copies.add(row, row, ("x", k)) for k in (1, 2, 3)]}

    def put(self, u, value):
        self.out[u, self.x, self.y] = value

    def start(self, axis):
        self.cp.start(self.ids[axis])

    def finish(self, axis):
        self.cp.arrived(self.ids[axis])


class SmallSum:
    def __init__(self, copies, src, half, r0, r1, by, bz, out):
        self.cp, self.src, self.half, self.r0, self.r1, self.by, self.bz, self.out = copies, src, half, r0, r1, by, bz, out
        at = copies.place.at
        self.c, self.x, self.y, self.z = at["c"], at["x"], at["y"], at["z"]
        own_half = lambda: out.at[self.c]
        own = lambda: out.at[self.c, self.x]
        self.ids = [
            [copies.add(lambda: src.at[1 - self.c], lambda: r0, ("c", 0))],
            [copies.add(lambda k=k: half.at[(self.x + k) % 4], lambda k=k: r1.at[k - 1], ("x", k)) for k in (1, 2, 3)],
            [copies.add(lambda: by.at[self.y], lambda: by.at[self.y], ("y", k)) for k in (1, 2, 3)],
            [copies.add(lambda: bz.at[self.z], lambda: bz.at[self.z], ("z", k)) for k in (1, 2, 3)],
            [copies.add(own, own, ("x", k)) for k in (1, 2, 3)],
            [copies.add(own_half, own_half, ("c", 0))],
        ]

    def step(self, i):
        if i:
            self.cp.arrived(self.ids[i - 1])
        if i == 1:
            for a in range(4):
                self.half[a] = (self.src[self.c, a].astype(f32) + self.r0[a].astype(f32)).astype(bf16)
        if i == 2:
            v = self.half[self.x].astype(f32)
            for k in range(3):
                v = v + self.r1[k].astype(f32)
            self.by[self.y] = v.astype(bf16)
        if i in (3, 4):
            b = self.by if i == 3 else self.bz
            v = (b[0].astype(f32) + b[1].astype(f32) + b[2].astype(f32) + b[3].astype(f32)).astype(bf16)
            if i == 3:
                self.bz[self.z] = v
            else:
                self.out[self.c, self.x] = v
        if i < 6:
            self.cp.start(self.ids[i])


ORDERS = ["xyz", "yzx", "zxy"]
BATCHES = [(0, 4), (4, 8), (8, 11)]
ALL_BATCHES = [(0, 3), (3, 6), (6, 8)]
UP_UNIT, DOWN_UNIT, WO_UNIT = [0, 1, 2, 4], [5, 6, 8, 9], [3, 7, 10]
UNITS = 11
STEPS = [(u, i) for i, u in enumerate(sorted(UP_UNIT + DOWN_UNIT))]


def expert_row(ex, piece, order):
    at = {"x": piece // 4, "y": piece % 4, "z": ex // 2}
    r = ex % 2
    for a in order:
        r = r * 4 + at[a]
    return r * 16


def store_expert(ref, units, ex0, value):
    low = value.astype(bf16)
    for o in range(2):
        for row in range(0, 768, 16):
            v, piece = row // 256, (row % 256) // 16
            ct, r = row // 192, row % 192
            base = expert_row(ex0 + o, piece, ORDERS[v])
            ref[units[v], base : base + 16, :] = low[o * 192 + r : o * 192 + r + 16, ct * 128 : (ct + 1) * 128]


KVR = T + 16


class Gather:
    def __init__(self, copies, out):
        self.cp, self.out = copies, out
        at, ex = copies.place.at, copies.place.ex
        own = lambda: out.at[ex]
        from_z = lambda k: out.at[((at["z"] - k + 4) % 4) * 2 + at["c"]]
        self.line = [copies.add(own, own, ("z", k)) for k in (1, 2, 3)]
        self.core = [copies.add(functools.partial(from_z, k), functools.partial(from_z, k), ("c", 0)) for k in (0, 1, 2, 3)]

    def start(self):
        self.cp.start(self.line)
        self.cp.start(self.core[:1])

    def forward(self):
        for k in range(3):
            self.cp.arrived(self.line[k : k + 1])
            self.cp.start(self.core[k + 1 : k + 2])

    def finish(self):
        self.cp.arrived(self.core)


def bounds_of(kv_ref):
    n0 = n1 = 0.0
    for b in range(NB):
        tail = kv_ref[b, T:KVR, :].astype(f32)
        n0 = n0 + 16.0 * tail[0:1] + tail[1:2]
        n1 = n1 + 16.0 * tail[2:3] + tail[3:4]
    return n0, n1


def prepare_keys(kv_ref, bounds, kaug, vaug):
    ln = lanes(T)
    for b in range(NB):
        kv = kv_ref[b, 0:T, :].astype(f32)
        pos = (lax.broadcasted_iota(i32, (T, 128), 0) + b * T).astype(f32)
        seg = segment_of(pos, bounds)
        feat = jnp.where((ln < H + 3) & (seg != ln - H), NEG, 0.0)
        feat = jnp.where((ln >= H + 3) & (ln < H + 6), 1.0, feat)
        kaug[b] = jnp.where(ln < H, kv, feat).astype(bf16)
        one = jnp.where(ln < H + 3, 1.0, 0.0)
        vaug[b] = jnp.where(ln < H, pltpu.roll(kv, H, 1), one).astype(bf16)


def project_queries(normed_ref, wq_ref, qall):
    normed = normed_ref[...]
    for c in range(4):
        w = wq_ref[2 * c : 2 * c + 2].reshape(2 * 3 * H, D)
        qall[:, c * 384 : (c + 1) * 384] = nt(normed, w) * 0.125


def pick_queries(cols_ref, bounds, me, qall, qa):
    R = 128
    ln = lanes(R)
    half = expert_lane(R)

    def chunk(i, _):
        r0 = pl.multiple_of(i * R, R)
        pos = (lax.broadcasted_iota(i32, (R, 128), 0) + me * T + r0).astype(f32)
        seg = segment_of(pos, bounds)
        feat = jnp.where((ln >= H) & (seg == ln - H), 1.0, 0.0)
        for j in range(J):
            rj = jnp.broadcast_to(cols_ref[pl.ds(r0, R), j : j + 1], (R, 128)) - half
            acc = jnp.zeros((R, 128), f32)
            for p in range(PAIRS):
                acc = jnp.where(rj == 2 * p, qall[pl.ds(r0, R), p * 128 : (p + 1) * 128], acc)
            acc = acc + pltpu.roll(acc, H, 1)
            qa[j, pl.ds(r0, R), :] = jnp.where(ln < H, acc, feat).astype(bf16)
        return 0

    lax.fori_loop(0, T // R, chunk, 0)

def attend_set(me, s, qa, kaug, vaug, att_ref, sbuf, mbuf, acc):
    mbuf[...] = jnp.full(mbuf.shape, NEG, f32)
    acc[...] = jnp.zeros(acc.shape, f32)

    def score(kb, masked):
        for j in range(HALF_J):
            sc = nt(qa[s * HALF_J + j], kaug[kb])
            if masked:
                sc = jnp.where(causal(T, T), sc, NEG)
            sbuf[kb, j] = sc
            m = jnp.maximum(sc[:, 0:128], jnp.maximum(sc[:, 128:256], sc[:, 256:384]))
            mbuf[j] = jnp.maximum(mbuf[j], m)

    lax.fori_loop(0, me, lambda kb, c: (score(kb, False), c)[1], 0)
    score(me, True)
    for j in range(HALF_J):
        mbuf[j] = jnp.broadcast_to(jnp.max(mbuf[j], axis=-1, keepdims=True), (T, 128))

    def weigh(kb, c):
        for j in range(HALF_J):
            m = mbuf[j]
            p = jnp.exp(sbuf[kb, j] - jnp.concatenate([m, m, m], axis=1)).astype(bf16)
            acc[j] += nn(p, vaug[kb])
        return c

    lax.fori_loop(0, me + 1, weigh, 0)
    ln = lanes(T)
    for j in range(HALF_J):
        a = acc[j]
        tot = jnp.broadcast_to(a[:, H : H + 1], (T, 128))
        att_ref[s * HALF_J + j] = (a / tot).astype(bf16)
        l1, l2, l3 = split3(-(mbuf[j] + jnp.log(tot)))
        lse = jnp.where(ln == H + 3, l1, jnp.where(ln == H + 4, l2, l3))
        old = qa[s * HALF_J + j].astype(f32)
        qa[s * HALF_J + j] = jnp.where((ln >= H + 3) & (ln < H + 6), lse, old).astype(bf16)


def kernel_ab(x_ref, gain_ref, kvw_ref, rw_ref, routes_ref, seg_ref, wq_in, wo_in,
              normed_ref, gate_ref, kv_ref, wq_ref, wo_ref, att_ref, qa_ref,
              qall, cols_ref, kaug, vaug, sbuf, mbuf, acc, send, recv):
    place = Place()
    me = place.ex
    copies = Copies(place, send, recv)
    gq, gk, go = Gather(copies, wq_ref), Gather(copies, kv_ref), Gather(copies, wo_ref)
    wq_ref[me] = wq_in[...]
    wo_ref[me] = wo_in[...]
    place.enter([("c", 0)] + [("z", k) for k in (1, 2, 3)])
    gq.start()
    x = x_ref[...].astype(f32)
    inv = lax.rsqrt(jnp.mean(x * x, axis=-1, keepdims=True) + eps)
    normed = (x * inv * gain_ref[...]).astype(bf16)
    normed_ref[...] = normed
    kv_ref[me, 0:T, :] = nn(normed, kvw_ref[...]).astype(bf16)
    seg = seg_ref[...]
    row = lax.broadcasted_iota(i32, (16, 128), 0)
    tail = jnp.zeros((16, 128), f32)
    for s in range(2):
        n = jnp.sum(jnp.sum((seg <= s).astype(f32), axis=0, keepdims=True), axis=1, keepdims=True)
        n = jnp.broadcast_to(n, (16, 128))
        hi = jnp.floor(n * 0.0625)
        tail = jnp.where(row == 2 * s, hi, jnp.where(row == 2 * s + 1, n - 16.0 * hi, tail))
    kv_ref[me, T:KVR, :] = tail.astype(bf16)
    gk.start()
    cols_ref[...] = jnp.transpose(routes_ref[...])
    cols = cols_ref[...]
    logits = nt(normed, rw_ref[...])
    eid = lax.broadcasted_iota(i32, (T, E), 1)
    chosen = cols[:, 0:1] == eid
    for j in range(1, J):
        chosen = chosen | (cols[:, j : j + 1] == eid)
    logits = jnp.where(chosen, logits, NEG)
    top = jnp.max(logits, axis=-1, keepdims=True)
    e = jnp.where(chosen, jnp.exp(logits - top), 0.0)
    gate_ref[...] = e / jnp.sum(e, axis=-1, keepdims=True)
    gq.forward()
    go.start()
    gk.forward()
    gq.finish()
    project_queries(normed_ref, wq_ref, qall)
    gk.finish()
    bounds = bounds_of(kv_ref)
    prepare_keys(kv_ref, bounds, kaug, vaug)
    pick_queries(cols_ref, bounds, me, qall, qa_ref)
    go.forward()
    lax.fori_loop(0, 2, lambda s, c: (attend_set(me, s, qa_ref, kaug, vaug, att_ref, sbuf, mbuf, acc), c)[1], 0)
    go.finish()
    copies.drain()


SCRATCH_AB = [VM((T, EW), f32), VM((T, J), i32), VM((NB, T, 128), bf16), VM((NB, T, 128), bf16),
              VM((NB, HALF_J, T, T), f32), VM((HALF_J, T, 128), f32), VM((HALF_J, T, 128), f32),
              pltpu.SemaphoreType.DMA((21,)), pltpu.SemaphoreType.DMA((21,))]


def kernel_c(x_ref, cot_ref, gate_ref, routes_ref, att_ref, wo_ref, up_ref, down_ref, fgain_ref, normed_ref, rw_ref,
             out_ref, da_ref, gm_ref, gn_ref, big_ref, drw_ref, dfg_ref,
             cols_ref, gcol, ga, gall, act, gmlow, gg):
    cols_ref[...] = jnp.transpose(routes_ref[...])
    R = 128
    ln = lanes(R)
    half = expert_lane(R)
    eidr = lax.broadcasted_iota(i32, (R, E), 1)

    def spread(i, _):
        r0 = pl.multiple_of(i * R, R)
        g = gate_ref[pl.ds(r0, R), :]
        tiles = []
        for j in range(J):
            rj = cols_ref[pl.ds(r0, R), j : j + 1]
            gj = jnp.sum(jnp.where(rj == eidr, g, 0.0), axis=-1, keepdims=True)
            gcol[j, pl.ds(r0, R), :] = jnp.broadcast_to(gj, (R, 128))
            a = att_ref[j, pl.ds(r0, R), :].astype(f32)
            a = jnp.where(ln < H, a, pltpu.roll(a, H, 1)) * gj
            tiles.append((jnp.broadcast_to(rj, (R, 128)) - half, a))
        for p in range(PAIRS):
            acc = jnp.zeros((R, 128), f32)
            for rj, a in tiles:
                acc = jnp.where(rj == 2 * p, a, acc)
            ga[pl.ds(r0, R), p * 128 : (p + 1) * 128] = acc.astype(bf16)
        return 0

    lax.fori_loop(0, T // R, spread, 0)
    x = x_ref[...].astype(f32)
    mixed = x + nn(ga[...], wo_ref[...])
    inv = lax.rsqrt(jnp.mean(mixed * mixed, axis=-1, keepdims=True) + eps)
    n = mixed * inv
    fgain = fgain_ref[...]
    second = (n * fgain).astype(bf16)
    cot = cot_ref[...]
    C = 512
    out = mixed
    gsec = jnp.zeros((T, D), f32)
    for c in range(FF // C):
        cs = slice(c * C, (c + 1) * C)
        v = nn(second, up_ref[:, cs])
        v2 = v * v
        th = jnp.tanh(0.7978845608028654 * (v + 0.044715 * v * v2))
        a = (0.5 * v * (1.0 + th)).astype(bf16)
        act[:, cs] = a
        dth = 0.5 * (1.0 + th) + 0.5 * v * (1.0 - th * th) * (0.7978845608028654 * (1.0 + 0.134145 * v2))
        gh = (nt(cot, down_ref[cs, :]) * dth).astype(bf16)
        out = out + nn(a, down_ref[cs, :])
        gsec = gsec + nt(gh, up_ref[:, cs])
        gdown = tn(a, cot).astype(bf16)
        gup = tn(second, gh).astype(bf16)
        for t in range(4):
            big_ref[DOWN_UNIT[t], cs, :] = gdown[:, t * 128 : (t + 1) * 128]
            big_ref[UP_UNIT[c], t * 512 : (t + 1) * 512, :] = gup[:, t * 128 : (t + 1) * 128]
    out_ref[...] = out.astype(bf16)
    dfg_ref[...] = jnp.sum(gsec * n, axis=0, keepdims=True)
    hh = gsec * fgain
    gm = cot.astype(f32) + inv * (hh - n * jnp.mean(hh * n, axis=-1, keepdims=True))
    gm_ref[...] = gm
    gml = gm.astype(bf16)
    gmlow[...] = gml
    for c in range(3):
        gall[:, c * 512 : (c + 1) * 512] = nt(gml, wo_ref[c * 512 : (c + 1) * 512, :])

    def grads(i, _):
        r0 = pl.multiple_of(i * R, R)
        inner = jnp.zeros((R, 1), f32)
        ggs = []
        for j in range(J):
            rj = cols_ref[pl.ds(r0, R), j : j + 1]
            rb = jnp.broadcast_to(rj, (R, 128)) - half
            acc = jnp.zeros((R, 128), f32)
            for p in range(PAIRS):
                acc = jnp.where(rb == 2 * p, gall[pl.ds(r0, R), p * 128 : (p + 1) * 128], acc)
            acc = acc + pltpu.roll(acc, H, 1)
            a = att_ref[j, pl.ds(r0, R), :].astype(f32)
            dot = jnp.sum(jnp.where(ln < H, acc * a, 0.0), axis=-1, keepdims=True)
            gj = gcol[j, pl.ds(r0, R), :]
            g1 = gj[:, 0:1]
            inner = inner + g1 * dot
            ggs.append((rj, g1, dot))
            da = acc * gj
            d1, d2, d3 = split3(-jnp.broadcast_to(dot * g1, (R, 128)))
            ft = jnp.where(ln == H, d1, jnp.where(ln == H + 1, d2, jnp.where(ln == H + 2, d3, 0.0)))
            da_ref[j, pl.ds(r0, R), :] = jnp.where(ln < H, da, ft).astype(bf16)
        gl = jnp.zeros((R, E), f32)
        for rj, g1, dot in ggs:
            gl = jnp.where(rj == eidr, g1 * (dot - inner), gl)
        gg[pl.ds(r0, R), :] = gl
        return 0

    lax.fori_loop(0, T // R, grads, 0)
    gl = gg[...]
    hi = gl.astype(bf16)
    lo = (gl - hi.astype(f32)).astype(bf16)
    rw = rw_ref[...]
    gn_ref[...] = nn(hi, rw) + nn(lo, rw)
    nm = normed_ref[...]
    drw_ref[...] = tn(hi, nm) + tn(lo, nm)
    for c in range(4):
        store_expert(big_ref, WO_UNIT, 2 * c, tn(ga[:, c * 384 : (c + 1) * 384], gmlow[...]))


SCRATCH_C = [VM((T, J), i32), VM((J, T, 128), f32), VM((T, EW), bf16), VM((T, EW), f32),
             VM((T, FF), bf16), VM((T, D), bf16), VM((T, E), f32)]


def kernel_d(kv_ref, qa_ref, da_ref, big_ref, dq_ref, gkv_ref, red_ref,
             kaug, vaug, qt, dat, dqacc, gsend, grecv, total, r0, r1, r2, r3, send, recv, ksend, krecv):
    place = Place()
    me = place.ex
    dp = lax.axis_index("dp")
    copies = Copies(place, send, recv)
    sums = [Scatter(copies, big_ref, total, (r0, r1, r2, r3), u0, u1, o) for (u0, u1), o in zip(BATCHES, ORDERS)]
    bar = pltpu.get_barrier_semaphore()
    for p in ALL_PEERS:
        pl.semaphore_signal(bar, inc=1, device_id=place.peers[p], device_id_type=MESH)
    for k in range(1, NB):
        pl.semaphore_signal(bar, inc=1, device_id=(dp, (me + k) % NB), device_id_type=MESH)
    pl.semaphore_wait(bar, len(ALL_PEERS) + NB - 1)
    for s in sums:
        s.start(0)
    prepare_keys(kv_ref, bounds_of(kv_ref), kaug, vaug)
    for j in range(J):
        qt[j] = jnp.transpose(qa_ref[j].astype(f32))[:H].astype(bf16)
        dat[j] = jnp.transpose(da_ref[j].astype(f32))[:H].astype(bf16)
    dqacc[...] = jnp.zeros(dqacc.shape, f32)

    def block(kb, masked):
        def rows(j, tot):
            p = jnp.exp(nt(qa_ref[j], kaug[kb]))
            if masked:
                p = jnp.where(causal(T, T), p, 0.0)
            ds = (p * nt(da_ref[j], vaug[kb])).astype(bf16)
            dqacc[j] += nn(ds, kv_ref[kb, 0:T, :])
            dk = nn(qt[j], ds)
            dv = nn(dat[j], p.astype(bf16))
            return tot + jnp.concatenate([dk, dv], axis=0)

        return jnp.transpose(lax.fori_loop(0, J, rows, jnp.zeros((128, T), f32)))

    def to_owner(kb):
        return pltpu.make_async_remote_copy(src_ref=gsend.at[kb], dst_ref=grecv.at[me], send_sem=ksend.at[kb],
                                            recv_sem=krecv.at[me], device_id=(dp, kb), device_id_type=MESH)

    def from_device(b):
        return pltpu.make_async_remote_copy(src_ref=gsend.at[b], dst_ref=grecv.at[b], send_sem=ksend.at[b],
                                            recv_sem=krecv.at[b], device_id=(dp, b), device_id_type=MESH)

    def step(i, carry):
        @pl.when(i < me)
        def _():
            gsend[i] = block(i, False).astype(bf16)
            to_owner(i).start()

        for at, level in ((1, 0), (4, 1), (5, 2), (6, 3)):
            @pl.when(i == at)
            def _(level=level):
                for s in sums:
                    s.finish(level)
                    if level < 3:
                        s.start(level + 1)

        return carry

    lax.fori_loop(0, NB - 1, step, 0)
    own = block(me, True)
    for j in range(J):
        dq_ref[j] = dqacc[j].astype(bf16)
    for s in sums:
        for u in range(s.u0, s.u1):
            red_ref[u] = s.result(u)
    gkv_ref[...] = own
    for b in range(1, NB):
        @pl.when(b > me)
        def _(b=b):
            from_device(b).wait_recv()
            gkv_ref[...] += grecv[b].astype(f32)
    for b in range(NB - 1):
        @pl.when(b < me)
        def _(b=b):
            to_owner(b).wait_send()
    copies.drain()


def dma_sems(n):
    return [pltpu.SemaphoreType.DMA((n,)), pltpu.SemaphoreType.DMA((n,))]


SCRATCH_D = [VM((NB, T, 128), bf16), VM((NB, T, 128), bf16), VM((J, H, T), bf16), VM((J, H, T), bf16), VM((J, T, 128), f32),
             VM((NB, T, 128), bf16), VM((NB, T, 128), bf16),
             VM((UNITS, 4, 4, 4, 16, 128), bf16), VM((UNITS, 4, 4, 4, 16, 128), bf16), VM((UNITS, 3, 4, 4, 16, 128), bf16),
             VM((UNITS, 3, 4, 16, 128), bf16), VM((UNITS, 3, 16, 128), bf16)] + dma_sems(30) + dma_sems(NB)


SMALL = 640


def kernel_e(dq_ref, routes_ref, wq_ref, normed_ref, gkv_ref, kvw_ref, gn_ref, x_ref, gain_ref, gm_ref, drw_ref, dfg_ref, red_ref,
             ing_ref, all_ref, wo_ref, dwq_ref, small_ref,
             cols_ref, dqs, big, total, r0, r1, r2, r3, ssrc, shalf, s0, s1, sy, sz, send, recv):
    place = Place()
    copies = Copies(place, send, recv)
    spreads = [Spread(copies, all_ref, u0, u1, o) for (u0, u1), o in zip(ALL_BATCHES, ORDERS)]
    plane_o = SpreadPlane(copies, wo_ref, 0, 3)
    plane_q = SpreadPlane(copies, dwq_ref, 0, 3)
    big7 = big.reshape(3, 2, 4, 4, 4, 16, 128)
    sums = [Scatter(copies, big7, total, (r0, r1, r2, r3), u, u + 1, o) for u, o in enumerate(ORDERS)]
    small = SmallSum(copies, ssrc, shalf, s0, s1, sy, sz, small_ref)
    for (u0, u1), s in zip(ALL_BATCHES, spreads):
        for u in range(u0, u1):
            s.put(u, red_ref[sorted(UP_UNIT + DOWN_UNIT)[u]])
    for v in range(3):
        plane_o.put(v, red_ref[WO_UNIT[v]])
    place.enter(ALL_PEERS)
    for s in spreads:
        s.start(3)
    plane_o.start("y")
    cols_ref[...] = jnp.transpose(routes_ref[...])
    R = 128
    ln = lanes(R)
    half = expert_lane(R)

    def spread(i, _):
        r_ = pl.multiple_of(i * R, R)
        tiles = []
        for j in range(J):
            a = dq_ref[j, pl.ds(r_, R), :].astype(f32)
            a = jnp.where(ln < H, a, pltpu.roll(a, H, 1)) * 0.125
            tiles.append((jnp.broadcast_to(cols_ref[pl.ds(r_, R), j : j + 1], (R, 128)) - half, a))
        for p in range(PAIRS):
            acc = jnp.zeros((R, 128), f32)
            for rj, a in tiles:
                acc = jnp.where(rj == 2 * p, a, acc)
            dqs[pl.ds(r_, R), p * 128 : (p + 1) * 128] = acc.astype(bf16)
        return 0

    lax.fori_loop(0, T // R, spread, 0)
    nm = normed_ref[...]
    for c in range(4):
        store_expert(big, [0, 1, 2], 2 * c, tn(dqs[:, c * 384 : (c + 1) * 384], nm))
    for s in sums:
        s.start(0)
    for s in spreads:
        s.finish(3)
        s.start(2)
    plane_o.finish("y")
    plane_o.start("x")
    gkv = gkv_ref[...].astype(bf16)
    dkvw = tn(nm, gkv).astype(bf16)
    gn = gn_ref[...] + nn(dqs[...], wq_ref[...]) + nt(gkv, kvw_ref[...])
    x = x_ref[...].astype(f32)
    inv = lax.rsqrt(jnp.mean(x * x, axis=-1, keepdims=True) + eps)
    n = x * inv
    dgain = jnp.sum(gn * n, axis=0, keepdims=True)
    drw = drw_ref[...]
    dfg = dfg_ref[...]
    rows = [dkvw.astype(f32)] + [drw[:, t * 128 : (t + 1) * 128] for t in range(4)]
    rows += [v[:, t * 128 : (t + 1) * 128] for v in (dgain, dfg) for t in range(4)] + [jnp.zeros((SMALL - 616, 128), f32)]
    ssrc[...] = jnp.concatenate(rows, axis=0).astype(bf16).reshape(2, 4, SMALL // 8, 128)
    small.step(0)
    for s in sums:
        s.finish(0)
        s.start(1)
    small.step(1)
    for s in spreads:
        s.finish(2)
        s.start(1)
    plane_o.finish("x")
    hh = gn * gain_ref[...]
    ing_ref[...] = (gm_ref[...] + inv * (hh - n * jnp.mean(hh * n, axis=-1, keepdims=True))).astype(bf16)
    small.step(2)
    for level in (1, 2):
        for s in sums:
            s.finish(level)
            s.start(level + 1)
        small.step(level + 2)
    for s in sums:
        s.finish(3)
    for v in range(3):
        plane_q.put(v, sums[v].result(v))
    plane_q.start("y")
    for s in spreads:
        s.finish(1)
        s.start(0)
    small.step(5)
    plane_q.finish("y")
    plane_q.start("x")
    small.step(6)
    plane_q.finish("x")
    for s in spreads:
        s.finish(0)
    copies.drain()


SCRATCH_E = [VM((T, J), i32), VM((T, EW), bf16), VM((3, 2048, 128), bf16),
             VM((3, 4, 4, 4, 16, 128), bf16), VM((3, 4, 4, 4, 16, 128), bf16), VM((3, 3, 4, 4, 16, 128), bf16),
             VM((3, 3, 4, 16, 128), bf16), VM((3, 3, 16, 128), bf16),
             VM((2, 4, SMALL // 8, 128), bf16), VM((4, SMALL // 8, 128), bf16), VM((4, SMALL // 8, 128), bf16),
             VM((3, SMALL // 8, 128), bf16), VM((4, SMALL // 8, 128), bf16), VM((4, SMALL // 8, 128), bf16)] + dma_sems(86)


def call(body, outs, scratch, vmem=56 << 20, flops=0, **kw):
    n = 0
    def run(*args):
        return pl.pallas_call(
            body,
            out_shape=[jax.ShapeDtypeStruct(s, t) for s, t in outs],
            in_specs=[pl.BlockSpec(memory_space=VM)] * len(args),
            out_specs=[pl.BlockSpec(memory_space=VM)] * len(outs),
            scratch_shapes=scratch,
            compiler_params=pltpu.CompilerParams(vmem_limit_bytes=vmem, **kw),
            cost_estimate=pl.CostEstimate(flops=flops, bytes_accessed=1 << 22, transcendentals=0),
        )(*args)
    return run


def columns(blocks, rows):
    return jnp.swapaxes(blocks, 0, 1).reshape(rows, -1).astype(f32)


def per_device(inputs, cotangent, norm_gain, ffn_gain, kv_weight, router_weight, query_weight, output_weight, up_weight,
               down_weight, routes, segment_ids):
    wq = jnp.swapaxes(query_weight, 1, 2).reshape(3 * H, D)
    wo = output_weight.reshape(3 * H, D)
    rw = router_weight.T
    rt = routes.T
    gain = norm_gain.reshape(1, D)
    fgain = ffn_gain.reshape(1, D)
    normed, gate, kv_all, wq_all, wo_all, att, qa = call(
        kernel_ab,
        [((T, D), bf16), ((T, E), f32), ((NB, KVR, 128), bf16), ((NB, 3 * H, D), bf16), ((NB, 3 * H, D), bf16),
         ((J, T, 128), bf16), ((J, T, 128), bf16)],
        SCRATCH_AB, flops=1 << 33, collective_id=1, has_side_effects=True)(
        inputs, gain, kv_weight, rw, rt, segment_ids.reshape(3, 128), wq, wo)
    wq_all, wo_all = wq_all.reshape(EW, D), wo_all.reshape(EW, D)
    out, da, gm, gn, big, drw, dfg = call(
        kernel_c,
        [((T, D), bf16), ((J, T, 128), bf16), ((T, D), f32), ((T, D), f32), ((UNITS, 2048, 128), bf16), ((E, D), f32), ((1, D), f32)],
        SCRATCH_C, flops=1 << 33)(inputs, cotangent, gate, rt, att, wo_all, up_weight, down_weight, fgain, normed, rw)
    dq, gkv, red = call(
        kernel_d, [((J, T, 128), bf16), ((T, 128), f32), ((UNITS, 16, 128), bf16)],
        SCRATCH_D, flops=1 << 35, collective_id=2, has_side_effects=True)(
        kv_all, qa, da, big.reshape(UNITS, 2, 4, 4, 4, 16, 128))
    ing, shared, dwo, dwq, small = call(
        kernel_e,
        [((T, D), bf16), ((8, 2, 4, 4, 4, 16, 128), bf16), ((3, 4, 4, 16, 128), bf16), ((3, 4, 4, 16, 128), bf16),
         ((2, 4, SMALL // 8, 128), bf16)],
        SCRATCH_E, flops=1 << 32, collective_id=3, has_side_effects=True)(
        dq, rt, wq_all, normed, gkv, kv_weight, gn, inputs, gain, gm, drw, dfg, red)
    shared = shared.reshape(8, 2048, 128)
    slot = {u: i for i, u in enumerate(sorted(UP_UNIT + DOWN_UNIT))}
    dup = columns(jnp.stack([shared[slot[u]] for u in UP_UNIT]).reshape(16, 512, 128), D)
    ddown = columns(jnp.stack([shared[slot[u]] for u in DOWN_UNIT]), FF)
    dwo = columns(dwo.reshape(4, 3 * H, 128), 3 * H).reshape(3, H, D)
    dwq = columns(dwq.reshape(4, 3 * H, 128), 3 * H).reshape(3, H, D)
    small = small.reshape(SMALL, 128).astype(f32)
    drw = columns(small[512:608].reshape(4, E, 128), E)
    return (out, ing, small[608:612].reshape(D), small[612:616].reshape(D), small[:512], drw.T,
            jnp.swapaxes(dwq, 1, 2), dwo, dup, ddown)


def solution(mesh):
    both = P(("dp", "expert"), None)
    ex = P("expert", None, None)
    return jax.shard_map(
        per_device, mesh=mesh,
        in_specs=(both, both, P(), P(), P(), P(), ex, ex, P(), P(), both, P(("dp", "expert"))),
        out_specs=(both, both, P(), P(), P(), P(), ex, ex, P(), P()),
        check_vma=False)
```

```python
import functools
import jax
import jax.numpy as jnp
from jax import lax
from jax.experimental import pallas as pl
from jax.experimental.pallas import tpu as pltpu
from jax.sharding import PartitionSpec as P

f32, bf16, i32 = jnp.float32, jnp.bfloat16, jnp.int32
T, D, H, J, E, FF, NB = 384, 512, 64, 8, 24, 2048, 8
EW = E * H
ROWS = J * T
SB = 2 * T
NSB = NB // 2
eps = 1e-06
NEG = -1e30
VM = pltpu.VMEM


def nn(a, b):
    return lax.dot_general(a, b, (((1,), (0,)), ((), ())), preferred_element_type=f32)


def nt(a, b):
    return lax.dot_general(a, b, (((1,), (1,)), ((), ())), preferred_element_type=f32)


def tn(a, b):
    return lax.dot_general(a, b, (((0,), (0,)), ((), ())), preferred_element_type=f32)


def lanes(rows):
    return lax.broadcasted_iota(i32, (rows, 128), 1)


def split3(v):
    a = v.astype(bf16).astype(f32)
    b = (v - a).astype(bf16).astype(f32)
    c = (v - a - b).astype(bf16).astype(f32)
    return a, b, c


MESH = pl.DeviceIdType.MESH
LINES = [(a, k) for a in "xyz" for k in (1, 2, 3)]
ALL_PEERS = [("c", 0)] + LINES


class Place:
    def __init__(self):
        dp, ex = lax.axis_index("dp"), lax.axis_index("expert")
        self.ex = ex
        self.at = {"x": dp // 4, "y": dp % 4, "z": ex // 2, "c": ex % 2}
        self.peers = {("c", 0): self.device(c=1 - self.at["c"])}
        for axis, k in LINES:
            self.peers[axis, k] = self.device(**{axis: (self.at[axis] + k) % 4})

    def device(self, **moved):
        at = {**self.at, **moved}
        return (at["x"] * 4 + at["y"], at["z"] * 2 + at["c"])

    def enter(self, peers):
        bar = pltpu.get_barrier_semaphore()
        for p in peers:
            pl.semaphore_signal(bar, inc=1, device_id=self.peers[p], device_id_type=MESH)
        pl.semaphore_wait(bar, len(peers))


class Copies:
    def __init__(self, place, send, recv):
        self.place, self.send, self.recv, self.made = place, send, recv, []

    def add(self, src, dst, peer):
        self.made.append((src, dst, peer))
        return len(self.made) - 1

    def get(self, i):
        src, dst, peer = self.made[i]
        return pltpu.make_async_remote_copy(src_ref=src(), dst_ref=dst(), send_sem=self.send.at[i], recv_sem=self.recv.at[i],
                                            device_id=self.place.peers[peer], device_id_type=MESH)

    def start(self, ids):
        for i in ids:
            self.get(i).start()

    def arrived(self, ids):
        for i in ids:
            self.get(i).wait_recv()

    def sent(self, ids):
        for i in ids:
            self.get(i).wait_send()

    def drain(self):
        self.sent(range(len(self.made)))


class Scatter:
    def __init__(self, copies, src, total, r, u0, u1, order):
        self.cp, self.src, self.total, self.r = copies, src, total, r
        self.u0, self.u1 = u0, u1
        at = copies.place.at
        self.c, self.m = at["c"], [at[a] for a in order]
        us = pl.ds(u0, u1 - u0)
        self.ids = [[copies.add(lambda: src.at[us, 1 - self.c], lambda: r[0].at[us], ("c", 0))]]
        for level in (1, 2, 3):
            def piece(k, level=level):
                pre = tuple(self.m[: level - 1])
                return total.at[(us,) + pre + ((self.m[level - 1] + k) % 4,)]
            self.ids.append([
                copies.add(functools.partial(piece, k), lambda k=k, level=level: r[level].at[us, k - 1], (order[level - 1], k))
                for k in (1, 2, 3)])

    def start(self, level):
        self.cp.start(self.ids[level])

    def finish(self, level):
        self.cp.arrived(self.ids[level])
        for u in range(self.u0, self.u1):
            if level == 0:
                for a in range(4):
                    v = self.src[u, self.c, a].astype(f32) + self.r[0][u, a].astype(f32)
                    self.total[u, a] = v.astype(bf16)
                continue
            at = (u,) + tuple(self.m[:level])
            v = self.total[at].astype(f32)
            for k in range(3):
                v = v + self.r[level][u, k].astype(f32)
            self.total[at] = v.astype(bf16)

    def result(self, u):
        return self.total[(u,) + tuple(self.m)]


class Spread:
    def __init__(self, copies, out, u0, u1, order):
        self.cp, self.out = copies, out
        at = copies.place.at
        self.c, self.m = at["c"], [at[a] for a in order]
        us = pl.ds(u0, u1 - u0)
        self.ids = []
        for level in range(4):
            ref = lambda level=level: out.at[(us, self.c) + tuple(self.m[:level])]
            peers = [("c", 0)] if level == 0 else [(order[level - 1], k) for k in (1, 2, 3)]
            self.ids.append([copies.add(ref, ref, p) for p in peers])

    def put(self, u, value):
        self.out[(u, self.c) + tuple(self.m)] = value

    def start(self, level):
        self.cp.start(self.ids[level])

    def finish(self, level):
        self.cp.arrived(self.ids[level])


class SpreadPlane:
    def __init__(self, copies, out, u0, u1):
        self.cp, self.out = copies, out
        self.x, self.y = copies.place.at["x"], copies.place.at["y"]
        us = pl.ds(u0, u1 - u0)
        one = lambda: out.at[us, self.x, self.y]
        row = lambda: out.at[us, self.x]
        self.ids = {"y": [copies.add(one, one, ("y", k)) for k in (1, 2, 3)],
                    "x": [copies.add(row, row, ("x", k)) for k in (1, 2, 3)]}

    def put(self, u, value):
        self.out[u, self.x, self.y] = value

    def start(self, axis):
        self.cp.start(self.ids[axis])

    def finish(self, axis):
        self.cp.arrived(self.ids[axis])


class SmallSum:
    def __init__(self, copies, src, half, r0, r1, by, bz, out):
        self.cp, self.src, self.half, self.r0, self.r1, self.by, self.bz, self.out = copies, src, half, r0, r1, by, bz, out
        at = copies.place.at
        self.c, self.x, self.y, self.z = at["c"], at["x"], at["y"], at["z"]
        own_half = lambda: out.at[self.c]
        own = lambda: out.at[self.c, self.x]
        self.ids = [
            [copies.add(lambda: src.at[1 - self.c], lambda: r0, ("c", 0))],
            [copies.add(lambda k=k: half.at[(self.x + k) % 4], lambda k=k: r1.at[k - 1], ("x", k)) for k in (1, 2, 3)],
            [copies.add(lambda: by.at[self.y], lambda: by.at[self.y], ("y", k)) for k in (1, 2, 3)],
            [copies.add(lambda: bz.at[self.z], lambda: bz.at[self.z], ("z", k)) for k in (1, 2, 3)],
            [copies.add(own, own, ("x", k)) for k in (1, 2, 3)],
            [copies.add(own_half, own_half, ("c", 0))],
        ]

    def step(self, i):
        if i:
            self.cp.arrived(self.ids[i - 1])
        if i == 1:
            for a in range(4):
                self.half[a] = (self.src[self.c, a].astype(f32) + self.r0[a].astype(f32)).astype(bf16)
        if i == 2:
            v = self.half[self.x].astype(f32)
            for k in range(3):
                v = v + self.r1[k].astype(f32)
            self.by[self.y] = v.astype(bf16)
        if i in (3, 4):
            b = self.by if i == 3 else self.bz
            v = (b[0].astype(f32) + b[1].astype(f32) + b[2].astype(f32) + b[3].astype(f32)).astype(bf16)
            if i == 3:
                self.bz[self.z] = v
            else:
                self.out[self.c, self.x] = v
        if i < 6:
            self.cp.start(self.ids[i])


ORDERS = ["xyz", "yzx", "zxy"]
BATCHES = [(0, 4), (4, 8), (8, 11)]
ALL_BATCHES = [(0, 3), (3, 6), (6, 8)]
UP_UNIT, DOWN_UNIT, WO_UNIT = [0, 1, 2, 4], [5, 6, 8, 9], [3, 7, 10]
UNITS = 11
STEPS = [(u, i) for i, u in enumerate(sorted(UP_UNIT + DOWN_UNIT))]


def expert_row(ex, piece, order):
    at = {"x": piece // 4, "y": piece % 4, "z": ex // 2}
    r = ex % 2
    for a in order:
        r = r * 4 + at[a]
    return r * 16


def store_expert(ref, units, ex0, value):
    low = value.astype(bf16)
    for o in range(2):
        for row in range(0, 768, 16):
            v, piece = row // 256, (row % 256) // 16
            ct, r = row // 192, row % 192
            base = expert_row(ex0 + o, piece, ORDERS[v])
            ref[units[v], base : base + 16, :] = low[o * 192 + r : o * 192 + r + 16, ct * 128 : (ct + 1) * 128]


KVR = T + 16


class Gather:
    def __init__(self, copies, out):
        self.cp, self.out = copies, out
        at, ex = copies.place.at, copies.place.ex
        own = lambda: out.at[ex]
        from_z = lambda k: out.at[((at["z"] - k + 4) % 4) * 2 + at["c"]]
        self.line = [copies.add(own, own, ("z", k)) for k in (1, 2, 3)]
        self.core = [copies.add(functools.partial(from_z, k), functools.partial(from_z, k), ("c", 0)) for k in (0, 1, 2, 3)]

    def start(self):
        self.cp.start(self.line)
        self.cp.start(self.core[:1])

    def forward(self):
        for k in range(3):
            self.cp.arrived(self.line[k : k + 1])
            self.cp.start(self.core[k + 1 : k + 2])

    def finish(self):
        self.cp.arrived(self.core)


def bounds_of(kv_ref):
    n0 = n1 = 0.0
    for b in range(NB):
        tail = kv_ref[b, T:KVR, :].astype(f32)
        n0 = n0 + 16.0 * tail[0:1] + tail[1:2]
        n1 = n1 + 16.0 * tail[2:3] + tail[3:4]
    return n0, n1


def segment_of(pos, bounds):
    return (pos >= bounds[0]).astype(i32) + (pos >= bounds[1]).astype(i32)


def sub8(v):
    return v.reshape(8, 8, v.shape[-1])


def route_rows(rt_ref):
    return [jnp.broadcast_to(rt_ref[j : j + 1, :], (8, T)) for j in range(J)]


def visible(me, sb):
    key = lax.broadcasted_iota(i32, (T, SB), 1)
    tok = lax.broadcasted_iota(i32, (T, SB), 0)
    ok = key - tok <= (me - 2 * sb) * T
    return ok


def prepare_keys(kv_ref, bounds, kaug, vaug, vt):
    ln = lanes(T)
    for b in range(NB):
        bs = slice(b * T, (b + 1) * T)
        kv = kv_ref[b, 0:T, :].astype(f32)
        pos = (lax.broadcasted_iota(i32, (T, 128), 0) + b * T).astype(f32)
        seg = segment_of(pos, bounds)
        feat = jnp.where((ln < H + 3) & (seg != ln - H), NEG, 0.0)
        feat = jnp.where((ln >= H + 3) & (ln < H + 6), 1.0, feat)
        kaug[bs, :] = jnp.where(ln < H, kv, feat).astype(bf16)
        if vaug is not None:
            one = jnp.where(ln < H + 3, 1.0, 0.0)
            vaug[bs, :] = jnp.where(ln < H, pltpu.roll(kv, H, 1), one).astype(bf16)
        if vt is not None:
            ones = jnp.where(lax.broadcasted_iota(i32, (16, T), 0) == 0, 1.0, 0.0)
            vt[:, bs] = jnp.concatenate([jnp.transpose(kv)[H:], ones], axis=0).astype(bf16)


def project_queries(normed, wq_ref, qall):
    for c in range(4):
        w = wq_ref[2 * c : 2 * c + 2].reshape(2 * 3 * H, D)
        qall[c * 48 : (c + 1) * 48] = (nt(w, normed) * 0.125).reshape(48, 8, T)


def choose(routes, table, j):
    acc = table[0:8]
    for e in range(1, E):
        acc = jnp.where((routes[j] == e)[None], table[e * 8 : (e + 1) * 8], acc)
    return acc


def to_experts(routes, rows, out):
    for e in range(E):
        acc = jnp.zeros((8, 8, T), f32)
        for j in range(J):
            acc = jnp.where((routes[j] == e)[None], rows[j], acc)
        out[e * H : (e + 1) * H, :] = acc.reshape(H, T).astype(bf16)


def pick_queries(rt_ref, bounds, me, qall, qt):
    routes = route_rows(rt_ref)
    pos = (lax.broadcasted_iota(i32, (H, T), 1) + me * T).astype(f32)
    seg = segment_of(pos, (bounds[0][:, 0:1], bounds[1][:, 0:1]))
    feat = jnp.where(lax.broadcasted_iota(i32, (H, T), 0) == seg, 1.0, 0.0).astype(bf16)
    for j in range(J):
        qt[0:H, j * T : (j + 1) * T] = choose(routes, qall, j).reshape(H, T).astype(bf16)
        qt[H:, j * T : (j + 1) * T] = feat


def attend(me, qt, kaug, vt, att, sbuf, macc, acc):
    last = me // 2

    def group(g, carry):
        gs = pl.ds(pl.multiple_of(g * SB, SB), SB)
        q = qt[:, gs]
        macc[...] = jnp.full(macc.shape, NEG, f32)

        def score(sb, masked):
            s = nn(kaug[pl.ds(pl.multiple_of(sb * SB, SB), SB), :], q)
            if masked:
                key = lax.broadcasted_iota(i32, (SB, T), 0)
                tok = lax.broadcasted_iota(i32, (SB, T), 1)
                ok = key - tok <= (me - 2 * sb) * T
                s = jnp.where(jnp.concatenate([ok, ok], axis=1), s, NEG)
            sbuf[sb] = s
            macc[...] = jnp.maximum(macc[...], jnp.max(s.reshape(SB // 8, 8, SB), axis=0))

        lax.fori_loop(0, last, lambda sb, c: (score(sb, False), c)[1], 0)
        score(last, True)
        m = jnp.max(macc[...], axis=0, keepdims=True)
        macc[...] = jnp.broadcast_to(m, macc.shape)
        acc[...] = jnp.zeros(acc.shape, f32)

        def weigh(sb, c):
            p = jnp.exp(sbuf[sb].reshape(SB // 8, 8, SB) - macc[...][None]).reshape(SB, SB).astype(bf16)
            acc[...] += nn(vt[:, pl.ds(pl.multiple_of(sb * SB, SB), SB)], p)
            return c

        lax.fori_loop(0, last + 1, weigh, 0)
        tot = acc[H : H + 1, :]
        att[:, gs] = (acc[0:H, :] / tot).astype(bf16)
        l1, l2, l3 = split3(-(m + jnp.log(tot)))
        row = lax.broadcasted_iota(i32, (16, SB), 0)
        old = q[H : H + 16].astype(f32)
        new = jnp.where(row == 3, l1, jnp.where(row == 4, l2, jnp.where(row == 5, l3, old)))
        qt[H : H + 16, gs] = new.astype(bf16)
        return carry

    lax.fori_loop(0, J // 2, group, 0)


def gates_of(normed, rw_ref, rt_ref, gate_ref):
    logits = nt(rw_ref[...], normed)
    eid = lax.broadcasted_iota(i32, (E, T), 0)
    per = [jnp.sum(jnp.where(rt_ref[j : j + 1, :] == eid, logits, 0.0), axis=0, keepdims=True) for j in range(J)]
    v = jnp.concatenate(per, axis=0)
    e = jnp.exp(v - jnp.max(v, axis=0, keepdims=True))
    gate_ref[...] = e / jnp.sum(e, axis=0, keepdims=True)


def kernel_ab(x_ref, gain_ref, kvw_ref, rw_ref, rt_ref, seg_ref, wq_in, wo_in,
              normed_ref, gate_ref, kv_ref, wq_ref, wo_ref, att_ref, qt_ref,
              qall, kaug, vt, sbuf, macc, acc, send, recv):
    place = Place()
    me = place.ex
    copies = Copies(place, send, recv)
    gq, gk, go = Gather(copies, wq_ref), Gather(copies, kv_ref), Gather(copies, wo_ref)
    wq_ref[me] = wq_in[...]
    wo_ref[me] = wo_in[...]
    place.enter([("c", 0)] + [("z", k) for k in (1, 2, 3)])
    gq.start()
    x = x_ref[...].astype(f32)
    inv = lax.rsqrt(jnp.mean(x * x, axis=-1, keepdims=True) + eps)
    normed = (x * inv * gain_ref[...]).astype(bf16)
    normed_ref[...] = normed
    kv_ref[me, 0:T, :] = nn(normed, kvw_ref[...]).astype(bf16)
    seg = seg_ref[...]
    row = lax.broadcasted_iota(i32, (16, 128), 0)
    tail = jnp.zeros((16, 128), f32)
    for s in range(2):
        n = jnp.sum(jnp.sum((seg <= s).astype(f32), axis=0, keepdims=True), axis=1, keepdims=True)
        n = jnp.broadcast_to(n, (16, 128))
        hi = jnp.floor(n * 0.0625)
        tail = jnp.where(row == 2 * s, hi, jnp.where(row == 2 * s + 1, n - 16.0 * hi, tail))
    kv_ref[me, T:KVR, :] = tail.astype(bf16)
    gk.start()
    gates_of(normed, rw_ref, rt_ref, gate_ref)
    gq.forward()
    go.start()
    gk.forward()
    gq.finish()
    project_queries(normed, wq_ref, qall)
    gk.finish()
    bounds = bounds_of(kv_ref)
    prepare_keys(kv_ref, bounds, kaug, None, vt)
    pick_queries(rt_ref, bounds, me, qall, qt_ref)
    go.forward()
    attend(me, qt_ref, kaug, vt, att_ref, sbuf, macc, acc)
    go.finish()
    copies.drain()


def dma_sems(n):
    return [pltpu.SemaphoreType.DMA((n,)), pltpu.SemaphoreType.DMA((n,))]


SCRATCH_AB = [VM((EW // 8, 8, T), f32), VM((ROWS, 128), bf16), VM((80, ROWS), bf16),
              VM((NSB, SB, SB), f32), VM((8, SB), f32), VM((80, SB), f32)] + dma_sems(21)


def kernel_c(x_ref, cot_ref, gate_ref, rt_ref, att_ref, wo_ref, up_ref, down_ref, fgain_ref, normed_ref, rw_ref,
             out_ref, dat_ref, gm_ref, gn_ref, big_ref, drw_ref, dfg_ref, rows, gat, gall):
    routes = route_rows(rt_ref)
    for j in range(J):
        rows[j] = sub8(att_ref[:, j * T : (j + 1) * T].astype(f32) * gate_ref[j : j + 1, :])
    to_experts(routes, rows, gat)
    x = x_ref[...].astype(f32)
    mixed = x + tn(gat[...], wo_ref[...])
    inv = lax.rsqrt(jnp.mean(mixed * mixed, axis=-1, keepdims=True) + eps)
    n = mixed * inv
    fgain = fgain_ref[...]
    second = (n * fgain).astype(bf16)
    second_t = jnp.transpose(n * fgain).astype(bf16)
    cot = cot_ref[...]
    C = 512
    out = mixed
    gsec = jnp.zeros((T, D), f32)
    for c in range(FF // C):
        cs = slice(c * C, (c + 1) * C)
        v = nn(second, up_ref[:, cs])
        v2 = v * v
        th = jnp.tanh(0.7978845608028654 * (v + 0.044715 * v * v2))
        a = (0.5 * v * (1.0 + th)).astype(bf16)
        dth = 0.5 * (1.0 + th) + 0.5 * v * (1.0 - th * th) * (0.7978845608028654 * (1.0 + 0.134145 * v2))
        gh = (nt(cot, down_ref[cs, :]) * dth).astype(bf16)
        out = out + nn(a, down_ref[cs, :])
        gsec = gsec + nt(gh, up_ref[:, cs])
        gdown = tn(a, cot).astype(bf16)
        gup = nn(second_t, gh).astype(bf16)
        for t in range(4):
            big_ref[DOWN_UNIT[t], cs, :] = gdown[:, t * 128 : (t + 1) * 128]
            big_ref[UP_UNIT[c], t * 512 : (t + 1) * 512, :] = gup[:, t * 128 : (t + 1) * 128]
    out_ref[...] = out.astype(bf16)
    dfg_ref[...] = jnp.sum(gsec * n, axis=0, keepdims=True)
    hh = gsec * fgain
    gm = cot.astype(f32) + inv * (hh - n * jnp.mean(hh * n, axis=-1, keepdims=True))
    gm_ref[...] = gm
    gml = gm.astype(bf16)
    for c in range(4):
        gall[c * 48 : (c + 1) * 48] = nt(wo_ref[c * 384 : (c + 1) * 384, :], gml).reshape(48, 8, T)
    dots = []
    row = lax.broadcasted_iota(i32, (H, T), 0)
    for j in range(J):
        js = slice(j * T, (j + 1) * T)
        g = choose(routes, gall, j).reshape(H, T)
        gate = gate_ref[j : j + 1, :]
        dot = jnp.sum(g * att_ref[:, js].astype(f32), axis=0, keepdims=True)
        dots.append(dot)
        d1, d2, d3 = split3(-(dot * gate))
        dat_ref[0:H, js] = (g * gate).astype(bf16)
        dat_ref[H:, js] = jnp.where(row == 0, d1, jnp.where(row == 1, d2, jnp.where(row == 2, d3, 0.0))).astype(bf16)
    dots = jnp.concatenate(dots, axis=0)
    gates = gate_ref[...]
    chosen = gates * (dots - jnp.sum(gates * dots, axis=0, keepdims=True))
    eid = lax.broadcasted_iota(i32, (E, T), 0)
    gl = jnp.zeros((E, T), f32)
    for j in range(J):
        gl = jnp.where(rt_ref[j : j + 1, :] == eid, chosen[j : j + 1, :], gl)
    hi = gl.astype(bf16)
    lo = (gl - hi.astype(f32)).astype(bf16)
    rw = rw_ref[...]
    gn_ref[...] = tn(hi, rw) + tn(lo, rw)
    nm = normed_ref[...]
    drw_ref[...] = nn(hi, nm) + nn(lo, nm)
    for c in range(4):
        store_expert(big_ref, WO_UNIT, 2 * c, nn(gat[c * 384 : (c + 1) * 384, :], gml))


SCRATCH_C = [VM((J, 8, 8, T), f32), VM((EW, T), bf16), VM((EW // 8, 8, T), f32)]


def kernel_d(kv_ref, qt_ref, dat_ref, big_ref, dq_ref, gkv_ref, red_ref,
             kaug, vaug, qa, da, dqacc, tot, gsend, grecv, total, r0, r1, r2, r3, send, recv, ksend, krecv):
    place = Place()
    me = place.ex
    dp = lax.axis_index("dp")
    copies = Copies(place, send, recv)
    sums = [Scatter(copies, big_ref, total, (r0, r1, r2, r3), u0, u1, o) for (u0, u1), o in zip(BATCHES, ORDERS)]
    bar = pltpu.get_barrier_semaphore()
    for p in ALL_PEERS:
        pl.semaphore_signal(bar, inc=1, device_id=place.peers[p], device_id_type=MESH)
    for k in range(1, NB):
        pl.semaphore_signal(bar, inc=1, device_id=(dp, (me + k) % NB), device_id_type=MESH)
    pl.semaphore_wait(bar, len(ALL_PEERS) + NB - 1)
    for s in sums:
        s.start(0)
    prepare_keys(kv_ref, bounds_of(kv_ref), kaug, vaug, None)
    for j in range(J):
        js = slice(j * T, (j + 1) * T)
        qa[js, :] = jnp.transpose(qt_ref[:, js].astype(f32)).astype(bf16)
        da[js, :] = jnp.transpose(dat_ref[:, js].astype(f32)).astype(bf16)
    dqacc[...] = jnp.zeros(dqacc.shape, f32)
    last = me // 2

    def block(sb, masked):
        ks = pl.ds(pl.multiple_of(sb * SB, SB), SB)
        tot[...] = jnp.zeros(tot.shape, f32)

        def rows(g):
            gs = pl.ds(pl.multiple_of(g * SB, SB), SB)
            p = jnp.exp(nt(qa[gs, :], kaug[ks, :]))
            if masked:
                ok = visible(me, sb)
                p = jnp.where(jnp.concatenate([ok, ok], axis=0), p, 0.0)
            ds = (p * nt(da[gs, :], vaug[ks, :])).astype(bf16)
            kv = jnp.concatenate([kv_ref[2 * sb, 0:T, :], kv_ref[2 * sb + 1, 0:T, :]], axis=0)
            dqacc[gs, :] += nn(ds, kv)
            tot[0:H, :] += nn(qt_ref[0:H, gs], ds)
            tot[H:, :] += nn(dat_ref[0:H, gs], p.astype(bf16))

        def two(i, c):
            rows(2 * i)
            rows(2 * i + 1)
            return c

        lax.fori_loop(0, J // 4, two, 0)
        low = jnp.transpose(tot[...]).astype(bf16)
        gsend[2 * sb] = low[0:T]
        gsend[2 * sb + 1] = low[T:]

    def to_owner(kb):
        return pltpu.make_async_remote_copy(src_ref=gsend.at[kb], dst_ref=grecv.at[me], send_sem=ksend.at[kb],
                                            recv_sem=krecv.at[me], device_id=(dp, kb), device_id_type=MESH)

    def from_device(b):
        return pltpu.make_async_remote_copy(src_ref=gsend.at[b], dst_ref=grecv.at[b], send_sem=ksend.at[b],
                                            recv_sem=krecv.at[b], device_id=(dp, b), device_id_type=MESH)

    def step(i, carry):
        @pl.when(i < last)
        def _():
            block(i, False)
            to_owner(2 * i).start()
            to_owner(2 * i + 1).start()

        for at, level in ((0, 0), (2, 1)):
            @pl.when(i == at)
            def _(level=level):
                for s in sums:
                    s.finish(level)
                    s.start(level + 1)

        return carry

    lax.fori_loop(0, NSB - 1, step, 0)
    block(last, True)

    @pl.when(2 * last < me)
    def _():
        to_owner(2 * last).start()

    for s in sums:
        s.finish(2)
        s.start(3)
    for j in range(J):
        js = slice(j * T, (j + 1) * T)
        dq_ref[:, js] = jnp.transpose(dqacc[js, :])[0:H].astype(bf16)
    for s in sums:
        s.finish(3)
        for u in range(s.u0, s.u1):
            red_ref[u] = s.result(u)
    gkv_ref[...] = gsend[me].astype(f32)
    for b in range(1, NB):
        @pl.when(b > me)
        def _(b=b):
            from_device(b).wait_recv()
            gkv_ref[...] += grecv[b].astype(f32)
    for b in range(NB - 1):
        @pl.when(b < me)
        def _(b=b):
            to_owner(b).wait_send()
    copies.drain()


SCRATCH_D = [VM((ROWS, 128), bf16), VM((ROWS, 128), bf16), VM((ROWS, 128), bf16), VM((ROWS, 128), bf16), VM((ROWS, 128), f32),
             VM((128, SB), f32), VM((NB, T, 128), bf16), VM((NB, T, 128), bf16),
             VM((UNITS, 4, 4, 4, 16, 128), bf16), VM((UNITS, 4, 4, 4, 16, 128), bf16), VM((UNITS, 3, 4, 4, 16, 128), bf16),
             VM((UNITS, 3, 4, 16, 128), bf16), VM((UNITS, 3, 16, 128), bf16)] + dma_sems(30) + dma_sems(NB)


SMALL = 640


def kernel_e(dq_ref, rt_ref, wq_ref, normed_ref, gkv_ref, kvw_ref, gn_ref, x_ref, gain_ref, gm_ref, drw_ref, dfg_ref, red_ref,
             ing_ref, all_ref, wo_ref, dwq_ref, small_ref,
             rows, dqs, big, total, r0, r1, r2, r3, ssrc, shalf, s0, s1, sy, sz, send, recv):
    place = Place()
    copies = Copies(place, send, recv)
    spreads = [Spread(copies, all_ref, u0, u1, o) for (u0, u1), o in zip(ALL_BATCHES, ORDERS)]
    plane_o = SpreadPlane(copies, wo_ref, 0, 3)
    plane_q = SpreadPlane(copies, dwq_ref, 0, 3)
    big7 = big.reshape(3, 2, 4, 4, 4, 16, 128)
    sums = [Scatter(copies, big7, total, (r0, r1, r2, r3), u, u + 1, o) for u, o in enumerate(ORDERS)]
    small = SmallSum(copies, ssrc, shalf, s0, s1, sy, sz, small_ref)
    for (u0, u1), s in zip(ALL_BATCHES, spreads):
        for u in range(u0, u1):
            s.put(u, red_ref[sorted(UP_UNIT + DOWN_UNIT)[u]])
    for v in range(3):
        plane_o.put(v, red_ref[WO_UNIT[v]])
    place.enter(ALL_PEERS)
    for s in spreads:
        s.start(3)
    plane_o.start("y")
    routes = route_rows(rt_ref)
    for j in range(J):
        rows[j] = sub8(dq_ref[:, j * T : (j + 1) * T].astype(f32) * 0.125)
    to_experts(routes, rows, dqs)
    nm = normed_ref[...]
    for c in range(4):
        store_expert(big, [0, 1, 2], 2 * c, nn(dqs[c * 384 : (c + 1) * 384, :], nm))
    for s in sums:
        s.start(0)
    for s in spreads:
        s.finish(3)
        s.start(2)
    plane_o.finish("y")
    plane_o.start("x")
    gkv = gkv_ref[...].astype(bf16)
    dkvw = tn(nm, gkv).astype(bf16)
    gn = gn_ref[...] + tn(dqs[...], wq_ref[...]) + nt(gkv, kvw_ref[...])
    x = x_ref[...].astype(f32)
    inv = lax.rsqrt(jnp.mean(x * x, axis=-1, keepdims=True) + eps)
    n = x * inv
    dgain = jnp.sum(gn * n, axis=0, keepdims=True)
    drw = drw_ref[...]
    dfg = dfg_ref[...]
    parts = [dkvw.astype(f32)] + [drw[:, t * 128 : (t + 1) * 128] for t in range(4)]
    parts += [v[:, t * 128 : (t + 1) * 128] for v in (dgain, dfg) for t in range(4)] + [jnp.zeros((SMALL - 616, 128), f32)]
    ssrc[...] = jnp.concatenate(parts, axis=0).astype(bf16).reshape(2, 4, SMALL // 8, 128)
    small.step(0)
    for s in sums:
        s.finish(0)
        s.start(1)
    small.step(1)
    for s in spreads:
        s.finish(2)
        s.start(1)
    plane_o.finish("x")
    hh = gn * gain_ref[...]
    ing_ref[...] = (gm_ref[...] + inv * (hh - n * jnp.mean(hh * n, axis=-1, keepdims=True))).astype(bf16)
    small.step(2)
    for level in (1, 2):
        for s in sums:
            s.finish(level)
            s.start(level + 1)
        small.step(level + 2)
    for s in sums:
        s.finish(3)
    for v in range(3):
        plane_q.put(v, sums[v].result(v))
    plane_q.start("y")
    for s in spreads:
        s.finish(1)
        s.start(0)
    small.step(5)
    plane_q.finish("y")
    plane_q.start("x")
    small.step(6)
    plane_q.finish("x")
    for s in spreads:
        s.finish(0)
    copies.drain()


SCRATCH_E = [VM((J, 8, 8, T), f32), VM((EW, T), bf16), VM((3, 2048, 128), bf16),
             VM((3, 4, 4, 4, 16, 128), bf16), VM((3, 4, 4, 4, 16, 128), bf16), VM((3, 3, 4, 4, 16, 128), bf16),
             VM((3, 3, 4, 16, 128), bf16), VM((3, 3, 16, 128), bf16),
             VM((2, 4, SMALL // 8, 128), bf16), VM((4, SMALL // 8, 128), bf16), VM((4, SMALL // 8, 128), bf16),
             VM((3, SMALL // 8, 128), bf16), VM((4, SMALL // 8, 128), bf16), VM((4, SMALL // 8, 128), bf16)] + dma_sems(86)


def kernel_f(all_ref, wo_ref, dwq_ref, small_ref, out_in, ing_in, dup_ref, ddown_ref, dwo_ref, dwqt_ref, dkvw_ref, drw_ref, dgain_ref,
             dfg_ref, out_ref, ing_ref):
    slot = {u: i for i, u in enumerate(sorted(UP_UNIT + DOWN_UNIT))}
    for t in range(4):
        ts = slice(t * 128, (t + 1) * 128)
        ddown_ref[:, ts] = all_ref[slot[DOWN_UNIT[t]]].astype(f32)
        for s in range(4):
            dup_ref[:, (4 * t + s) * 128 : (4 * t + s + 1) * 128] = all_ref[slot[UP_UNIT[t]], s * 512 : (s + 1) * 512, :].astype(f32)
        dwo_ref[:, ts] = wo_ref[t * 192 : (t + 1) * 192, :].astype(f32)
        dwqt_ref[:, ts] = dwq_ref[t * 192 : (t + 1) * 192, :].astype(f32)
    small = small_ref[512:SMALL, :].astype(f32)
    dkvw_ref[...] = small_ref[0:512, :].astype(f32)
    for t in range(4):
        ts = slice(t * 128, (t + 1) * 128)
        drw_ref[:, ts] = small[t * E : (t + 1) * E]
        dgain_ref[:, ts] = small[96 + t : 97 + t]
        dfg_ref[:, ts] = small[100 + t : 101 + t]
    out_ref[...] = out_in[...]
    ing_ref[...] = ing_in[...]


def call(body, outs, scratch, vmem=56 << 20, flops=0, **kw):
    n = 0
    def run(*args):
        return pl.pallas_call(
            body,
            out_shape=[jax.ShapeDtypeStruct(s, t) for s, t in outs],
            in_specs=[pl.BlockSpec(memory_space=VM)] * len(args),
            out_specs=[pl.BlockSpec(memory_space=VM)] * len(outs),
            scratch_shapes=scratch,
            compiler_params=pltpu.CompilerParams(vmem_limit_bytes=vmem, **kw),
            cost_estimate=pl.CostEstimate(flops=flops, bytes_accessed=1 << 22, transcendentals=0),
        )(*args)
    return run


def per_device(inputs, cotangent, norm_gain, ffn_gain, kv_weight, router_weight, query_weight, output_weight, up_weight,
               down_weight, routes, segment_ids):
    wq = jnp.swapaxes(query_weight, 1, 2).reshape(3 * H, D)
    wo = output_weight.reshape(3 * H, D)
    rw = router_weight.T
    rt = routes.T
    gain = norm_gain.reshape(1, D)
    fgain = ffn_gain.reshape(1, D)
    normed, gate, kv_all, wq_all, wo_all, att, qt = call(
        kernel_ab,
        [((T, D), bf16), ((J, T), f32), ((NB, KVR, 128), bf16), ((NB, 3 * H, D), bf16), ((NB, 3 * H, D), bf16),
         ((H, ROWS), bf16), ((128, ROWS), bf16)],
        SCRATCH_AB, flops=1 << 33, collective_id=1, has_side_effects=True)(
        inputs, gain, kv_weight, rw, rt, segment_ids.reshape(3, 128), wq, wo)
    wq_all, wo_all = wq_all.reshape(EW, D), wo_all.reshape(EW, D)
    out, dat, gm, gn, big, drw, dfg = call(
        kernel_c,
        [((T, D), bf16), ((128, ROWS), bf16), ((T, D), f32), ((T, D), f32), ((UNITS, 2048, 128), bf16), ((E, D), f32), ((1, D), f32)],
        SCRATCH_C, flops=1 << 33)(inputs, cotangent, gate, rt, att, wo_all, up_weight, down_weight, fgain, normed, rw)
    dq, gkv, red = call(
        kernel_d, [((H, ROWS), bf16), ((T, 128), f32), ((UNITS, 16, 128), bf16)],
        SCRATCH_D, flops=1 << 35, collective_id=2, has_side_effects=True)(
        kv_all, qt, dat, big.reshape(UNITS, 2, 4, 4, 4, 16, 128))
    ing, shared, dwo, dwq, small = call(
        kernel_e,
        [((T, D), bf16), ((8, 2, 4, 4, 4, 16, 128), bf16), ((3, 4, 4, 16, 128), bf16), ((3, 4, 4, 16, 128), bf16),
         ((2, 4, SMALL // 8, 128), bf16)],
        SCRATCH_E, flops=1 << 32, collective_id=3, has_side_effects=True)(
        dq, rt, wq_all, normed, gkv, kv_weight, gn, inputs, gain, gm, drw, dfg, red)
    dup, ddown, dwo, dwqt, dkvw, drw, dgain, dfg, out, ing = call(
        kernel_f,
        [((D, FF), f32), ((FF, D), f32), ((3 * H, D), f32), ((3 * H, D), f32), ((D, 128), f32), ((E, D), f32), ((1, D), f32),
         ((1, D), f32), ((T, D), bf16), ((T, D), bf16)], [])(
        shared.reshape(8, 2048, 128), dwo.reshape(768, 128), dwq.reshape(768, 128), small.reshape(SMALL, 128), out, ing)
    return (out, ing, dgain.reshape(D), dfg.reshape(D), dkvw, drw.T,
            jnp.swapaxes(dwqt.reshape(3, H, D), 1, 2), dwo.reshape(3, H, D), dup, ddown)


def solution(mesh):
    both = P(("dp", "expert"), None)
    ex = P("expert", None, None)
    return jax.shard_map(
        per_device, mesh=mesh,
        in_specs=(both, both, P(), P(), P(), P(), ex, ex, P(), P(), both, P(("dp", "expert"))),
        out_specs=(both, both, P(), P(), P(), P(), ex, ex, P(), P()),
        check_vma=False)
```

```python
import functools
import jax
import jax.numpy as jnp
from jax import lax
from jax.experimental import pallas as pl
from jax.experimental.pallas import tpu as pltpu
from jax.sharding import PartitionSpec as P

f32, bf16, i32 = jnp.float32, jnp.bfloat16, jnp.int32
T, D, H, J, E, FF, NB = 384, 512, 64, 8, 24, 2048, 8
EW = E * H
ROWS = J * T
SB = 2 * T
NSB = NB // 2
eps = 1e-06
NEG = -1e30
VM = pltpu.VMEM


def nn(a, b):
    return lax.dot_general(a, b, (((1,), (0,)), ((), ())), preferred_element_type=f32)


def nt(a, b):
    return lax.dot_general(a, b, (((1,), (1,)), ((), ())), preferred_element_type=f32)


def tn(a, b):
    return lax.dot_general(a, b, (((0,), (0,)), ((), ())), preferred_element_type=f32)


def lanes(rows):
    return lax.broadcasted_iota(i32, (rows, 128), 1)


def split3(v):
    a = v.astype(bf16).astype(f32)
    b = (v - a).astype(bf16).astype(f32)
    c = (v - a - b).astype(bf16).astype(f32)
    return a, b, c


MESH = pl.DeviceIdType.MESH
LINES = [(a, k) for a in "xyz" for k in (1, 2, 3)]
ALL_PEERS = [("c", 0)] + LINES


class Place:
    def __init__(self):
        dp, ex = lax.axis_index("dp"), lax.axis_index("expert")
        self.ex = ex
        self.at = {"x": dp // 4, "y": dp % 4, "z": ex // 2, "c": ex % 2}
        self.peers = {("c", 0): self.device(c=1 - self.at["c"])}
        for axis, k in LINES:
            self.peers[axis, k] = self.device(**{axis: (self.at[axis] + k) % 4})

    def device(self, **moved):
        at = {**self.at, **moved}
        return (at["x"] * 4 + at["y"], at["z"] * 2 + at["c"])

    def enter(self, peers):
        bar = pltpu.get_barrier_semaphore()
        for p in peers:
            pl.semaphore_signal(bar, inc=1, device_id=self.peers[p], device_id_type=MESH)
        pl.semaphore_wait(bar, len(peers))


class Copies:
    def __init__(self, place, send, recv):
        self.place, self.send, self.recv, self.made = place, send, recv, []

    def add(self, src, dst, peer):
        self.made.append((src, dst, peer))
        return len(self.made) - 1

    def get(self, i):
        src, dst, peer = self.made[i]
        return pltpu.make_async_remote_copy(src_ref=src(), dst_ref=dst(), send_sem=self.send.at[i], recv_sem=self.recv.at[i],
                                            device_id=self.place.peers[peer], device_id_type=MESH)

    def start(self, ids):
        for i in ids:
            self.get(i).start()

    def arrived(self, ids):
        for i in ids:
            self.get(i).wait_recv()

    def sent(self, ids):
        for i in ids:
            self.get(i).wait_send()

    def drain(self):
        self.sent(range(len(self.made)))


class Scatter:
    def __init__(self, copies, big, r, parts, order):
        self.cp, self.big, self.r = copies, big, r
        self.u0, self.u1 = parts[0][0], parts[-1][1]
        at = copies.place.at
        self.m = [at[a] for a in order]
        us = pl.ds(self.u0, self.u1 - self.u0)
        self.part_ids = [
            copies.add(lambda s=s: big.at[1, pl.ds(s[0], s[1] - s[0])], lambda s=s: r[0].at[pl.ds(s[0], s[1] - s[0])], ("c", 0))
            for s in parts]
        self.ids = [self.part_ids]
        for level in (1, 2, 3):
            def piece(k, level=level):
                pre = tuple(self.m[: level - 1])
                return big.at[(0, us) + pre + ((self.m[level - 1] + k) % 4,)]
            self.ids.append([
                copies.add(functools.partial(piece, k), lambda k=k, level=level: r[level].at[us, k - 1], (order[level - 1], k))
                for k in (1, 2, 3)])

    def start_part(self, i):
        self.cp.start([self.part_ids[i]])

    def start(self, level):
        self.cp.start(self.ids[level])

    def finish(self, level):
        self.cp.arrived(self.ids[level])
        for u in range(self.u0, self.u1):
            if level == 0:
                for a in range(4):
                    v = self.big[0, u, a].astype(f32) + self.r[0][u, a].astype(f32)
                    self.big[0, u, a] = v.astype(bf16)
                continue
            at = (0, u) + tuple(self.m[:level])
            v = self.big[at].astype(f32)
            for k in range(3):
                v = v + self.r[level][u, k].astype(f32)
            self.big[at] = v.astype(bf16)

    def result(self, u):
        return self.big[(0, u) + tuple(self.m)]


class Spread:
    def __init__(self, copies, out, u0, u1, order):
        self.cp, self.out = copies, out
        at = copies.place.at
        self.c, self.m = at["c"], [at[a] for a in order]
        us = pl.ds(u0, u1 - u0)
        self.ids = []
        for level in range(4):
            ref = lambda level=level: out.at[(us, self.c) + tuple(self.m[:level])]
            peers = [("c", 0)] if level == 0 else [(order[level - 1], k) for k in (1, 2, 3)]
            self.ids.append([copies.add(ref, ref, p) for p in peers])

    def put(self, u, value):
        self.out[(u, self.c) + tuple(self.m)] = value

    def start(self, level):
        self.cp.start(self.ids[level])

    def finish(self, level):
        self.cp.arrived(self.ids[level])


class SpreadPlane:
    def __init__(self, copies, out, u0, u1):
        self.cp, self.out = copies, out
        self.x, self.y = copies.place.at["x"], copies.place.at["y"]
        us = pl.ds(u0, u1 - u0)
        one = lambda: out.at[us, self.x, self.y]
        row = lambda: out.at[us, self.x]
        self.ids = {"y": [copies.add(one, one, ("y", k)) for k in (1, 2, 3)],
                    "x": [copies.add(row, row, ("x", k)) for k in (1, 2, 3)]}

    def put(self, u, value):
        self.out[u, self.x, self.y] = value

    def start(self, axis):
        self.cp.start(self.ids[axis])

    def finish(self, axis):
        self.cp.arrived(self.ids[axis])


class SmallSum:
    def __init__(self, copies, src, half, r0, r1, by, bz, out):
        self.cp, self.src, self.half, self.r0, self.r1, self.by, self.bz, self.out = copies, src, half, r0, r1, by, bz, out
        at = copies.place.at
        self.c, self.x, self.y, self.z = at["c"], at["x"], at["y"], at["z"]
        own_half = lambda: out.at[self.c]
        own = lambda: out.at[self.c, self.x]
        self.ids = [
            [copies.add(lambda: src.at[1 - self.c], lambda: r0, ("c", 0))],
            [copies.add(lambda k=k: half.at[(self.x + k) % 4], lambda k=k: r1.at[k - 1], ("x", k)) for k in (1, 2, 3)],
            [copies.add(lambda: by.at[self.y], lambda: by.at[self.y], ("y", k)) for k in (1, 2, 3)],
            [copies.add(lambda: bz.at[self.z], lambda: bz.at[self.z], ("z", k)) for k in (1, 2, 3)],
            [copies.add(own, own, ("x", k)) for k in (1, 2, 3)],
            [copies.add(own_half, own_half, ("c", 0))],
        ]

    def step(self, i):
        if i:
            self.cp.arrived(self.ids[i - 1])
        if i == 1:
            for a in range(4):
                self.half[a] = (self.src[self.c, a].astype(f32) + self.r0[a].astype(f32)).astype(bf16)
        if i == 2:
            v = self.half[self.x].astype(f32)
            for k in range(3):
                v = v + self.r1[k].astype(f32)
            self.by[self.y] = v.astype(bf16)
        if i in (3, 4):
            b = self.by if i == 3 else self.bz
            v = (b[0].astype(f32) + b[1].astype(f32) + b[2].astype(f32) + b[3].astype(f32)).astype(bf16)
            if i == 3:
                self.bz[self.z] = v
            else:
                self.out[self.c, self.x] = v
        if i < 6:
            self.cp.start(self.ids[i])


ORDERS = ["xyz", "yzx", "zxy"]
BATCHES = [[(0, 3), (3, 4)], [(4, 7), (7, 8)], [(8, 10), (10, 11)]]
ALL_BATCHES = [(0, 3), (3, 6), (6, 8)]
UP_UNIT, DOWN_UNIT, WO_UNIT = [0, 1, 2, 4], [5, 6, 8, 9], [3, 7, 10]
UNITS = 11
STEPS = [(u, i) for i, u in enumerate(sorted(UP_UNIT + DOWN_UNIT))]


def expert_row(ex, piece, order):
    at = {"x": piece // 4, "y": piece % 4, "z": ex // 2}
    r = ex % 2
    for a in order:
        r = r * 4 + at[a]
    return r * 16


def store_expert(big, core, units, ex0, value):
    low = value.astype(bf16)
    for o in range(2):
        slot = (core + (ex0 + o) % 2) % 2
        for row in range(0, 768, 16):
            v, piece = row // 256, (row % 256) // 16
            ct, r = row // 192, row % 192
            base = expert_row(ex0 + o, piece, ORDERS[v]) % 1024
            big[slot, units[v], base : base + 16, :] = low[o * 192 + r : o * 192 + r + 16, ct * 128 : (ct + 1) * 128]


KVR = T + 16


class Gather:
    def __init__(self, copies, out):
        self.cp, self.out = copies, out
        at, ex = copies.place.at, copies.place.ex
        own = lambda: out.at[ex]
        from_z = lambda k: out.at[((at["z"] - k + 4) % 4) * 2 + at["c"]]
        self.line = [copies.add(own, own, ("z", k)) for k in (1, 2, 3)]
        self.core = [copies.add(functools.partial(from_z, k), functools.partial(from_z, k), ("c", 0)) for k in (0, 1, 2, 3)]

    def start(self):
        self.cp.start(self.line)
        self.cp.start(self.core[:1])

    def forward(self):
        for k in range(3):
            self.cp.arrived(self.line[k : k + 1])
            self.cp.start(self.core[k + 1 : k + 2])

    def finish(self):
        self.cp.arrived(self.core)


def bounds_of(kv_ref):
    n0 = n1 = 0.0
    for b in range(NB):
        tail = kv_ref[b, T:KVR, :].astype(f32)
        n0 = n0 + 16.0 * tail[0:1] + tail[1:2]
        n1 = n1 + 16.0 * tail[2:3] + tail[3:4]
    return n0, n1


def segment_of(pos, bounds):
    return (pos >= bounds[0]).astype(i32) + (pos >= bounds[1]).astype(i32)


def sub8(v):
    return v.reshape(8, 8, v.shape[-1])


def route_rows(rt_ref):
    return [jnp.broadcast_to(rt_ref[j : j + 1, :], (8, T)) for j in range(J)]


def visible(me, sb):
    key = lax.broadcasted_iota(i32, (T, SB), 1)
    tok = lax.broadcasted_iota(i32, (T, SB), 0)
    ok = key - tok <= (me - 2 * sb) * T
    return ok


def prepare_keys(kv_ref, bounds, kaug, vaug, vt):
    ln = lanes(T)
    for b in range(NB):
        bs = slice(b * T, (b + 1) * T)
        kv = kv_ref[b, 0:T, :].astype(f32)
        pos = (lax.broadcasted_iota(i32, (T, 128), 0) + b * T).astype(f32)
        seg = segment_of(pos, bounds)
        feat = jnp.where((ln < H + 3) & (seg != ln - H), NEG, 0.0)
        feat = jnp.where((ln >= H + 3) & (ln < H + 6), 1.0, feat)
        kaug[bs, :] = jnp.where(ln < H, kv, feat).astype(bf16)
        if vaug is not None:
            one = jnp.where(ln < H + 3, 1.0, 0.0)
            vaug[bs, :] = jnp.where(ln < H, pltpu.roll(kv, H, 1), one).astype(bf16)
        if vt is not None:
            ones = jnp.where(lax.broadcasted_iota(i32, (16, T), 0) == 0, 1.0, 0.0)
            vt[:, bs] = jnp.concatenate([jnp.transpose(kv)[H:], ones], axis=0).astype(bf16)


def project_queries(normed, wq_ref, qall):
    for c in range(4):
        w = wq_ref[2 * c : 2 * c + 2].reshape(2 * 3 * H, D)
        qall[c * 48 : (c + 1) * 48] = (nt(w, normed) * 0.125).reshape(48, 8, T)


def choose(routes, table, j):
    acc = table[0:8]
    for e in range(1, E):
        acc = jnp.where((routes[j] == e)[None], table[e * 8 : (e + 1) * 8], acc)
    return acc


def to_experts(routes, rows, out):
    for e in range(E):
        acc = jnp.zeros((8, 8, T), f32)
        for j in range(J):
            acc = jnp.where((routes[j] == e)[None], rows[j], acc)
        out[e * H : (e + 1) * H, :] = acc.reshape(H, T).astype(bf16)


def pick_queries(rt_ref, bounds, me, qall, qt):
    routes = route_rows(rt_ref)
    pos = (lax.broadcasted_iota(i32, (H, T), 1) + me * T).astype(f32)
    seg = segment_of(pos, (bounds[0][:, 0:1], bounds[1][:, 0:1]))
    feat = jnp.where(lax.broadcasted_iota(i32, (H, T), 0) == seg, 1.0, 0.0).astype(bf16)
    for j in range(J):
        qt[0:H, j * T : (j + 1) * T] = choose(routes, qall, j).reshape(H, T).astype(bf16)
        qt[H:, j * T : (j + 1) * T] = feat


def attend(me, qt, kaug, vt, att, macc, acc):
    last = me // 2
    macc[...] = jnp.full(macc.shape, NEG, f32)
    acc[...] = jnp.zeros(acc.shape, f32)

    def block(sb, masked):
        ks = pl.ds(pl.multiple_of(sb * SB, SB), SB)
        for g in range(J // 2):
            gs = slice(g * SB, (g + 1) * SB)
            s = nn(kaug[ks, :], qt[:, gs])
            if masked:
                key = lax.broadcasted_iota(i32, (SB, T), 0)
                tok = lax.broadcasted_iota(i32, (SB, T), 1)
                ok = key - tok <= (me - 2 * sb) * T
                s = jnp.where(jnp.concatenate([ok, ok], axis=1), s, NEG)
            s = s.reshape(SB // 8, 8, SB)
            old = macc[:, gs]
            top = jnp.max(jnp.maximum(old, jnp.max(s, axis=0)), axis=0, keepdims=True)
            top = jnp.broadcast_to(top, (8, SB))
            p = jnp.exp(s - top[None]).reshape(SB, SB).astype(bf16)
            kept = acc[:, gs].reshape(10, 8, SB) * jnp.exp(old - top)[None]
            acc[:, gs] = kept.reshape(80, SB) + nn(vt[:, ks], p)
            macc[:, gs] = top

    lax.fori_loop(0, last, lambda sb, c: (block(sb, False), c)[1], 0)
    block(last, True)
    for g in range(J // 2):
        gs = slice(g * SB, (g + 1) * SB)
        tot = acc[H : H + 1, gs]
        att[:, gs] = (acc[0:H, gs] / tot).astype(bf16)
        l1, l2, l3 = split3(-(macc[0:1, gs] + jnp.log(tot)))
        row = lax.broadcasted_iota(i32, (16, SB), 0)
        feat = qt[H : H + 16, gs].astype(f32)
        feat = jnp.where(row == 3, l1, jnp.where(row == 4, l2, jnp.where(row == 5, l3, feat)))
        qt[H : H + 16, gs] = feat.astype(bf16)


def gates_of(normed, rw_ref, rt_ref, gate_ref):
    logits = nt(rw_ref[...], normed)
    eid = lax.broadcasted_iota(i32, (E, T), 0)
    per = [jnp.sum(jnp.where(rt_ref[j : j + 1, :] == eid, logits, 0.0), axis=0, keepdims=True) for j in range(J)]
    v = jnp.concatenate(per, axis=0)
    e = jnp.exp(v - jnp.max(v, axis=0, keepdims=True))
    gate_ref[...] = e / jnp.sum(e, axis=0, keepdims=True)


SMALL = 640


def dma_sems(n):
    return [pltpu.SemaphoreType.DMA((n,)), pltpu.SemaphoreType.DMA((n,))]


def kernel_all(x_ref, cot_ref, gain_ref, fgain_ref, kvw_ref, rw_ref, rt_ref, seg_ref, wq_in, wo_in, up_hbm, down_hbm,
               out_ref, ing_ref, all_ref, dwo_ref, dwq_ref, small_ref,
               up_ref, down_ref, wsem, normed_ref, gate_ref, kv_ref, wq_ref, wo_ref, att_ref, qt_ref, table, kaug, vaug, vt, macc, acc,
               rows, gat, gm_ref, gn_ref, drw_ref, dfg_ref, big, r0, r1, r2, r3,
               dat_ref, qa, da, dqacc, tot, gsend, grecv, lbig, l0, l1, l2, l3, ssrc, shalf, s0, s1, sy, sz, send, recv, ksend, krecv):
    place = Place()
    me, core = place.ex, place.at["c"]
    dp = lax.axis_index("dp")
    copies = Copies(place, send, recv)
    gq, gk, go = Gather(copies, wq_ref), Gather(copies, kv_ref), Gather(copies, wo_ref)
    big7 = big.reshape(2, UNITS, 4, 4, 4, 16, 128)
    lbig7 = lbig.reshape(2, 3, 4, 4, 4, 16, 128)
    early = [Scatter(copies, big7, (r0, r1, r2, r3), parts, o) for parts, o in zip(BATCHES, ORDERS)]
    late = [Scatter(copies, lbig7, (l0, l1, l2, l3), [(u, u + 1)], o) for u, o in enumerate(ORDERS)]
    spreads = [Spread(copies, all_ref, u0, u1, o) for (u0, u1), o in zip(ALL_BATCHES, ORDERS)]
    plane_o = SpreadPlane(copies, dwo_ref, 0, 3)
    plane_q = SpreadPlane(copies, dwq_ref, 0, 3)
    small = SmallSum(copies, ssrc, shalf, s0, s1, sy, sz, small_ref)

    bar = pltpu.get_barrier_semaphore()
    for p in ALL_PEERS:
        pl.semaphore_signal(bar, inc=1, device_id=place.peers[p], device_id_type=MESH)
    for k in range(1, NB):
        pl.semaphore_signal(bar, inc=1, device_id=(dp, (me + k) % NB), device_id_type=MESH)
    loads = [pltpu.make_async_copy(up_hbm, up_ref, wsem.at[0]), pltpu.make_async_copy(down_hbm, down_ref, wsem.at[1])]
    for cp in loads:
        cp.start()
    wq_ref[me] = wq_in[...]
    wo_ref[me] = wo_in[...]
    pl.semaphore_wait(bar, len(ALL_PEERS) + NB - 1)
    gq.start()

    x = x_ref[...].astype(f32)
    inv = lax.rsqrt(jnp.mean(x * x, axis=-1, keepdims=True) + eps)
    normed = (x * inv * gain_ref[...]).astype(bf16)
    normed_ref[...] = normed
    kv_ref[me, 0:T, :] = nn(normed, kvw_ref[...]).astype(bf16)
    seg = seg_ref[...]
    row = lax.broadcasted_iota(i32, (16, 128), 0)
    tail = jnp.zeros((16, 128), f32)
    for s in range(2):
        n = jnp.sum(jnp.sum((seg <= s).astype(f32), axis=0, keepdims=True), axis=1, keepdims=True)
        n = jnp.broadcast_to(n, (16, 128))
        hi = jnp.floor(n * 0.0625)
        tail = jnp.where(row == 2 * s, hi, jnp.where(row == 2 * s + 1, n - 16.0 * hi, tail))
    kv_ref[me, T:KVR, :] = tail.astype(bf16)
    gk.start()
    gates_of(normed, rw_ref, rt_ref, gate_ref)
    gq.forward()
    go.start()
    gk.forward()
    gq.finish()
    project_queries(normed, wq_ref, table)
    gk.finish()
    bounds = bounds_of(kv_ref)
    prepare_keys(kv_ref, bounds, kaug, vaug, vt)
    pick_queries(rt_ref, bounds, me, table, qt_ref)
    attend(me, qt_ref, kaug, vt, att_ref, macc, acc)

    go.forward()
    routes = route_rows(rt_ref)
    for j in range(J):
        rows[j] = sub8(att_ref[:, j * T : (j + 1) * T].astype(f32) * gate_ref[j : j + 1, :])
    to_experts(routes, rows, gat)
    go.finish()
    x = x_ref[...].astype(f32)
    wo_all = wo_ref[...].reshape(EW, D)
    mixed = x + tn(gat[...], wo_all)
    inv = lax.rsqrt(jnp.mean(mixed * mixed, axis=-1, keepdims=True) + eps)
    n = mixed * inv
    fgain = fgain_ref[...]
    second = (n * fgain).astype(bf16)
    second_t = jnp.transpose(n * fgain).astype(bf16)
    cot = cot_ref[...]
    for cp in loads:
        cp.wait()
    C = 512
    out = mixed
    gsec = jnp.zeros((T, D), f32)
    for c in range(FF // C):
        cs = slice(c * C, (c + 1) * C)
        v = nn(second, up_ref[:, cs])
        v2 = v * v
        th = jnp.tanh(0.7978845608028654 * (v + 0.044715 * v * v2))
        a = (0.5 * v * (1.0 + th)).astype(bf16)
        dth = 0.5 * (1.0 + th) + 0.5 * v * (1.0 - th * th) * (0.7978845608028654 * (1.0 + 0.134145 * v2))
        gh = (nt(cot, down_ref[cs, :]) * dth).astype(bf16)
        out = out + nn(a, down_ref[cs, :])
        gsec = gsec + nt(gh, up_ref[:, cs])
        gdown = tn(a, cot).astype(bf16)
        gup = nn(second_t, gh).astype(bf16)
        for t in range(4):
            ts = slice(t * 128, (t + 1) * 128)
            big[(core + c // 2) % 2, DOWN_UNIT[t], c % 2 * C : c % 2 * C + C, :] = gdown[:, ts]
            big[(core + t // 2) % 2, UP_UNIT[c], t % 2 * 512 : t % 2 * 512 + 512, :] = gup[:, ts]
    for s in early:
        s.start_part(0)
    out_ref[...] = out.astype(bf16)
    dfg_ref[...] = jnp.sum(gsec * n, axis=0, keepdims=True)
    hh = gsec * fgain
    gm = cot.astype(f32) + inv * (hh - n * jnp.mean(hh * n, axis=-1, keepdims=True))
    gm_ref[...] = gm
    gml = gm.astype(bf16)
    for c in range(4):
        store_expert(big, core, WO_UNIT, 2 * c, nn(gat[c * 384 : (c + 1) * 384, :], gml))
    for s in early:
        s.start_part(1)
    for c in range(4):
        w = wo_ref[2 * c : 2 * c + 2].reshape(2 * 3 * H, D)
        table[c * 48 : (c + 1) * 48] = nt(w, gml).reshape(48, 8, T)
    dots = []
    row = lax.broadcasted_iota(i32, (H, T), 0)
    for j in range(J):
        js = slice(j * T, (j + 1) * T)
        g = choose(routes, table, j).reshape(H, T)
        gate = gate_ref[j : j + 1, :]
        dot = jnp.sum(g * att_ref[:, js].astype(f32), axis=0, keepdims=True)
        dots.append(dot)
        d1, d2, d3 = split3(-(dot * gate))
        dat_ref[0:H, js] = (g * gate).astype(bf16)
        dat_ref[H:, js] = jnp.where(row == 0, d1, jnp.where(row == 1, d2, jnp.where(row == 2, d3, 0.0))).astype(bf16)
    dots = jnp.concatenate(dots, axis=0)
    gates = gate_ref[...]
    chosen = gates * (dots - jnp.sum(gates * dots, axis=0, keepdims=True))
    eid = lax.broadcasted_iota(i32, (E, T), 0)
    gl = jnp.zeros((E, T), f32)
    for j in range(J):
        gl = jnp.where(rt_ref[j : j + 1, :] == eid, chosen[j : j + 1, :], gl)
    hi = gl.astype(bf16)
    lo = (gl - hi.astype(f32)).astype(bf16)
    rw = rw_ref[...]
    gn_ref[...] = tn(hi, rw) + tn(lo, rw)
    nm = normed_ref[...]
    drw_ref[...] = nn(hi, nm) + nn(lo, nm)

    for j in range(J):
        js = slice(j * T, (j + 1) * T)
        qa[js, :] = jnp.transpose(qt_ref[:, js].astype(f32)).astype(bf16)
        da[js, :] = jnp.transpose(dat_ref[:, js].astype(f32)).astype(bf16)
    for s in early:
        s.finish(0)
        s.start(1)
    dqacc[...] = jnp.zeros(dqacc.shape, f32)
    last = me // 2

    def half_block(sb, half, masked):
        ks = pl.ds(pl.multiple_of(sb * SB, SB), SB)

        @pl.when(half == 0)
        def _():
            tot[...] = jnp.zeros(tot.shape, f32)

        for i in range(2):
            gs = pl.ds(pl.multiple_of((half * 2 + i) * SB, SB), SB)
            p = jnp.exp(nt(qa[gs, :], kaug[ks, :]))
            if masked:
                ok = visible(me, sb)
                p = jnp.where(jnp.concatenate([ok, ok], axis=0), p, 0.0)
            ds = (p * nt(da[gs, :], vaug[ks, :])).astype(bf16)
            kv = jnp.concatenate([kv_ref[2 * sb, 0:T, :], kv_ref[2 * sb + 1, 0:T, :]], axis=0)
            dqacc[gs, :] += nn(ds, kv)
            tot[0:H, :] += nn(qt_ref[0:H, gs], ds)
            tot[H:, :] += nn(dat_ref[0:H, gs], p.astype(bf16))

        @pl.when(half == 1)
        def _():
            low = jnp.transpose(tot[...]).astype(bf16)
            gsend[2 * sb] = low[0:T]
            gsend[2 * sb + 1] = low[T:]

    def to_owner(kb):
        return pltpu.make_async_remote_copy(src_ref=gsend.at[kb], dst_ref=grecv.at[me], send_sem=ksend.at[kb],
                                            recv_sem=krecv.at[me], device_id=(dp, kb), device_id_type=MESH)

    def from_device(b):
        return pltpu.make_async_remote_copy(src_ref=gsend.at[b], dst_ref=grecv.at[b], send_sem=ksend.at[b],
                                            recv_sem=krecv.at[b], device_id=(dp, b), device_id_type=MESH)

    def level(i):
        for s in early:
            s.finish(i)
            if i < 3:
                s.start(i + 1)

    def share_start():
        for (u0, u1), s in zip(ALL_BATCHES, spreads):
            for u in range(u0, u1):
                real = sorted(UP_UNIT + DOWN_UNIT)[u]
                s.put(u, early[u // 3].result(real))
            s.start(3)
        for v in range(3):
            plane_o.put(v, early[v].result(WO_UNIT[v]))
        plane_o.start("y")

    def step(i, carry):
        sb, half = i // 2, i % 2

        @pl.when(sb < last)
        def _():
            half_block(sb, half, False)

            @pl.when(half == 1)
            def _():
                to_owner(2 * sb).start()
                to_owner(2 * sb + 1).start()

        for at, lv in ((3, 1), (4, 2), (5, 3)):
            @pl.when(i == at)
            def _(lv=lv):
                level(lv)
                if lv == 3:
                    share_start()

        return carry

    lax.fori_loop(0, 2 * (NSB - 1), step, 0)

    def last_step(half, carry):
        half_block(last, half, True)

        @pl.when(half == 0)
        def _():
            for s in spreads:
                s.finish(3)
                s.start(2)
            plane_o.finish("y")
            plane_o.start("x")

        return carry

    lax.fori_loop(0, 2, last_step, 0)

    @pl.when(2 * last < me)
    def _():
        to_owner(2 * last).start()

    for s in spreads:
        s.finish(2)
        s.start(1)
    plane_o.finish("x")
    for j in range(J):
        js = slice(j * T, (j + 1) * T)
        rows[j] = sub8(jnp.transpose(dqacc[js, :])[0:H].astype(bf16).astype(f32) * 0.125)
    to_experts(routes, rows, gat)
    for c in range(4):
        store_expert(lbig, core, [0, 1, 2], 2 * c, nn(gat[c * 384 : (c + 1) * 384, :], nm))
    for s in late:
        s.start(0)
    gkv = gsend[me].astype(f32)
    acc_kv = tot
    acc_kv[:, 0:T] = jnp.transpose(gkv)
    for b in range(1, NB):
        @pl.when(b > me)
        def _(b=b):
            from_device(b).wait_recv()
            acc_kv[:, 0:T] += jnp.transpose(grecv[b].astype(f32))
    gkv = jnp.transpose(acc_kv[:, 0:T]).astype(bf16)
    dkvw = tn(nm, gkv).astype(bf16)
    gn = gn_ref[...] + tn(gat[...], wq_ref[...].reshape(EW, D)) + nt(gkv, kvw_ref[...])
    x = x_ref[...].astype(f32)
    inv = lax.rsqrt(jnp.mean(x * x, axis=-1, keepdims=True) + eps)
    n = x * inv
    dgain = jnp.sum(gn * n, axis=0, keepdims=True)
    drw = drw_ref[...]
    dfg = dfg_ref[...]
    parts = [dkvw.astype(f32)] + [drw[:, t * 128 : (t + 1) * 128] for t in range(4)]
    parts += [v[:, t * 128 : (t + 1) * 128] for v in (dgain, dfg) for t in range(4)] + [jnp.zeros((SMALL - 616, 128), f32)]
    ssrc[...] = jnp.concatenate(parts, axis=0).astype(bf16).reshape(2, 4, SMALL // 8, 128)
    small.step(0)
    for s in late:
        s.finish(0)
        s.start(1)
    small.step(1)
    hh = gn * gain_ref[...]
    ing_ref[...] = (gm_ref[...] + inv * (hh - n * jnp.mean(hh * n, axis=-1, keepdims=True))).astype(bf16)
    small.step(2)
    for lv in (1, 2):
        for s in late:
            s.finish(lv)
            s.start(lv + 1)
        small.step(lv + 2)
    for s in late:
        s.finish(3)
    for v in range(3):
        plane_q.put(v, late[v].result(v))
    plane_q.start("y")
    for s in spreads:
        s.finish(1)
        s.start(0)
    small.step(5)
    plane_q.finish("y")
    plane_q.start("x")
    small.step(6)
    plane_q.finish("x")
    for s in spreads:
        s.finish(0)
    for b in range(NB - 1):
        @pl.when(b < me)
        def _(b=b):
            to_owner(b).wait_send()
    copies.drain()


SCRATCH = [
    VM((D, FF), bf16), VM((FF, D), bf16), pltpu.SemaphoreType.DMA((2,)), VM((T, D), bf16), VM((J, T), f32), VM((NB, KVR, 128), bf16),
    VM((NB, 3 * H, D), bf16), VM((NB, 3 * H, D), bf16), VM((H, ROWS), bf16), VM((128, ROWS), bf16), VM((EW // 8, 8, T), f32),
    VM((ROWS, 128), bf16), VM((ROWS, 128), bf16), VM((80, ROWS), bf16), VM((8, ROWS), f32), VM((80, ROWS), f32),
    VM((J, 8, 8, T), f32), VM((EW, T), bf16), VM((T, D), f32), VM((T, D), f32), VM((E, D), f32), VM((1, D), f32),
    VM((2, UNITS, 1024, 128), bf16), VM((UNITS, 4, 4, 4, 16, 128), bf16), VM((UNITS, 3, 4, 4, 16, 128), bf16),
    VM((UNITS, 3, 4, 16, 128), bf16), VM((UNITS, 3, 16, 128), bf16),
    VM((128, ROWS), bf16), VM((ROWS, 128), bf16), VM((ROWS, 128), bf16), VM((ROWS, 128), f32), VM((128, SB), f32),
    VM((NB, T, 128), bf16), VM((NB, T, 128), bf16),
    VM((2, 3, 1024, 128), bf16), VM((3, 4, 4, 4, 16, 128), bf16), VM((3, 3, 4, 4, 16, 128), bf16), VM((3, 3, 4, 16, 128), bf16),
    VM((3, 3, 16, 128), bf16),
    VM((2, 4, SMALL // 8, 128), bf16), VM((4, SMALL // 8, 128), bf16), VM((4, SMALL // 8, 128), bf16),
    VM((3, SMALL // 8, 128), bf16), VM((4, SMALL // 8, 128), bf16), VM((4, SMALL // 8, 128), bf16),
] + dma_sems(143) + dma_sems(NB)


def kernel_f(up_in, down_in, wo_ref, dwq_ref, small_ref, out_in, ing_in, dup_ref, ddown_ref, dwo_ref, dwqt_ref, dkvw_ref, drw_ref,
             dgain_ref, dfg_ref, out_ref, ing_ref):
    ddown_ref[...] = down_in[0].astype(f32)
    for s in range(4):
        dup_ref[:, s * 128 : (s + 1) * 128] = up_in[0, s * 512 : (s + 1) * 512, :].astype(f32)

    @pl.when(pl.program_id(0) == 0)
    def _():
        for t in range(4):
            ts = slice(t * 128, (t + 1) * 128)
            dwo_ref[:, ts] = wo_ref[t * 192 : (t + 1) * 192, :].astype(f32)
            dwqt_ref[:, ts] = dwq_ref[t * 192 : (t + 1) * 192, :].astype(f32)
        small = small_ref[512:SMALL, :].astype(f32)
        dkvw_ref[...] = small_ref[0:512, :].astype(f32)
        for t in range(4):
            ts = slice(t * 128, (t + 1) * 128)
            drw_ref[:, ts] = small[t * E : (t + 1) * E]
            dgain_ref[:, ts] = small[96 + t : 97 + t]
            dfg_ref[:, ts] = small[100 + t : 101 + t]
        out_ref[...] = out_in[...]
        ing_ref[...] = ing_in[...]


def per_device(inputs, cotangent, norm_gain, ffn_gain, kv_weight, router_weight, query_weight, output_weight, up_weight,
               down_weight, routes, segment_ids):
    wq = jnp.swapaxes(query_weight, 1, 2).reshape(3 * H, D)
    wo = output_weight.reshape(3 * H, D)
    vmem, anywhere = pl.BlockSpec(memory_space=VM), pl.BlockSpec(memory_space=pl.ANY)
    S = jax.ShapeDtypeStruct
    out, ing, shared, dwo, dwq, small = pl.pallas_call(
        kernel_all,
        out_shape=[S((T, D), bf16), S((T, D), bf16), S((8, 2, 4, 4, 4, 16, 128), bf16), S((3, 4, 4, 16, 128), bf16),
                   S((3, 4, 4, 16, 128), bf16), S((2, 4, SMALL // 8, 128), bf16)],
        in_specs=[vmem] * 10 + [anywhere] * 2,
        out_specs=[vmem] * 6,
        scratch_shapes=SCRATCH,
        compiler_params=pltpu.CompilerParams(vmem_limit_bytes=62 << 20, collective_id=1, has_side_effects=True),
        cost_estimate=pl.CostEstimate(flops=1 << 35, bytes_accessed=1 << 24, transcendentals=0),
    )(inputs, cotangent, norm_gain.reshape(1, D), ffn_gain.reshape(1, D), kv_weight, router_weight.T, routes.T,
      segment_ids.reshape(3, 128), wq, wo, up_weight, down_weight)
    shared = shared.reshape(8, 2048, 128)

    def whole(*shape):
        return pl.BlockSpec(shape, lambda i: (0,) * len(shape))

    dup, ddown, dwo, dwqt, dkvw, drw, dgain, dfg, out, ing = pl.pallas_call(
        kernel_f,
        grid=(4,),
        out_shape=[S((D, FF), f32), S((FF, D), f32), S((3 * H, D), f32), S((3 * H, D), f32), S((D, 128), f32), S((E, D), f32),
                   S((1, D), f32), S((1, D), f32), S((T, D), bf16), S((T, D), bf16)],
        in_specs=[pl.BlockSpec((1, 2048, 128), lambda i: (i, 0, 0)), pl.BlockSpec((1, 2048, 128), lambda i: (4 + i, 0, 0)),
                  whole(768, 128), whole(768, 128), whole(SMALL, 128), whole(T, D), whole(T, D)],
        out_specs=[pl.BlockSpec((D, 512), lambda i: (0, i)), pl.BlockSpec((FF, 128), lambda i: (0, i)), whole(3 * H, D),
                   whole(3 * H, D), whole(D, 128), whole(E, D), whole(1, D), whole(1, D), whole(T, D), whole(T, D)],
        compiler_params=pltpu.CompilerParams(vmem_limit_bytes=40 << 20),
    )(shared, shared, dwo.reshape(768, 128), dwq.reshape(768, 128), small.reshape(SMALL, 128), out, ing)
    return (out, ing, dgain.reshape(D), dfg.reshape(D), dkvw, drw.T,
            jnp.swapaxes(dwqt.reshape(3, H, D), 1, 2), dwo.reshape(3, H, D), dup, ddown)


def solution(mesh):
    both = P(("dp", "expert"), None)
    ex = P("expert", None, None)
    return jax.shard_map(
        per_device, mesh=mesh,
        in_specs=(both, both, P(), P(), P(), P(), ex, ex, P(), P(), both, P(("dp", "expert"))),
        out_specs=(both, both, P(), P(), P(), P(), ex, ex, P(), P()),
        check_vma=False)
```

```python
import functools
import jax
import jax.numpy as jnp
from jax import lax
from jax.experimental import pallas as pl
from jax.experimental.pallas import tpu as pltpu
from jax.sharding import PartitionSpec as P

f32, bf16, i32 = jnp.float32, jnp.bfloat16, jnp.int32
T, D, H, J, E, FF, NB = 384, 512, 64, 8, 24, 2048, 8
EW = E * H
ROWS = J * T
SB = 2 * T
NSB = NB // 2
eps = 1e-06
NEG = -1e30
VM = pltpu.VMEM


def nn(a, b):
    return lax.dot_general(a, b, (((1,), (0,)), ((), ())), preferred_element_type=f32)


def nt(a, b):
    return lax.dot_general(a, b, (((1,), (1,)), ((), ())), preferred_element_type=f32)


def tn(a, b):
    return lax.dot_general(a, b, (((0,), (0,)), ((), ())), preferred_element_type=f32)


def lanes(rows):
    return lax.broadcasted_iota(i32, (rows, 128), 1)


def split3(v):
    a = v.astype(bf16).astype(f32)
    b = (v - a).astype(bf16).astype(f32)
    c = (v - a - b).astype(bf16).astype(f32)
    return a, b, c


MESH = pl.DeviceIdType.MESH
LINES = [(a, k) for a in "xyz" for k in (1, 2, 3)]
ALL_PEERS = [("c", 0)] + LINES


class Place:
    def __init__(self):
        dp, ex = lax.axis_index("dp"), lax.axis_index("expert")
        self.ex = ex
        self.at = {"x": dp // 4, "y": dp % 4, "z": ex // 2, "c": ex % 2}
        self.peers = {("c", 0): self.device(c=1 - self.at["c"])}
        for axis, k in LINES:
            self.peers[axis, k] = self.device(**{axis: (self.at[axis] + k) % 4})

    def device(self, **moved):
        at = {**self.at, **moved}
        return (at["x"] * 4 + at["y"], at["z"] * 2 + at["c"])

    def enter(self, peers):
        bar = pltpu.get_barrier_semaphore()
        for p in peers:
            pl.semaphore_signal(bar, inc=1, device_id=self.peers[p], device_id_type=MESH)
        pl.semaphore_wait(bar, len(peers))


class Copies:
    def __init__(self, place, send, recv):
        self.place, self.send, self.recv, self.made = place, send, recv, []

    def add(self, src, dst, peer):
        self.made.append((src, dst, peer))
        return len(self.made) - 1

    def get(self, i):
        src, dst, peer = self.made[i]
        return pltpu.make_async_remote_copy(src_ref=src(), dst_ref=dst(), send_sem=self.send.at[i], recv_sem=self.recv.at[i],
                                            device_id=self.place.peers[peer], device_id_type=MESH)

    def start(self, ids):
        for i in ids:
            self.get(i).start()

    def arrived(self, ids):
        for i in ids:
            self.get(i).wait_recv()

    def sent(self, ids):
        for i in ids:
            self.get(i).wait_send()

    def drain(self):
        self.sent(range(len(self.made)))


class Scatter:
    def __init__(self, copies, big, r, parts, order):
        self.cp, self.big, self.r = copies, big, r
        self.u0, self.u1 = parts[0][0], parts[-1][1]
        at = copies.place.at
        self.m = [at[a] for a in order]
        us = pl.ds(self.u0, self.u1 - self.u0)
        self.part_ids = [
            copies.add(lambda s=s: big.at[1, pl.ds(s[0], s[1] - s[0])], lambda s=s: r[0].at[pl.ds(s[0], s[1] - s[0])], ("c", 0))
            for s in parts]
        self.ids = [self.part_ids]
        for level in (1, 2, 3):
            def piece(k, level=level):
                pre = tuple(self.m[: level - 1])
                return big.at[(0, us) + pre + ((self.m[level - 1] + k) % 4,)]
            self.ids.append([
                copies.add(functools.partial(piece, k), lambda k=k, level=level: r[level].at[us, k - 1], (order[level - 1], k))
                for k in (1, 2, 3)])

    def start_part(self, i):
        self.cp.start([self.part_ids[i]])

    def start(self, level):
        self.cp.start(self.ids[level])

    def finish(self, level):
        self.cp.arrived(self.ids[level])
        for u in range(self.u0, self.u1):
            if level == 0:
                for a in range(4):
                    v = self.big[0, u, a].astype(f32) + self.r[0][u, a].astype(f32)
                    self.big[0, u, a] = v.astype(bf16)
                continue
            at = (0, u) + tuple(self.m[:level])
            v = self.big[at].astype(f32)
            for k in range(3):
                v = v + self.r[level][u, k].astype(f32)
            self.big[at] = v.astype(bf16)

    def result(self, u):
        return self.big[(0, u) + tuple(self.m)]


class Spread:
    def __init__(self, copies, out, u0, u1, order):
        self.cp, self.out = copies, out
        at = copies.place.at
        self.c, self.m = at["c"], [at[a] for a in order]
        us = pl.ds(u0, u1 - u0)
        self.ids = []
        for level in range(4):
            ref = lambda level=level: out.at[(us, self.c) + tuple(self.m[:level])]
            piece = lambda k=0: out.at[us, self.c, (self.m[0] - k + 4) % 4]
            if level == 0:
                self.ids.append([copies.add(lambda k=k: piece(k), lambda k=k: piece(k), ("c", 0)) for k in range(4)])
            else:
                self.ids.append([copies.add(ref, ref, (order[level - 1], k)) for k in (1, 2, 3)])

    def put(self, u, value):
        self.out[(u, self.c) + tuple(self.m)] = value

    def start(self, level):
        self.cp.start(self.ids[level])
        if level == 1:
            self.cp.start(self.ids[0][:1])

    def forward(self, k):
        self.cp.arrived(self.ids[1][k - 1 : k])
        self.cp.start(self.ids[0][k : k + 1])

    def finish(self, level):
        self.cp.arrived(self.ids[level])


class SpreadPlane:
    def __init__(self, copies, out, u0, u1):
        self.cp, self.out = copies, out
        self.x, self.y = copies.place.at["x"], copies.place.at["y"]
        us = pl.ds(u0, u1 - u0)
        one = lambda: out.at[us, self.x, self.y]
        row = lambda: out.at[us, self.x]
        self.ids = {"y": [copies.add(one, one, ("y", k)) for k in (1, 2, 3)],
                    "x": [copies.add(row, row, ("x", k)) for k in (1, 2, 3)]}

    def put(self, u, value):
        self.out[u, self.x, self.y] = value

    def start(self, axis):
        self.cp.start(self.ids[axis])

    def finish(self, axis):
        self.cp.arrived(self.ids[axis])


class SmallSum:
    def __init__(self, copies, src, half, r0, r1, by, bz, out):
        self.cp, self.src, self.half, self.r0, self.r1, self.by, self.bz, self.out = copies, src, half, r0, r1, by, bz, out
        at = copies.place.at
        self.c, self.x, self.y, self.z = at["c"], at["x"], at["y"], at["z"]
        own_half = lambda: out.at[self.c]
        own = lambda: out.at[self.c, self.x]
        self.ids = [
            [copies.add(lambda: src.at[1 - self.c], lambda: r0, ("c", 0))],
            [copies.add(lambda k=k: half.at[(self.x + k) % 4], lambda k=k: r1.at[k - 1], ("x", k)) for k in (1, 2, 3)],
            [copies.add(lambda: by.at[self.y], lambda: by.at[self.y], ("y", k)) for k in (1, 2, 3)],
            [copies.add(lambda: bz.at[self.z], lambda: bz.at[self.z], ("z", k)) for k in (1, 2, 3)],
            [copies.add(own, own, ("x", k)) for k in (1, 2, 3)],
            [copies.add(own_half, own_half, ("c", 0))],
        ]

    def step(self, i):
        if i:
            self.cp.arrived(self.ids[i - 1])
        if i == 1:
            for a in range(4):
                self.half[a] = (self.src[self.c, a].astype(f32) + self.r0[a].astype(f32)).astype(bf16)
        if i == 2:
            v = self.half[self.x].astype(f32)
            for k in range(3):
                v = v + self.r1[k].astype(f32)
            self.by[self.y] = v.astype(bf16)
        if i in (3, 4):
            b = self.by if i == 3 else self.bz
            v = (b[0].astype(f32) + b[1].astype(f32) + b[2].astype(f32) + b[3].astype(f32)).astype(bf16)
            if i == 3:
                self.bz[self.z] = v
            else:
                self.out[self.c, self.x] = v
        if i < 6:
            self.cp.start(self.ids[i])


ORDERS = ["xyz", "yzx", "zxy"]
BATCHES = [[(0, 1), (1, 2), (2, 3), (3, 4)], [(4, 5), (5, 7), (7, 8)], [(8, 10), (10, 11)]]
UP_PART, DOWN_PARTS, WO_PARTS = [(0, 0), (0, 1), (0, 2), (1, 0)], [(1, 1), (2, 0)], [(0, 3), (1, 2), (2, 1)]
ALL_BATCHES = [(0, 3), (3, 6), (6, 8)]
UP_UNIT, DOWN_UNIT, WO_UNIT = [0, 1, 2, 4], [5, 6, 8, 9], [3, 7, 10]
UNITS = 11
STEPS = [(u, i) for i, u in enumerate(sorted(UP_UNIT + DOWN_UNIT))]


def expert_row(ex, piece, order):
    at = {"x": piece // 4, "y": piece % 4, "z": ex // 2}
    r = ex % 2
    for a in order:
        r = r * 4 + at[a]
    return r * 16


def store_expert(big, core, units, ex0, value):
    low = value.astype(bf16)
    for o in range(2):
        slot = (core + (ex0 + o) % 2) % 2
        for row in range(0, 768, 16):
            v, piece = row // 256, (row % 256) // 16
            ct, r = row // 192, row % 192
            base = expert_row(ex0 + o, piece, ORDERS[v]) % 1024
            big[slot, units[v], base : base + 16, :] = low[o * 192 + r : o * 192 + r + 16, ct * 128 : (ct + 1) * 128]


KVR = T + 16


class Gather:
    def __init__(self, copies, out):
        self.cp, self.out = copies, out
        at, ex = copies.place.at, copies.place.ex
        own = lambda: out.at[ex]
        from_z = lambda k: out.at[((at["z"] - k + 4) % 4) * 2 + at["c"]]
        self.line = [copies.add(own, own, ("z", k)) for k in (1, 2, 3)]
        self.core = [copies.add(functools.partial(from_z, k), functools.partial(from_z, k), ("c", 0)) for k in (0, 1, 2, 3)]

    def start(self):
        self.cp.start(self.line)
        self.cp.start(self.core[:1])

    def forward(self):
        for k in range(3):
            self.cp.arrived(self.line[k : k + 1])
            self.cp.start(self.core[k + 1 : k + 2])

    def finish(self):
        self.cp.arrived(self.core)


def bounds_of(kv_ref):
    n0 = n1 = 0.0
    for b in range(NB):
        tail = kv_ref[b, T:KVR, :].astype(f32)
        n0 = n0 + 16.0 * tail[0:1] + tail[1:2]
        n1 = n1 + 16.0 * tail[2:3] + tail[3:4]
    return n0, n1


def segment_of(pos, bounds):
    return (pos >= bounds[0]).astype(i32) + (pos >= bounds[1]).astype(i32)


def sub8(v):
    return v.reshape(8, 8, v.shape[-1])


def route_rows(rt_ref):
    return [jnp.broadcast_to(rt_ref[j : j + 1, :], (8, T)) for j in range(J)]


def visible(me, sb):
    key = lax.broadcasted_iota(i32, (T, SB), 1)
    tok = lax.broadcasted_iota(i32, (T, SB), 0)
    ok = key - tok <= (me - 2 * sb) * T
    return ok


def prepare_keys(kv_ref, bounds, kaug, vaug, vt):
    ln = lanes(T)
    for b in range(NB):
        bs = slice(b * T, (b + 1) * T)
        kv = kv_ref[b, 0:T, :].astype(f32)
        pos = (lax.broadcasted_iota(i32, (T, 128), 0) + b * T).astype(f32)
        seg = segment_of(pos, bounds)
        feat = jnp.where((ln < H + 3) & (seg != ln - H), NEG, 0.0)
        feat = jnp.where((ln >= H + 3) & (ln < H + 6), 1.0, feat)
        kaug[bs, :] = jnp.where(ln < H, kv, feat).astype(bf16)
        if vaug is not None:
            one = jnp.where(ln < H + 3, 1.0, 0.0)
            vaug[bs, :] = jnp.where(ln < H, pltpu.roll(kv, H, 1), one).astype(bf16)
        if vt is not None:
            ones = jnp.where(lax.broadcasted_iota(i32, (16, T), 0) == 0, 1.0, 0.0)
            vt[:, bs] = jnp.concatenate([jnp.transpose(kv)[H:], ones], axis=0).astype(bf16)


def project_queries(normed, wq_ref, qall):
    for c in range(4):
        w = wq_ref[2 * c : 2 * c + 2].reshape(2 * 3 * H, D)
        qall[c * 48 : (c + 1) * 48] = (nt(w, normed) * 0.125).reshape(48, 8, T)


def choose(routes, table, j):
    acc = table[0:8]
    for e in range(1, E):
        acc = jnp.where((routes[j] == e)[None], table[e * 8 : (e + 1) * 8], acc)
    return acc


def to_experts(routes, rows, out):
    for e in range(E):
        acc = jnp.zeros((8, 8, T), f32)
        for j in range(J):
            acc = jnp.where((routes[j] == e)[None], rows[j], acc)
        out[e * H : (e + 1) * H, :] = acc.reshape(H, T).astype(bf16)


def pick_queries(rt_ref, table, qt):
    routes = route_rows(rt_ref)
    for j in range(J):
        qt[0:H, j * T : (j + 1) * T] = choose(routes, table, j).reshape(H, T).astype(bf16)


def mark_queries(bounds, me, qt):
    pos = (lax.broadcasted_iota(i32, (H, T), 1) + me * T).astype(f32)
    seg = segment_of(pos, (bounds[0][:, 0:1], bounds[1][:, 0:1]))
    feat = jnp.where(lax.broadcasted_iota(i32, (H, T), 0) == seg, 1.0, 0.0).astype(bf16)
    for j in range(J):
        qt[H:, j * T : (j + 1) * T] = feat


def attend(me, qt, kaug, vt, att, macc, acc):
    last = me // 2
    macc[...] = jnp.full(macc.shape, NEG, f32)
    acc[...] = jnp.zeros(acc.shape, f32)

    def score(sb, g, masked):
        s = nn(kaug[pl.ds(pl.multiple_of(sb * SB, SB), SB), :], qt[:, g * SB : (g + 1) * SB])
        if masked:
            key = lax.broadcasted_iota(i32, (SB, T), 0)
            tok = lax.broadcasted_iota(i32, (SB, T), 1)
            ok = key - tok <= (me - 2 * sb) * T
            s = jnp.where(jnp.concatenate([ok, ok], axis=1), s, NEG)
        return s.reshape(SB // 8, 8, SB)

    def soften(s, g):
        gs = slice(g * SB, (g + 1) * SB)
        old = macc[:, gs]
        top = jnp.max(jnp.maximum(old, jnp.max(s, axis=0)), axis=0, keepdims=True)
        top = jnp.broadcast_to(top, (8, SB))
        macc[:, gs] = top
        return jnp.exp(s - top[None]).reshape(SB, SB).astype(bf16), jnp.exp(old - top)

    def weigh(sb, g, p, kept):
        gs = slice(g * SB, (g + 1) * SB)
        old = acc[:, gs].reshape(10, 8, SB) * kept[None]
        acc[:, gs] = old.reshape(80, SB) + nn(vt[:, pl.ds(pl.multiple_of(sb * SB, SB), SB)], p)

    def block(sb, masked):
        s = score(sb, 0, masked)
        held = None
        for g in range(J // 2):
            ahead = score(sb, g + 1, masked) if g + 1 < J // 2 else None
            new = soften(s, g)
            if g:
                weigh(sb, g - 1, *held)
            held, s = new, ahead
        weigh(sb, J // 2 - 1, *held)

    lax.fori_loop(0, last, lambda sb, c: (block(sb, False), c)[1], 0)
    block(last, True)
    for g in range(J // 2):
        gs = slice(g * SB, (g + 1) * SB)
        tot = acc[H : H + 1, gs]
        att[:, gs] = (acc[0:H, gs] / tot).astype(bf16)
        l1, l2, l3 = split3(-(macc[0:1, gs] + jnp.log(tot)))
        row = lax.broadcasted_iota(i32, (16, SB), 0)
        feat = qt[H : H + 16, gs].astype(f32)
        feat = jnp.where(row == 3, l1, jnp.where(row == 4, l2, jnp.where(row == 5, l3, feat)))
        qt[H : H + 16, gs] = feat.astype(bf16)


def gates_of(normed, rw_ref, rt_ref, gate_ref):
    logits = nt(rw_ref[...], normed)
    eid = lax.broadcasted_iota(i32, (E, T), 0)
    per = [jnp.sum(jnp.where(rt_ref[j : j + 1, :] == eid, logits, 0.0), axis=0, keepdims=True) for j in range(J)]
    v = jnp.concatenate(per, axis=0)
    e = jnp.exp(v - jnp.max(v, axis=0, keepdims=True))
    gate_ref[...] = e / jnp.sum(e, axis=0, keepdims=True)


SMALL = 640


def dma_sems(n):
    return [pltpu.SemaphoreType.DMA((n,)), pltpu.SemaphoreType.DMA((n,))]


def kernel_all(x_ref, cot_ref, gain_ref, fgain_ref, kvw_ref, rw_ref, rt_ref, seg_ref, wq_in, wo_in, up_hbm, down_hbm,
               out_ref, ing_ref, all_ref, dwo_ref, dwq_ref, small_ref,
               up_ref, down_ref, wsem, normed_ref, gate_ref, kv_ref, wq_ref, wo_ref, att_ref, qt_ref, table, kaug, vaug, vt, macc, acc,
               rows, gat, gm_ref, gn_ref, drw_ref, dfg_ref, big, r0, r1, r2, r3,
               dat_ref, qa, da, dqacc, tot, gsend, grecv, lbig, l0, l1, l2, l3, ssrc, shalf, s0, s1, sy, sz, send, recv, ksend, krecv):
    place = Place()
    me, core = place.ex, place.at["c"]
    dp = lax.axis_index("dp")
    copies = Copies(place, send, recv)
    gq, gk, go = Gather(copies, wq_ref), Gather(copies, kv_ref), Gather(copies, wo_ref)
    big7 = big.reshape(2, UNITS, 4, 4, 4, 16, 128)
    lbig7 = lbig.reshape(2, 3, 4, 4, 4, 16, 128)
    early = [Scatter(copies, big7, (r0, r1, r2, r3), parts, o) for parts, o in zip(BATCHES, ORDERS)]
    late = [Scatter(copies, lbig7, (l0, l1, l2, l3), [(u, u + 1)], o) for u, o in enumerate(ORDERS)]
    spreads = [Spread(copies, all_ref, u0, u1, o) for (u0, u1), o in zip(ALL_BATCHES, ORDERS)]
    plane_o = SpreadPlane(copies, dwo_ref, 0, 3)
    plane_q = SpreadPlane(copies, dwq_ref, 0, 3)
    small = SmallSum(copies, ssrc, shalf, s0, s1, sy, sz, small_ref)

    bar = pltpu.get_barrier_semaphore()
    for p in ALL_PEERS:
        pl.semaphore_signal(bar, inc=1, device_id=place.peers[p], device_id_type=MESH)
    for k in range(1, NB):
        pl.semaphore_signal(bar, inc=1, device_id=(dp, (me + k) % NB), device_id_type=MESH)
    loads = [pltpu.make_async_copy(up_hbm, up_ref, wsem.at[0]), pltpu.make_async_copy(down_hbm, down_ref, wsem.at[1])]
    for cp in loads:
        cp.start()
    wq_ref[me] = wq_in[...]
    wo_ref[me] = wo_in[...]
    pl.semaphore_wait(bar, len(ALL_PEERS) + NB - 1)
    gq.start()

    x = x_ref[...].astype(f32)
    inv = lax.rsqrt(jnp.mean(x * x, axis=-1, keepdims=True) + eps)
    normed = (x * inv * gain_ref[...]).astype(bf16)
    normed_ref[...] = normed
    kv_ref[me, 0:T, :] = nn(normed, kvw_ref[...]).astype(bf16)
    seg = seg_ref[...]
    row = lax.broadcasted_iota(i32, (16, 128), 0)
    tail = jnp.zeros((16, 128), f32)
    for s in range(2):
        n = jnp.sum(jnp.sum((seg <= s).astype(f32), axis=0, keepdims=True), axis=1, keepdims=True)
        n = jnp.broadcast_to(n, (16, 128))
        hi = jnp.floor(n * 0.0625)
        tail = jnp.where(row == 2 * s, hi, jnp.where(row == 2 * s + 1, n - 16.0 * hi, tail))
    kv_ref[me, T:KVR, :] = tail.astype(bf16)
    gk.start()
    gates_of(normed, rw_ref, rt_ref, gate_ref)
    gq.forward()
    gq.finish()
    project_queries(normed, wq_ref, table)
    pick_queries(rt_ref, table, qt_ref)
    gk.forward()
    gk.finish()
    bounds = bounds_of(kv_ref)
    prepare_keys(kv_ref, bounds, kaug, vaug, vt)
    mark_queries(bounds, me, qt_ref)
    go.start()
    attend(me, qt_ref, kaug, vt, att_ref, macc, acc)

    go.forward()
    routes = route_rows(rt_ref)
    for j in range(J):
        rows[j] = sub8(att_ref[:, j * T : (j + 1) * T].astype(f32) * gate_ref[j : j + 1, :])
    to_experts(routes, rows, gat)
    go.finish()
    x = x_ref[...].astype(f32)
    wo_all = wo_ref[...].reshape(EW, D)
    mixed = x + tn(gat[...], wo_all)
    inv = lax.rsqrt(jnp.mean(mixed * mixed, axis=-1, keepdims=True) + eps)
    n = mixed * inv
    fgain = fgain_ref[...]
    second = (n * fgain).astype(bf16)
    second_t = jnp.transpose(n * fgain).astype(bf16)
    cot = cot_ref[...]
    for cp in loads:
        cp.wait()
    C = 512
    out = mixed
    gsec = jnp.zeros((T, D), f32)
    for c in range(FF // C):
        cs = slice(c * C, (c + 1) * C)
        v = nn(second, up_ref[:, cs])
        v2 = v * v
        th = jnp.tanh(0.7978845608028654 * (v + 0.044715 * v * v2))
        a = (0.5 * v * (1.0 + th)).astype(bf16)
        dth = 0.5 * (1.0 + th) + 0.5 * v * (1.0 - th * th) * (0.7978845608028654 * (1.0 + 0.134145 * v2))
        gh = (nt(cot, down_ref[cs, :]) * dth).astype(bf16)
        out = out + nn(a, down_ref[cs, :])
        gsec = gsec + nt(gh, up_ref[:, cs])
        gdown = tn(a, cot).astype(bf16)
        gup = nn(second_t, gh).astype(bf16)
        for t in range(4):
            ts = slice(t * 128, (t + 1) * 128)
            big[(core + c // 2) % 2, DOWN_UNIT[t], c % 2 * C : c % 2 * C + C, :] = gdown[:, ts]
            big[(core + t // 2) % 2, UP_UNIT[c], t % 2 * 512 : t % 2 * 512 + 512, :] = gup[:, ts]
        early[UP_PART[c][0]].start_part(UP_PART[c][1])
    for b, i in DOWN_PARTS:
        early[b].start_part(i)
    out_ref[...] = out.astype(bf16)
    dfg_ref[...] = jnp.sum(gsec * n, axis=0, keepdims=True)
    hh = gsec * fgain
    gm = cot.astype(f32) + inv * (hh - n * jnp.mean(hh * n, axis=-1, keepdims=True))
    gm_ref[...] = gm
    gml = gm.astype(bf16)
    for c in range(4):
        store_expert(big, core, WO_UNIT, 2 * c, nn(gat[c * 384 : (c + 1) * 384, :], gml))
    for b, i in WO_PARTS:
        early[b].start_part(i)
    for c in range(4):
        w = wo_ref[2 * c : 2 * c + 2].reshape(2 * 3 * H, D)
        table[c * 48 : (c + 1) * 48] = nt(w, gml).reshape(48, 8, T)
    dots = []
    row = lax.broadcasted_iota(i32, (H, T), 0)
    for j in range(J):
        js = slice(j * T, (j + 1) * T)
        g = choose(routes, table, j).reshape(H, T)
        gate = gate_ref[j : j + 1, :]
        dot = jnp.sum(g * att_ref[:, js].astype(f32), axis=0, keepdims=True)
        dots.append(dot)
        d1, d2, d3 = split3(-(dot * gate))
        dat_ref[0:H, js] = (g * gate).astype(bf16)
        dat_ref[H:, js] = jnp.where(row == 0, d1, jnp.where(row == 1, d2, jnp.where(row == 2, d3, 0.0))).astype(bf16)
    dots = jnp.concatenate(dots, axis=0)
    gates = gate_ref[...]
    chosen = gates * (dots - jnp.sum(gates * dots, axis=0, keepdims=True))
    eid = lax.broadcasted_iota(i32, (E, T), 0)
    gl = jnp.zeros((E, T), f32)
    for j in range(J):
        gl = jnp.where(rt_ref[j : j + 1, :] == eid, chosen[j : j + 1, :], gl)
    hi = gl.astype(bf16)
    lo = (gl - hi.astype(f32)).astype(bf16)
    rw = rw_ref[...]
    gn_ref[...] = tn(hi, rw) + tn(lo, rw)
    nm = normed_ref[...]
    drw_ref[...] = nn(hi, nm) + nn(lo, nm)

    for j in range(J):
        js = slice(j * T, (j + 1) * T)
        qa[js, :] = jnp.transpose(qt_ref[:, js].astype(f32)).astype(bf16)
        da[js, :] = jnp.transpose(dat_ref[:, js].astype(f32)).astype(bf16)
    dqacc[...] = jnp.zeros(dqacc.shape, f32)
    last = me // 2

    def half_block(sb, half, masked):
        ks = pl.ds(pl.multiple_of(sb * SB, SB), SB)

        @pl.when(half == 0)
        def _():
            tot[...] = jnp.zeros(tot.shape, f32)

        for i in range(2):
            gs = pl.ds(pl.multiple_of((half * 2 + i) * SB, SB), SB)
            p = jnp.exp(nt(qa[gs, :], kaug[ks, :]))
            if masked:
                ok = visible(me, sb)
                p = jnp.where(jnp.concatenate([ok, ok], axis=0), p, 0.0)
            ds = (p * nt(da[gs, :], vaug[ks, :])).astype(bf16)
            kv = jnp.concatenate([kv_ref[2 * sb, 0:T, :], kv_ref[2 * sb + 1, 0:T, :]], axis=0)
            dqacc[gs, :] += nn(ds, kv)
            tot[0:H, :] += nn(qt_ref[0:H, gs], ds)
            tot[H:, :] += nn(dat_ref[0:H, gs], p.astype(bf16))

        @pl.when(half == 1)
        def _():
            low = jnp.transpose(tot[...]).astype(bf16)
            gsend[2 * sb] = low[0:T]
            gsend[2 * sb + 1] = low[T:]

    def to_owner(kb):
        return pltpu.make_async_remote_copy(src_ref=gsend.at[kb], dst_ref=grecv.at[me], send_sem=ksend.at[kb],
                                            recv_sem=krecv.at[me], device_id=(dp, kb), device_id_type=MESH)

    def from_device(b):
        return pltpu.make_async_remote_copy(src_ref=gsend.at[b], dst_ref=grecv.at[b], send_sem=ksend.at[b],
                                            recv_sem=krecv.at[b], device_id=(dp, b), device_id_type=MESH)

    def level(i):
        for s in early:
            s.finish(i)
            if i < 3:
                s.start(i + 1)

    def share_start():
        for (u0, u1), s in zip(ALL_BATCHES, spreads):
            for u in range(u0, u1):
                real = sorted(UP_UNIT + DOWN_UNIT)[u]
                s.put(u, early[u // 3].result(real))
            s.start(3)
        for v in range(3):
            plane_o.put(v, early[v].result(WO_UNIT[v]))
        plane_o.start("y")

    def step(i, carry):
        sb, half = i // 2, i % 2

        @pl.when(sb < last)
        def _():
            half_block(sb, half, False)

            @pl.when(half == 1)
            def _():
                to_owner(2 * sb).start()
                to_owner(2 * sb + 1).start()

        for at, lv in ((0, 0), (4, 1), (5, 2)):
            @pl.when(i == at)
            def _(lv=lv):
                level(lv)

        return carry

    lax.fori_loop(0, 2 * (NSB - 1), step, 0)

    def last_step(half, carry):
        half_block(last, half, True)

        @pl.when(half == 0)
        def _():
            level(3)
            share_start()

        return carry

    lax.fori_loop(0, 2, last_step, 0)

    @pl.when(2 * last < me)
    def _():
        to_owner(2 * last).start()

    for s in spreads:
        s.finish(3)
        s.start(2)
    plane_o.finish("y")
    plane_o.start("x")
    for j in range(J):
        js = slice(j * T, (j + 1) * T)
        rows[j] = sub8(jnp.transpose(dqacc[js, :])[0:H].astype(bf16).astype(f32) * 0.125)
    to_experts(routes, rows, gat)
    for c in range(4):
        store_expert(lbig, core, [0, 1, 2], 2 * c, nn(gat[c * 384 : (c + 1) * 384, :], nm))
    for s in late:
        s.start(0)
    acc_kv = tot
    acc_kv[:, 0:T] = jnp.transpose(gsend[me].astype(f32))
    for b in range(1, NB):
        @pl.when(b > me)
        def _(b=b):
            from_device(b).wait_recv()
            acc_kv[:, 0:T] += jnp.transpose(grecv[b].astype(f32))
    gkv = jnp.transpose(acc_kv[:, 0:T]).astype(bf16)
    dkvw = tn(nm, gkv).astype(bf16)
    for s in late:
        s.finish(0)
        s.start(1)
    for s in spreads:
        s.finish(2)
        s.start(1)
    plane_o.finish("x")
    gn = gn_ref[...] + tn(gat[...], wq_ref[...].reshape(EW, D)) + nt(gkv, kvw_ref[...])
    x = x_ref[...].astype(f32)
    inv = lax.rsqrt(jnp.mean(x * x, axis=-1, keepdims=True) + eps)
    n = x * inv
    dgain = jnp.sum(gn * n, axis=0, keepdims=True)
    drw = drw_ref[...]
    dfg = dfg_ref[...]
    parts = [dkvw.astype(f32)] + [drw[:, t * 128 : (t + 1) * 128] for t in range(4)]
    parts += [v[:, t * 128 : (t + 1) * 128] for v in (dgain, dfg) for t in range(4)] + [jnp.zeros((SMALL - 616, 128), f32)]
    ssrc[...] = jnp.concatenate(parts, axis=0).astype(bf16).reshape(2, 4, SMALL // 8, 128)
    small.step(0)
    for s in late:
        s.finish(1)
        s.start(2)
    small.step(1)
    hh = gn * gain_ref[...]
    ing_ref[...] = (gm_ref[...] + inv * (hh - n * jnp.mean(hh * n, axis=-1, keepdims=True))).astype(bf16)
    for s in late:
        s.finish(2)
        s.start(3)
    small.step(2)
    for s in late:
        s.finish(3)
    for v in range(3):
        plane_q.put(v, late[v].result(v))
    plane_q.start("y")
    small.step(3)
    for k in (1, 2, 3):
        for s in spreads:
            s.forward(k)
    plane_q.finish("y")
    plane_q.start("x")
    small.step(4)
    small.step(5)
    plane_q.finish("x")
    small.step(6)
    for s in spreads:
        s.finish(0)
    for b in range(NB - 1):
        @pl.when(b < me)
        def _(b=b):
            to_owner(b).wait_send()
    copies.drain()


SCRATCH = [
    VM((D, FF), bf16), VM((FF, D), bf16), pltpu.SemaphoreType.DMA((2,)), VM((T, D), bf16), VM((J, T), f32), VM((NB, KVR, 128), bf16),
    VM((NB, 3 * H, D), bf16), VM((NB, 3 * H, D), bf16), VM((H, ROWS), bf16), VM((128, ROWS), bf16), VM((EW // 8, 8, T), f32),
    VM((ROWS, 128), bf16), VM((ROWS, 128), bf16), VM((80, ROWS), bf16), VM((8, ROWS), f32), VM((80, ROWS), f32),
    VM((J, 8, 8, T), f32), VM((EW, T), bf16), VM((T, D), f32), VM((T, D), f32), VM((E, D), f32), VM((1, D), f32),
    VM((2, UNITS, 1024, 128), bf16), VM((UNITS, 4, 4, 4, 16, 128), bf16), VM((UNITS, 3, 4, 4, 16, 128), bf16),
    VM((UNITS, 3, 4, 16, 128), bf16), VM((UNITS, 3, 16, 128), bf16),
    VM((128, ROWS), bf16), VM((ROWS, 128), bf16), VM((ROWS, 128), bf16), VM((ROWS, 128), f32), VM((128, SB), f32),
    VM((NB, T, 128), bf16), VM((NB, T, 128), bf16),
    VM((2, 3, 1024, 128), bf16), VM((3, 4, 4, 4, 16, 128), bf16), VM((3, 3, 4, 4, 16, 128), bf16), VM((3, 3, 4, 16, 128), bf16),
    VM((3, 3, 16, 128), bf16),
    VM((2, 4, SMALL // 8, 128), bf16), VM((4, SMALL // 8, 128), bf16), VM((4, SMALL // 8, 128), bf16),
    VM((3, SMALL // 8, 128), bf16), VM((4, SMALL // 8, 128), bf16), VM((4, SMALL // 8, 128), bf16),
] + dma_sems(152) + dma_sems(NB)


def kernel_f(up_in, down_in, wo_ref, dwq_ref, small_ref, out_in, ing_in, dup_ref, ddown_ref, dwo_ref, dwqt_ref, dkvw_ref, drw_ref,
             dgain_ref, dfg_ref, out_ref, ing_ref):
    ddown_ref[...] = down_in[0].astype(f32)
    for s in range(4):
        dup_ref[:, s * 128 : (s + 1) * 128] = up_in[0, s * 512 : (s + 1) * 512, :].astype(f32)

    @pl.when(pl.program_id(0) == 0)
    def _():
        for t in range(4):
            ts = slice(t * 128, (t + 1) * 128)
            dwo_ref[:, ts] = wo_ref[t * 192 : (t + 1) * 192, :].astype(f32)
            dwqt_ref[:, ts] = dwq_ref[t * 192 : (t + 1) * 192, :].astype(f32)
        small = small_ref[512:SMALL, :].astype(f32)
        dkvw_ref[...] = small_ref[0:512, :].astype(f32)
        for t in range(4):
            ts = slice(t * 128, (t + 1) * 128)
            drw_ref[:, ts] = small[t * E : (t + 1) * E]
            dgain_ref[:, ts] = small[96 + t : 97 + t]
            dfg_ref[:, ts] = small[100 + t : 101 + t]
        out_ref[...] = out_in[...]
        ing_ref[...] = ing_in[...]


def per_device(inputs, cotangent, norm_gain, ffn_gain, kv_weight, router_weight, query_weight, output_weight, up_weight,
               down_weight, routes, segment_ids):
    wq = jnp.swapaxes(query_weight, 1, 2).reshape(3 * H, D)
    wo = output_weight.reshape(3 * H, D)
    vmem, anywhere = pl.BlockSpec(memory_space=VM), pl.BlockSpec(memory_space=pl.ANY)
    S = jax.ShapeDtypeStruct
    out, ing, shared, dwo, dwq, small = pl.pallas_call(
        kernel_all,
        out_shape=[S((T, D), bf16), S((T, D), bf16), S((8, 2, 4, 4, 4, 16, 128), bf16), S((3, 4, 4, 16, 128), bf16),
                   S((3, 4, 4, 16, 128), bf16), S((2, 4, SMALL // 8, 128), bf16)],
        in_specs=[vmem] * 10 + [anywhere] * 2,
        out_specs=[vmem] * 6,
        scratch_shapes=SCRATCH,
        compiler_params=pltpu.CompilerParams(vmem_limit_bytes=62 << 20, collective_id=1, has_side_effects=True),
        cost_estimate=pl.CostEstimate(flops=1 << 35, bytes_accessed=1 << 24, transcendentals=0),
    )(inputs, cotangent, norm_gain.reshape(1, D), ffn_gain.reshape(1, D), kv_weight, router_weight.T, routes.T,
      segment_ids.reshape(3, 128), wq, wo, up_weight, down_weight)
    shared = shared.reshape(8, 2048, 128)

    def whole(*shape):
        return pl.BlockSpec(shape, lambda i: (0,) * len(shape))

    dup, ddown, dwo, dwqt, dkvw, drw, dgain, dfg, out, ing = pl.pallas_call(
        kernel_f,
        grid=(4,),
        out_shape=[S((D, FF), f32), S((FF, D), f32), S((3 * H, D), f32), S((3 * H, D), f32), S((D, 128), f32), S((E, D), f32),
                   S((1, D), f32), S((1, D), f32), S((T, D), bf16), S((T, D), bf16)],
        in_specs=[pl.BlockSpec((1, 2048, 128), lambda i: (i, 0, 0)), pl.BlockSpec((1, 2048, 128), lambda i: (4 + i, 0, 0)),
                  whole(768, 128), whole(768, 128), whole(SMALL, 128), whole(T, D), whole(T, D)],
        out_specs=[pl.BlockSpec((D, 512), lambda i: (0, i)), pl.BlockSpec((FF, 128), lambda i: (0, i)), whole(3 * H, D),
                   whole(3 * H, D), whole(D, 128), whole(E, D), whole(1, D), whole(1, D), whole(T, D), whole(T, D)],
        compiler_params=pltpu.CompilerParams(vmem_limit_bytes=62 << 20),
    )(shared, shared, dwo.reshape(768, 128), dwq.reshape(768, 128), small.reshape(SMALL, 128), out, ing)
    return (out, ing, dgain.reshape(D), dfg.reshape(D), dkvw, drw.T,
            jnp.swapaxes(dwqt.reshape(3, H, D), 1, 2), dwo.reshape(3, H, D), dup, ddown)


def solution(mesh):
    both = P(("dp", "expert"), None)
    ex = P("expert", None, None)
    return jax.shard_map(
        per_device, mesh=mesh,
        in_specs=(both, both, P(), P(), P(), P(), ex, ex, P(), P(), both, P(("dp", "expert"))),
        out_specs=(both, both, P(), P(), P(), P(), ex, ex, P(), P()),
        check_vma=False)
```

```python
import functools
import jax
import jax.numpy as jnp
from jax import lax
from jax.experimental import pallas as pl
from jax.experimental.pallas import tpu as pltpu
from jax.sharding import PartitionSpec as P

f32, bf16, i32 = jnp.float32, jnp.bfloat16, jnp.int32
T, D, H, J, E, FF, NB = 384, 512, 64, 8, 24, 2048, 8
EW = E * H
ROWS = J * T
SB = 2 * T
NSB = NB // 2
eps = 1e-06
NEG = -1e30
VM = pltpu.VMEM


def nn(a, b):
    return lax.dot_general(a, b, (((1,), (0,)), ((), ())), preferred_element_type=f32)


def nt(a, b):
    return lax.dot_general(a, b, (((1,), (1,)), ((), ())), preferred_element_type=f32)


def tn(a, b):
    return lax.dot_general(a, b, (((0,), (0,)), ((), ())), preferred_element_type=f32)


def lanes(rows):
    return lax.broadcasted_iota(i32, (rows, 128), 1)


def split3(v):
    a = v.astype(bf16).astype(f32)
    b = (v - a).astype(bf16).astype(f32)
    c = (v - a - b).astype(bf16).astype(f32)
    return a, b, c


MESH = pl.DeviceIdType.MESH
LINES = [(a, k) for a in "xyz" for k in (1, 2, 3)]
ALL_PEERS = [("c", 0)] + LINES


class Place:
    def __init__(self):
        dp, ex = lax.axis_index("dp"), lax.axis_index("expert")
        self.ex = ex
        self.at = {"x": dp // 4, "y": dp % 4, "z": ex // 2, "c": ex % 2}
        self.peers = {("c", 0): self.device(c=1 - self.at["c"])}
        for axis, k in LINES:
            self.peers[axis, k] = self.device(**{axis: (self.at[axis] + k) % 4})

    def device(self, **moved):
        at = {**self.at, **moved}
        return (at["x"] * 4 + at["y"], at["z"] * 2 + at["c"])

    def enter(self, peers):
        bar = pltpu.get_barrier_semaphore()
        for p in peers:
            pl.semaphore_signal(bar, inc=1, device_id=self.peers[p], device_id_type=MESH)
        pl.semaphore_wait(bar, len(peers))


class Copies:
    def __init__(self, place, send, recv):
        self.place, self.send, self.recv, self.made = place, send, recv, []

    def add(self, src, dst, peer):
        self.made.append((src, dst, peer))
        return len(self.made) - 1

    def get(self, i):
        src, dst, peer = self.made[i]
        return pltpu.make_async_remote_copy(src_ref=src(), dst_ref=dst(), send_sem=self.send.at[i], recv_sem=self.recv.at[i],
                                            device_id=self.place.peers[peer], device_id_type=MESH)

    def start(self, ids):
        for i in ids:
            self.get(i).start()

    def arrived(self, ids):
        for i in ids:
            self.get(i).wait_recv()

    def sent(self, ids):
        for i in ids:
            self.get(i).wait_send()

    def drain(self):
        self.sent(range(len(self.made)))


class Scatter:
    def __init__(self, copies, big, r, ex, parts, groups, order):
        self.cp, self.big, self.r, self.ex = copies, big, r, ex
        self.parts, self.groups, self.u0, self.u1 = parts, groups, parts[0][0], parts[-1][1]
        at = copies.place.at
        self.m = m = [at[a] for a in order]
        rng = lambda g: pl.ds(g[0], g[1] - g[0])
        us = rng((self.u0, self.u1))
        self.part_ids = [copies.add(lambda g=g: big.at[1, rng(g)], lambda g=g: r[0].at[rng(g)], ("c", 0)) for g in parts]
        self.group_ids = [
            [copies.add(lambda g=g, k=k: big.at[0, rng(g), (m[0] + k) % 4], lambda g=g, k=k: r[1].at[rng(g), k - 1], (order[0], k))
             for k in (1, 2, 3)] for g in groups]
        self.ids2 = [copies.add(lambda k=k: big.at[0, us, m[0], (m[1] + k) % 4], lambda k=k: r[2].at[us, k - 1], (order[1], k))
                     for k in (1, 2, 3)]
        own = lambda: ex.at[us, m[2]]
        self.ids3 = [copies.add(own, own, (order[2], k)) for k in (1, 2, 3)]

    def start0(self, i):
        self.cp.start([self.part_ids[i]])

    def pass0(self, h):
        g = self.groups[h]
        self.cp.arrived([i for i, p in zip(self.part_ids, self.parts) if g[0] <= p[0] < g[1]])
        for u in range(*g):
            for a in range(4):
                v = self.big[0, u, a].astype(f32) + self.r[0][u, a].astype(f32)
                self.big[0, u, a] = v.astype(bf16)
        self.cp.start(self.group_ids[h])

    def add3(self, u, at, r):
        v = self.big[at].astype(f32)
        for k in range(3):
            v = v + r[u, k].astype(f32)
        return v.astype(bf16)

    def pass1(self):
        for h, g in enumerate(self.groups):
            self.cp.arrived(self.group_ids[h])
            for u in range(*g):
                at = (0, u, self.m[0])
                self.big[at] = self.add3(u, at, self.r[1])
        self.cp.start(self.ids2)

    def pass2(self):
        self.cp.arrived(self.ids2)
        for u in range(self.u0, self.u1):
            self.ex[u, self.m[2]] = self.add3(u, (0, u, self.m[0], self.m[1]), self.r[2])
        self.cp.start(self.ids3)

    def pass3(self):
        self.cp.arrived(self.ids3)

    def result(self, u):
        e = [self.ex[u, i].astype(f32) for i in range(4)]
        return (e[0] + e[1] + e[2] + e[3]).astype(bf16)


class Spread:
    def __init__(self, copies, out, u0, u1, order):
        self.cp, self.out, self.u0, self.u1 = copies, out, u0, u1
        at = copies.place.at
        self.c, self.m = at["c"], [at[a] for a in order]
        us = pl.ds(u0, u1 - u0)
        piece = lambda k=0: out.at[us, self.c, (self.m[0] - k + 4) % 4]
        quarter = lambda: out.at[us, self.c, self.m[0], self.m[1]]
        self.ids2 = [copies.add(quarter, quarter, (order[1], k)) for k in (1, 2, 3)]
        self.ids1 = [copies.add(piece, piece, (order[0], k)) for k in (1, 2, 3)]
        self.ids0 = [copies.add(lambda k=k: piece(k), lambda k=k: piece(k), ("c", 0)) for k in range(4)]

    def begin(self, values):
        for u, v in zip(range(self.u0, self.u1), values):
            self.out[u, self.c, self.m[0], self.m[1]] = v
        self.cp.start(self.ids2)

    def pass2(self):
        self.cp.arrived(self.ids2)
        self.cp.start(self.ids1 + self.ids0[:1])

    def forward(self, k):
        self.cp.arrived(self.ids1[k - 1 : k])
        self.cp.start(self.ids0[k : k + 1])

    def finish(self):
        self.cp.arrived(self.ids0)


class SpreadOwner:
    def __init__(self, copies, out, u, axis):
        self.cp, self.out, self.u, self.p = copies, out, u, copies.place.at[axis]
        ref = lambda: out.at[u, self.p]
        self.ids = [copies.add(ref, ref, (axis, k)) for k in (1, 2, 3)]

    def begin(self, value):
        self.out[self.u, self.p] = value
        self.cp.start(self.ids)

    def finish(self):
        self.cp.arrived(self.ids)


class SmallSum:
    def __init__(self, copies, src, half, r0, r1, by, bz, out):
        self.cp, self.src, self.half, self.r0, self.r1, self.by, self.bz, self.out = copies, src, half, r0, r1, by, bz, out
        at = copies.place.at
        self.c, self.x, self.y, self.z = at["c"], at["x"], at["y"], at["z"]
        own_half = lambda: out.at[self.c]
        own = lambda: out.at[self.c, self.x]
        self.ids = [
            [copies.add(lambda: src.at[1 - self.c], lambda: r0, ("c", 0))],
            [copies.add(lambda k=k: half.at[(self.x + k) % 4], lambda k=k: r1.at[k - 1], ("x", k)) for k in (1, 2, 3)],
            [copies.add(lambda: by.at[self.y], lambda: by.at[self.y], ("y", k)) for k in (1, 2, 3)],
            [copies.add(lambda: bz.at[self.z], lambda: bz.at[self.z], ("z", k)) for k in (1, 2, 3)],
            [copies.add(own, own, ("x", k)) for k in (1, 2, 3)],
            [copies.add(own_half, own_half, ("c", 0))],
        ]

    def step(self, i):
        if i:
            self.cp.arrived(self.ids[i - 1])
        if i == 1:
            for a in range(4):
                self.half[a] = (self.src[self.c, a].astype(f32) + self.r0[a].astype(f32)).astype(bf16)
        if i == 2:
            v = self.half[self.x].astype(f32)
            for k in range(3):
                v = v + self.r1[k].astype(f32)
            self.by[self.y] = v.astype(bf16)
        if i in (3, 4):
            b = self.by if i == 3 else self.bz
            v = (b[0].astype(f32) + b[1].astype(f32) + b[2].astype(f32) + b[3].astype(f32)).astype(bf16)
            if i == 3:
                self.bz[self.z] = v
            else:
                self.out[self.c, self.x] = v
        if i < 6:
            self.cp.start(self.ids[i])


UNITS = 11
UP_UNIT, DOWN_UNIT, WO_UNIT = [0, 4, 5, 8], [1, 2, 6, 9], [3, 7, 10]
SHARED = sorted(UP_UNIT + DOWN_UNIT)
OWNER_ORDERS = ["zxy", "xzy", "yzx"]
EARLY = [([(0, 1), (1, 3), (3, 4)], [(0, 1), (1, 4)], "zxy"), ([(4, 5), (5, 6), (6, 7)], [(4, 6), (6, 7)], "xyz"),
         ([(7, 8)], [(7, 8)], "xzy"), ([(8, 9), (9, 10), (10, 11)], [(8, 9), (9, 11)], "yzx")]
UP_PART, DOWN_PARTS, WO_PARTS = [(0, 0), (1, 0), (1, 1), (3, 0)], [(0, 1), (1, 2), (3, 1)], [(0, 2), (2, 0), (3, 2)]
SPREADS = [(0, 3, "zxy"), (3, 6, "xyz"), (6, 8, "yzx")]


def plane_axes(order):
    return [a for a in order if a != "z"]


def expert_row(ex, piece, order):
    p, q = plane_axes(order)
    at = {p: piece // 4, q: piece % 4, "z": ex // 2}
    r = ex % 2
    for a in order:
        r = r * 4 + at[a]
    return r * 16


def store_expert(big, core, units, ex0, value):
    low = value.astype(bf16)
    for o in range(2):
        slot = (core + (ex0 + o) % 2) % 2
        for row in range(0, 768, 16):
            v, piece = row // 256, (row % 256) // 16
            ct, r = row // 192, row % 192
            base = expert_row(ex0 + o, piece, OWNER_ORDERS[v]) % 1024
            big[slot, units[v], base : base + 16, :] = low[o * 192 + r : o * 192 + r + 16, ct * 128 : (ct + 1) * 128]


KVR = T + 16


class Gather:
    def __init__(self, copies, out):
        self.cp, self.out = copies, out
        at, ex = copies.place.at, copies.place.ex
        own = lambda: out.at[ex]
        from_z = lambda k: out.at[((at["z"] - k + 4) % 4) * 2 + at["c"]]
        self.line = [copies.add(own, own, ("z", k)) for k in (1, 2, 3)]
        self.core = [copies.add(functools.partial(from_z, k), functools.partial(from_z, k), ("c", 0)) for k in (0, 1, 2, 3)]

    def start(self):
        self.cp.start(self.line)
        self.cp.start(self.core[:1])

    def forward(self):
        for k in range(3):
            self.cp.arrived(self.line[k : k + 1])
            self.cp.start(self.core[k + 1 : k + 2])

    def finish(self):
        self.cp.arrived(self.core)


def bounds_of(kv_ref):
    n0 = n1 = 0.0
    for b in range(NB):
        tail = kv_ref[b, T:KVR, :].astype(f32)
        n0 = n0 + 16.0 * tail[0:1] + tail[1:2]
        n1 = n1 + 16.0 * tail[2:3] + tail[3:4]
    return n0, n1


def segment_of(pos, bounds):
    return (pos >= bounds[0]).astype(i32) + (pos >= bounds[1]).astype(i32)


def sub8(v):
    return v.reshape(8, 8, v.shape[-1])


def route_rows(rt_ref):
    return [jnp.broadcast_to(rt_ref[j : j + 1, :], (8, T)) for j in range(J)]


def visible(me, sb):
    key = lax.broadcasted_iota(i32, (T, SB), 1)
    tok = lax.broadcasted_iota(i32, (T, SB), 0)
    ok = key - tok <= (me - 2 * sb) * T
    return ok


def prepare_keys(kv_ref, bounds, kaug, vaug, vt):
    ln = lanes(T)
    for b in range(NB):
        bs = slice(b * T, (b + 1) * T)
        kv = kv_ref[b, 0:T, :].astype(f32)
        pos = (lax.broadcasted_iota(i32, (T, 128), 0) + b * T).astype(f32)
        seg = segment_of(pos, bounds)
        feat = jnp.where((ln < H + 3) & (seg != ln - H), NEG, 0.0)
        feat = jnp.where((ln >= H + 3) & (ln < H + 6), 1.0, feat)
        kaug[bs, :] = jnp.where(ln < H, kv, feat).astype(bf16)
        if vaug is not None:
            one = jnp.where(ln < H + 3, 1.0, 0.0)
            vaug[bs, :] = jnp.where(ln < H, pltpu.roll(kv, H, 1), one).astype(bf16)
        if vt is not None:
            ones = jnp.where(lax.broadcasted_iota(i32, (16, T), 0) == 0, 1.0, 0.0)
            vt[:, bs] = jnp.concatenate([jnp.transpose(kv)[H:], ones], axis=0).astype(bf16)


def project_queries(normed, wq_ref, qall):
    for c in range(4):
        w = wq_ref[2 * c : 2 * c + 2].reshape(2 * 3 * H, D)
        qall[c * 48 : (c + 1) * 48] = (nt(w, normed) * 0.125).reshape(48, 8, T)


def choose(routes, table, j):
    acc = table[0:8]
    for e in range(1, E):
        acc = jnp.where((routes[j] == e)[None], table[e * 8 : (e + 1) * 8], acc)
    return acc


def to_experts(routes, rows, out):
    for e in range(E):
        acc = jnp.zeros((8, 8, T), f32)
        for j in range(J):
            acc = jnp.where((routes[j] == e)[None], rows[j], acc)
        out[e * H : (e + 1) * H, :] = acc.reshape(H, T).astype(bf16)


def pick_queries(rt_ref, table, qt):
    routes = route_rows(rt_ref)
    for j in range(J):
        qt[0:H, j * T : (j + 1) * T] = choose(routes, table, j).reshape(H, T).astype(bf16)


def mark_queries(bounds, me, qt):
    pos = (lax.broadcasted_iota(i32, (H, T), 1) + me * T).astype(f32)
    seg = segment_of(pos, (bounds[0][:, 0:1], bounds[1][:, 0:1]))
    feat = jnp.where(lax.broadcasted_iota(i32, (H, T), 0) == seg, 1.0, 0.0).astype(bf16)
    for j in range(J):
        qt[H:, j * T : (j + 1) * T] = feat


def attend(me, qt, kaug, vt, att, macc, acc):
    last = me // 2
    macc[...] = jnp.full(macc.shape, NEG, f32)
    acc[...] = jnp.zeros(acc.shape, f32)

    def score(sb, g, masked):
        s = nn(kaug[pl.ds(pl.multiple_of(sb * SB, SB), SB), :], qt[:, g * SB : (g + 1) * SB])
        if masked:
            key = lax.broadcasted_iota(i32, (SB, T), 0)
            tok = lax.broadcasted_iota(i32, (SB, T), 1)
            ok = key - tok <= (me - 2 * sb) * T
            s = jnp.where(jnp.concatenate([ok, ok], axis=1), s, NEG)
        return s.reshape(SB // 8, 8, SB)

    def soften(s, g):
        gs = slice(g * SB, (g + 1) * SB)
        old = macc[:, gs]
        top = jnp.max(jnp.maximum(old, jnp.max(s, axis=0)), axis=0, keepdims=True)
        top = jnp.broadcast_to(top, (8, SB))
        macc[:, gs] = top
        return jnp.exp(s - top[None]).reshape(SB, SB).astype(bf16), jnp.exp(old - top)

    def weigh(sb, g, p, kept):
        gs = slice(g * SB, (g + 1) * SB)
        old = acc[:, gs].reshape(10, 8, SB) * kept[None]
        acc[:, gs] = old.reshape(80, SB) + nn(vt[:, pl.ds(pl.multiple_of(sb * SB, SB), SB)], p)

    def block(sb, masked):
        s = score(sb, 0, masked)
        held = None
        for g in range(J // 2):
            ahead = score(sb, g + 1, masked) if g + 1 < J // 2 else None
            new = soften(s, g)
            if g:
                weigh(sb, g - 1, *held)
            held, s = new, ahead
        weigh(sb, J // 2 - 1, *held)

    lax.fori_loop(0, last, lambda sb, c: (block(sb, False), c)[1], 0)
    block(last, True)
    for g in range(J // 2):
        gs = slice(g * SB, (g + 1) * SB)
        tot = acc[H : H + 1, gs]
        att[:, gs] = (acc[0:H, gs] / tot).astype(bf16)
        l1, l2, l3 = split3(-(macc[0:1, gs] + jnp.log(tot)))
        row = lax.broadcasted_iota(i32, (16, SB), 0)
        feat = qt[H : H + 16, gs].astype(f32)
        feat = jnp.where(row == 3, l1, jnp.where(row == 4, l2, jnp.where(row == 5, l3, feat)))
        qt[H : H + 16, gs] = feat.astype(bf16)


def gates_of(normed, rw_ref, rt_ref, gate_ref):
    logits = nt(rw_ref[...], normed)
    eid = lax.broadcasted_iota(i32, (E, T), 0)
    per = [jnp.sum(jnp.where(rt_ref[j : j + 1, :] == eid, logits, 0.0), axis=0, keepdims=True) for j in range(J)]
    v = jnp.concatenate(per, axis=0)
    e = jnp.exp(v - jnp.max(v, axis=0, keepdims=True))
    gate_ref[...] = e / jnp.sum(e, axis=0, keepdims=True)


SMALL = 640


def dma_sems(n):
    return [pltpu.SemaphoreType.DMA((n,)), pltpu.SemaphoreType.DMA((n,))]


def kernel_all(x_ref, cot_ref, gain_ref, fgain_ref, kvw_ref, rw_ref, rt_ref, seg_ref, wq_in, wo_in, up_hbm, down_hbm,
               out_ref, ing_ref, all_ref, dwo_ref, dwq_ref, small_ref,
               up_ref, down_ref, wsem, normed_ref, gate_ref, kv_ref, wq_ref, wo_ref, att_ref, qt_ref, table, kaug, vaug, vt, macc, acc,
               rows, gat, gm_ref, gn_ref, drw_ref, dfg_ref, big, r0, r1, r2, ex,
               dat_ref, qa, da, dqacc, tot, gsend, grecv, lbig, l0, l1, l2, lex, ssrc, shalf, s0, s1, sy, sz, send, recv, ksend, krecv):
    place = Place()
    me, core = place.ex, place.at["c"]
    dp = lax.axis_index("dp")
    copies = Copies(place, send, recv)
    gq, gk, go = Gather(copies, wq_ref), Gather(copies, kv_ref), Gather(copies, wo_ref)
    big7 = big.reshape(2, UNITS, 4, 4, 4, 16, 128)
    lbig7 = lbig.reshape(2, 3, 4, 4, 4, 16, 128)
    early = [Scatter(copies, big7, (r0, r1, r2), ex, parts, groups, o) for parts, groups, o in EARLY]
    late = [Scatter(copies, lbig7, (l0, l1, l2), lex, [(u, u + 1)], [(u, u + 1)], o) for u, o in enumerate(OWNER_ORDERS)]
    spreads = [Spread(copies, all_ref, u0, u1, o) for u0, u1, o in SPREADS]
    owned_o = [SpreadOwner(copies, dwo_ref, u, plane_axes(o)[0]) for u, o in enumerate(OWNER_ORDERS)]
    owned_q = [SpreadOwner(copies, dwq_ref, u, plane_axes(o)[0]) for u, o in enumerate(OWNER_ORDERS)]
    small = SmallSum(copies, ssrc, shalf, s0, s1, sy, sz, small_ref)

    bar = pltpu.get_barrier_semaphore()
    for p in ALL_PEERS:
        pl.semaphore_signal(bar, inc=1, device_id=place.peers[p], device_id_type=MESH)
    for k in range(1, NB):
        pl.semaphore_signal(bar, inc=1, device_id=(dp, (me + k) % NB), device_id_type=MESH)
    loads = [pltpu.make_async_copy(up_hbm, up_ref, wsem.at[0]), pltpu.make_async_copy(down_hbm, down_ref, wsem.at[1])]
    for cp in loads:
        cp.start()
    wq_ref[me] = wq_in[...]
    wo_ref[me] = wo_in[...]
    pl.semaphore_wait(bar, len(ALL_PEERS) + NB - 1)
    gq.start()

    x = x_ref[...].astype(f32)
    inv = lax.rsqrt(jnp.mean(x * x, axis=-1, keepdims=True) + eps)
    normed = (x * inv * gain_ref[...]).astype(bf16)
    normed_ref[...] = normed
    kv_ref[me, 0:T, :] = nn(normed, kvw_ref[...]).astype(bf16)
    seg = seg_ref[...]
    row = lax.broadcasted_iota(i32, (16, 128), 0)
    tail = jnp.zeros((16, 128), f32)
    for s in range(2):
        n = jnp.sum(jnp.sum((seg <= s).astype(f32), axis=0, keepdims=True), axis=1, keepdims=True)
        n = jnp.broadcast_to(n, (16, 128))
        hi = jnp.floor(n * 0.0625)
        tail = jnp.where(row == 2 * s, hi, jnp.where(row == 2 * s + 1, n - 16.0 * hi, tail))
    kv_ref[me, T:KVR, :] = tail.astype(bf16)
    gk.start()
    gates_of(normed, rw_ref, rt_ref, gate_ref)
    gq.forward()
    gq.finish()
    project_queries(normed, wq_ref, table)
    pick_queries(rt_ref, table, qt_ref)
    gk.forward()
    gk.finish()
    bounds = bounds_of(kv_ref)
    prepare_keys(kv_ref, bounds, kaug, vaug, vt)
    mark_queries(bounds, me, qt_ref)
    go.start()
    attend(me, qt_ref, kaug, vt, att_ref, macc, acc)

    go.forward()
    routes = route_rows(rt_ref)
    for j in range(J):
        rows[j] = sub8(att_ref[:, j * T : (j + 1) * T].astype(f32) * gate_ref[j : j + 1, :])
    to_experts(routes, rows, gat)
    go.finish()
    x = x_ref[...].astype(f32)
    wo_all = wo_ref[...].reshape(EW, D)
    mixed = x + tn(gat[...], wo_all)
    inv = lax.rsqrt(jnp.mean(mixed * mixed, axis=-1, keepdims=True) + eps)
    n = mixed * inv
    fgain = fgain_ref[...]
    second = (n * fgain).astype(bf16)
    second_t = jnp.transpose(n * fgain).astype(bf16)
    cot = cot_ref[...]
    for cp in loads:
        cp.wait()
    C = 512
    out = mixed
    gsec = jnp.zeros((T, D), f32)
    for c in range(FF // C):
        cs = slice(c * C, (c + 1) * C)
        v = nn(second, up_ref[:, cs])
        v2 = v * v
        th = jnp.tanh(0.7978845608028654 * (v + 0.044715 * v * v2))
        a = (0.5 * v * (1.0 + th)).astype(bf16)
        dth = 0.5 * (1.0 + th) + 0.5 * v * (1.0 - th * th) * (0.7978845608028654 * (1.0 + 0.134145 * v2))
        gh = (nt(cot, down_ref[cs, :]) * dth).astype(bf16)
        out = out + nn(a, down_ref[cs, :])
        gsec = gsec + nt(gh, up_ref[:, cs])
        gdown = tn(a, cot).astype(bf16)
        gup = nn(second_t, gh).astype(bf16)
        for t in range(4):
            ts = slice(t * 128, (t + 1) * 128)
            big[(core + c // 2) % 2, DOWN_UNIT[t], c % 2 * C : c % 2 * C + C, :] = gdown[:, ts]
            big[(core + t // 2) % 2, UP_UNIT[c], t % 2 * 512 : t % 2 * 512 + 512, :] = gup[:, ts]
        early[UP_PART[c][0]].start0(UP_PART[c][1])
    for b, i in DOWN_PARTS:
        early[b].start0(i)
    out_ref[...] = out.astype(bf16)
    dfg_ref[...] = jnp.sum(gsec * n, axis=0, keepdims=True)
    hh = gsec * fgain
    gm = cot.astype(f32) + inv * (hh - n * jnp.mean(hh * n, axis=-1, keepdims=True))
    gm_ref[...] = gm
    gml = gm.astype(bf16)
    for c in range(4):
        store_expert(big, core, WO_UNIT, 2 * c, nn(gat[c * 384 : (c + 1) * 384, :], gml))
    for b, i in WO_PARTS:
        early[b].start0(i)
    for c in range(4):
        w = wo_ref[2 * c : 2 * c + 2].reshape(2 * 3 * H, D)
        table[c * 48 : (c + 1) * 48] = nt(w, gml).reshape(48, 8, T)
    for i in (0, 1, 3):
        early[i].pass0(0)
    dots = []
    row = lax.broadcasted_iota(i32, (H, T), 0)
    for j in range(J):
        js = slice(j * T, (j + 1) * T)
        g = choose(routes, table, j).reshape(H, T)
        gate = gate_ref[j : j + 1, :]
        dot = jnp.sum(g * att_ref[:, js].astype(f32), axis=0, keepdims=True)
        dots.append(dot)
        d1, d2, d3 = split3(-(dot * gate))
        dat_ref[0:H, js] = (g * gate).astype(bf16)
        dat_ref[H:, js] = jnp.where(row == 0, d1, jnp.where(row == 1, d2, jnp.where(row == 2, d3, 0.0))).astype(bf16)
    dots = jnp.concatenate(dots, axis=0)
    gates = gate_ref[...]
    chosen = gates * (dots - jnp.sum(gates * dots, axis=0, keepdims=True))
    eid = lax.broadcasted_iota(i32, (E, T), 0)
    gl = jnp.zeros((E, T), f32)
    for j in range(J):
        gl = jnp.where(rt_ref[j : j + 1, :] == eid, chosen[j : j + 1, :], gl)
    hi = gl.astype(bf16)
    lo = (gl - hi.astype(f32)).astype(bf16)
    rw = rw_ref[...]
    gn_ref[...] = tn(hi, rw) + tn(lo, rw)
    nm = normed_ref[...]
    drw_ref[...] = nn(hi, nm) + nn(lo, nm)

    for j in range(J):
        js = slice(j * T, (j + 1) * T)
        qa[js, :] = jnp.transpose(qt_ref[:, js].astype(f32)).astype(bf16)
        da[js, :] = jnp.transpose(dat_ref[:, js].astype(f32)).astype(bf16)
    dqacc[...] = jnp.zeros(dqacc.shape, f32)
    last = me // 2

    def half_block(sb, half, masked):
        ks = pl.ds(pl.multiple_of(sb * SB, SB), SB)

        @pl.when(half == 0)
        def _():
            tot[...] = jnp.zeros(tot.shape, f32)

        for i in range(2):
            gs = pl.ds(pl.multiple_of((half * 2 + i) * SB, SB), SB)
            p = jnp.exp(nt(qa[gs, :], kaug[ks, :]))
            if masked:
                ok = visible(me, sb)
                p = jnp.where(jnp.concatenate([ok, ok], axis=0), p, 0.0)
            ds = (p * nt(da[gs, :], vaug[ks, :])).astype(bf16)
            kv = jnp.concatenate([kv_ref[2 * sb, 0:T, :], kv_ref[2 * sb + 1, 0:T, :]], axis=0)
            dqacc[gs, :] += nn(ds, kv)
            tot[0:H, :] += nn(qt_ref[0:H, gs], ds)
            tot[H:, :] += nn(dat_ref[0:H, gs], p.astype(bf16))

        @pl.when(half == 1)
        def _():
            low = jnp.transpose(tot[...]).astype(bf16)
            gsend[2 * sb] = low[0:T]
            gsend[2 * sb + 1] = low[T:]

    def to_owner(kb):
        return pltpu.make_async_remote_copy(src_ref=gsend.at[kb], dst_ref=grecv.at[me], send_sem=ksend.at[kb],
                                            recv_sem=krecv.at[me], device_id=(dp, kb), device_id_type=MESH)

    def from_device(b):
        return pltpu.make_async_remote_copy(src_ref=gsend.at[b], dst_ref=grecv.at[b], send_sem=ksend.at[b],
                                            recv_sem=krecv.at[b], device_id=(dp, b), device_id_type=MESH)

    def at_0():
        for i, h in ((0, 1), (1, 1), (2, 0), (3, 1)):
            early[i].pass0(h)

    def at_4():
        for s in early:
            s.pass1()

    def at_6():
        for s in early:
            s.pass2()

    def step(i, carry):
        sb, half = i // 2, i % 2

        @pl.when(sb < last)
        def _():
            half_block(sb, half, False)

            @pl.when(half == 1)
            def _():
                to_owner(2 * sb).start()
                to_owner(2 * sb + 1).start()

        pl.when(i == 0)(at_0)
        pl.when(i == 4)(at_4)

        return carry

    lax.fori_loop(0, 2 * (NSB - 1), step, 0)

    def last_step(half, carry):
        half_block(last, half, True)

        pl.when(half == 0)(at_6)
        return carry

    lax.fori_loop(0, 2, last_step, 0)

    @pl.when(2 * last < me)
    def _():
        to_owner(2 * last).start()

    for j in range(J):
        js = slice(j * T, (j + 1) * T)
        rows[j] = sub8(jnp.transpose(dqacc[js, :])[0:H].astype(bf16).astype(f32) * 0.125)
    to_experts(routes, rows, gat)
    for c in range(4):
        store_expert(lbig, core, [0, 1, 2], 2 * c, nn(gat[c * 384 : (c + 1) * 384, :], nm))
    for s in late:
        s.start0(0)
    for s in early:
        s.pass3()
    for s, (u0, u1, _) in zip(spreads, SPREADS):
        s.begin([early[{0: 0, 4: 1, 8: 3}[4 * (SHARED[u] // 4)]].result(SHARED[u]) for u in range(u0, u1)])
    for s, e, u in zip(owned_o, (early[0], early[2], early[3]), WO_UNIT):
        s.begin(e.result(u))
    acc_kv = tot
    acc_kv[:, 0:T] = jnp.transpose(gsend[me].astype(f32))
    for b in range(1, NB):
        @pl.when(b > me)
        def _(b=b):
            from_device(b).wait_recv()
            acc_kv[:, 0:T] += jnp.transpose(grecv[b].astype(f32))
    gkv = jnp.transpose(acc_kv[:, 0:T]).astype(bf16)
    dkvw = tn(nm, gkv).astype(bf16)
    for s in late:
        s.pass0(0)
    for s in spreads:
        s.pass2()
    gn = gn_ref[...] + tn(gat[...], wq_ref[...].reshape(EW, D)) + nt(gkv, kvw_ref[...])
    x = x_ref[...].astype(f32)
    inv = lax.rsqrt(jnp.mean(x * x, axis=-1, keepdims=True) + eps)
    n = x * inv
    dgain = jnp.sum(gn * n, axis=0, keepdims=True)
    drw = drw_ref[...]
    dfg = dfg_ref[...]
    parts = [dkvw.astype(f32)] + [drw[:, t * 128 : (t + 1) * 128] for t in range(4)]
    parts += [v[:, t * 128 : (t + 1) * 128] for v in (dgain, dfg) for t in range(4)] + [jnp.zeros((SMALL - 616, 128), f32)]
    ssrc[...] = jnp.concatenate(parts, axis=0).astype(bf16).reshape(2, 4, SMALL // 8, 128)
    small.step(0)
    for s in late:
        s.pass1()
    small.step(1)
    hh = gn * gain_ref[...]
    ing_ref[...] = (gm_ref[...] + inv * (hh - n * jnp.mean(hh * n, axis=-1, keepdims=True))).astype(bf16)
    for s in late:
        s.pass2()
    small.step(2)
    for s, t, u in zip(owned_q, late, range(3)):
        t.pass3()
        s.begin(t.result(u))
    small.step(3)
    for k in (1, 2, 3):
        for s in spreads:
            s.forward(k)
    for s in owned_o + owned_q:
        s.finish()
    small.step(4)
    small.step(5)
    small.step(6)
    for s in spreads:
        s.finish()
    for b in range(NB - 1):
        @pl.when(b < me)
        def _(b=b):
            to_owner(b).wait_send()
    copies.drain()


SCRATCH = [
    VM((D, FF), bf16), VM((FF, D), bf16), pltpu.SemaphoreType.DMA((2,)), VM((T, D), bf16), VM((J, T), f32), VM((NB, KVR, 128), bf16),
    VM((NB, 3 * H, D), bf16), VM((NB, 3 * H, D), bf16), VM((H, ROWS), bf16), VM((128, ROWS), bf16), VM((EW // 8, 8, T), f32),
    VM((ROWS, 128), bf16), VM((ROWS, 128), bf16), VM((80, ROWS), bf16), VM((8, ROWS), f32), VM((80, ROWS), f32),
    VM((J, 8, 8, T), f32), VM((EW, T), bf16), VM((T, D), f32), VM((T, D), f32), VM((E, D), f32), VM((1, D), f32),
    VM((2, UNITS, 1024, 128), bf16), VM((UNITS, 4, 4, 4, 16, 128), bf16), VM((UNITS, 3, 4, 4, 16, 128), bf16),
    VM((UNITS, 3, 4, 16, 128), bf16), VM((UNITS, 4, 4, 16, 128), bf16),
    VM((128, ROWS), bf16), VM((ROWS, 128), bf16), VM((ROWS, 128), bf16), VM((ROWS, 128), f32), VM((128, SB), f32),
    VM((NB, T, 128), bf16), VM((NB, T, 128), bf16),
    VM((2, 3, 1024, 128), bf16), VM((3, 4, 4, 4, 16, 128), bf16), VM((3, 3, 4, 4, 16, 128), bf16), VM((3, 3, 4, 16, 128), bf16),
    VM((3, 4, 4, 16, 128), bf16),
    VM((2, 4, SMALL // 8, 128), bf16), VM((4, SMALL // 8, 128), bf16), VM((4, SMALL // 8, 128), bf16),
    VM((3, SMALL // 8, 128), bf16), VM((4, SMALL // 8, 128), bf16), VM((4, SMALL // 8, 128), bf16),
] + dma_sems(168) + dma_sems(NB)


def kernel_f(u0, u1, u2, u3, d0, d1, d2, d3, wo_ref, dwq_ref, small_ref, out_in, ing_in, dup_ref, ddown_ref, dwo_ref, dwqt_ref, dkvw_ref,
             drw_ref, dgain_ref, dfg_ref, out_ref, ing_ref):
    for t, (u, d) in enumerate(zip((u0, u1, u2, u3), (d0, d1, d2, d3))):
        ddown_ref[:, t * 128 : (t + 1) * 128] = d[0].astype(f32)
        for s in range(4):
            dup_ref[:, (4 * t + s) * 128 : (4 * t + s + 1) * 128] = u[0, s].astype(f32)

    @pl.when(pl.program_id(0) == 0)
    def _():
        for t in range(4):
            ts = slice(t * 128, (t + 1) * 128)
            dwo_ref[:, ts] = wo_ref[t * 192 : (t + 1) * 192, :].astype(f32)
            dwqt_ref[:, ts] = dwq_ref[t * 192 : (t + 1) * 192, :].astype(f32)
        small = small_ref[512:SMALL, :].astype(f32)
        dkvw_ref[...] = small_ref[0:512, :].astype(f32)
        for t in range(4):
            ts = slice(t * 128, (t + 1) * 128)
            drw_ref[:, ts] = small[t * E : (t + 1) * E]
            dgain_ref[:, ts] = small[96 + t : 97 + t]
            dfg_ref[:, ts] = small[100 + t : 101 + t]
        out_ref[...] = out_in[...]
        ing_ref[...] = ing_in[...]


def per_device(inputs, cotangent, norm_gain, ffn_gain, kv_weight, router_weight, query_weight, output_weight, up_weight,
               down_weight, routes, segment_ids):
    wq = jnp.swapaxes(query_weight, 1, 2).reshape(3 * H, D)
    wo = output_weight.reshape(3 * H, D)
    vmem, anywhere = pl.BlockSpec(memory_space=VM), pl.BlockSpec(memory_space=pl.ANY)
    S = jax.ShapeDtypeStruct
    out, ing, shared, dwo, dwq, small = pl.pallas_call(
        kernel_all,
        out_shape=[S((T, D), bf16), S((T, D), bf16), S((8, 2, 4, 4, 4, 16, 128), bf16), S((3, 4, 4, 16, 128), bf16),
                   S((3, 4, 4, 16, 128), bf16), S((2, 4, SMALL // 8, 128), bf16)],
        in_specs=[vmem] * 10 + [anywhere] * 2,
        out_specs=[vmem] * 6,
        scratch_shapes=SCRATCH,
        compiler_params=pltpu.CompilerParams(vmem_limit_bytes=62 << 20, collective_id=1, has_side_effects=True),
        cost_estimate=pl.CostEstimate(flops=1 << 35, bytes_accessed=1 << 24, transcendentals=0),
    )(inputs, cotangent, norm_gain.reshape(1, D), ffn_gain.reshape(1, D), kv_weight, router_weight.T, routes.T,
      segment_ids.reshape(3, 128), wq, wo, up_weight, down_weight)
    up_slots, down_slots = ([SHARED.index(u) for u in units] for units in (UP_UNIT, DOWN_UNIT))
    ups = [pl.BlockSpec((1, 4, 128, 128), lambda i, k=k: (k, 0, i, 0)) for k in up_slots]
    downs = [pl.BlockSpec((1, 512, 128), lambda i, k=k: (k, i, 0)) for k in down_slots]

    def whole(*shape):
        return pl.BlockSpec(shape, lambda i: (0,) * len(shape))

    dup, ddown, dwo, dwqt, dkvw, drw, dgain, dfg, out, ing = pl.pallas_call(
        kernel_f,
        grid=(4,),
        out_shape=[S((D, FF), f32), S((FF, D), f32), S((3 * H, D), f32), S((3 * H, D), f32), S((D, 128), f32), S((E, D), f32),
                   S((1, D), f32), S((1, D), f32), S((T, D), bf16), S((T, D), bf16)],
        in_specs=ups + downs + [
                  whole(768, 128), whole(768, 128), whole(SMALL, 128), whole(T, D), whole(T, D)],
        out_specs=[pl.BlockSpec((128, FF), lambda i: (i, 0)), pl.BlockSpec((512, D), lambda i: (i, 0)), whole(3 * H, D),
                   whole(3 * H, D), whole(D, 128), whole(E, D), whole(1, D), whole(1, D), whole(T, D), whole(T, D)],
        compiler_params=pltpu.CompilerParams(vmem_limit_bytes=62 << 20),
    )(*[shared.reshape(8, 4, 512, 128)] * 4, *[shared.reshape(8, 2048, 128)] * 4, dwo.reshape(768, 128), dwq.reshape(768, 128), small.reshape(SMALL, 128), out, ing)
    return (out, ing, dgain.reshape(D), dfg.reshape(D), dkvw, drw.T,
            jnp.swapaxes(dwqt.reshape(3, H, D), 1, 2), dwo.reshape(3, H, D), dup, ddown)


def solution(mesh):
    both = P(("dp", "expert"), None)
    ex = P("expert", None, None)
    return jax.shard_map(
        per_device, mesh=mesh,
        in_specs=(both, both, P(), P(), P(), P(), ex, ex, P(), P(), both, P(("dp", "expert"))),
        out_specs=(both, both, P(), P(), P(), P(), ex, ex, P(), P()),
        check_vma=False)
```

```python
import functools
import jax
import jax.numpy as jnp
from jax import lax
from jax.experimental import pallas as pl
from jax.experimental.pallas import tpu as pltpu
from jax.sharding import PartitionSpec as P

f32, bf16, i32 = jnp.float32, jnp.bfloat16, jnp.int32
T, D, H, J, E, FF, NB = 384, 512, 64, 8, 24, 2048, 8
EW = E * H
ROWS = J * T
SB = 2 * T
NSB = NB // 2
eps = 1e-06
NEG = -1e30
VM = pltpu.VMEM


def nn(a, b):
    return lax.dot_general(a, b, (((1,), (0,)), ((), ())), preferred_element_type=f32)


def nt(a, b):
    return lax.dot_general(a, b, (((1,), (1,)), ((), ())), preferred_element_type=f32)


def tn(a, b):
    return lax.dot_general(a, b, (((0,), (0,)), ((), ())), preferred_element_type=f32)


def lanes(rows):
    return lax.broadcasted_iota(i32, (rows, 128), 1)


def split3(v):
    a = v.astype(bf16).astype(f32)
    b = (v - a).astype(bf16).astype(f32)
    c = (v - a - b).astype(bf16).astype(f32)
    return a, b, c


MESH = pl.DeviceIdType.MESH
LINES = [(a, k) for a in "xyz" for k in (1, 2, 3)]
ALL_PEERS = [("c", 0)] + LINES


class Place:
    def __init__(self):
        dp, ex = lax.axis_index("dp"), lax.axis_index("expert")
        self.ex = ex
        self.at = {"x": dp // 4, "y": dp % 4, "z": ex // 2, "c": ex % 2}
        self.peers = {("c", 0): self.device(c=1 - self.at["c"])}
        for axis, k in LINES:
            self.peers[axis, k] = self.device(**{axis: (self.at[axis] + k) % 4})

    def device(self, **moved):
        at = {**self.at, **moved}
        return (at["x"] * 4 + at["y"], at["z"] * 2 + at["c"])

    def enter(self, peers):
        bar = pltpu.get_barrier_semaphore()
        for p in peers:
            pl.semaphore_signal(bar, inc=1, device_id=self.peers[p], device_id_type=MESH)
        pl.semaphore_wait(bar, len(peers))


class Copies:
    def __init__(self, place, send, recv):
        self.place, self.send, self.recv, self.made = place, send, recv, []

    def add(self, src, dst, peer):
        self.made.append((src, dst, peer))
        return len(self.made) - 1

    def get(self, i):
        src, dst, peer = self.made[i]
        return pltpu.make_async_remote_copy(src_ref=src(), dst_ref=dst(), send_sem=self.send.at[i], recv_sem=self.recv.at[i],
                                            device_id=self.place.peers[peer], device_id_type=MESH)

    def start(self, ids):
        for i in ids:
            self.get(i).start()

    def arrived(self, ids):
        for i in ids:
            self.get(i).wait_recv()

    def sent(self, ids):
        for i in ids:
            self.get(i).wait_send()

    def drain(self):
        self.sent(range(len(self.made)))


class Scatter:
    def __init__(self, copies, big, r, ex, parts, groups, order):
        self.cp, self.big, self.r, self.ex = copies, big, r, ex
        self.parts, self.groups, self.u0, self.u1 = parts, groups, parts[0][0], parts[-1][1]
        at = copies.place.at
        self.m = m = [at[a] for a in order]
        rng = lambda g: pl.ds(g[0], g[1] - g[0])
        us = rng((self.u0, self.u1))
        self.part_ids = [copies.add(lambda g=g: big.at[1, rng(g)], lambda g=g: r[0].at[rng(g)], ("c", 0)) for g in parts]
        self.group_ids = [
            [copies.add(lambda g=g, k=k: big.at[0, rng(g), (m[0] + k) % 4], lambda g=g, k=k: r[1].at[rng(g), k - 1], (order[0], k))
             for k in (1, 2, 3)] for g in groups]
        self.ids2 = [copies.add(lambda k=k: big.at[0, us, m[0], (m[1] + k) % 4], lambda k=k: r[2].at[us, k - 1], (order[1], k))
                     for k in (1, 2, 3)]
        own = lambda: ex.at[us, m[2]]
        self.ids3 = [copies.add(own, own, (order[2], k)) for k in (1, 2, 3)]

    def start0(self, i):
        self.cp.start([self.part_ids[i]])

    def pass0(self, h):
        g = self.groups[h]
        self.cp.arrived([i for i, p in zip(self.part_ids, self.parts) if g[0] <= p[0] < g[1]])
        for u in range(*g):
            for a in range(4):
                v = self.big[0, u, a].astype(f32) + self.r[0][u, a].astype(f32)
                self.big[0, u, a] = v.astype(bf16)
        self.cp.start(self.group_ids[h])

    def add3(self, u, at, r):
        v = self.big[at].astype(f32)
        for k in range(3):
            v = v + r[u, k].astype(f32)
        return v.astype(bf16)

    def pass1(self):
        for h, g in enumerate(self.groups):
            self.cp.arrived(self.group_ids[h])
            for u in range(*g):
                at = (0, u, self.m[0])
                self.big[at] = self.add3(u, at, self.r[1])
        self.cp.start(self.ids2)

    def pass2(self):
        self.cp.arrived(self.ids2)
        for u in range(self.u0, self.u1):
            self.ex[u, self.m[2]] = self.add3(u, (0, u, self.m[0], self.m[1]), self.r[2])
        self.cp.start(self.ids3)

    def pass3(self):
        self.cp.arrived(self.ids3)

    def result(self, u):
        e = [self.ex[u, i].astype(f32) for i in range(4)]
        return (e[0] + e[1] + e[2] + e[3]).astype(bf16)


class Spread:
    def __init__(self, copies, out, u0, u1, order):
        self.cp, self.out, self.u0, self.u1 = copies, out, u0, u1
        at = copies.place.at
        self.c, self.m = at["c"], [at[a] for a in order]
        us = pl.ds(u0, u1 - u0)
        quarter = lambda: out.at[us, self.c, self.m[0], self.m[1]]
        self.ids2 = [copies.add(quarter, quarter, (order[1], k)) for k in (1, 2, 3)]
        self.ids1, self.ids0 = [], []
        for u in range(u0, u1):
            piece = lambda k=0, u=u: out.at[u, self.c, (self.m[0] - k + 4) % 4]
            self.ids1.append([copies.add(piece, piece, (order[0], k)) for k in (1, 2, 3)])
            self.ids0.append([copies.add(functools.partial(piece, k), functools.partial(piece, k), ("c", 0)) for k in range(4)])

    def begin(self, values):
        for u, v in zip(range(self.u0, self.u1), values):
            self.out[u, self.c, self.m[0], self.m[1]] = v
        self.cp.start(self.ids2)

    def pass2(self):
        self.cp.arrived(self.ids2)

    def send(self, i):
        if i < len(self.ids1):
            self.cp.start(self.ids1[i] + self.ids0[i][:1])

    def forward(self, i):
        if i < len(self.ids1):
            for k in (1, 2, 3):
                self.cp.arrived(self.ids1[i][k - 1 : k])
                self.cp.start(self.ids0[i][k : k + 1])

    def finish(self):
        for ids in self.ids0:
            self.cp.arrived(ids)


class SpreadOwner:
    def __init__(self, copies, out, u, axis):
        self.cp, self.out, self.u, self.p = copies, out, u, copies.place.at[axis]
        ref = lambda: out.at[u, self.p]
        self.ids = [copies.add(ref, ref, (axis, k)) for k in (1, 2, 3)]

    def begin(self, value):
        self.out[self.u, self.p] = value
        self.cp.start(self.ids)

    def finish(self):
        self.cp.arrived(self.ids)


class SmallSum:
    def __init__(self, copies, src, half, r0, r1, by, bz, out):
        self.cp, self.src, self.half, self.r0, self.r1, self.by, self.bz, self.out = copies, src, half, r0, r1, by, bz, out
        at = copies.place.at
        self.c, self.x, self.y, self.z = at["c"], at["x"], at["y"], at["z"]
        own_half = lambda: out.at[self.c]
        own = lambda: out.at[self.c, self.x]
        self.ids = [
            [copies.add(lambda: src.at[1 - self.c], lambda: r0, ("c", 0))],
            [copies.add(lambda k=k: half.at[(self.x + k) % 4], lambda k=k: r1.at[k - 1], ("x", k)) for k in (1, 2, 3)],
            [copies.add(lambda: by.at[self.y], lambda: by.at[self.y], ("y", k)) for k in (1, 2, 3)],
            [copies.add(lambda: bz.at[self.z], lambda: bz.at[self.z], ("z", k)) for k in (1, 2, 3)],
            [copies.add(own, own, ("x", k)) for k in (1, 2, 3)],
            [copies.add(own_half, own_half, ("c", 0))],
        ]

    def step(self, i):
        if i:
            self.cp.arrived(self.ids[i - 1])
        if i == 1:
            for a in range(4):
                self.half[a] = (self.src[self.c, a].astype(f32) + self.r0[a].astype(f32)).astype(bf16)
        if i == 2:
            v = self.half[self.x].astype(f32)
            for k in range(3):
                v = v + self.r1[k].astype(f32)
            self.by[self.y] = v.astype(bf16)
        if i in (3, 4):
            b = self.by if i == 3 else self.bz
            v = (b[0].astype(f32) + b[1].astype(f32) + b[2].astype(f32) + b[3].astype(f32)).astype(bf16)
            if i == 3:
                self.bz[self.z] = v
            else:
                self.out[self.c, self.x] = v
        if i < 6:
            self.cp.start(self.ids[i])


UNITS = 11
UP_UNIT, DOWN_UNIT, WO_UNIT = [0, 4, 5, 8], [1, 2, 6, 9], [3, 7, 10]
SHARED = sorted(UP_UNIT + DOWN_UNIT)
OWNER_ORDERS = ["zxy", "xzy", "yzx"]
EARLY = [([(0, 1), (1, 3), (3, 4)], [(0, 1), (1, 4)], "zxy"), ([(4, 5), (5, 6), (6, 7)], [(4, 6), (6, 7)], "xyz"),
         ([(7, 8)], [(7, 8)], "xzy"), ([(8, 9), (9, 10), (10, 11)], [(8, 9), (9, 11)], "yzx")]
UP_PART, DOWN_PARTS, WO_PARTS = [(0, 0), (1, 0), (1, 1), (3, 0)], [(0, 1), (1, 2), (3, 1)], [(0, 2), (2, 0), (3, 2)]
SPREADS = [(0, 3, "zxy"), (3, 6, "xyz"), (6, 8, "yzx")]


def plane_axes(order):
    return [a for a in order if a != "z"]


def expert_row(ex, piece, order):
    p, q = plane_axes(order)
    at = {p: piece // 4, q: piece % 4, "z": ex // 2}
    r = ex % 2
    for a in order:
        r = r * 4 + at[a]
    return r * 16


def store_expert(big, core, units, ex0, value):
    low = value.astype(bf16)
    for o in range(2):
        slot = (core + (ex0 + o) % 2) % 2
        for row in range(0, 768, 16):
            v, piece = row // 256, (row % 256) // 16
            ct, r = row // 192, row % 192
            base = expert_row(ex0 + o, piece, OWNER_ORDERS[v]) % 1024
            big[slot, units[v], base : base + 16, :] = low[o * 192 + r : o * 192 + r + 16, ct * 128 : (ct + 1) * 128]


KVR = T + 16


class Gather:
    def __init__(self, copies, out):
        self.cp, self.out = copies, out
        at, ex = copies.place.at, copies.place.ex
        own = lambda: out.at[ex]
        from_z = lambda k: out.at[((at["z"] - k + 4) % 4) * 2 + at["c"]]
        self.line = [copies.add(own, own, ("z", k)) for k in (1, 2, 3)]
        self.core = [copies.add(functools.partial(from_z, k), functools.partial(from_z, k), ("c", 0)) for k in (0, 1, 2, 3)]

    def start(self):
        self.cp.start(self.line)
        self.cp.start(self.core[:1])

    def forward(self):
        for k in range(3):
            self.cp.arrived(self.line[k : k + 1])
            self.cp.start(self.core[k + 1 : k + 2])

    def finish(self):
        self.cp.arrived(self.core)


def bounds_of(kv_ref):
    n0 = n1 = 0.0
    for b in range(NB):
        tail = kv_ref[b, T:KVR, :].astype(f32)
        n0 = n0 + 16.0 * tail[0:1] + tail[1:2]
        n1 = n1 + 16.0 * tail[2:3] + tail[3:4]
    return n0, n1


def segment_of(pos, bounds):
    return (pos >= bounds[0]).astype(i32) + (pos >= bounds[1]).astype(i32)


def sub8(v):
    return v.reshape(8, 8, v.shape[-1])


def route_rows(rt_ref):
    return [jnp.broadcast_to(rt_ref[j : j + 1, :], (8, T)) for j in range(J)]


def visible(me, sb):
    key = lax.broadcasted_iota(i32, (T, SB), 1)
    tok = lax.broadcasted_iota(i32, (T, SB), 0)
    ok = key - tok <= (me - 2 * sb) * T
    return ok


def prepare_keys(kv_ref, bounds, kaug, vaug, vt):
    ln = lanes(T)
    for b in range(NB):
        bs = slice(b * T, (b + 1) * T)
        kv = kv_ref[b, 0:T, :].astype(f32)
        pos = (lax.broadcasted_iota(i32, (T, 128), 0) + b * T).astype(f32)
        seg = segment_of(pos, bounds)
        feat = jnp.where((ln < H + 3) & (seg != ln - H), NEG, 0.0)
        feat = jnp.where((ln >= H + 3) & (ln < H + 6), 1.0, feat)
        kaug[bs, :] = jnp.where(ln < H, kv, feat).astype(bf16)
        if vaug is not None:
            one = jnp.where(ln < H + 3, 1.0, 0.0)
            vaug[bs, :] = jnp.where(ln < H, pltpu.roll(kv, H, 1), one).astype(bf16)
        if vt is not None:
            ones = jnp.where(lax.broadcasted_iota(i32, (16, T), 0) == 0, 1.0, 0.0)
            vt[:, bs] = jnp.concatenate([jnp.transpose(kv)[H:], ones], axis=0).astype(bf16)


def project_queries(normed, wq_ref, qall):
    for c in range(4):
        w = wq_ref[2 * c : 2 * c + 2].reshape(2 * 3 * H, D)
        qall[c * 48 : (c + 1) * 48] = (nt(w, normed) * 0.125).reshape(48, 8, T)


def choose(routes, table, j):
    acc = table[0:8]
    for e in range(1, E):
        acc = jnp.where((routes[j] == e)[None], table[e * 8 : (e + 1) * 8], acc)
    return acc


def to_experts(routes, rows, out):
    for e in range(E):
        acc = jnp.zeros((8, 8, T), f32)
        for j in range(J):
            acc = jnp.where((routes[j] == e)[None], rows[j], acc)
        out[e * H : (e + 1) * H, :] = acc.reshape(H, T).astype(bf16)


def pick_queries(rt_ref, table, qt):
    routes = route_rows(rt_ref)
    for j in range(J):
        qt[0:H, j * T : (j + 1) * T] = choose(routes, table, j).reshape(H, T).astype(bf16)


def mark_queries(bounds, me, qt):
    pos = (lax.broadcasted_iota(i32, (H, T), 1) + me * T).astype(f32)
    seg = segment_of(pos, (bounds[0][:, 0:1], bounds[1][:, 0:1]))
    feat = jnp.where(lax.broadcasted_iota(i32, (H, T), 0) == seg, 1.0, 0.0).astype(bf16)
    for j in range(J):
        qt[H:, j * T : (j + 1) * T] = feat


def attend(me, qt, kaug, vt, att, macc, acc):
    last = me // 2
    macc[...] = jnp.full(macc.shape, NEG, f32)
    acc[...] = jnp.zeros(acc.shape, f32)

    def score(sb, g, masked):
        s = nn(kaug[pl.ds(pl.multiple_of(sb * SB, SB), SB), :], qt[:, g * SB : (g + 1) * SB])
        if masked:
            key = lax.broadcasted_iota(i32, (SB, T), 0)
            tok = lax.broadcasted_iota(i32, (SB, T), 1)
            ok = key - tok <= (me - 2 * sb) * T
            s = jnp.where(jnp.concatenate([ok, ok], axis=1), s, NEG)
        return s.reshape(SB // 8, 8, SB)

    def soften(s, g):
        gs = slice(g * SB, (g + 1) * SB)
        old = macc[:, gs]
        top = jnp.max(jnp.maximum(old, jnp.max(s, axis=0)), axis=0, keepdims=True)
        top = jnp.broadcast_to(top, (8, SB))
        macc[:, gs] = top
        return jnp.exp(s - top[None]).reshape(SB, SB).astype(bf16), jnp.exp(old - top)

    def weigh(sb, g, p, kept):
        gs = slice(g * SB, (g + 1) * SB)
        old = acc[:, gs].reshape(10, 8, SB) * kept[None]
        acc[:, gs] = old.reshape(80, SB) + nn(vt[:, pl.ds(pl.multiple_of(sb * SB, SB), SB)], p)

    def block(sb, masked):
        s = score(sb, 0, masked)
        held = None
        for g in range(J // 2):
            ahead = score(sb, g + 1, masked) if g + 1 < J // 2 else None
            new = soften(s, g)
            if g:
                weigh(sb, g - 1, *held)
            held, s = new, ahead
        weigh(sb, J // 2 - 1, *held)

    lax.fori_loop(0, last, lambda sb, c: (block(sb, False), c)[1], 0)
    block(last, True)
    for g in range(J // 2):
        gs = slice(g * SB, (g + 1) * SB)
        tot = acc[H : H + 1, gs]
        att[:, gs] = (acc[0:H, gs] / tot).astype(bf16)
        l1, l2, l3 = split3(-(macc[0:1, gs] + jnp.log(tot)))
        row = lax.broadcasted_iota(i32, (16, SB), 0)
        feat = qt[H : H + 16, gs].astype(f32)
        feat = jnp.where(row == 3, l1, jnp.where(row == 4, l2, jnp.where(row == 5, l3, feat)))
        qt[H : H + 16, gs] = feat.astype(bf16)


def gates_of(normed, rw_ref, rt_ref, gate_ref):
    logits = nt(rw_ref[...], normed)
    eid = lax.broadcasted_iota(i32, (E, T), 0)
    per = [jnp.sum(jnp.where(rt_ref[j : j + 1, :] == eid, logits, 0.0), axis=0, keepdims=True) for j in range(J)]
    v = jnp.concatenate(per, axis=0)
    e = jnp.exp(v - jnp.max(v, axis=0, keepdims=True))
    gate_ref[...] = e / jnp.sum(e, axis=0, keepdims=True)


SMALL = 640


def dma_sems(n):
    return [pltpu.SemaphoreType.DMA((n,)), pltpu.SemaphoreType.DMA((n,))]


def kernel_all(x_ref, cot_ref, gain_ref, fgain_ref, kvw_ref, rw_ref, rt_ref, seg_ref, wq_in, wo_in, up_hbm, down_hbm,
               out_ref, ing_ref, all_ref, dwo_ref, dwq_ref, small_ref,
               up_ref, down_ref, wsem, normed_ref, gate_ref, kv_ref, wq_ref, wo_ref, att_ref, qt_ref, table, kaug, vaug, vt, macc, acc,
               rows, gat, gm_ref, gn_ref, drw_ref, dfg_ref, big, r0, r1, r2, ex,
               dat_ref, qa, da, dqacc, tot, gsend, grecv, lbig, l0, l1, l2, lex, ssrc, shalf, s0, s1, sy, sz, send, recv, ksend, krecv):
    place = Place()
    me, core = place.ex, place.at["c"]
    dp = lax.axis_index("dp")
    copies = Copies(place, send, recv)
    gq, gk, go = Gather(copies, wq_ref), Gather(copies, kv_ref), Gather(copies, wo_ref)
    big7 = big.reshape(2, UNITS, 4, 4, 4, 16, 128)
    lbig7 = lbig.reshape(2, 3, 4, 4, 4, 16, 128)
    early = [Scatter(copies, big7, (r0, r1, r2), ex, parts, groups, o) for parts, groups, o in EARLY]
    late = [Scatter(copies, lbig7, (l0, l1, l2), lex, [(u, u + 1)], [(u, u + 1)], o) for u, o in enumerate(OWNER_ORDERS)]
    spreads = [Spread(copies, all_ref, u0, u1, o) for u0, u1, o in SPREADS]
    owned_o = [SpreadOwner(copies, dwo_ref, u, plane_axes(o)[0]) for u, o in enumerate(OWNER_ORDERS)]
    owned_q = [SpreadOwner(copies, dwq_ref, u, plane_axes(o)[0]) for u, o in enumerate(OWNER_ORDERS)]
    small = SmallSum(copies, ssrc, shalf, s0, s1, sy, sz, small_ref)

    bar = pltpu.get_barrier_semaphore()
    for p in ALL_PEERS:
        pl.semaphore_signal(bar, inc=1, device_id=place.peers[p], device_id_type=MESH)
    for k in range(1, NB):
        pl.semaphore_signal(bar, inc=1, device_id=(dp, (me + k) % NB), device_id_type=MESH)
    loads = [pltpu.make_async_copy(up_hbm, up_ref, wsem.at[0]), pltpu.make_async_copy(down_hbm, down_ref, wsem.at[1])]
    for cp in loads:
        cp.start()
    wq_ref[me] = wq_in[...]
    wo_ref[me] = wo_in[...]
    pl.semaphore_wait(bar, len(ALL_PEERS) + NB - 1)
    gq.start()

    x = x_ref[...].astype(f32)
    inv = lax.rsqrt(jnp.mean(x * x, axis=-1, keepdims=True) + eps)
    normed = (x * inv * gain_ref[...]).astype(bf16)
    normed_ref[...] = normed
    kv_ref[me, 0:T, :] = nn(normed, kvw_ref[...]).astype(bf16)
    seg = seg_ref[...]
    row = lax.broadcasted_iota(i32, (16, 128), 0)
    tail = jnp.zeros((16, 128), f32)
    for s in range(2):
        n = jnp.sum(jnp.sum((seg <= s).astype(f32), axis=0, keepdims=True), axis=1, keepdims=True)
        n = jnp.broadcast_to(n, (16, 128))
        hi = jnp.floor(n * 0.0625)
        tail = jnp.where(row == 2 * s, hi, jnp.where(row == 2 * s + 1, n - 16.0 * hi, tail))
    kv_ref[me, T:KVR, :] = tail.astype(bf16)
    gk.start()
    gates_of(normed, rw_ref, rt_ref, gate_ref)
    gq.forward()
    gq.finish()
    project_queries(normed, wq_ref, table)
    pick_queries(rt_ref, table, qt_ref)
    gk.forward()
    gk.finish()
    bounds = bounds_of(kv_ref)
    prepare_keys(kv_ref, bounds, kaug, vaug, vt)
    mark_queries(bounds, me, qt_ref)
    go.start()
    attend(me, qt_ref, kaug, vt, att_ref, macc, acc)

    go.forward()
    routes = route_rows(rt_ref)
    for j in range(J):
        rows[j] = sub8(att_ref[:, j * T : (j + 1) * T].astype(f32) * gate_ref[j : j + 1, :])
    to_experts(routes, rows, gat)
    go.finish()
    x = x_ref[...].astype(f32)
    wo_all = wo_ref[...].reshape(EW, D)
    mixed = x + tn(gat[...], wo_all)
    inv = lax.rsqrt(jnp.mean(mixed * mixed, axis=-1, keepdims=True) + eps)
    n = mixed * inv
    fgain = fgain_ref[...]
    second = (n * fgain).astype(bf16)
    second_t = jnp.transpose(n * fgain).astype(bf16)
    cot = cot_ref[...]
    for cp in loads:
        cp.wait()
    C = 512
    out = mixed
    gsec = jnp.zeros((T, D), f32)
    for c in range(FF // C):
        cs = slice(c * C, (c + 1) * C)
        v = nn(second, up_ref[:, cs])
        v2 = v * v
        th = jnp.tanh(0.7978845608028654 * (v + 0.044715 * v * v2))
        a = (0.5 * v * (1.0 + th)).astype(bf16)
        dth = 0.5 * (1.0 + th) + 0.5 * v * (1.0 - th * th) * (0.7978845608028654 * (1.0 + 0.134145 * v2))
        gh = (nt(cot, down_ref[cs, :]) * dth).astype(bf16)
        out = out + nn(a, down_ref[cs, :])
        gsec = gsec + nt(gh, up_ref[:, cs])
        gdown = tn(a, cot).astype(bf16)
        gup = nn(second_t, gh).astype(bf16)
        for t in range(4):
            ts = slice(t * 128, (t + 1) * 128)
            big[(core + c // 2) % 2, DOWN_UNIT[t], c % 2 * C : c % 2 * C + C, :] = gdown[:, ts]
            big[(core + t // 2) % 2, UP_UNIT[c], t % 2 * 512 : t % 2 * 512 + 512, :] = gup[:, ts]
        early[UP_PART[c][0]].start0(UP_PART[c][1])
    for b, i in DOWN_PARTS:
        early[b].start0(i)
    out_ref[...] = out.astype(bf16)
    dfg_ref[...] = jnp.sum(gsec * n, axis=0, keepdims=True)
    hh = gsec * fgain
    gm = cot.astype(f32) + inv * (hh - n * jnp.mean(hh * n, axis=-1, keepdims=True))
    gm_ref[...] = gm
    gml = gm.astype(bf16)
    for c in range(4):
        store_expert(big, core, WO_UNIT, 2 * c, nn(gat[c * 384 : (c + 1) * 384, :], gml))
    for b, i in WO_PARTS:
        early[b].start0(i)
    for c in range(4):
        w = wo_ref[2 * c : 2 * c + 2].reshape(2 * 3 * H, D)
        table[c * 48 : (c + 1) * 48] = nt(w, gml).reshape(48, 8, T)
    for i in (0, 1, 3):
        early[i].pass0(0)
    dots = []
    row = lax.broadcasted_iota(i32, (H, T), 0)
    for j in range(J):
        js = slice(j * T, (j + 1) * T)
        g = choose(routes, table, j).reshape(H, T)
        gate = gate_ref[j : j + 1, :]
        dot = jnp.sum(g * att_ref[:, js].astype(f32), axis=0, keepdims=True)
        dots.append(dot)
        d1, d2, d3 = split3(-(dot * gate))
        dat_ref[0:H, js] = (g * gate).astype(bf16)
        dat_ref[H:, js] = jnp.where(row == 0, d1, jnp.where(row == 1, d2, jnp.where(row == 2, d3, 0.0))).astype(bf16)
    dots = jnp.concatenate(dots, axis=0)
    gates = gate_ref[...]
    chosen = gates * (dots - jnp.sum(gates * dots, axis=0, keepdims=True))
    eid = lax.broadcasted_iota(i32, (E, T), 0)
    gl = jnp.zeros((E, T), f32)
    for j in range(J):
        gl = jnp.where(rt_ref[j : j + 1, :] == eid, chosen[j : j + 1, :], gl)
    hi = gl.astype(bf16)
    lo = (gl - hi.astype(f32)).astype(bf16)
    rw = rw_ref[...]
    gn_ref[...] = tn(hi, rw) + tn(lo, rw)
    nm = normed_ref[...]
    drw_ref[...] = nn(hi, nm) + nn(lo, nm)

    for j in range(J):
        js = slice(j * T, (j + 1) * T)
        qa[js, :] = jnp.transpose(qt_ref[:, js].astype(f32)).astype(bf16)
        da[js, :] = jnp.transpose(dat_ref[:, js].astype(f32)).astype(bf16)
    dqacc[...] = jnp.zeros(dqacc.shape, f32)
    last = me // 2

    def half_block(sb, half, masked):
        ks = pl.ds(pl.multiple_of(sb * SB, SB), SB)

        @pl.when(half == 0)
        def _():
            tot[...] = jnp.zeros(tot.shape, f32)

        for i in range(2):
            gs = pl.ds(pl.multiple_of((half * 2 + i) * SB, SB), SB)
            p = jnp.exp(nt(qa[gs, :], kaug[ks, :]))
            if masked:
                ok = visible(me, sb)
                p = jnp.where(jnp.concatenate([ok, ok], axis=0), p, 0.0)
            ds = (p * nt(da[gs, :], vaug[ks, :])).astype(bf16)
            kv = jnp.concatenate([kv_ref[2 * sb, 0:T, :], kv_ref[2 * sb + 1, 0:T, :]], axis=0)
            dqacc[gs, :] += nn(ds, kv)
            tot[0:H, :] += nn(qt_ref[0:H, gs], ds)
            tot[H:, :] += nn(dat_ref[0:H, gs], p.astype(bf16))

        @pl.when(half == 1)
        def _():
            low = jnp.transpose(tot[...]).astype(bf16)
            gsend[2 * sb] = low[0:T]
            gsend[2 * sb + 1] = low[T:]

    def to_owner(kb):
        return pltpu.make_async_remote_copy(src_ref=gsend.at[kb], dst_ref=grecv.at[me], send_sem=ksend.at[kb],
                                            recv_sem=krecv.at[me], device_id=(dp, kb), device_id_type=MESH)

    def from_device(b):
        return pltpu.make_async_remote_copy(src_ref=gsend.at[b], dst_ref=grecv.at[b], send_sem=ksend.at[b],
                                            recv_sem=krecv.at[b], device_id=(dp, b), device_id_type=MESH)

    def at_0():
        for i, h in ((0, 1), (1, 1), (2, 0), (3, 1)):
            early[i].pass0(h)

    def at_4():
        for s in early:
            s.pass1()

    def at_6():
        for s in early:
            s.pass2()

    def step(i, carry):
        sb, half = i // 2, i % 2

        @pl.when(sb < last)
        def _():
            half_block(sb, half, False)

            @pl.when(half == 1)
            def _():
                to_owner(2 * sb).start()
                to_owner(2 * sb + 1).start()

        pl.when(i == 0)(at_0)
        pl.when(i == 4)(at_4)

        return carry

    lax.fori_loop(0, 2 * (NSB - 1), step, 0)

    def last_step(half, carry):
        half_block(last, half, True)

        pl.when(half == 0)(at_6)
        return carry

    lax.fori_loop(0, 2, last_step, 0)

    @pl.when(2 * last < me)
    def _():
        to_owner(2 * last).start()

    for s in early:
        s.pass3()
    for s, (u0, u1, _) in zip(spreads, SPREADS):
        s.begin([early[{0: 0, 4: 1, 8: 3}[4 * (SHARED[u] // 4)]].result(SHARED[u]) for u in range(u0, u1)])
    for s, e, u in zip(owned_o, (early[0], early[2], early[3]), WO_UNIT):
        s.begin(e.result(u))
    for j in range(J):
        js = slice(j * T, (j + 1) * T)
        rows[j] = sub8(jnp.transpose(dqacc[js, :])[0:H].astype(bf16).astype(f32) * 0.125)
    to_experts(routes, rows, gat)
    for c in range(4):
        store_expert(lbig, core, [0, 1, 2], 2 * c, nn(gat[c * 384 : (c + 1) * 384, :], nm))
    for s in late:
        s.start0(0)
    acc_kv = tot
    acc_kv[:, 0:T] = jnp.transpose(gsend[me].astype(f32))
    for b in range(1, NB):
        @pl.when(b > me)
        def _(b=b):
            from_device(b).wait_recv()
            acc_kv[:, 0:T] += jnp.transpose(grecv[b].astype(f32))
    gkv = jnp.transpose(acc_kv[:, 0:T]).astype(bf16)
    dkvw = tn(nm, gkv).astype(bf16)
    for s in late:
        s.pass0(0)
    for s in spreads:
        s.pass2()
        s.send(0)
    gn = gn_ref[...] + tn(gat[...], wq_ref[...].reshape(EW, D)) + nt(gkv, kvw_ref[...])
    x = x_ref[...].astype(f32)
    inv = lax.rsqrt(jnp.mean(x * x, axis=-1, keepdims=True) + eps)
    n = x * inv
    dgain = jnp.sum(gn * n, axis=0, keepdims=True)
    drw = drw_ref[...]
    dfg = dfg_ref[...]
    parts = [dkvw.astype(f32)] + [drw[:, t * 128 : (t + 1) * 128] for t in range(4)]
    parts += [v[:, t * 128 : (t + 1) * 128] for v in (dgain, dfg) for t in range(4)] + [jnp.zeros((SMALL - 616, 128), f32)]
    ssrc[...] = jnp.concatenate(parts, axis=0).astype(bf16).reshape(2, 4, SMALL // 8, 128)
    small.step(0)
    small.step(1)
    for s in late:
        s.pass1()
    for s in spreads:
        s.send(1)
    small.step(2)
    hh = gn * gain_ref[...]
    ing_ref[...] = (gm_ref[...] + inv * (hh - n * jnp.mean(hh * n, axis=-1, keepdims=True))).astype(bf16)
    for s in late:
        s.pass2()
    for s in spreads:
        s.send(2)
        s.forward(0)
    small.step(3)
    for s, t, u in zip(owned_q, late, range(3)):
        t.pass3()
        s.begin(t.result(u))
    for s in spreads:
        s.forward(1)
    small.step(4)
    for s in owned_o + owned_q:
        s.finish()
    small.step(5)
    for s in spreads:
        s.forward(2)
    small.step(6)
    for s in spreads:
        s.finish()
    for b in range(NB - 1):
        @pl.when(b < me)
        def _(b=b):
            to_owner(b).wait_send()
    copies.drain()


SCRATCH = [
    VM((D, FF), bf16), VM((FF, D), bf16), pltpu.SemaphoreType.DMA((2,)), VM((T, D), bf16), VM((J, T), f32), VM((NB, KVR, 128), bf16),
    VM((NB, 3 * H, D), bf16), VM((NB, 3 * H, D), bf16), VM((H, ROWS), bf16), VM((128, ROWS), bf16), VM((EW // 8, 8, T), f32),
    VM((ROWS, 128), bf16), VM((ROWS, 128), bf16), VM((80, ROWS), bf16), VM((8, ROWS), f32), VM((80, ROWS), f32),
    VM((J, 8, 8, T), f32), VM((EW, T), bf16), VM((T, D), f32), VM((T, D), f32), VM((E, D), f32), VM((1, D), f32),
    VM((2, UNITS, 1024, 128), bf16), VM((UNITS, 4, 4, 4, 16, 128), bf16), VM((UNITS, 3, 4, 4, 16, 128), bf16),
    VM((UNITS, 3, 4, 16, 128), bf16), VM((UNITS, 4, 4, 16, 128), bf16),
    VM((128, ROWS), bf16), VM((ROWS, 128), bf16), VM((ROWS, 128), bf16), VM((ROWS, 128), f32), VM((128, SB), f32),
    VM((NB, T, 128), bf16), VM((NB, T, 128), bf16),
    VM((2, 3, 1024, 128), bf16), VM((3, 4, 4, 4, 16, 128), bf16), VM((3, 3, 4, 4, 16, 128), bf16), VM((3, 3, 4, 16, 128), bf16),
    VM((3, 4, 4, 16, 128), bf16),
    VM((2, 4, SMALL // 8, 128), bf16), VM((4, SMALL // 8, 128), bf16), VM((4, SMALL // 8, 128), bf16),
    VM((3, SMALL // 8, 128), bf16), VM((4, SMALL // 8, 128), bf16), VM((4, SMALL // 8, 128), bf16),
] + dma_sems(203) + dma_sems(NB)


def kernel_f(u0, u1, u2, u3, d0, d1, d2, d3, wo_ref, dwq_ref, small_ref, out_in, ing_in, dup_ref, ddown_ref, dwo_ref, dwqt_ref, dkvw_ref,
             drw_ref, dgain_ref, dfg_ref, out_ref, ing_ref):
    for t, (u, d) in enumerate(zip((u0, u1, u2, u3), (d0, d1, d2, d3))):
        ddown_ref[:, t * 128 : (t + 1) * 128] = d[0].astype(f32)
        for s in range(4):
            dup_ref[:, (4 * t + s) * 128 : (4 * t + s + 1) * 128] = u[0, s].astype(f32)

    @pl.when(pl.program_id(0) == 0)
    def _():
        for t in range(4):
            ts = slice(t * 128, (t + 1) * 128)
            dwo_ref[:, ts] = wo_ref[t * 192 : (t + 1) * 192, :].astype(f32)
            dwqt_ref[:, ts] = dwq_ref[t * 192 : (t + 1) * 192, :].astype(f32)
        small = small_ref[512:SMALL, :].astype(f32)
        dkvw_ref[...] = small_ref[0:512, :].astype(f32)
        for t in range(4):
            ts = slice(t * 128, (t + 1) * 128)
            drw_ref[:, ts] = small[t * E : (t + 1) * E]
            dgain_ref[:, ts] = small[96 + t : 97 + t]
            dfg_ref[:, ts] = small[100 + t : 101 + t]
        out_ref[...] = out_in[...]
        ing_ref[...] = ing_in[...]


def per_device(inputs, cotangent, norm_gain, ffn_gain, kv_weight, router_weight, query_weight, output_weight, up_weight,
               down_weight, routes, segment_ids):
    wq = jnp.swapaxes(query_weight, 1, 2).reshape(3 * H, D)
    wo = output_weight.reshape(3 * H, D)
    vmem, anywhere = pl.BlockSpec(memory_space=VM), pl.BlockSpec(memory_space=pl.ANY)
    S = jax.ShapeDtypeStruct
    out, ing, shared, dwo, dwq, small = pl.pallas_call(
        kernel_all,
        out_shape=[S((T, D), bf16), S((T, D), bf16), S((8, 2, 4, 4, 4, 16, 128), bf16), S((3, 4, 4, 16, 128), bf16),
                   S((3, 4, 4, 16, 128), bf16), S((2, 4, SMALL // 8, 128), bf16)],
        in_specs=[vmem] * 10 + [anywhere] * 2,
        out_specs=[vmem] * 6,
        scratch_shapes=SCRATCH,
        compiler_params=pltpu.CompilerParams(vmem_limit_bytes=62 << 20, collective_id=1, has_side_effects=True),
        cost_estimate=pl.CostEstimate(flops=1 << 35, bytes_accessed=1 << 24, transcendentals=0),
    )(inputs, cotangent, norm_gain.reshape(1, D), ffn_gain.reshape(1, D), kv_weight, router_weight.T, routes.T,
      segment_ids.reshape(3, 128), wq, wo, up_weight, down_weight)
    up_slots, down_slots = ([SHARED.index(u) for u in units] for units in (UP_UNIT, DOWN_UNIT))
    ups = [pl.BlockSpec((1, 4, 128, 128), lambda i, k=k: (k, 0, i, 0)) for k in up_slots]
    downs = [pl.BlockSpec((1, 512, 128), lambda i, k=k: (k, i, 0)) for k in down_slots]

    def whole(*shape):
        return pl.BlockSpec(shape, lambda i: (0,) * len(shape))

    dup, ddown, dwo, dwqt, dkvw, drw, dgain, dfg, out, ing = pl.pallas_call(
        kernel_f,
        grid=(4,),
        out_shape=[S((D, FF), f32), S((FF, D), f32), S((3 * H, D), f32), S((3 * H, D), f32), S((D, 128), f32), S((E, D), f32),
                   S((1, D), f32), S((1, D), f32), S((T, D), bf16), S((T, D), bf16)],
        in_specs=ups + downs + [
                  whole(768, 128), whole(768, 128), whole(SMALL, 128), whole(T, D), whole(T, D)],
        out_specs=[pl.BlockSpec((128, FF), lambda i: (i, 0)), pl.BlockSpec((512, D), lambda i: (i, 0)), whole(3 * H, D),
                   whole(3 * H, D), whole(D, 128), whole(E, D), whole(1, D), whole(1, D), whole(T, D), whole(T, D)],
        compiler_params=pltpu.CompilerParams(vmem_limit_bytes=62 << 20),
    )(*[shared.reshape(8, 4, 512, 128)] * 4, *[shared.reshape(8, 2048, 128)] * 4, dwo.reshape(768, 128), dwq.reshape(768, 128), small.reshape(SMALL, 128), out, ing)
    return (out, ing, dgain.reshape(D), dfg.reshape(D), dkvw, drw.T,
            jnp.swapaxes(dwqt.reshape(3, H, D), 1, 2), dwo.reshape(3, H, D), dup, ddown)


def solution(mesh):
    both = P(("dp", "expert"), None)
    ex = P("expert", None, None)
    return jax.shard_map(
        per_device, mesh=mesh,
        in_specs=(both, both, P(), P(), P(), P(), ex, ex, P(), P(), both, P(("dp", "expert"))),
        out_specs=(both, both, P(), P(), P(), P(), ex, ex, P(), P()),
        check_vma=False)
```

```python
import functools
import jax
import jax.numpy as jnp
from jax import lax
from jax.experimental import pallas as pl
from jax.experimental.pallas import tpu as pltpu
from jax.sharding import PartitionSpec as P

f32, bf16, i32 = jnp.float32, jnp.bfloat16, jnp.int32
T, D, H, J, E, FF, NB = 384, 512, 64, 8, 24, 2048, 8
EW = E * H
ROWS = J * T
SB = 2 * T
NSB = NB // 2
eps = 1e-06
NEG = -1e30
VM = pltpu.VMEM


def nn(a, b):
    return lax.dot_general(a, b, (((1,), (0,)), ((), ())), preferred_element_type=f32)


def nt(a, b):
    return lax.dot_general(a, b, (((1,), (1,)), ((), ())), preferred_element_type=f32)


def tn(a, b):
    return lax.dot_general(a, b, (((0,), (0,)), ((), ())), preferred_element_type=f32)


def lanes(rows):
    return lax.broadcasted_iota(i32, (rows, 128), 1)


def split3(v):
    a = v.astype(bf16).astype(f32)
    b = (v - a).astype(bf16).astype(f32)
    c = (v - a - b).astype(bf16).astype(f32)
    return a, b, c


MESH = pl.DeviceIdType.MESH
LINES = [(a, k) for a in "xyz" for k in (1, 2, 3)]
ALL_PEERS = [("c", 0)] + LINES


class Place:
    def __init__(self):
        dp, ex = lax.axis_index("dp"), lax.axis_index("expert")
        self.ex = ex
        self.at = {"x": dp // 4, "y": dp % 4, "z": ex // 2, "c": ex % 2}
        self.peers = {("c", 0): self.device(c=1 - self.at["c"])}
        for axis, k in LINES:
            self.peers[axis, k] = self.device(**{axis: (self.at[axis] + k) % 4})

    def device(self, **moved):
        at = {**self.at, **moved}
        return (at["x"] * 4 + at["y"], at["z"] * 2 + at["c"])


class Copies:
    def __init__(self, place, send, recv):
        self.place, self.send, self.recv, self.made = place, send, recv, []

    def add(self, src, dst, peer):
        self.made.append((src, dst, peer))
        return len(self.made) - 1

    def get(self, i):
        src, dst, peer = self.made[i]
        return pltpu.make_async_remote_copy(src_ref=src(), dst_ref=dst(), send_sem=self.send.at[i], recv_sem=self.recv.at[i],
                                            device_id=self.place.peers[peer], device_id_type=MESH)

    def start(self, ids):
        for i in ids:
            self.get(i).start()

    def arrived(self, ids):
        for i in ids:
            self.get(i).wait_recv()

    def sent(self, ids):
        for i in ids:
            self.get(i).wait_send()

    def drain(self):
        self.sent(range(len(self.made)))


class Scatter:
    def __init__(self, copies, big, r, ex, parts, groups, order):
        self.cp, self.big, self.r, self.ex = copies, big, r, ex
        self.parts, self.groups, self.u0, self.u1 = parts, groups, parts[0][0], parts[-1][1]
        at = copies.place.at
        self.m = m = [at[a] for a in order]
        rng = lambda g: pl.ds(g[0], g[1] - g[0])
        us = rng((self.u0, self.u1))
        self.part_ids = [copies.add(lambda g=g: big.at[1, rng(g)], lambda g=g: r[0].at[rng(g)], ("c", 0)) for g in parts]
        self.group_ids = [
            [copies.add(lambda g=g, k=k: big.at[0, rng(g), (m[0] + k) % 4], lambda g=g, k=k: r[1].at[rng(g), k - 1], (order[0], k))
             for k in (1, 2, 3)] for g in groups]
        self.ids2 = [copies.add(lambda k=k: big.at[0, us, m[0], (m[1] + k) % 4], lambda k=k: r[2].at[us, k - 1], (order[1], k))
                     for k in (1, 2, 3)]
        own = lambda: ex.at[us, m[2]]
        self.ids3 = [copies.add(own, own, (order[2], k)) for k in (1, 2, 3)]

    def start0(self, i):
        self.cp.start([self.part_ids[i]])

    def pass0(self, h):
        g = self.groups[h]
        self.cp.arrived([i for i, p in zip(self.part_ids, self.parts) if g[0] <= p[0] < g[1]])
        for u in range(*g):
            for a in range(4):
                v = self.big[0, u, a].astype(f32) + self.r[0][u, a].astype(f32)
                self.big[0, u, a] = v.astype(bf16)
        self.cp.start(self.group_ids[h])

    def add3(self, u, at, r):
        v = self.big[at].astype(f32)
        for k in range(3):
            v = v + r[u, k].astype(f32)
        return v.astype(bf16)

    def pass1(self):
        for h, g in enumerate(self.groups):
            self.cp.arrived(self.group_ids[h])
            for u in range(*g):
                at = (0, u, self.m[0])
                self.big[at] = self.add3(u, at, self.r[1])
        self.cp.start(self.ids2)

    def pass2(self):
        self.cp.arrived(self.ids2)
        for u in range(self.u0, self.u1):
            self.ex[u, self.m[2]] = self.add3(u, (0, u, self.m[0], self.m[1]), self.r[2])
        self.cp.start(self.ids3)

    def pass3(self):
        self.cp.arrived(self.ids3)

    def result(self, u):
        e = [self.ex[u, i].astype(f32) for i in range(4)]
        return (e[0] + e[1] + e[2] + e[3]).astype(bf16)


class Spread:
    def __init__(self, copies, out, kept, kept_sem, u0, u1, order):
        self.cp, self.out, self.kept, self.kept_sem, self.u0, self.u1 = copies, out, kept, kept_sem, u0, u1
        at = copies.place.at
        self.c, self.m = at["c"], [at[a] for a in order]
        us = pl.ds(u0, u1 - u0)
        quarter = lambda: out.at[us, self.c, self.m[0], self.m[1]]
        self.ids2 = [copies.add(quarter, quarter, (order[1], k)) for k in (1, 2, 3)]
        self.ids1, self.ids0 = [], []
        for u in range(u0, u1):
            piece = lambda k=0, u=u: out.at[u, self.c, (self.m[0] - k + 4) % 4]
            self.ids1.append([copies.add(piece, piece, (order[0], k)) for k in (1, 2, 3)])
            self.ids0.append([copies.add(functools.partial(piece, k), functools.partial(piece, k), ("c", 0)) for k in range(4)])

    def begin(self, values):
        for u, v in zip(range(self.u0, self.u1), values):
            self.out[u, self.c, self.m[0], self.m[1]] = v
        self.cp.start(self.ids2)

    def pass2(self):
        self.cp.arrived(self.ids2)

    def send(self, i):
        if i < len(self.ids1):
            self.cp.start(self.ids1[i] + self.ids0[i][:1])

    def forward(self, i):
        if i < len(self.ids1):
            for k in (1, 2, 3):
                self.cp.arrived(self.ids1[i][k - 1 : k])
                self.cp.start(self.ids0[i][k : k + 1])

    def finish(self, i):
        if i < len(self.ids0):
            self.cp.arrived(self.ids0[i])
            self.keep(self.u0 + i).start()

    def keep(self, u):
        return pltpu.make_async_copy(self.out.at[u], self.kept.at[u], self.kept_sem.at[u])


class SpreadOwner:
    def __init__(self, copies, out, u, axis):
        self.cp, self.out, self.u, self.p = copies, out, u, copies.place.at[axis]
        ref = lambda: out.at[u, self.p]
        self.ids = [copies.add(ref, ref, (axis, k)) for k in (1, 2, 3)]

    def begin(self, value):
        self.out[self.u, self.p] = value
        self.cp.start(self.ids)

    def finish(self):
        self.cp.arrived(self.ids)


class SmallSum:
    def __init__(self, copies, src, half, r0, r1, by, bz, out):
        self.cp, self.src, self.half, self.r0, self.r1, self.by, self.bz, self.out = copies, src, half, r0, r1, by, bz, out
        at = copies.place.at
        self.c, self.x, self.y, self.z = at["c"], at["x"], at["y"], at["z"]
        own_half = lambda: out.at[self.c]
        own = lambda: out.at[self.c, self.x]
        self.ids = [
            [copies.add(lambda: src.at[1 - self.c], lambda: r0, ("c", 0))],
            [copies.add(lambda k=k: half.at[(self.x + k) % 4], lambda k=k: r1.at[k - 1], ("x", k)) for k in (1, 2, 3)],
            [copies.add(lambda: by.at[self.y], lambda: by.at[self.y], ("y", k)) for k in (1, 2, 3)],
            [copies.add(lambda: bz.at[self.z], lambda: bz.at[self.z], ("z", k)) for k in (1, 2, 3)],
            [copies.add(own, own, ("x", k)) for k in (1, 2, 3)],
            [copies.add(own_half, own_half, ("c", 0))],
        ]

    def step(self, i):
        if i:
            self.cp.arrived(self.ids[i - 1])
        if i == 1:
            for a in range(4):
                self.half[a] = (self.src[self.c, a].astype(f32) + self.r0[a].astype(f32)).astype(bf16)
        if i == 2:
            v = self.half[self.x].astype(f32)
            for k in range(3):
                v = v + self.r1[k].astype(f32)
            self.by[self.y] = v.astype(bf16)
        if i in (3, 4):
            b = self.by if i == 3 else self.bz
            v = (b[0].astype(f32) + b[1].astype(f32) + b[2].astype(f32) + b[3].astype(f32)).astype(bf16)
            if i == 3:
                self.bz[self.z] = v
            else:
                self.out[self.c, self.x] = v
        if i < 6:
            self.cp.start(self.ids[i])


UNITS = 11
UP_UNIT, DOWN_UNIT, WO_UNIT = [0, 4, 8, 2], [1, 5, 9, 6], [3, 7, 10]
SHARED = sorted(UP_UNIT + DOWN_UNIT)
OWNER_ORDERS = ["zxy", "xzy", "yzx"]
EARLY = [([(0, 2), (2, 3), (3, 4)], [(0, 2), (2, 4)], "zxy"), ([(4, 6), (6, 7)], [(4, 6), (6, 7)], "xyz"),
         ([(7, 8)], [(7, 8)], "xzy"), ([(8, 10), (10, 11)], [(8, 10), (10, 11)], "yzx")]
CHUNK_PARTS, WO_PARTS = [[(0, 0)], [(1, 0)], [(3, 0)], [(0, 1), (1, 1)]], [(0, 2), (2, 0), (3, 1)]
SPREADS = [(0, 3, "zxy"), (3, 6, "xyz"), (6, 8, "yzx")]


def plane_axes(order):
    return [a for a in order if a != "z"]


def expert_row(ex, piece, order):
    p, q = plane_axes(order)
    at = {p: piece // 4, q: piece % 4, "z": ex // 2}
    r = ex % 2
    for a in order:
        r = r * 4 + at[a]
    return r * 16


def store_expert(big, core, units, ex0, value):
    low = value.astype(bf16)
    for o in range(2):
        slot = (core + (ex0 + o) % 2) % 2
        for row in range(0, 768, 16):
            v, piece = row // 256, (row % 256) // 16
            ct, r = row // 192, row % 192
            base = expert_row(ex0 + o, piece, OWNER_ORDERS[v]) % 1024
            big[slot, units[v], base : base + 16, :] = low[o * 192 + r : o * 192 + r + 16, ct * 128 : (ct + 1) * 128]


KVR = T + 16


class Gather:
    def __init__(self, copies, out):
        self.cp, self.out = copies, out
        at, ex = copies.place.at, copies.place.ex
        own = lambda: out.at[ex]
        from_z = lambda k: out.at[((at["z"] - k + 4) % 4) * 2 + at["c"]]
        self.line = [copies.add(own, own, ("z", k)) for k in (1, 2, 3)]
        self.core = [copies.add(functools.partial(from_z, k), functools.partial(from_z, k), ("c", 0)) for k in (0, 1, 2, 3)]

    def start(self):
        self.cp.start(self.line)
        self.cp.start(self.core[:1])

    def forward(self):
        for k in range(3):
            self.cp.arrived(self.line[k : k + 1])
            self.cp.start(self.core[k + 1 : k + 2])

    def finish(self):
        self.cp.arrived(self.core)


def bounds_of(kv_ref):
    n0 = n1 = 0.0
    for b in range(NB):
        tail = kv_ref[b, T:KVR, :].astype(f32)
        n0 = n0 + 16.0 * tail[0:1] + tail[1:2]
        n1 = n1 + 16.0 * tail[2:3] + tail[3:4]
    return n0, n1


def segment_of(pos, bounds):
    return (pos >= bounds[0]).astype(i32) + (pos >= bounds[1]).astype(i32)


def sub8(v):
    return v.reshape(8, 8, v.shape[-1])


def route_rows(rt_ref):
    return [jnp.broadcast_to(rt_ref[j : j + 1, :], (8, T)) for j in range(J)]


def visible(me, sb):
    key = lax.broadcasted_iota(i32, (T, SB), 1)
    tok = lax.broadcasted_iota(i32, (T, SB), 0)
    ok = key - tok <= (me - 2 * sb) * T
    return ok


def prepare_keys(kv_ref, bounds, kaug, vaug, vt):
    ln = lanes(T)
    for b in range(NB):
        bs = slice(b * T, (b + 1) * T)
        kv = kv_ref[b, 0:T, :].astype(f32)
        pos = (lax.broadcasted_iota(i32, (T, 128), 0) + b * T).astype(f32)
        seg = segment_of(pos, bounds)
        feat = jnp.where((ln < H + 3) & (seg != ln - H), NEG, 0.0)
        feat = jnp.where((ln >= H + 3) & (ln < H + 6), 1.0, feat)
        kaug[bs, :] = jnp.where(ln < H, kv, feat).astype(bf16)
        if vaug is not None:
            one = jnp.where(ln < H + 3, 1.0, 0.0)
            vaug[bs, :] = jnp.where(ln < H, pltpu.roll(kv, H, 1), one).astype(bf16)
        if vt is not None:
            ones = jnp.where(lax.broadcasted_iota(i32, (16, T), 0) == 0, 1.0, 0.0)
            vt[:, bs] = jnp.concatenate([jnp.transpose(kv)[H:], ones], axis=0).astype(bf16)


def project_queries(normed, wq_ref, qall):
    for c in range(4):
        w = wq_ref[2 * c : 2 * c + 2].reshape(2 * 3 * H, D)
        qall[c * 48 : (c + 1) * 48] = (nt(w, normed) * 0.125).reshape(48, 8, T)


def choose(routes, table, j):
    acc = table[0:8]
    for e in range(1, E):
        acc = jnp.where((routes[j] == e)[None], table[e * 8 : (e + 1) * 8], acc)
    return acc


def to_experts(routes, rows, out):
    for e in range(E):
        acc = jnp.zeros((8, 8, T), f32)
        for j in range(J):
            acc = jnp.where((routes[j] == e)[None], rows[j], acc)
        out[e * H : (e + 1) * H, :] = acc.reshape(H, T).astype(bf16)


def pick_queries(rt_ref, table, qt):
    routes = route_rows(rt_ref)
    for j in range(J):
        qt[0:H, j * T : (j + 1) * T] = choose(routes, table, j).reshape(H, T).astype(bf16)


def mark_queries(bounds, me, qt):
    pos = (lax.broadcasted_iota(i32, (H, T), 1) + me * T).astype(f32)
    seg = segment_of(pos, (bounds[0][:, 0:1], bounds[1][:, 0:1]))
    feat = jnp.where(lax.broadcasted_iota(i32, (H, T), 0) == seg, 1.0, 0.0).astype(bf16)
    for j in range(J):
        qt[H:, j * T : (j + 1) * T] = feat


def attend(me, qt, kaug, vt, att, macc, acc):
    last = me // 2
    macc[...] = jnp.full(macc.shape, NEG, f32)
    acc[...] = jnp.zeros(acc.shape, f32)

    def score(sb, g, masked):
        s = nn(kaug[pl.ds(pl.multiple_of(sb * SB, SB), SB), :], qt[:, g * SB : (g + 1) * SB])
        if masked:
            key = lax.broadcasted_iota(i32, (SB, T), 0)
            tok = lax.broadcasted_iota(i32, (SB, T), 1)
            ok = key - tok <= (me - 2 * sb) * T
            s = jnp.where(jnp.concatenate([ok, ok], axis=1), s, NEG)
        return s.reshape(SB // 8, 8, SB)

    def soften(s, g):
        gs = slice(g * SB, (g + 1) * SB)
        old = macc[:, gs]
        top = jnp.max(jnp.maximum(old, jnp.max(s, axis=0)), axis=0, keepdims=True)
        top = jnp.broadcast_to(top, (8, SB))
        macc[:, gs] = top
        return jnp.exp(s - top[None]).reshape(SB, SB).astype(bf16), jnp.exp(old - top)

    def weigh(sb, g, p, kept):
        gs = slice(g * SB, (g + 1) * SB)
        old = acc[:, gs].reshape(10, 8, SB) * kept[None]
        acc[:, gs] = old.reshape(80, SB) + nn(vt[:, pl.ds(pl.multiple_of(sb * SB, SB), SB)], p)

    def block(sb, masked):
        s = score(sb, 0, masked)
        held = None
        for g in range(J // 2):
            ahead = score(sb, g + 1, masked) if g + 1 < J // 2 else None
            new = soften(s, g)
            if g:
                weigh(sb, g - 1, *held)
            held, s = new, ahead
        weigh(sb, J // 2 - 1, *held)

    lax.fori_loop(0, last, lambda sb, c: (block(sb, False), c)[1], 0)
    block(last, True)
    for g in range(J // 2):
        gs = slice(g * SB, (g + 1) * SB)
        tot = acc[H : H + 1, gs]
        att[:, gs] = (acc[0:H, gs] / tot).astype(bf16)
        l1, l2, l3 = split3(-(macc[0:1, gs] + jnp.log(tot)))
        row = lax.broadcasted_iota(i32, (16, SB), 0)
        feat = qt[H : H + 16, gs].astype(f32)
        feat = jnp.where(row == 3, l1, jnp.where(row == 4, l2, jnp.where(row == 5, l3, feat)))
        qt[H : H + 16, gs] = feat.astype(bf16)


def gates_of(normed, rw_ref, rt_ref, gate_ref):
    logits = nt(rw_ref[...], normed)
    eid = lax.broadcasted_iota(i32, (E, T), 0)
    per = [jnp.sum(jnp.where(rt_ref[j : j + 1, :] == eid, logits, 0.0), axis=0, keepdims=True) for j in range(J)]
    v = jnp.concatenate(per, axis=0)
    e = jnp.exp(v - jnp.max(v, axis=0, keepdims=True))
    gate_ref[...] = e / jnp.sum(e, axis=0, keepdims=True)


SMALL = 640


def dma_sems(n):
    return [pltpu.SemaphoreType.DMA((n,)), pltpu.SemaphoreType.DMA((n,))]


def kernel_all(x_ref, cot_ref, gain_ref, fgain_ref, kvw_ref, rw_ref, rt_ref, seg_ref, wq_in, wo_in, up_hbm, down_hbm,
               out_ref, ing_ref, all_hbm, dwo_ref, dwq_ref, small_ref,
               shared, all_sem, up_ref, down_ref, wsem, normed_ref, gate_ref, kv_ref, wq_ref, wo_ref, att_ref, qt_ref, table, kaug, vaug, vt, macc, acc,
               rows, gat, gm_ref, gn_ref, drw_ref, dfg_ref, big, r0, r1, r2, ex,
               dat_ref, qa, da, dqacc, tot, gsend, grecv, lbig, l0, l1, l2, lex, ssrc, shalf, s0, s1, sy, sz, send, recv, ksend, krecv):
    place = Place()
    me, core = place.ex, place.at["c"]
    dp = lax.axis_index("dp")
    copies = Copies(place, send, recv)
    gq, gk, go = Gather(copies, wq_ref), Gather(copies, kv_ref), Gather(copies, wo_ref)
    big7 = big.reshape(2, UNITS, 4, 4, 4, 16, 128)
    lbig7 = lbig.reshape(2, 3, 4, 4, 4, 16, 128)
    early = [Scatter(copies, big7, (r0, r1, r2), ex, parts, groups, o) for parts, groups, o in EARLY]
    late = [Scatter(copies, lbig7, (l0, l1, l2), lex, [(u, u + 1)], [(u, u + 1)], o) for u, o in enumerate(OWNER_ORDERS)]
    spreads = [Spread(copies, shared, all_hbm, all_sem, u0, u1, o) for u0, u1, o in SPREADS]
    owned_o = [SpreadOwner(copies, dwo_ref, u, plane_axes(o)[0]) for u, o in enumerate(OWNER_ORDERS)]
    owned_q = [SpreadOwner(copies, dwq_ref, u, plane_axes(o)[0]) for u, o in enumerate(OWNER_ORDERS)]
    small = SmallSum(copies, ssrc, shalf, s0, s1, sy, sz, small_ref)

    bar = pltpu.get_barrier_semaphore()
    for p in ALL_PEERS:
        pl.semaphore_signal(bar, inc=1, device_id=place.peers[p], device_id_type=MESH)
    for k in range(1, NB):
        pl.semaphore_signal(bar, inc=1, device_id=(dp, (me + k) % NB), device_id_type=MESH)
    loads = [pltpu.make_async_copy(up_hbm, up_ref, wsem.at[0]), pltpu.make_async_copy(down_hbm, down_ref, wsem.at[1])]
    for cp in loads:
        cp.start()
    wq_ref[me] = wq_in[...]
    wo_ref[me] = wo_in[...]

    x = x_ref[...].astype(f32)
    inv = lax.rsqrt(jnp.mean(x * x, axis=-1, keepdims=True) + eps)
    normed = (x * inv * gain_ref[...]).astype(bf16)
    normed_ref[...] = normed
    kv_ref[me, 0:T, :] = nn(normed, kvw_ref[...]).astype(bf16)
    seg = seg_ref[...]
    row = lax.broadcasted_iota(i32, (16, 128), 0)
    tail = jnp.zeros((16, 128), f32)
    for s in range(2):
        n = jnp.sum(jnp.sum((seg <= s).astype(f32), axis=0, keepdims=True), axis=1, keepdims=True)
        n = jnp.broadcast_to(n, (16, 128))
        hi = jnp.floor(n * 0.0625)
        tail = jnp.where(row == 2 * s, hi, jnp.where(row == 2 * s + 1, n - 16.0 * hi, tail))
    kv_ref[me, T:KVR, :] = tail.astype(bf16)
    pl.semaphore_wait(bar, len(ALL_PEERS) + NB - 1)
    gq.start()
    gk.start()
    gates_of(normed, rw_ref, rt_ref, gate_ref)
    gq.forward()
    gq.finish()
    project_queries(normed, wq_ref, table)
    pick_queries(rt_ref, table, qt_ref)
    gk.forward()
    gk.finish()
    bounds = bounds_of(kv_ref)
    prepare_keys(kv_ref, bounds, kaug, vaug, vt)
    mark_queries(bounds, me, qt_ref)
    go.start()
    attend(me, qt_ref, kaug, vt, att_ref, macc, acc)

    go.forward()
    routes = route_rows(rt_ref)
    for j in range(J):
        rows[j] = sub8(att_ref[:, j * T : (j + 1) * T].astype(f32) * gate_ref[j : j + 1, :])
    to_experts(routes, rows, gat)
    go.finish()
    x = x_ref[...].astype(f32)
    wo_all = wo_ref[...].reshape(EW, D)
    mixed = x + tn(gat[...], wo_all)
    inv = lax.rsqrt(jnp.mean(mixed * mixed, axis=-1, keepdims=True) + eps)
    n = mixed * inv
    fgain = fgain_ref[...]
    second = (n * fgain).astype(bf16)
    second_t = jnp.transpose(n * fgain).astype(bf16)
    cot = cot_ref[...]
    for cp in loads:
        cp.wait()
    C = 512
    out = mixed
    gsec = jnp.zeros((T, D), f32)
    ahead = nn(second, up_ref[:, 0:C]), nt(cot, down_ref[0:C, :])
    for c in range(FF // C):
        cs = slice(c * C, (c + 1) * C)
        v, gact = ahead
        if c + 1 < FF // C:
            ns = slice((c + 1) * C, (c + 2) * C)
            ahead = nn(second, up_ref[:, ns]), nt(cot, down_ref[ns, :])
        v2 = v * v
        th = jnp.tanh(0.7978845608028654 * (v + 0.044715 * v * v2))
        a = (0.5 * v * (1.0 + th)).astype(bf16)
        dth = 0.5 * (1.0 + th) + 0.5 * v * (1.0 - th * th) * (0.7978845608028654 * (1.0 + 0.134145 * v2))
        gh = (gact * dth).astype(bf16)
        out = out + nn(a, down_ref[cs, :])
        gsec = gsec + nt(gh, up_ref[:, cs])
        gdown = tn(a, cot).astype(bf16)
        gup = nn(second_t, gh).astype(bf16)
        for t in range(4):
            ts = slice(t * 128, (t + 1) * 128)
            big[(core + t // 2) % 2, DOWN_UNIT[c], t % 2 * 512 : t % 2 * 512 + 512, :] = gdown[:, ts]
            big[(core + t // 2) % 2, UP_UNIT[c], t % 2 * 512 : t % 2 * 512 + 512, :] = gup[:, ts]
        for b, i in CHUNK_PARTS[c]:
            early[b].start0(i)
    for i in (0, 1, 3):
        early[i].pass0(0)
    out_ref[...] = out.astype(bf16)
    dfg_ref[...] = jnp.sum(gsec * n, axis=0, keepdims=True)
    hh = gsec * fgain
    gm = cot.astype(f32) + inv * (hh - n * jnp.mean(hh * n, axis=-1, keepdims=True))
    gm_ref[...] = gm
    gml = gm.astype(bf16)
    for c in range(4):
        store_expert(big, core, WO_UNIT, 2 * c, nn(gat[c * 384 : (c + 1) * 384, :], gml))
    for b, i in WO_PARTS:
        early[b].start0(i)
    for c in range(4):
        w = wo_ref[2 * c : 2 * c + 2].reshape(2 * 3 * H, D)
        table[c * 48 : (c + 1) * 48] = nt(w, gml).reshape(48, 8, T)
    dots = []
    row = lax.broadcasted_iota(i32, (H, T), 0)
    for j in range(J):
        js = slice(j * T, (j + 1) * T)
        g = choose(routes, table, j).reshape(H, T)
        gate = gate_ref[j : j + 1, :]
        dot = jnp.sum(g * att_ref[:, js].astype(f32), axis=0, keepdims=True)
        dots.append(dot)
        d1, d2, d3 = split3(-(dot * gate))
        dat_ref[0:H, js] = (g * gate).astype(bf16)
        dat_ref[H:, js] = jnp.where(row == 0, d1, jnp.where(row == 1, d2, jnp.where(row == 2, d3, 0.0))).astype(bf16)
    dots = jnp.concatenate(dots, axis=0)
    gates = gate_ref[...]
    chosen = gates * (dots - jnp.sum(gates * dots, axis=0, keepdims=True))
    eid = lax.broadcasted_iota(i32, (E, T), 0)
    gl = jnp.zeros((E, T), f32)
    for j in range(J):
        gl = jnp.where(rt_ref[j : j + 1, :] == eid, chosen[j : j + 1, :], gl)
    hi = gl.astype(bf16)
    lo = (gl - hi.astype(f32)).astype(bf16)
    rw = rw_ref[...]
    gn_ref[...] = tn(hi, rw) + tn(lo, rw)
    nm = normed_ref[...]
    drw_ref[...] = nn(hi, nm) + nn(lo, nm)

    for j in range(J):
        js = slice(j * T, (j + 1) * T)
        qa[js, :] = jnp.transpose(qt_ref[:, js].astype(f32)).astype(bf16)
        da[js, :] = jnp.transpose(dat_ref[:, js].astype(f32)).astype(bf16)
    dqacc[...] = jnp.zeros(dqacc.shape, f32)
    for i, h in ((0, 1), (1, 1), (2, 0), (3, 1)):
        early[i].pass0(h)
    last = me // 2

    def half_block(sb, half, masked):
        ks = pl.ds(pl.multiple_of(sb * SB, SB), SB)

        @pl.when(half == 0)
        def _():
            tot[...] = jnp.zeros(tot.shape, f32)

        for i in range(2):
            gs = pl.ds(pl.multiple_of((half * 2 + i) * SB, SB), SB)
            p = jnp.exp(nt(qa[gs, :], kaug[ks, :]))
            if masked:
                ok = visible(me, sb)
                p = jnp.where(jnp.concatenate([ok, ok], axis=0), p, 0.0)
            ds = (p * nt(da[gs, :], vaug[ks, :])).astype(bf16)
            kv = jnp.concatenate([kv_ref[2 * sb, 0:T, :], kv_ref[2 * sb + 1, 0:T, :]], axis=0)
            dqacc[gs, :] += nn(ds, kv)
            tot[0:H, :] += nn(qt_ref[0:H, gs], ds)
            tot[H:, :] += nn(dat_ref[0:H, gs], p.astype(bf16))

        @pl.when(half == 1)
        def _():
            low = jnp.transpose(tot[...]).astype(bf16)
            gsend[2 * sb] = low[0:T]
            gsend[2 * sb + 1] = low[T:]

    def to_owner(kb):
        return pltpu.make_async_remote_copy(src_ref=gsend.at[kb], dst_ref=grecv.at[me], send_sem=ksend.at[kb],
                                            recv_sem=krecv.at[me], device_id=(dp, kb), device_id_type=MESH)

    def from_device(b):
        return pltpu.make_async_remote_copy(src_ref=gsend.at[b], dst_ref=grecv.at[b], send_sem=ksend.at[b],
                                            recv_sem=krecv.at[b], device_id=(dp, b), device_id_type=MESH)

    def at_3():
        for s in early:
            s.pass1()

    def at_5():
        for s in early:
            s.pass2()

    def step(i, carry):
        sb, half = i // 2, i % 2

        @pl.when(sb < last)
        def _():
            half_block(sb, half, False)

            @pl.when(half == 1)
            def _():
                to_owner(2 * sb).start()
                to_owner(2 * sb + 1).start()

        pl.when(i == 3)(at_3)
        pl.when(i == 5)(at_5)

        return carry

    lax.fori_loop(0, 2 * (NSB - 1), step, 0)

    def last_step(half, carry):
        half_block(last, half, True)

        return carry

    lax.fori_loop(0, 2, last_step, 0)

    @pl.when(2 * last < me)
    def _():
        to_owner(2 * last).start()

    for s in early:
        s.pass3()
    for s, e, (u0, u1, _) in zip(spreads, (early[0], early[1], early[3]), SPREADS):
        s.begin([e.result(SHARED[u]) for u in range(u0, u1)])
    for s, e, u in zip(owned_o, (early[0], early[2], early[3]), WO_UNIT):
        s.begin(e.result(u))
    for j in range(J):
        js = slice(j * T, (j + 1) * T)
        rows[j] = sub8(jnp.transpose(dqacc[js, :])[0:H].astype(bf16).astype(f32) * 0.125)
    to_experts(routes, rows, gat)
    for s in spreads:
        s.pass2()
        s.send(0)
    for c in range(4):
        store_expert(lbig, core, [0, 1, 2], 2 * c, nn(gat[c * 384 : (c + 1) * 384, :], nm))
    for s in late:
        s.start0(0)
    for s in spreads:
        s.send(1)
    dqacc[0:T, :] = gsend[me].astype(f32)
    for b in range(1, NB):
        @pl.when(b > me)
        def _(b=b):
            from_device(b).wait_recv()
            dqacc[0:T, :] += grecv[b].astype(f32)
    gkv = dqacc[0:T, :].astype(bf16)
    dkvw = tn(nm, gkv).astype(bf16)
    for s in late:
        s.pass0(0)
    for s in spreads:
        s.send(2)
    gn = gn_ref[...] + tn(gat[...], wq_ref[...].reshape(EW, D)) + nt(gkv, kvw_ref[...])
    x = x_ref[...].astype(f32)
    inv = lax.rsqrt(jnp.mean(x * x, axis=-1, keepdims=True) + eps)
    n = x * inv
    dgain = jnp.sum(gn * n, axis=0, keepdims=True)
    drw = drw_ref[...]
    dfg = dfg_ref[...]
    parts = [dkvw.astype(f32)] + [drw[:, t * 128 : (t + 1) * 128] for t in range(4)]
    parts += [v[:, t * 128 : (t + 1) * 128] for v in (dgain, dfg) for t in range(4)] + [jnp.zeros((SMALL - 616, 128), f32)]
    ssrc[...] = jnp.concatenate(parts, axis=0).astype(bf16).reshape(2, 4, SMALL // 8, 128)
    small.step(0)
    small.step(1)
    for s in late:
        s.pass1()
    for s in spreads:
        s.forward(0)
    small.step(2)
    hh = gn * gain_ref[...]
    ing_ref[...] = (gm_ref[...] + inv * (hh - n * jnp.mean(hh * n, axis=-1, keepdims=True))).astype(bf16)
    for s in late:
        s.pass2()
    for s in spreads:
        s.finish(0)
        s.forward(1)
    small.step(3)
    for s, t, u in zip(owned_q, late, range(3)):
        t.pass3()
        s.begin(t.result(u))
    for s in spreads:
        s.finish(1)
        s.forward(2)
    small.step(4)
    for s in owned_o + owned_q:
        s.finish()
    small.step(5)
    for s in spreads:
        s.finish(2)
    small.step(6)
    for s in spreads:
        for u in range(s.u0, s.u1):
            s.keep(u).wait()
    for b in range(NB - 1):
        @pl.when(b < me)
        def _(b=b):
            to_owner(b).wait_send()
    copies.drain()


SCRATCH = [
    VM((8, 2, 4, 4, 4, 16, 128), bf16), pltpu.SemaphoreType.DMA((8,)),
    VM((D, FF), bf16), VM((FF, D), bf16), pltpu.SemaphoreType.DMA((2,)), VM((T, D), bf16), VM((J, T), f32), VM((NB, KVR, 128), bf16),
    VM((NB, 3 * H, D), bf16), VM((NB, 3 * H, D), bf16), VM((H, ROWS), bf16), VM((128, ROWS), bf16), VM((EW // 8, 8, T), f32),
    VM((ROWS, 128), bf16), VM((ROWS, 128), bf16), VM((80, ROWS), bf16), VM((8, ROWS), f32), VM((80, ROWS), f32),
    VM((J, 8, 8, T), f32), VM((EW, T), bf16), VM((T, D), f32), VM((T, D), f32), VM((E, D), f32), VM((1, D), f32),
    VM((2, UNITS, 1024, 128), bf16), VM((UNITS, 4, 4, 4, 16, 128), bf16), VM((UNITS, 3, 4, 4, 16, 128), bf16),
    VM((UNITS, 3, 4, 16, 128), bf16), VM((UNITS, 4, 4, 16, 128), bf16),
    VM((128, ROWS), bf16), VM((ROWS, 128), bf16), VM((ROWS, 128), bf16), VM((ROWS, 128), f32), VM((128, SB), f32),
    VM((NB, T, 128), bf16), VM((NB, T, 128), bf16),
    VM((2, 3, 1024, 128), bf16), VM((3, 4, 4, 4, 16, 128), bf16), VM((3, 3, 4, 4, 16, 128), bf16), VM((3, 3, 4, 16, 128), bf16),
    VM((3, 4, 4, 16, 128), bf16),
    VM((2, 4, SMALL // 8, 128), bf16), VM((4, SMALL // 8, 128), bf16), VM((4, SMALL // 8, 128), bf16),
    VM((3, SMALL // 8, 128), bf16), VM((4, SMALL // 8, 128), bf16), VM((4, SMALL // 8, 128), bf16),
] + dma_sems(201) + dma_sems(NB)


def kernel_f(u0, u1, u2, u3, down, wo_ref, dwq_ref, small_ref, out_in, ing_in, dup_ref, ddown_ref, dwo_ref, dwqt_ref, dkvw_ref,
             drw_ref, dgain_ref, dfg_ref, out_ref, ing_ref):
    for t, u in enumerate((u0, u1, u2, u3)):
        ddown_ref[:, t * 128 : (t + 1) * 128] = down[0, t].astype(f32)
        for s in range(4):
            dup_ref[:, (4 * t + s) * 128 : (4 * t + s + 1) * 128] = u[0, s].astype(f32)

    @pl.when(pl.program_id(0) == 0)
    def _():
        for t in range(4):
            ts = slice(t * 128, (t + 1) * 128)
            dwo_ref[:, ts] = wo_ref[t * 192 : (t + 1) * 192, :].astype(f32)
            dwqt_ref[:, ts] = dwq_ref[t * 192 : (t + 1) * 192, :].astype(f32)
        small = small_ref[512:SMALL, :].astype(f32)
        dkvw_ref[...] = small_ref[0:512, :].astype(f32)
        for t in range(4):
            ts = slice(t * 128, (t + 1) * 128)
            drw_ref[:, ts] = small[t * E : (t + 1) * E]
            dgain_ref[:, ts] = small[96 + t : 97 + t]
            dfg_ref[:, ts] = small[100 + t : 101 + t]
        out_ref[...] = out_in[...]
        ing_ref[...] = ing_in[...]


def per_device(inputs, cotangent, norm_gain, ffn_gain, kv_weight, router_weight, query_weight, output_weight, up_weight,
               down_weight, routes, segment_ids):
    wq = jnp.swapaxes(query_weight, 1, 2).reshape(3 * H, D)
    wo = output_weight.reshape(3 * H, D)
    vmem, anywhere = pl.BlockSpec(memory_space=VM), pl.BlockSpec(memory_space=pl.ANY)
    S = jax.ShapeDtypeStruct
    out, ing, shared, dwo, dwq, small = pl.pallas_call(
        kernel_all,
        out_shape=[S((T, D), bf16), S((T, D), bf16), S((8, 2, 4, 4, 4, 16, 128), bf16), S((3, 4, 4, 16, 128), bf16),
                   S((3, 4, 4, 16, 128), bf16), S((2, 4, SMALL // 8, 128), bf16)],
        in_specs=[vmem] * 10 + [anywhere] * 2,
        out_specs=[vmem, vmem, anywhere, vmem, vmem, vmem],
        scratch_shapes=SCRATCH,
        compiler_params=pltpu.CompilerParams(vmem_limit_bytes=62 << 20, collective_id=1, has_side_effects=True),
        cost_estimate=pl.CostEstimate(flops=1 << 35, bytes_accessed=1 << 24, transcendentals=0),
    )(inputs, cotangent, norm_gain.reshape(1, D), ffn_gain.reshape(1, D), kv_weight, router_weight.T, routes.T,
      segment_ids.reshape(3, 128), wq, wo, up_weight, down_weight)
    up_slots, down_slots = ([SHARED.index(u) for u in units] for units in (UP_UNIT, DOWN_UNIT))
    assert down_slots == [1, 4, 7, 5]
    ups = [pl.BlockSpec((1, 4, 128, 128), lambda i, k=k: (k, 0, i, 0)) for k in up_slots]
    downs = [pl.BlockSpec((1, 4, 512, 128), lambda i: (1 + 3 * i - 5 * (i // 3), 0, 0, 0))]

    def whole(*shape):
        return pl.BlockSpec(shape, lambda i: (0,) * len(shape))

    dup, ddown, dwo, dwqt, dkvw, drw, dgain, dfg, out, ing = pl.pallas_call(
        kernel_f,
        grid=(4,),
        out_shape=[S((D, FF), f32), S((FF, D), f32), S((3 * H, D), f32), S((3 * H, D), f32), S((D, 128), f32), S((E, D), f32),
                   S((1, D), f32), S((1, D), f32), S((T, D), bf16), S((T, D), bf16)],
        in_specs=ups + downs + [
                  whole(768, 128), whole(768, 128), whole(SMALL, 128), whole(T, D), whole(T, D)],
        out_specs=[pl.BlockSpec((128, FF), lambda i: (i, 0)), pl.BlockSpec((512, D), lambda i: (i, 0)), whole(3 * H, D),
                   whole(3 * H, D), whole(D, 128), whole(E, D), whole(1, D), whole(1, D), whole(T, D), whole(T, D)],
        compiler_params=pltpu.CompilerParams(vmem_limit_bytes=62 << 20),
    )(*[shared.reshape(8, 4, 512, 128)] * 5, dwo.reshape(768, 128), dwq.reshape(768, 128), small.reshape(SMALL, 128), out, ing)
    return (out, ing, dgain.reshape(D), dfg.reshape(D), dkvw, drw.T,
            jnp.swapaxes(dwqt.reshape(3, H, D), 1, 2), dwo.reshape(3, H, D), dup, ddown)


def solution(mesh):
    both = P(("dp", "expert"), None)
    ex = P("expert", None, None)
    return jax.shard_map(
        per_device, mesh=mesh,
        in_specs=(both, both, P(), P(), P(), P(), ex, ex, P(), P(), both, P(("dp", "expert"))),
        out_specs=(both, both, P(), P(), P(), P(), ex, ex, P(), P()),
        check_vma=False)
```

```python
import functools
import jax
import jax.numpy as jnp
from jax import lax
from jax.experimental import pallas as pl
from jax.experimental.pallas import tpu as pltpu
from jax.sharding import PartitionSpec as P

f32, bf16, i32 = jnp.float32, jnp.bfloat16, jnp.int32
T, D, H, J, E, FF, NB = 384, 512, 64, 8, 24, 2048, 8
EW = E * H
ROWS = J * T
SB = 2 * T
NSB = NB // 2
eps = 1e-06
NEG = -1e30
VM = pltpu.VMEM


def nn(a, b):
    return lax.dot_general(a, b, (((1,), (0,)), ((), ())), preferred_element_type=f32)


def nt(a, b):
    return lax.dot_general(a, b, (((1,), (1,)), ((), ())), preferred_element_type=f32)


def tn(a, b):
    return lax.dot_general(a, b, (((0,), (0,)), ((), ())), preferred_element_type=f32)


def lanes(rows):
    return lax.broadcasted_iota(i32, (rows, 128), 1)


def split3(v):
    a = v.astype(bf16).astype(f32)
    b = (v - a).astype(bf16).astype(f32)
    c = (v - a - b).astype(bf16).astype(f32)
    return a, b, c


MESH = pl.DeviceIdType.MESH
LINES = [(a, k) for a in "xyz" for k in (1, 2, 3)]
ALL_PEERS = [("c", 0)] + LINES


class Place:
    def __init__(self):
        dp, ex = lax.axis_index("dp"), lax.axis_index("expert")
        self.ex = ex
        self.at = {"x": dp // 4, "y": dp % 4, "z": ex // 2, "c": ex % 2}
        self.peers = {("c", 0): self.device(c=1 - self.at["c"])}
        for axis, k in LINES:
            self.peers[axis, k] = self.device(**{axis: (self.at[axis] + k) % 4})

    def device(self, **moved):
        at = {**self.at, **moved}
        return (at["x"] * 4 + at["y"], at["z"] * 2 + at["c"])


class Copies:
    def __init__(self, place, send, recv):
        self.place, self.send, self.recv, self.made = place, send, recv, []

    def add(self, src, dst, peer):
        self.made.append((src, dst, peer))
        return len(self.made) - 1

    def get(self, i):
        src, dst, peer = self.made[i]
        return pltpu.make_async_remote_copy(src_ref=src(), dst_ref=dst(), send_sem=self.send.at[i], recv_sem=self.recv.at[i],
                                            device_id=self.place.peers[peer], device_id_type=MESH)

    def start(self, ids):
        for i in ids:
            self.get(i).start()

    def arrived(self, ids):
        for i in ids:
            self.get(i).wait_recv()

    def sent(self, ids):
        for i in ids:
            self.get(i).wait_send()

    def drain(self):
        self.sent(range(len(self.made)))


class Scatter:
    def __init__(self, copies, big, r, ex, parts, groups, order):
        self.cp, self.big, self.r, self.ex = copies, big, r, ex
        self.parts, self.groups, self.u0, self.u1 = parts, groups, parts[0][0], parts[-1][1]
        at = copies.place.at
        self.m = m = [at[a] for a in order]
        rng = lambda g: pl.ds(g[0], g[1] - g[0])
        us = rng((self.u0, self.u1))
        self.part_ids = [copies.add(lambda g=g: big.at[1, rng(g)], lambda g=g: r[0].at[rng(g)], ("c", 0)) for g in parts]
        self.group_ids = [
            [copies.add(lambda g=g, k=k: big.at[0, rng(g), (m[0] + k) % 4], lambda g=g, k=k: r[1].at[rng(g), k - 1], (order[0], k))
             for k in (1, 2, 3)] for g in groups]
        self.ids2 = [copies.add(lambda k=k: big.at[0, us, m[0], (m[1] + k) % 4], lambda k=k: r[2].at[us, k - 1], (order[1], k))
                     for k in (1, 2, 3)]
        own = lambda: ex.at[us, m[2]]
        self.ids3 = [copies.add(own, own, (order[2], k)) for k in (1, 2, 3)]

    def start0(self, i):
        self.cp.start([self.part_ids[i]])

    def pass0(self, h):
        g = self.groups[h]
        self.cp.arrived([i for i, p in zip(self.part_ids, self.parts) if g[0] <= p[0] < g[1]])
        for u in range(*g):
            for a in range(4):
                v = self.big[0, u, a].astype(f32) + self.r[0][u, a].astype(f32)
                self.big[0, u, a] = v.astype(bf16)
        self.cp.start(self.group_ids[h])

    def add3(self, u, at, r):
        v = self.big[at].astype(f32)
        for k in range(3):
            v = v + r[u, k].astype(f32)
        return v.astype(bf16)

    def pass1(self):
        for h, g in enumerate(self.groups):
            self.cp.arrived(self.group_ids[h])
            for u in range(*g):
                at = (0, u, self.m[0])
                self.big[at] = self.add3(u, at, self.r[1])
        self.cp.start(self.ids2)

    def pass2(self):
        self.cp.arrived(self.ids2)
        for u in range(self.u0, self.u1):
            self.ex[u, self.m[2]] = self.add3(u, (0, u, self.m[0], self.m[1]), self.r[2])
        self.cp.start(self.ids3)

    def pass3(self):
        self.cp.arrived(self.ids3)

    def result(self, u):
        e = [self.ex[u, i].astype(f32) for i in range(4)]
        return (e[0] + e[1] + e[2] + e[3]).astype(bf16)


class Spread:
    def __init__(self, copies, out, kept, kept_sem, u0, u1, order):
        self.cp, self.out, self.kept, self.kept_sem, self.u0, self.u1 = copies, out, kept, kept_sem, u0, u1
        at = copies.place.at
        self.c, self.m = at["c"], [at[a] for a in order]
        us = pl.ds(u0, u1 - u0)
        quarter = lambda: out.at[us, self.c, self.m[0], self.m[1]]
        self.ids2 = [copies.add(quarter, quarter, (order[1], k)) for k in (1, 2, 3)]
        self.ids1, self.ids0 = [], []
        for u in range(u0, u1):
            piece = lambda k=0, u=u: out.at[u, self.c, (self.m[0] - k + 4) % 4]
            self.ids1.append([copies.add(piece, piece, (order[0], k)) for k in (1, 2, 3)])
            self.ids0.append([copies.add(functools.partial(piece, k), functools.partial(piece, k), ("c", 0)) for k in range(4)])

    def begin(self, values):
        for u, v in zip(range(self.u0, self.u1), values):
            self.out[u, self.c, self.m[0], self.m[1]] = v
        self.cp.start(self.ids2)

    def pass2(self):
        self.cp.arrived(self.ids2)

    def send(self, i):
        if i < len(self.ids1):
            self.cp.start(self.ids1[i] + self.ids0[i][:1])

    def forward(self, i):
        if i < len(self.ids1):
            for k in (1, 2, 3):
                self.cp.arrived(self.ids1[i][k - 1 : k])
                self.cp.start(self.ids0[i][k : k + 1])

    def finish(self, i):
        if i < len(self.ids0):
            self.cp.arrived(self.ids0[i])
            self.keep(self.u0 + i).start()

    def keep(self, u):
        return pltpu.make_async_copy(self.out.at[u], self.kept.at[u], self.kept_sem.at[u])


class SpreadOwner:
    def __init__(self, copies, out, u, axis):
        self.cp, self.out, self.u, self.p = copies, out, u, copies.place.at[axis]
        ref = lambda: out.at[u, self.p]
        self.ids = [copies.add(ref, ref, (axis, k)) for k in (1, 2, 3)]

    def begin(self, value):
        self.out[self.u, self.p] = value
        self.cp.start(self.ids)

    def finish(self):
        self.cp.arrived(self.ids)


class SmallSum:
    def __init__(self, copies, src, half, r0, r1, by, bz, out):
        self.cp, self.src, self.half, self.r0, self.r1, self.by, self.bz, self.out = copies, src, half, r0, r1, by, bz, out
        at = copies.place.at
        self.c, self.x, self.y, self.z = at["c"], at["x"], at["y"], at["z"]
        own_half = lambda: out.at[self.c]
        own = lambda: out.at[self.c, self.x]
        self.ids = [
            [copies.add(lambda: src.at[1 - self.c], lambda: r0, ("c", 0))],
            [copies.add(lambda k=k: half.at[(self.x + k) % 4], lambda k=k: r1.at[k - 1], ("x", k)) for k in (1, 2, 3)],
            [copies.add(lambda: by.at[self.y], lambda: by.at[self.y], ("y", k)) for k in (1, 2, 3)],
            [copies.add(lambda: bz.at[self.z], lambda: bz.at[self.z], ("z", k)) for k in (1, 2, 3)],
            [copies.add(own, own, ("x", k)) for k in (1, 2, 3)],
            [copies.add(own_half, own_half, ("c", 0))],
        ]

    def step(self, i):
        if i:
            self.cp.arrived(self.ids[i - 1])
        if i == 1:
            for a in range(4):
                self.half[a] = (self.src[self.c, a].astype(f32) + self.r0[a].astype(f32)).astype(bf16)
        if i == 2:
            v = self.half[self.x].astype(f32)
            for k in range(3):
                v = v + self.r1[k].astype(f32)
            self.by[self.y] = v.astype(bf16)
        if i in (3, 4):
            b = self.by if i == 3 else self.bz
            v = (b[0].astype(f32) + b[1].astype(f32) + b[2].astype(f32) + b[3].astype(f32)).astype(bf16)
            if i == 3:
                self.bz[self.z] = v
            else:
                self.out[self.c, self.x] = v
        if i < 6:
            self.cp.start(self.ids[i])


UNITS = 11
UP_UNIT, DOWN_UNIT, WO_UNIT = [0, 4, 8, 2], [1, 5, 9, 6], [3, 7, 10]
SHARED = sorted(UP_UNIT + DOWN_UNIT)
OWNER_ORDERS = ["zxy", "xzy", "yzx"]
EARLY = [([(0, 2), (2, 3), (3, 4)], [(0, 2), (2, 4)], "zxy"), ([(4, 6), (6, 7)], [(4, 6), (6, 7)], "xyz"),
         ([(7, 8)], [(7, 8)], "xzy"), ([(8, 10), (10, 11)], [(8, 10), (10, 11)], "yzx")]
CHUNK_PARTS, WO_PARTS = [[(0, 0)], [(1, 0)], [(3, 0)], [(0, 1), (1, 1)]], [(0, 2), (2, 0), (3, 1)]
SPREADS = [(0, 3, "zxy"), (3, 6, "xyz"), (6, 8, "yzx")]


def plane_axes(order):
    return [a for a in order if a != "z"]


def expert_row(ex, piece, order):
    p, q = plane_axes(order)
    at = {p: piece // 4, q: piece % 4, "z": ex // 2}
    r = ex % 2
    for a in order:
        r = r * 4 + at[a]
    return r * 16


def store_expert(big, core, units, ex0, value):
    low = value.astype(bf16)
    for o in range(2):
        slot = (core + (ex0 + o) % 2) % 2
        for row in range(0, 768, 16):
            v, piece = row // 256, (row % 256) // 16
            ct, r = row // 192, row % 192
            base = expert_row(ex0 + o, piece, OWNER_ORDERS[v]) % 1024
            big[slot, units[v], base : base + 16, :] = low[o * 192 + r : o * 192 + r + 16, ct * 128 : (ct + 1) * 128]


KVR = T + 16


class Gather:
    def __init__(self, copies, out):
        self.cp, self.out = copies, out
        at, ex = copies.place.at, copies.place.ex
        own = lambda: out.at[ex]
        from_z = lambda k: out.at[((at["z"] - k + 4) % 4) * 2 + at["c"]]
        self.line = [copies.add(own, own, ("z", k)) for k in (1, 2, 3)]
        self.core = [copies.add(functools.partial(from_z, k), functools.partial(from_z, k), ("c", 0)) for k in (0, 1, 2, 3)]

    def start(self):
        self.cp.start(self.line)
        self.cp.start(self.core[:1])

    def forward(self):
        for k in range(3):
            self.cp.arrived(self.line[k : k + 1])
            self.cp.start(self.core[k + 1 : k + 2])

    def finish(self):
        self.cp.arrived(self.core)


def bounds_of(kv_ref):
    n0 = n1 = 0.0
    for b in range(NB):
        tail = kv_ref[b, T:KVR, :].astype(f32)
        n0 = n0 + 16.0 * tail[0:1] + tail[1:2]
        n1 = n1 + 16.0 * tail[2:3] + tail[3:4]
    return n0, n1


def segment_of(pos, bounds):
    return (pos >= bounds[0]).astype(i32) + (pos >= bounds[1]).astype(i32)


def sub8(v):
    return v.reshape(8, 8, v.shape[-1])


def route_rows(rt_ref):
    return [jnp.broadcast_to(rt_ref[j : j + 1, :], (8, T)) for j in range(J)]


def visible(me, sb):
    key = lax.broadcasted_iota(i32, (T, SB), 1)
    tok = lax.broadcasted_iota(i32, (T, SB), 0)
    ok = key - tok <= (me - 2 * sb) * T
    return ok


def prepare_keys(kv_ref, bounds, kaug, vaug, vt):
    ln = lanes(T)
    for b in range(NB):
        bs = slice(b * T, (b + 1) * T)
        kv = kv_ref[b, 0:T, :].astype(f32)
        pos = (lax.broadcasted_iota(i32, (T, 128), 0) + b * T).astype(f32)
        seg = segment_of(pos, bounds)
        feat = jnp.where((ln < H + 3) & (seg != ln - H), NEG, 0.0)
        feat = jnp.where((ln >= H + 3) & (ln < H + 6), 1.0, feat)
        kaug[bs, :] = jnp.where(ln < H, kv, feat).astype(bf16)
        if vaug is not None:
            one = jnp.where(ln < H + 3, 1.0, 0.0)
            vaug[bs, :] = jnp.where(ln < H, pltpu.roll(kv, H, 1), one).astype(bf16)
        if vt is not None:
            ones = jnp.where(lax.broadcasted_iota(i32, (16, T), 0) == 0, 1.0, 0.0)
            vt[:, bs] = jnp.concatenate([jnp.transpose(kv)[H:], ones], axis=0).astype(bf16)


def project_queries(normed, wq_ref, qall):
    for c in range(4):
        w = wq_ref[2 * c : 2 * c + 2].reshape(2 * 3 * H, D)
        qall[c * 48 : (c + 1) * 48] = (nt(w, normed) * 0.125).reshape(48, 8, T)


def choose(routes, table, j):
    acc = table[0:8]
    for e in range(1, E):
        acc = jnp.where((routes[j] == e)[None], table[e * 8 : (e + 1) * 8], acc)
    return acc


def to_experts(routes, rows, out):
    for e in range(E):
        acc = jnp.zeros((8, 8, T), f32)
        for j in range(J):
            acc = jnp.where((routes[j] == e)[None], rows[j], acc)
        out[e * H : (e + 1) * H, :] = acc.reshape(H, T).astype(bf16)


def pick_queries(rt_ref, table, qt):
    routes = route_rows(rt_ref)
    for j in range(J):
        qt[0:H, j * T : (j + 1) * T] = choose(routes, table, j).reshape(H, T).astype(bf16)


def mark_queries(bounds, me, qt):
    pos = (lax.broadcasted_iota(i32, (H, T), 1) + me * T).astype(f32)
    seg = segment_of(pos, (bounds[0][:, 0:1], bounds[1][:, 0:1]))
    feat = jnp.where(lax.broadcasted_iota(i32, (H, T), 0) == seg, 1.0, 0.0).astype(bf16)
    for j in range(J):
        qt[H:, j * T : (j + 1) * T] = feat


def attend(me, qt, kaug, vt, att, macc, acc):
    last = me // 2
    macc[...] = jnp.full(macc.shape, NEG, f32)
    acc[...] = jnp.zeros(acc.shape, f32)

    def score(sb, g, masked):
        s = nn(kaug[pl.ds(pl.multiple_of(sb * SB, SB), SB), :], qt[:, g * SB : (g + 1) * SB])
        if masked:
            key = lax.broadcasted_iota(i32, (SB, T), 0)
            tok = lax.broadcasted_iota(i32, (SB, T), 1)
            ok = key - tok <= (me - 2 * sb) * T
            s = jnp.where(jnp.concatenate([ok, ok], axis=1), s, NEG)
        return s.reshape(SB // 8, 8, SB)

    def soften(s, g):
        gs = slice(g * SB, (g + 1) * SB)
        old = macc[:, gs]
        top = jnp.max(jnp.maximum(old, jnp.max(s, axis=0)), axis=0, keepdims=True)
        top = jnp.broadcast_to(top, (8, SB))
        macc[:, gs] = top
        return jnp.exp(s - top[None]).reshape(SB, SB).astype(bf16), jnp.exp(old - top)

    def weigh(sb, g, p, kept):
        gs = slice(g * SB, (g + 1) * SB)
        old = acc[:, gs].reshape(10, 8, SB) * kept[None]
        acc[:, gs] = old.reshape(80, SB) + nn(vt[:, pl.ds(pl.multiple_of(sb * SB, SB), SB)], p)

    def block(sb, masked):
        s = score(sb, 0, masked)
        held = None
        for g in range(J // 2):
            ahead = score(sb, g + 1, masked) if g + 1 < J // 2 else None
            new = soften(s, g)
            if g:
                weigh(sb, g - 1, *held)
            held, s = new, ahead
        weigh(sb, J // 2 - 1, *held)

    lax.fori_loop(0, last, lambda sb, c: (block(sb, False), c)[1], 0)
    block(last, True)
    for g in range(J // 2):
        gs = slice(g * SB, (g + 1) * SB)
        tot = acc[H : H + 1, gs]
        att[:, gs] = (acc[0:H, gs] / tot).astype(bf16)
        l1, l2, l3 = split3(-(macc[0:1, gs] + jnp.log(tot)))
        row = lax.broadcasted_iota(i32, (16, SB), 0)
        feat = qt[H : H + 16, gs].astype(f32)
        feat = jnp.where(row == 3, l1, jnp.where(row == 4, l2, jnp.where(row == 5, l3, feat)))
        qt[H : H + 16, gs] = feat.astype(bf16)


def gates_of(normed, rw_ref, rt_ref, gate_ref):
    logits = nt(rw_ref[...], normed)
    eid = lax.broadcasted_iota(i32, (E, T), 0)
    per = [jnp.sum(jnp.where(rt_ref[j : j + 1, :] == eid, logits, 0.0), axis=0, keepdims=True) for j in range(J)]
    v = jnp.concatenate(per, axis=0)
    e = jnp.exp(v - jnp.max(v, axis=0, keepdims=True))
    gate_ref[...] = e / jnp.sum(e, axis=0, keepdims=True)


SMALL = 640


def dma_sems(n):
    return [pltpu.SemaphoreType.DMA((n,)), pltpu.SemaphoreType.DMA((n,))]


def kernel_all(x_ref, cot_ref, gain_ref, fgain_ref, kvw_ref, rw_ref, rt_ref, seg_ref, wq_in, wo_in, up_hbm, down_hbm,
               out_ref, ing_ref, all_hbm, dwo_ref, dwq_ref, small_ref,
               shared, all_sem, up_ref, down_ref, wsem, normed_ref, gate_ref, kv_ref, wq_ref, wo_ref, att_ref, qt_ref, table, kaug, vaug, vt, macc, acc,
               rows, gat, gm_ref, gn_ref, drw_ref, dfg_ref, big, r0, r1, r2, ex,
               dat_ref, qa, da, dqacc, tot, gsend, grecv, lbig, l0, l1, l2, lex, ssrc, shalf, s0, s1, sy, sz, send, recv, ksend, krecv):
    place = Place()
    me, core = place.ex, place.at["c"]
    dp = lax.axis_index("dp")
    copies = Copies(place, send, recv)
    gq, gk, go = Gather(copies, wq_ref), Gather(copies, kv_ref), Gather(copies, wo_ref)
    big7 = big.reshape(2, UNITS, 4, 4, 4, 16, 128)
    lbig7 = lbig.reshape(2, 3, 4, 4, 4, 16, 128)
    early = [Scatter(copies, big7, (r0, r1, r2), ex, parts, groups, o) for parts, groups, o in EARLY]
    late = [Scatter(copies, lbig7, (l0, l1, l2), lex, [(u, u + 1)], [(u, u + 1)], o) for u, o in enumerate(OWNER_ORDERS)]
    spreads = [Spread(copies, shared, all_hbm, all_sem, u0, u1, o) for u0, u1, o in SPREADS]
    owned_o = [SpreadOwner(copies, dwo_ref, u, plane_axes(o)[0]) for u, o in enumerate(OWNER_ORDERS)]
    owned_q = [SpreadOwner(copies, dwq_ref, u, plane_axes(o)[0]) for u, o in enumerate(OWNER_ORDERS)]
    small = SmallSum(copies, ssrc, shalf, s0, s1, sy, sz, small_ref)

    bar = pltpu.get_barrier_semaphore()
    for p in ALL_PEERS:
        pl.semaphore_signal(bar, inc=1, device_id=place.peers[p], device_id_type=MESH)
    for k in range(1, NB):
        pl.semaphore_signal(bar, inc=1, device_id=(dp, (me + k) % NB), device_id_type=MESH)
    loads = [pltpu.make_async_copy(up_hbm, up_ref, wsem.at[0]), pltpu.make_async_copy(down_hbm, down_ref, wsem.at[1])]
    for cp in loads:
        cp.start()
    wq_ref[me] = wq_in[...]
    wo_ref[me] = wo_in[...]

    x = x_ref[...].astype(f32)
    inv = lax.rsqrt(jnp.mean(x * x, axis=-1, keepdims=True) + eps)
    normed = (x * inv * gain_ref[...]).astype(bf16)
    normed_ref[...] = normed
    kv_ref[me, 0:T, :] = nn(normed, kvw_ref[...]).astype(bf16)
    seg = seg_ref[...]
    row = lax.broadcasted_iota(i32, (16, 128), 0)
    tail = jnp.zeros((16, 128), f32)
    for s in range(2):
        n = jnp.sum(jnp.sum((seg <= s).astype(f32), axis=0, keepdims=True), axis=1, keepdims=True)
        n = jnp.broadcast_to(n, (16, 128))
        hi = jnp.floor(n * 0.0625)
        tail = jnp.where(row == 2 * s, hi, jnp.where(row == 2 * s + 1, n - 16.0 * hi, tail))
    kv_ref[me, T:KVR, :] = tail.astype(bf16)
    pl.semaphore_wait(bar, len(ALL_PEERS) + NB - 1)
    gq.start()
    gk.start()
    gates_of(normed, rw_ref, rt_ref, gate_ref)
    gq.forward()
    gq.finish()
    project_queries(normed, wq_ref, table)
    pick_queries(rt_ref, table, qt_ref)
    gk.forward()
    gk.finish()
    bounds = bounds_of(kv_ref)
    prepare_keys(kv_ref, bounds, kaug, vaug, vt)
    mark_queries(bounds, me, qt_ref)
    go.start()
    attend(me, qt_ref, kaug, vt, att_ref, macc, acc)

    go.forward()
    routes = route_rows(rt_ref)
    for j in range(J):
        rows[j] = sub8(att_ref[:, j * T : (j + 1) * T].astype(f32) * gate_ref[j : j + 1, :])
    to_experts(routes, rows, gat)
    go.finish()
    x = x_ref[...].astype(f32)
    wo_all = wo_ref[...].reshape(EW, D)
    mixed = x + tn(gat[...], wo_all)
    inv = lax.rsqrt(jnp.mean(mixed * mixed, axis=-1, keepdims=True) + eps)
    n = mixed * inv
    fgain = fgain_ref[...]
    second = (n * fgain).astype(bf16)
    second_t = jnp.transpose(n * fgain).astype(bf16)
    cot = cot_ref[...]
    for cp in loads:
        cp.wait()
    C = 512
    out = mixed
    gsec = jnp.zeros((T, D), f32)
    ahead = nn(second, up_ref[:, 0:C]), nt(cot, down_ref[0:C, :])
    for c in range(FF // C):
        cs = slice(c * C, (c + 1) * C)
        v, gact = ahead
        if c + 1 < FF // C:
            ns = slice((c + 1) * C, (c + 2) * C)
            ahead = nn(second, up_ref[:, ns]), nt(cot, down_ref[ns, :])
        v2 = v * v
        th = jnp.tanh(0.7978845608028654 * (v + 0.044715 * v * v2))
        a = (0.5 * v * (1.0 + th)).astype(bf16)
        dth = 0.5 * (1.0 + th) + 0.5 * v * (1.0 - th * th) * (0.7978845608028654 * (1.0 + 0.134145 * v2))
        gh = (gact * dth).astype(bf16)
        out = out + nn(a, down_ref[cs, :])
        gsec = gsec + nt(gh, up_ref[:, cs])
        gdown = tn(a, cot).astype(bf16)
        gup = nn(second_t, gh).astype(bf16)
        for t in range(4):
            ts = slice(t * 128, (t + 1) * 128)
            big[(core + t // 2) % 2, DOWN_UNIT[c], t % 2 * 512 : t % 2 * 512 + 512, :] = gdown[:, ts]
            big[(core + t // 2) % 2, UP_UNIT[c], t % 2 * 512 : t % 2 * 512 + 512, :] = gup[:, ts]
        for b, i in CHUNK_PARTS[c]:
            early[b].start0(i)
    for i in (0, 1, 3):
        early[i].pass0(0)
    out_ref[...] = out.astype(bf16)
    dfg_ref[...] = jnp.sum(gsec * n, axis=0, keepdims=True)
    hh = gsec * fgain
    gm = cot.astype(f32) + inv * (hh - n * jnp.mean(hh * n, axis=-1, keepdims=True))
    gm_ref[...] = gm
    gml = gm.astype(bf16)
    for c in range(4):
        store_expert(big, core, WO_UNIT, 2 * c, nn(gat[c * 384 : (c + 1) * 384, :], gml))
    for b, i in WO_PARTS:
        early[b].start0(i)
    for c in range(4):
        w = wo_ref[2 * c : 2 * c + 2].reshape(2 * 3 * H, D)
        table[c * 48 : (c + 1) * 48] = nt(w, gml).reshape(48, 8, T)
    dots = []
    row = lax.broadcasted_iota(i32, (H, T), 0)
    for j in range(J):
        js = slice(j * T, (j + 1) * T)
        g = choose(routes, table, j).reshape(H, T)
        gate = gate_ref[j : j + 1, :]
        dot = jnp.sum(g * att_ref[:, js].astype(f32), axis=0, keepdims=True)
        dots.append(dot)
        d1, d2, d3 = split3(-(dot * gate))
        dat_ref[0:H, js] = (g * gate).astype(bf16)
        dat_ref[H:, js] = jnp.where(row == 0, d1, jnp.where(row == 1, d2, jnp.where(row == 2, d3, 0.0))).astype(bf16)
    dots = jnp.concatenate(dots, axis=0)
    gates = gate_ref[...]
    chosen = gates * (dots - jnp.sum(gates * dots, axis=0, keepdims=True))
    eid = lax.broadcasted_iota(i32, (E, T), 0)
    gl = jnp.zeros((E, T), f32)
    for j in range(J):
        gl = jnp.where(rt_ref[j : j + 1, :] == eid, chosen[j : j + 1, :], gl)
    hi = gl.astype(bf16)
    lo = (gl - hi.astype(f32)).astype(bf16)
    rw = rw_ref[...]
    gn_ref[...] = tn(hi, rw) + tn(lo, rw)
    nm = normed_ref[...]
    drw_ref[...] = nn(hi, nm) + nn(lo, nm)

    for j in range(J):
        js = slice(j * T, (j + 1) * T)
        qa[js, :] = jnp.transpose(qt_ref[:, js].astype(f32)).astype(bf16)
        da[js, :] = jnp.transpose(dat_ref[:, js].astype(f32)).astype(bf16)
    dqacc[...] = jnp.zeros(dqacc.shape, f32)
    for i, h in ((0, 1), (1, 1), (2, 0), (3, 1)):
        early[i].pass0(h)
    last = me // 2

    def half_block(sb, half, masked):
        ks = pl.ds(pl.multiple_of(sb * SB, SB), SB)

        @pl.when(half == 0)
        def _():
            tot[...] = jnp.zeros(tot.shape, f32)

        for i in range(2):
            gs = pl.ds(pl.multiple_of((half * 2 + i) * SB, SB), SB)
            p = jnp.exp(nt(qa[gs, :], kaug[ks, :]))
            if masked:
                ok = visible(me, sb)
                p = jnp.where(jnp.concatenate([ok, ok], axis=0), p, 0.0)
            ds = (p * nt(da[gs, :], vaug[ks, :])).astype(bf16)
            kv = jnp.concatenate([kv_ref[2 * sb, 0:T, :], kv_ref[2 * sb + 1, 0:T, :]], axis=0)
            dqacc[gs, :] += nn(ds, kv)
            tot[0:H, :] += nn(qt_ref[0:H, gs], ds)
            tot[H:, :] += nn(dat_ref[0:H, gs], p.astype(bf16))

        @pl.when(half == 1)
        def _():
            low = jnp.transpose(tot[...]).astype(bf16)
            gsend[2 * sb] = low[0:T]
            gsend[2 * sb + 1] = low[T:]

    def to_owner(kb):
        return pltpu.make_async_remote_copy(src_ref=gsend.at[kb], dst_ref=grecv.at[me], send_sem=ksend.at[kb],
                                            recv_sem=krecv.at[me], device_id=(dp, kb), device_id_type=MESH)

    def from_device(b):
        return pltpu.make_async_remote_copy(src_ref=gsend.at[b], dst_ref=grecv.at[b], send_sem=ksend.at[b],
                                            recv_sem=krecv.at[b], device_id=(dp, b), device_id_type=MESH)

    def at_3():
        for s in early:
            s.pass1()

    def at_5():
        for s in early:
            s.pass2()

    def step(i, carry):
        sb, half = i // 2, i % 2

        @pl.when(sb < last)
        def _():
            half_block(sb, half, False)

            @pl.when(half == 1)
            def _():
                to_owner(2 * sb).start()
                to_owner(2 * sb + 1).start()

        pl.when(i == 3)(at_3)
        pl.when(i == 5)(at_5)

        return carry

    lax.fori_loop(0, 2 * (NSB - 1), step, 0)

    def last_step(half, carry):
        half_block(last, half, True)

        return carry

    lax.fori_loop(0, 2, last_step, 0)

    @pl.when(2 * last < me)
    def _():
        to_owner(2 * last).start()

    for s in early:
        s.pass3()
    for s, e, (u0, u1, _) in zip(spreads, (early[0], early[1], early[3]), SPREADS):
        s.begin([e.result(SHARED[u]) for u in range(u0, u1)])
    for s, e, u in zip(owned_o, (early[0], early[2], early[3]), WO_UNIT):
        s.begin(e.result(u))
    for j in range(J):
        js = slice(j * T, (j + 1) * T)
        rows[j] = sub8(jnp.transpose(dqacc[js, :])[0:H].astype(bf16).astype(f32) * 0.125)
    to_experts(routes, rows, gat)
    for c in range(4):
        store_expert(lbig, core, [0, 1, 2], 2 * c, nn(gat[c * 384 : (c + 1) * 384, :], nm))
    for s in late:
        s.start0(0)
    for s in spreads:
        s.pass2()
        s.send(0)
    dqacc[0:T, :] = gsend[me].astype(f32)
    for b in range(1, NB):
        @pl.when(b > me)
        def _(b=b):
            from_device(b).wait_recv()
            dqacc[0:T, :] += grecv[b].astype(f32)
    gkv = dqacc[0:T, :].astype(bf16)
    dkvw = tn(nm, gkv).astype(bf16)
    for s in late:
        s.pass0(0)
    for s in spreads:
        s.send(1)
    gn = gn_ref[...] + tn(gat[...], wq_ref[...].reshape(EW, D)) + nt(gkv, kvw_ref[...])
    x = x_ref[...].astype(f32)
    inv = lax.rsqrt(jnp.mean(x * x, axis=-1, keepdims=True) + eps)
    n = x * inv
    dgain = jnp.sum(gn * n, axis=0, keepdims=True)
    drw = drw_ref[...]
    dfg = dfg_ref[...]
    parts = [dkvw.astype(f32)] + [drw[:, t * 128 : (t + 1) * 128] for t in range(4)]
    parts += [v[:, t * 128 : (t + 1) * 128] for v in (dgain, dfg) for t in range(4)] + [jnp.zeros((SMALL - 616, 128), f32)]
    ssrc[...] = jnp.concatenate(parts, axis=0).astype(bf16).reshape(2, 4, SMALL // 8, 128)
    small.step(0)
    small.step(1)
    for s in late:
        s.pass1()
    small.step(2)
    for s in spreads:
        s.send(2)
        s.forward(0)
    hh = gn * gain_ref[...]
    ing_ref[...] = (gm_ref[...] + inv * (hh - n * jnp.mean(hh * n, axis=-1, keepdims=True))).astype(bf16)
    for s in late:
        s.pass2()
    small.step(3)
    for s in spreads:
        s.finish(0)
        s.forward(1)
    for s, t, u in zip(owned_q, late, range(3)):
        t.pass3()
        s.begin(t.result(u))
    small.step(4)
    for s in spreads:
        s.finish(1)
        s.forward(2)
    for s in owned_o + owned_q:
        s.finish()
    small.step(5)
    for s in spreads:
        s.finish(2)
    small.step(6)
    for s in spreads:
        for u in range(s.u0, s.u1):
            s.keep(u).wait()
    for b in range(NB - 1):
        @pl.when(b < me)
        def _(b=b):
            to_owner(b).wait_send()
    copies.drain()


SCRATCH = [
    VM((8, 2, 4, 4, 4, 16, 128), bf16), pltpu.SemaphoreType.DMA((8,)),
    VM((D, FF), bf16), VM((FF, D), bf16), pltpu.SemaphoreType.DMA((2,)), VM((T, D), bf16), VM((J, T), f32), VM((NB, KVR, 128), bf16),
    VM((NB, 3 * H, D), bf16), VM((NB, 3 * H, D), bf16), VM((H, ROWS), bf16), VM((128, ROWS), bf16), VM((EW // 8, 8, T), f32),
    VM((ROWS, 128), bf16), VM((ROWS, 128), bf16), VM((80, ROWS), bf16), VM((8, ROWS), f32), VM((80, ROWS), f32),
    VM((J, 8, 8, T), f32), VM((EW, T), bf16), VM((T, D), f32), VM((T, D), f32), VM((E, D), f32), VM((1, D), f32),
    VM((2, UNITS, 1024, 128), bf16), VM((UNITS, 4, 4, 4, 16, 128), bf16), VM((UNITS, 3, 4, 4, 16, 128), bf16),
    VM((UNITS, 3, 4, 16, 128), bf16), VM((UNITS, 4, 4, 16, 128), bf16),
    VM((128, ROWS), bf16), VM((ROWS, 128), bf16), VM((ROWS, 128), bf16), VM((ROWS, 128), f32), VM((128, SB), f32),
    VM((NB, T, 128), bf16), VM((NB, T, 128), bf16),
    VM((2, 3, 1024, 128), bf16), VM((3, 4, 4, 4, 16, 128), bf16), VM((3, 3, 4, 4, 16, 128), bf16), VM((3, 3, 4, 16, 128), bf16),
    VM((3, 4, 4, 16, 128), bf16),
    VM((2, 4, SMALL // 8, 128), bf16), VM((4, SMALL // 8, 128), bf16), VM((4, SMALL // 8, 128), bf16),
    VM((3, SMALL // 8, 128), bf16), VM((4, SMALL // 8, 128), bf16), VM((4, SMALL // 8, 128), bf16),
] + dma_sems(201) + dma_sems(NB)


def kernel_f(u0, u1, u2, u3, down, wo_ref, dwq_ref, small_ref, out_in, ing_in, dup_ref, ddown_ref, dwo_ref, dwqt_ref, dkvw_ref,
             drw_ref, dgain_ref, dfg_ref, out_ref, ing_ref):
    for t, u in enumerate((u0, u1, u2, u3)):
        ddown_ref[:, t * 128 : (t + 1) * 128] = down[0, t].astype(f32)
        for s in range(4):
            dup_ref[:, (4 * t + s) * 128 : (4 * t + s + 1) * 128] = u[0, s].astype(f32)

    @pl.when(pl.program_id(0) == 0)
    def _():
        for t in range(4):
            ts = slice(t * 128, (t + 1) * 128)
            dwo_ref[:, ts] = wo_ref[t * 192 : (t + 1) * 192, :].astype(f32)
            dwqt_ref[:, ts] = dwq_ref[t * 192 : (t + 1) * 192, :].astype(f32)
        small = small_ref[512:SMALL, :].astype(f32)
        dkvw_ref[...] = small_ref[0:512, :].astype(f32)
        for t in range(4):
            ts = slice(t * 128, (t + 1) * 128)
            drw_ref[:, ts] = small[t * E : (t + 1) * E]
            dgain_ref[:, ts] = small[96 + t : 97 + t]
            dfg_ref[:, ts] = small[100 + t : 101 + t]
        out_ref[...] = out_in[...]
        ing_ref[...] = ing_in[...]


def per_device(inputs, cotangent, norm_gain, ffn_gain, kv_weight, router_weight, query_weight, output_weight, up_weight,
               down_weight, routes, segment_ids):
    wq = jnp.swapaxes(query_weight, 1, 2).reshape(3 * H, D)
    wo = output_weight.reshape(3 * H, D)
    vmem, anywhere = pl.BlockSpec(memory_space=VM), pl.BlockSpec(memory_space=pl.ANY)
    S = jax.ShapeDtypeStruct
    out, ing, shared, dwo, dwq, small = pl.pallas_call(
        kernel_all,
        out_shape=[S((T, D), bf16), S((T, D), bf16), S((8, 2, 4, 4, 4, 16, 128), bf16), S((3, 4, 4, 16, 128), bf16),
                   S((3, 4, 4, 16, 128), bf16), S((2, 4, SMALL // 8, 128), bf16)],
        in_specs=[vmem] * 10 + [anywhere] * 2,
        out_specs=[vmem, vmem, anywhere, vmem, vmem, vmem],
        scratch_shapes=SCRATCH,
        compiler_params=pltpu.CompilerParams(vmem_limit_bytes=62 << 20, collective_id=1, has_side_effects=True),
        cost_estimate=pl.CostEstimate(flops=1 << 35, bytes_accessed=1 << 24, transcendentals=0),
    )(inputs, cotangent, norm_gain.reshape(1, D), ffn_gain.reshape(1, D), kv_weight, router_weight.T, routes.T,
      segment_ids.reshape(3, 128), wq, wo, up_weight, down_weight)
    up_slots, down_slots = ([SHARED.index(u) for u in units] for units in (UP_UNIT, DOWN_UNIT))
    assert down_slots == [1, 4, 7, 5]
    ups = [pl.BlockSpec((1, 4, 128, 128), lambda i, k=k: (k, 0, i, 0)) for k in up_slots]
    downs = [pl.BlockSpec((1, 4, 512, 128), lambda i: (1 + 3 * i - 5 * (i // 3), 0, 0, 0))]

    def whole(*shape):
        return pl.BlockSpec(shape, lambda i: (0,) * len(shape))

    dup, ddown, dwo, dwqt, dkvw, drw, dgain, dfg, out, ing = pl.pallas_call(
        kernel_f,
        grid=(4,),
        out_shape=[S((D, FF), f32), S((FF, D), f32), S((3 * H, D), f32), S((3 * H, D), f32), S((D, 128), f32), S((E, D), f32),
                   S((1, D), f32), S((1, D), f32), S((T, D), bf16), S((T, D), bf16)],
        in_specs=ups + downs + [
                  whole(768, 128), whole(768, 128), whole(SMALL, 128), whole(T, D), whole(T, D)],
        out_specs=[pl.BlockSpec((128, FF), lambda i: (i, 0)), pl.BlockSpec((512, D), lambda i: (i, 0)), whole(3 * H, D),
                   whole(3 * H, D), whole(D, 128), whole(E, D), whole(1, D), whole(1, D), whole(T, D), whole(T, D)],
        compiler_params=pltpu.CompilerParams(vmem_limit_bytes=62 << 20),
    )(*[shared.reshape(8, 4, 512, 128)] * 5, dwo.reshape(768, 128), dwq.reshape(768, 128), small.reshape(SMALL, 128), out, ing)
    return (out, ing, dgain.reshape(D), dfg.reshape(D), dkvw, drw.T,
            jnp.swapaxes(dwqt.reshape(3, H, D), 1, 2), dwo.reshape(3, H, D), dup, ddown)


def solution(mesh):
    both = P(("dp", "expert"), None)
    ex = P("expert", None, None)
    return jax.shard_map(
        per_device, mesh=mesh,
        in_specs=(both, both, P(), P(), P(), P(), ex, ex, P(), P(), both, P(("dp", "expert"))),
        out_specs=(both, both, P(), P(), P(), P(), ex, ex, P(), P()),
        check_vma=False)
```

```python
import functools
import jax
import jax.numpy as jnp
from jax import lax
from jax.experimental import pallas as pl
from jax.experimental.pallas import tpu as pltpu
from jax.sharding import PartitionSpec as P

f32, bf16, i32 = jnp.float32, jnp.bfloat16, jnp.int32
T, D, H, J, E, FF, NB = 384, 512, 64, 8, 24, 2048, 8
EW = E * H
ROWS = J * T
SB = 2 * T
NSB = NB // 2
eps = 1e-06
NEG = -1e30
VM = pltpu.VMEM


def nn(a, b):
    return lax.dot_general(a, b, (((1,), (0,)), ((), ())), preferred_element_type=f32)


def nt(a, b):
    return lax.dot_general(a, b, (((1,), (1,)), ((), ())), preferred_element_type=f32)


def tn(a, b):
    return lax.dot_general(a, b, (((0,), (0,)), ((), ())), preferred_element_type=f32)


def lanes(rows):
    return lax.broadcasted_iota(i32, (rows, 128), 1)


def split3(v):
    a = v.astype(bf16).astype(f32)
    b = (v - a).astype(bf16).astype(f32)
    c = (v - a - b).astype(bf16).astype(f32)
    return a, b, c


MESH = pl.DeviceIdType.MESH
LINES = [(a, k) for a in "xyz" for k in (1, 2, 3)]
ALL_PEERS = [("c", 0)] + LINES


class Place:
    def __init__(self):
        dp, ex = lax.axis_index("dp"), lax.axis_index("expert")
        self.ex = ex
        self.at = {"x": dp // 4, "y": dp % 4, "z": ex // 2, "c": ex % 2}
        self.peers = {("c", 0): self.device(c=1 - self.at["c"])}
        for axis, k in LINES:
            self.peers[axis, k] = self.device(**{axis: (self.at[axis] + k) % 4})

    def device(self, **moved):
        at = {**self.at, **moved}
        return (at["x"] * 4 + at["y"], at["z"] * 2 + at["c"])


class Copies:
    def __init__(self, place, send, recv):
        self.place, self.send, self.recv, self.made, self.open = place, send, recv, [], set()

    def add(self, src, dst, peer):
        self.made.append((src, dst, peer))
        return len(self.made) - 1

    def get(self, i):
        src, dst, peer = self.made[i]
        return pltpu.make_async_remote_copy(src_ref=src(), dst_ref=dst(), send_sem=self.send.at[i], recv_sem=self.recv.at[i],
                                            device_id=self.place.peers[peer], device_id_type=MESH)

    def start(self, ids):
        self.open |= set(ids)
        for i in ids:
            self.get(i).start()

    def arrived(self, ids):
        for i in ids:
            self.get(i).wait_recv()

    def drain(self, keep=()):
        for i in sorted(self.open - set(keep)):
            self.get(i).wait_send()
        self.open &= set(keep)


class Scatter:
    def __init__(self, copies, big, r, ex, parts, groups, order, cut=False):
        self.cp, self.big, self.r, self.ex = copies, big, r, ex
        self.parts, self.groups, self.u0, self.u1 = parts, groups, parts[0][0], parts[-1][1]
        at = copies.place.at
        self.m = m = [at[a] for a in order]
        rng = lambda g: pl.ds(g[0], g[1] - g[0])
        us = rng((self.u0, self.u1))
        if cut:
            self.parts = parts * 4
            z = order.index("z")
            at_z = lambda q: (parts[0][0],) + (slice(None),) * z + (q,)
            self.part_ids = [copies.add(lambda q=q: big.at[(1,) + at_z(q)], lambda q=q: r[0].at[at_z(q)], ("c", 0)) for q in range(4)]
        else:
            self.part_ids = [copies.add(lambda g=g: big.at[1, rng(g)], lambda g=g: r[0].at[rng(g)], ("c", 0)) for g in parts]
        self.group_ids = [
            [copies.add(lambda g=g, k=k: big.at[0, rng(g), (m[0] + k) % 4], lambda g=g, k=k: r[1].at[rng(g), k - 1], (order[0], k))
             for k in (1, 2, 3)] for g in groups]
        self.ids2 = [copies.add(lambda k=k: big.at[0, us, m[0], (m[1] + k) % 4], lambda k=k: r[2].at[us, k - 1], (order[1], k))
                     for k in (1, 2, 3)]
        own = lambda: ex.at[us, m[2]]
        self.ids3 = [copies.add(own, own, (order[2], k)) for k in (1, 2, 3)]

    def start0(self, i):
        self.cp.start([self.part_ids[i]])

    def pass0(self, h):
        g = self.groups[h]
        self.cp.arrived([i for i, p in zip(self.part_ids, self.parts) if g[0] <= p[0] < g[1]])
        for u in range(*g):
            for a in range(4):
                v = self.big[0, u, a].astype(f32) + self.r[0][u, a].astype(f32)
                self.big[0, u, a] = v.astype(bf16)
        self.cp.start(self.group_ids[h])

    def add3(self, u, at, r):
        v = self.big[at].astype(f32)
        for k in range(3):
            v = v + r[u, k].astype(f32)
        return v.astype(bf16)

    def pass1(self):
        for h, g in enumerate(self.groups):
            self.cp.arrived(self.group_ids[h])
            for u in range(*g):
                at = (0, u, self.m[0])
                self.big[at] = self.add3(u, at, self.r[1])
        self.cp.start(self.ids2)

    def pass2(self):
        self.cp.arrived(self.ids2)
        for u in range(self.u0, self.u1):
            self.ex[u, self.m[2]] = self.add3(u, (0, u, self.m[0], self.m[1]), self.r[2])
        self.cp.start(self.ids3)

    def pass3(self):
        self.cp.arrived(self.ids3)

    def result(self, u):
        e = [self.ex[u, i].astype(f32) for i in range(4)]
        return (e[0] + e[1] + e[2] + e[3]).astype(bf16)


class Spread:
    def __init__(self, copies, out, kept, kept_sem, u0, u1, order):
        self.cp, self.out, self.kept, self.kept_sem, self.u0, self.u1 = copies, out, kept, kept_sem, u0, u1
        at = copies.place.at
        self.c, self.m = at["c"], [at[a] for a in order]
        us = pl.ds(u0, u1 - u0)
        quarter = lambda: out.at[us, self.c, self.m[0], self.m[1]]
        self.ids2 = [copies.add(quarter, quarter, (order[1], k)) for k in (1, 2, 3)]
        self.ids1, self.ids0 = [], []
        for u in range(u0, u1):
            piece = lambda k=0, u=u: out.at[u, self.c, (self.m[0] - k + 4) % 4]
            self.ids1.append([copies.add(piece, piece, (order[0], k)) for k in (1, 2, 3)])
            self.ids0.append([copies.add(functools.partial(piece, k), functools.partial(piece, k), ("c", 0)) for k in range(4)])

    def begin(self, values):
        for u, v in zip(range(self.u0, self.u1), values):
            self.out[u, self.c, self.m[0], self.m[1]] = v
        self.cp.start(self.ids2)

    def pass2(self):
        self.cp.arrived(self.ids2)

    def send(self, i):
        if i < len(self.ids1):
            self.cp.start(self.ids1[i] + self.ids0[i][:1])

    def forward(self, i):
        if i < len(self.ids1):
            for k in (1, 2, 3):
                self.cp.arrived(self.ids1[i][k - 1 : k])
                self.cp.start(self.ids0[i][k : k + 1])

    def finish(self, i):
        if i < len(self.ids0):
            self.cp.arrived(self.ids0[i])
            self.keep(self.u0 + i).start()

    def keep(self, u):
        return pltpu.make_async_copy(self.out.at[u], self.kept.at[u], self.kept_sem.at[u])


class SpreadOwner:
    def __init__(self, copies, out, u, axis):
        self.cp, self.out, self.u, self.p = copies, out, u, copies.place.at[axis]
        ref = lambda: out.at[u, self.p]
        self.ids = [copies.add(ref, ref, (axis, k)) for k in (1, 2, 3)]

    def begin(self, value):
        self.out[self.u, self.p] = value
        self.cp.start(self.ids)

    def finish(self):
        self.cp.arrived(self.ids)


class SmallSum:
    def __init__(self, copies, src, half, r0, r1, by, bz, out):
        self.cp, self.src, self.half, self.r0, self.r1, self.by, self.bz, self.out = copies, src, half, r0, r1, by, bz, out
        at = copies.place.at
        self.c, self.x, self.y, self.z = at["c"], at["x"], at["y"], at["z"]
        own_half = lambda: out.at[self.c]
        own = lambda: out.at[self.c, self.x]
        self.ids = [
            [copies.add(lambda: src.at[1 - self.c], lambda: r0, ("c", 0))],
            [copies.add(lambda k=k: half.at[(self.x + k) % 4], lambda k=k: r1.at[k - 1], ("x", k)) for k in (1, 2, 3)],
            [copies.add(lambda: by.at[self.y], lambda: by.at[self.y], ("y", k)) for k in (1, 2, 3)],
            [copies.add(lambda: bz.at[self.z], lambda: bz.at[self.z], ("z", k)) for k in (1, 2, 3)],
            [copies.add(own, own, ("x", k)) for k in (1, 2, 3)],
            [copies.add(own_half, own_half, ("c", 0))],
        ]

    def step(self, i):
        if i:
            self.cp.arrived(self.ids[i - 1])
        if i == 1:
            for a in range(4):
                self.half[a] = (self.src[self.c, a].astype(f32) + self.r0[a].astype(f32)).astype(bf16)
        if i == 2:
            v = self.half[self.x].astype(f32)
            for k in range(3):
                v = v + self.r1[k].astype(f32)
            self.by[self.y] = v.astype(bf16)
        if i in (3, 4):
            b = self.by if i == 3 else self.bz
            v = (b[0].astype(f32) + b[1].astype(f32) + b[2].astype(f32) + b[3].astype(f32)).astype(bf16)
            if i == 3:
                self.bz[self.z] = v
            else:
                self.out[self.c, self.x] = v
        if i < 6:
            self.cp.start(self.ids[i])


UNITS = 11
UP_UNIT, DOWN_UNIT, WO_UNIT = [0, 4, 8, 2], [1, 5, 9, 6], [3, 7, 10]
SHARED = sorted(UP_UNIT + DOWN_UNIT)
OWNER_ORDERS = ["zxy", "xzy", "yzx"]
EARLY = [([(0, 2), (2, 3), (3, 4)], [(0, 2), (2, 4)], "zxy"), ([(4, 6), (6, 7)], [(4, 6), (6, 7)], "xyz"),
         ([(7, 8)], [(7, 8)], "xzy"), ([(8, 10), (10, 11)], [(8, 10), (10, 11)], "yzx")]
CHUNK_PARTS, WO_PARTS = [[(0, 0)], [(1, 0)], [(3, 0)], [(0, 1), (1, 1)]], [(0, 2), (2, 0), (3, 1)]
SPREADS = [(0, 3, "zxy"), (3, 6, "xyz"), (6, 8, "yzx")]


def plane_axes(order):
    return [a for a in order if a != "z"]


def expert_row(ex, piece, order):
    p, q = plane_axes(order)
    at = {p: piece // 4, q: piece % 4, "z": ex // 2}
    r = ex % 2
    for a in order:
        r = r * 4 + at[a]
    return r * 16


def store_expert(big, core, units, ex0, value):
    low = value.astype(bf16)
    for o in range(2):
        slot = (core + (ex0 + o) % 2) % 2
        for row in range(0, 768, 16):
            v, piece = row // 256, (row % 256) // 16
            ct, r = row // 192, row % 192
            base = expert_row(ex0 + o, piece, OWNER_ORDERS[v]) % 1024
            big[slot, units[v], base : base + 16, :] = low[o * 192 + r : o * 192 + r + 16, ct * 128 : (ct + 1) * 128]


KVR = T + 16


class Gather:
    def __init__(self, copies, out):
        self.cp, self.out = copies, out
        at, ex = copies.place.at, copies.place.ex
        own = lambda: out.at[ex]
        from_z = lambda k: out.at[((at["z"] - k + 4) % 4) * 2 + at["c"]]
        self.line = [copies.add(own, own, ("z", k)) for k in (1, 2, 3)]
        self.core = [copies.add(functools.partial(from_z, k), functools.partial(from_z, k), ("c", 0)) for k in (0, 1, 2, 3)]

    def start(self):
        self.cp.start(self.line)
        self.cp.start(self.core[:1])

    def forward(self):
        for k in range(3):
            self.cp.arrived(self.line[k : k + 1])
            self.cp.start(self.core[k + 1 : k + 2])

    def finish(self):
        self.cp.arrived(self.core)


def bounds_of(kv_ref):
    n0 = n1 = 0.0
    for b in range(NB):
        tail = kv_ref[b, T:KVR, :].astype(f32)
        n0 = n0 + 16.0 * tail[0:1] + tail[1:2]
        n1 = n1 + 16.0 * tail[2:3] + tail[3:4]
    return n0, n1


def segment_of(pos, bounds):
    return (pos >= bounds[0]).astype(i32) + (pos >= bounds[1]).astype(i32)


def sub8(v):
    return v.reshape(8, 8, v.shape[-1])


def route_rows(rt_ref):
    return [jnp.broadcast_to(rt_ref[j : j + 1, :], (8, T)) for j in range(J)]


def visible(me, sb):
    key = lax.broadcasted_iota(i32, (T, SB), 1)
    tok = lax.broadcasted_iota(i32, (T, SB), 0)
    ok = key - tok <= (me - 2 * sb) * T
    return ok


def prepare_keys(kv_ref, bounds, kaug, vaug, vt):
    ln = lanes(T)
    for b in range(NB):
        bs = slice(b * T, (b + 1) * T)
        kv = kv_ref[b, 0:T, :].astype(f32)
        pos = (lax.broadcasted_iota(i32, (T, 128), 0) + b * T).astype(f32)
        seg = segment_of(pos, bounds)
        feat = jnp.where((ln < H + 3) & (seg != ln - H), NEG, 0.0)
        feat = jnp.where((ln >= H + 3) & (ln < H + 6), 1.0, feat)
        kaug[bs, :] = jnp.where(ln < H, kv, feat).astype(bf16)
        if vaug is not None:
            one = jnp.where(ln < H + 3, 1.0, 0.0)
            vaug[bs, :] = jnp.where(ln < H, pltpu.roll(kv, H, 1), one).astype(bf16)
        if vt is not None:
            ones = jnp.where(lax.broadcasted_iota(i32, (16, T), 0) == 0, 1.0, 0.0)
            vt[:, bs] = jnp.concatenate([jnp.transpose(kv)[H:], ones], axis=0).astype(bf16)


def project_queries(normed, wq_ref, qall):
    for c in range(4):
        w = wq_ref[2 * c : 2 * c + 2].reshape(2 * 3 * H, D)
        qall[c * 48 : (c + 1) * 48] = (nt(w, normed) * 0.125).reshape(48, 8, T)


def choose(routes, table, j):
    acc = table[0:8]
    for e in range(1, E):
        acc = jnp.where((routes[j] == e)[None], table[e * 8 : (e + 1) * 8], acc)
    return acc


def to_experts(routes, rows, out, experts=range(E)):
    for e in experts:
        acc = jnp.zeros((8, 8, T), f32)
        for j in range(J):
            acc = jnp.where((routes[j] == e)[None], rows[j], acc)
        out[e * H : (e + 1) * H, :] = acc.reshape(H, T).astype(bf16)


def pick_queries(rt_ref, table, qt):
    routes = route_rows(rt_ref)
    for j in range(J):
        qt[0:H, j * T : (j + 1) * T] = choose(routes, table, j).reshape(H, T).astype(bf16)


def mark_queries(bounds, me, qt):
    pos = (lax.broadcasted_iota(i32, (H, T), 1) + me * T).astype(f32)
    seg = segment_of(pos, (bounds[0][:, 0:1], bounds[1][:, 0:1]))
    feat = jnp.where(lax.broadcasted_iota(i32, (H, T), 0) == seg, 1.0, 0.0).astype(bf16)
    for j in range(J):
        qt[H:, j * T : (j + 1) * T] = feat


def attend(me, qt, kaug, vt, att, macc, acc):
    last = me // 2
    macc[...] = jnp.full(macc.shape, NEG, f32)
    acc[...] = jnp.zeros(acc.shape, f32)

    def score(sb, g, masked):
        s = nn(kaug[pl.ds(pl.multiple_of(sb * SB, SB), SB), :], qt[:, g * SB : (g + 1) * SB])
        if masked:
            key = lax.broadcasted_iota(i32, (SB, T), 0)
            tok = lax.broadcasted_iota(i32, (SB, T), 1)
            ok = key - tok <= (me - 2 * sb) * T
            s = jnp.where(jnp.concatenate([ok, ok], axis=1), s, NEG)
        return s.reshape(SB // 8, 8, SB)

    def soften(s, g):
        gs = slice(g * SB, (g + 1) * SB)
        old = macc[:, gs]
        top = jnp.max(jnp.maximum(old, jnp.max(s, axis=0)), axis=0, keepdims=True)
        top = jnp.broadcast_to(top, (8, SB))
        macc[:, gs] = top
        return jnp.exp(s - top[None]).reshape(SB, SB).astype(bf16), jnp.exp(old - top)

    def weigh(sb, g, p, kept):
        gs = slice(g * SB, (g + 1) * SB)
        old = acc[:, gs].reshape(10, 8, SB) * kept[None]
        acc[:, gs] = old.reshape(80, SB) + nn(vt[:, pl.ds(pl.multiple_of(sb * SB, SB), SB)], p)

    def block(sb, masked):
        s = score(sb, 0, masked)
        held = None
        for g in range(J // 2):
            ahead = score(sb, g + 1, masked) if g + 1 < J // 2 else None
            new = soften(s, g)
            if g:
                weigh(sb, g - 1, *held)
            held, s = new, ahead
        weigh(sb, J // 2 - 1, *held)

    lax.fori_loop(0, last, lambda sb, c: (block(sb, False), c)[1], 0)
    block(last, True)
    for g in range(J // 2):
        gs = slice(g * SB, (g + 1) * SB)
        tot = acc[H : H + 1, gs]
        att[:, gs] = (acc[0:H, gs] / tot).astype(bf16)
        l1, l2, l3 = split3(-(macc[0:1, gs] + jnp.log(tot)))
        row = lax.broadcasted_iota(i32, (16, SB), 0)
        feat = qt[H : H + 16, gs].astype(f32)
        feat = jnp.where(row == 3, l1, jnp.where(row == 4, l2, jnp.where(row == 5, l3, feat)))
        qt[H : H + 16, gs] = feat.astype(bf16)


def gates_of(normed, rw_ref, rt_ref, gate_ref):
    logits = nt(rw_ref[...], normed)
    eid = lax.broadcasted_iota(i32, (E, T), 0)
    per = [jnp.sum(jnp.where(rt_ref[j : j + 1, :] == eid, logits, 0.0), axis=0, keepdims=True) for j in range(J)]
    v = jnp.concatenate(per, axis=0)
    e = jnp.exp(v - jnp.max(v, axis=0, keepdims=True))
    gate_ref[...] = e / jnp.sum(e, axis=0, keepdims=True)


SMALL = 640


def dma_sems(n):
    return [pltpu.SemaphoreType.DMA((n,)), pltpu.SemaphoreType.DMA((n,))]


def kernel_all(x_ref, cot_ref, gain_ref, fgain_ref, kvw_ref, rw_ref, rt_ref, seg_ref, wq_in, wo_in, up_hbm, down_hbm,
               out_ref, ing_ref, all_hbm, dwo_ref, dwq_ref, small_ref,
               shared, all_sem, up_ref, down_ref, wsem, normed_ref, gate_ref, kv_ref, wq_ref, wo_ref, att_ref, qt_ref, table, kaug, vaug, vt, macc, acc,
               rows, gat, gm_ref, gn_ref, drw_ref, dfg_ref, big, r0, r1, r2, ex,
               dat_ref, qa, da, dqacc, tot, gsend, grecv, lbig, l0, l1, l2, lex, ssrc, shalf, s0, s1, sy, sz, send, recv, ksend, krecv):
    place = Place()
    me, core = place.ex, place.at["c"]
    dp = lax.axis_index("dp")
    copies = Copies(place, send, recv)
    gq, gk, go = Gather(copies, wq_ref), Gather(copies, kv_ref), Gather(copies, wo_ref)
    big7 = big.reshape(2, UNITS, 4, 4, 4, 16, 128)
    lbig7 = lbig.reshape(2, 3, 4, 4, 4, 16, 128)
    early = [Scatter(copies, big7, (r0, r1, r2), ex, parts, groups, o) for parts, groups, o in EARLY]
    late = [Scatter(copies, lbig7, (l0, l1, l2), lex, [(u, u + 1)], [(u, u + 1)], o, cut=True) for u, o in enumerate(OWNER_ORDERS)]
    spreads = [Spread(copies, shared, all_hbm, all_sem, u0, u1, o) for u0, u1, o in SPREADS]
    owned_o = [SpreadOwner(copies, dwo_ref, u, plane_axes(o)[0]) for u, o in enumerate(OWNER_ORDERS)]
    owned_q = [SpreadOwner(copies, dwq_ref, u, plane_axes(o)[0]) for u, o in enumerate(OWNER_ORDERS)]
    small = SmallSum(copies, ssrc, shalf, s0, s1, sy, sz, small_ref)

    bar = pltpu.get_barrier_semaphore()
    for p in ALL_PEERS:
        pl.semaphore_signal(bar, inc=1, device_id=place.peers[p], device_id_type=MESH)
    for k in range(1, NB):
        pl.semaphore_signal(bar, inc=1, device_id=(dp, (me + k) % NB), device_id_type=MESH)
    loads = [pltpu.make_async_copy(up_hbm, up_ref, wsem.at[0]), pltpu.make_async_copy(down_hbm, down_ref, wsem.at[1])]
    for cp in loads:
        cp.start()
    wq_ref[me] = wq_in[...]
    wo_ref[me] = wo_in[...]

    x = x_ref[...].astype(f32)
    inv = lax.rsqrt(jnp.mean(x * x, axis=-1, keepdims=True) + eps)
    normed = (x * inv * gain_ref[...]).astype(bf16)
    normed_ref[...] = normed
    kv_ref[me, 0:T, :] = nn(normed, kvw_ref[...]).astype(bf16)
    seg = seg_ref[...]
    row = lax.broadcasted_iota(i32, (16, 128), 0)
    tail = jnp.zeros((16, 128), f32)
    for s in range(2):
        n = jnp.sum(jnp.sum((seg <= s).astype(f32), axis=0, keepdims=True), axis=1, keepdims=True)
        n = jnp.broadcast_to(n, (16, 128))
        hi = jnp.floor(n * 0.0625)
        tail = jnp.where(row == 2 * s, hi, jnp.where(row == 2 * s + 1, n - 16.0 * hi, tail))
    kv_ref[me, T:KVR, :] = tail.astype(bf16)
    pl.semaphore_wait(bar, len(ALL_PEERS) + NB - 1)
    gq.start()
    gk.start()
    gates_of(normed, rw_ref, rt_ref, gate_ref)
    gq.forward()
    gq.finish()
    project_queries(normed, wq_ref, table)
    pick_queries(rt_ref, table, qt_ref)
    gk.forward()
    gk.finish()
    bounds = bounds_of(kv_ref)
    prepare_keys(kv_ref, bounds, kaug, vaug, vt)
    mark_queries(bounds, me, qt_ref)
    go.start()
    attend(me, qt_ref, kaug, vt, att_ref, macc, acc)

    go.forward()
    routes = route_rows(rt_ref)
    for j in range(J):
        rows[j] = sub8(att_ref[:, j * T : (j + 1) * T].astype(f32) * gate_ref[j : j + 1, :])
    to_experts(routes, rows, gat)
    go.finish()
    x = x_ref[...].astype(f32)
    wo_all = wo_ref[...].reshape(EW, D)
    mixed = x + tn(gat[...], wo_all)
    inv = lax.rsqrt(jnp.mean(mixed * mixed, axis=-1, keepdims=True) + eps)
    n = mixed * inv
    fgain = fgain_ref[...]
    second = (n * fgain).astype(bf16)
    second_t = jnp.transpose(n * fgain).astype(bf16)
    cot = cot_ref[...]
    for cp in loads:
        cp.wait()
    C = 512
    out = mixed
    gsec = jnp.zeros((T, D), f32)
    ahead = nn(second, up_ref[:, 0:C]), nt(cot, down_ref[0:C, :])
    for c in range(FF // C):
        cs = slice(c * C, (c + 1) * C)
        v, gact = ahead
        if c + 1 < FF // C:
            ns = slice((c + 1) * C, (c + 2) * C)
            ahead = nn(second, up_ref[:, ns]), nt(cot, down_ref[ns, :])
        v2 = v * v
        th = jnp.tanh(0.7978845608028654 * (v + 0.044715 * v * v2))
        a = (0.5 * v * (1.0 + th)).astype(bf16)
        dth = 0.5 * (1.0 + th) + 0.5 * v * (1.0 - th * th) * (0.7978845608028654 * (1.0 + 0.134145 * v2))
        gh = (gact * dth).astype(bf16)
        out = out + nn(a, down_ref[cs, :])
        gsec = gsec + nt(gh, up_ref[:, cs])
        gdown = tn(a, cot).astype(bf16)
        gup = nn(second_t, gh).astype(bf16)
        for t in range(4):
            ts = slice(t * 128, (t + 1) * 128)
            big[(core + t // 2) % 2, DOWN_UNIT[c], t % 2 * 512 : t % 2 * 512 + 512, :] = gdown[:, ts]
            big[(core + t // 2) % 2, UP_UNIT[c], t % 2 * 512 : t % 2 * 512 + 512, :] = gup[:, ts]
        for b, i in CHUNK_PARTS[c]:
            early[b].start0(i)
    for i in (0, 1, 3):
        early[i].pass0(0)
    out_ref[...] = out.astype(bf16)
    dfg_ref[...] = jnp.sum(gsec * n, axis=0, keepdims=True)
    hh = gsec * fgain
    gm = cot.astype(f32) + inv * (hh - n * jnp.mean(hh * n, axis=-1, keepdims=True))
    gm_ref[...] = gm
    gml = gm.astype(bf16)
    for c in range(4):
        store_expert(big, core, WO_UNIT, 2 * c, nn(gat[c * 384 : (c + 1) * 384, :], gml))
    for b, i in WO_PARTS:
        early[b].start0(i)
    for c in range(4):
        w = wo_ref[2 * c : 2 * c + 2].reshape(2 * 3 * H, D)
        table[c * 48 : (c + 1) * 48] = nt(w, gml).reshape(48, 8, T)
    dots = []
    row = lax.broadcasted_iota(i32, (H, T), 0)
    for j in range(J):
        js = slice(j * T, (j + 1) * T)
        g = choose(routes, table, j).reshape(H, T)
        gate = gate_ref[j : j + 1, :]
        dot = jnp.sum(g * att_ref[:, js].astype(f32), axis=0, keepdims=True)
        dots.append(dot)
        d1, d2, d3 = split3(-(dot * gate))
        dat_ref[0:H, js] = (g * gate).astype(bf16)
        dat_ref[H:, js] = jnp.where(row == 0, d1, jnp.where(row == 1, d2, jnp.where(row == 2, d3, 0.0))).astype(bf16)
    dots = jnp.concatenate(dots, axis=0)
    gates = gate_ref[...]
    chosen = gates * (dots - jnp.sum(gates * dots, axis=0, keepdims=True))
    eid = lax.broadcasted_iota(i32, (E, T), 0)
    gl = jnp.zeros((E, T), f32)
    for j in range(J):
        gl = jnp.where(rt_ref[j : j + 1, :] == eid, chosen[j : j + 1, :], gl)
    hi = gl.astype(bf16)
    lo = (gl - hi.astype(f32)).astype(bf16)
    rw = rw_ref[...]
    gn_ref[...] = tn(hi, rw) + tn(lo, rw)
    nm = normed_ref[...]
    drw_ref[...] = nn(hi, nm) + nn(lo, nm)

    for j in range(J):
        js = slice(j * T, (j + 1) * T)
        qa[js, :] = jnp.transpose(qt_ref[:, js].astype(f32)).astype(bf16)
        da[js, :] = jnp.transpose(dat_ref[:, js].astype(f32)).astype(bf16)
    dqacc[...] = jnp.zeros(dqacc.shape, f32)
    for i, h in ((0, 1), (1, 1), (2, 0), (3, 1)):
        early[i].pass0(h)
    last = me // 2

    def half_block(sb, half, masked):
        ks = pl.ds(pl.multiple_of(sb * SB, SB), SB)

        @pl.when(half == 0)
        def _():
            tot[...] = jnp.zeros(tot.shape, f32)

        for i in range(2):
            gs = pl.ds(pl.multiple_of((half * 2 + i) * SB, SB), SB)
            p = jnp.exp(nt(qa[gs, :], kaug[ks, :]))
            if masked:
                ok = visible(me, sb)
                p = jnp.where(jnp.concatenate([ok, ok], axis=0), p, 0.0)
            ds = (p * nt(da[gs, :], vaug[ks, :])).astype(bf16)
            kv = jnp.concatenate([kv_ref[2 * sb, 0:T, :], kv_ref[2 * sb + 1, 0:T, :]], axis=0)
            dqacc[gs, :] += nn(ds, kv)
            tot[0:H, :] += nn(qt_ref[0:H, gs], ds)
            tot[H:, :] += nn(dat_ref[0:H, gs], p.astype(bf16))

        @pl.when(half == 1)
        def _():
            low = jnp.transpose(tot[...]).astype(bf16)
            gsend[2 * sb] = low[0:T]
            gsend[2 * sb + 1] = low[T:]

    def to_owner(kb):
        return pltpu.make_async_remote_copy(src_ref=gsend.at[kb], dst_ref=grecv.at[me], send_sem=ksend.at[kb],
                                            recv_sem=krecv.at[me], device_id=(dp, kb), device_id_type=MESH)

    def from_device(b):
        return pltpu.make_async_remote_copy(src_ref=gsend.at[b], dst_ref=grecv.at[b], send_sem=ksend.at[b],
                                            recv_sem=krecv.at[b], device_id=(dp, b), device_id_type=MESH)

    def at_3():
        for s in early:
            s.pass1()

    def at_5():
        for s in early:
            s.pass2()

    def step(i, carry):
        sb, half = i // 2, i % 2

        @pl.when(sb < last)
        def _():
            half_block(sb, half, False)

            @pl.when(half == 1)
            def _():
                to_owner(2 * sb).start()
                to_owner(2 * sb + 1).start()

        pl.when(i == 3)(at_3)
        pl.when(i == 5)(at_5)

        return carry

    lax.fori_loop(0, 2 * (NSB - 1), step, 0)

    def last_step(half, carry):
        half_block(last, half, True)

        return carry

    lax.fori_loop(0, 2, last_step, 0)

    @pl.when(2 * last < me)
    def _():
        to_owner(2 * last).start()

    for s in early:
        s.pass3()
    for s, e, (u0, u1, _) in zip(spreads, (early[0], early[1], early[3]), SPREADS):
        s.begin([e.result(SHARED[u]) for u in range(u0, u1)])
    for s, e, u in zip(owned_o, (early[0], early[2], early[3]), WO_UNIT):
        s.begin(e.result(u))
    for j in range(J):
        js = slice(j * T, (j + 1) * T)
        rows[j] = sub8(jnp.transpose(dqacc[js, :])[0:H].astype(bf16).astype(f32) * 0.125)
    for c in range(4):
        to_experts(routes, rows, gat, range(6 * c, 6 * c + 6))
        store_expert(lbig, core, [0, 1, 2], 2 * c, nn(gat[c * 384 : (c + 1) * 384, :], nm))
        for s in late:
            s.start0(c)
    for s in spreads:
        s.pass2()
        s.send(0)
    dqacc[0:T, :] = gsend[me].astype(f32)
    for b in range(1, NB):
        @pl.when(b > me)
        def _(b=b):
            from_device(b).wait_recv()
            dqacc[0:T, :] += grecv[b].astype(f32)
    gkv = dqacc[0:T, :].astype(bf16)
    dkvw = tn(nm, gkv).astype(bf16)
    done = set(copies.open)
    for s in late:
        s.pass0(0)
    for s in spreads:
        s.send(1)
    gn = gn_ref[...] + tn(gat[...], wq_ref[...].reshape(EW, D)) + nt(gkv, kvw_ref[...])
    x = x_ref[...].astype(f32)
    inv = lax.rsqrt(jnp.mean(x * x, axis=-1, keepdims=True) + eps)
    n = x * inv
    dgain = jnp.sum(gn * n, axis=0, keepdims=True)
    drw = drw_ref[...]
    dfg = dfg_ref[...]
    parts = [dkvw.astype(f32)] + [drw[:, t * 128 : (t + 1) * 128] for t in range(4)]
    parts += [v[:, t * 128 : (t + 1) * 128] for v in (dgain, dfg) for t in range(4)] + [jnp.zeros((SMALL - 616, 128), f32)]
    ssrc[...] = jnp.concatenate(parts, axis=0).astype(bf16).reshape(2, 4, SMALL // 8, 128)
    small.step(0)
    copies.drain(copies.open - done)
    small.step(1)
    for s in late:
        s.pass1()
    small.step(2)
    for s in spreads:
        s.send(2)
        s.forward(0)
    hh = gn * gain_ref[...]
    ing_ref[...] = (gm_ref[...] + inv * (hh - n * jnp.mean(hh * n, axis=-1, keepdims=True))).astype(bf16)
    for s in late:
        s.pass2()
    small.step(3)
    for s in spreads:
        s.finish(0)
        s.forward(1)
    for s, t, u in zip(owned_q, late, range(3)):
        t.pass3()
        s.begin(t.result(u))
    small.step(4)
    for s in spreads:
        s.finish(1)
        s.forward(2)
    copies.drain([i for s in owned_q for i in s.ids] + small.ids[4])
    for s in owned_o + owned_q:
        s.finish()
    small.step(5)
    for s in spreads:
        s.finish(2)
    small.step(6)
    for s in spreads:
        for u in range(s.u0, s.u1):
            s.keep(u).wait()
    for b in range(NB - 1):
        @pl.when(b < me)
        def _(b=b):
            to_owner(b).wait_send()
    copies.drain()


SCRATCH = [
    VM((8, 2, 4, 4, 4, 16, 128), bf16), pltpu.SemaphoreType.DMA((8,)),
    VM((D, FF), bf16), VM((FF, D), bf16), pltpu.SemaphoreType.DMA((2,)), VM((T, D), bf16), VM((J, T), f32), VM((NB, KVR, 128), bf16),
    VM((NB, 3 * H, D), bf16), VM((NB, 3 * H, D), bf16), VM((H, ROWS), bf16), VM((128, ROWS), bf16), VM((EW // 8, 8, T), f32),
    VM((ROWS, 128), bf16), VM((ROWS, 128), bf16), VM((80, ROWS), bf16), VM((8, ROWS), f32), VM((80, ROWS), f32),
    VM((J, 8, 8, T), f32), VM((EW, T), bf16), VM((T, D), f32), VM((T, D), f32), VM((E, D), f32), VM((1, D), f32),
    VM((2, UNITS, 1024, 128), bf16), VM((UNITS, 4, 4, 4, 16, 128), bf16), VM((UNITS, 3, 4, 4, 16, 128), bf16),
    VM((UNITS, 3, 4, 16, 128), bf16), VM((UNITS, 4, 4, 16, 128), bf16),
    VM((128, ROWS), bf16), VM((ROWS, 128), bf16), VM((ROWS, 128), bf16), VM((ROWS, 128), f32), VM((128, SB), f32),
    VM((NB, T, 128), bf16), VM((NB, T, 128), bf16),
    VM((2, 3, 1024, 128), bf16), VM((3, 4, 4, 4, 16, 128), bf16), VM((3, 3, 4, 4, 16, 128), bf16), VM((3, 3, 4, 16, 128), bf16),
    VM((3, 4, 4, 16, 128), bf16),
    VM((2, 4, SMALL // 8, 128), bf16), VM((4, SMALL // 8, 128), bf16), VM((4, SMALL // 8, 128), bf16),
    VM((3, SMALL // 8, 128), bf16), VM((4, SMALL // 8, 128), bf16), VM((4, SMALL // 8, 128), bf16),
] + dma_sems(210) + dma_sems(NB)


def kernel_f(all_hbm, wo_hbm, dwq_hbm, small_hbm, out_in, ing_in,
             dup_hbm, ddown_hbm, dwo_ref, dwqt_ref, dkvw_ref, drw_ref, dgain_ref, dfg_ref, out_hbm, ing_hbm,
             units, wo_ref, dwq_ref, small_ref, up, down, held, in_sem, out_sem):
    order = [SHARED.index(u) for pair in zip(UP_UNIT, DOWN_UNIT) for u in pair]
    loads = [pltpu.make_async_copy(all_hbm.at[u], units.at[u], in_sem.at[i]) for i, u in enumerate(order)]
    loads += [pltpu.make_async_copy(src, dst, in_sem.at[8 + i])
              for i, (src, dst) in enumerate(((wo_hbm, wo_ref), (dwq_hbm, dwq_ref), (small_hbm, small_ref),
                                              (out_in, held.at[0]), (ing_in, held.at[1])))]
    for cp in loads:
        cp.start()
    stores = []
    for c in range(4):
        cs = slice(c * 512, (c + 1) * 512)
        u, d = order[2 * c : 2 * c + 2]
        loads[2 * c].wait()
        for t in range(4):
            up[:, c * 512 + t * 128 : c * 512 + (t + 1) * 128] = units[u, t].astype(f32)
        stores.append(pltpu.make_async_copy(up.at[:, cs], dup_hbm.at[:, cs], out_sem.at[2 * c]))
        stores[-1].start()
        loads[2 * c + 1].wait()
        for t in range(4):
            down[cs, t * 128 : (t + 1) * 128] = units[d, t].astype(f32)
        stores.append(pltpu.make_async_copy(down.at[cs], ddown_hbm.at[cs], out_sem.at[2 * c + 1]))
        stores[-1].start()
    for cp in loads[8:]:
        cp.wait()
    for i, dst in enumerate((out_hbm, ing_hbm)):
        stores.append(pltpu.make_async_copy(held.at[i], dst, out_sem.at[8 + i]))
        stores[-1].start()
    for t in range(4):
        ts = slice(t * 128, (t + 1) * 128)
        dwo_ref[:, ts] = wo_ref[t * 192 : (t + 1) * 192, :].astype(f32)
        dwqt_ref[:, ts] = dwq_ref[t * 192 : (t + 1) * 192, :].astype(f32)
    small = small_ref[512:SMALL, :].astype(f32)
    dkvw_ref[...] = small_ref[0:512, :].astype(f32)
    for t in range(4):
        ts = slice(t * 128, (t + 1) * 128)
        drw_ref[:, ts] = small[t * E : (t + 1) * E]
        dgain_ref[:, ts] = small[96 + t : 97 + t]
        dfg_ref[:, ts] = small[100 + t : 101 + t]
    for cp in stores:
        cp.wait()


def per_device(inputs, cotangent, norm_gain, ffn_gain, kv_weight, router_weight, query_weight, output_weight, up_weight,
               down_weight, routes, segment_ids):
    wq = jnp.swapaxes(query_weight, 1, 2).reshape(3 * H, D)
    wo = output_weight.reshape(3 * H, D)
    vmem, anywhere = pl.BlockSpec(memory_space=VM), pl.BlockSpec(memory_space=pl.ANY)
    S = jax.ShapeDtypeStruct
    out, ing, shared, dwo, dwq, small = pl.pallas_call(
        kernel_all,
        out_shape=[S((T, D), bf16), S((T, D), bf16), S((8, 2, 4, 4, 4, 16, 128), bf16), S((3, 4, 4, 16, 128), bf16),
                   S((3, 4, 4, 16, 128), bf16), S((2, 4, SMALL // 8, 128), bf16)],
        in_specs=[vmem] * 10 + [anywhere] * 2,
        out_specs=[vmem, vmem, anywhere, vmem, vmem, vmem],
        scratch_shapes=SCRATCH,
        compiler_params=pltpu.CompilerParams(vmem_limit_bytes=62 << 20, collective_id=1, has_side_effects=True),
        cost_estimate=pl.CostEstimate(flops=1 << 35, bytes_accessed=1 << 24, transcendentals=0),
    )(inputs, cotangent, norm_gain.reshape(1, D), ffn_gain.reshape(1, D), kv_weight, router_weight.T, routes.T,
      segment_ids.reshape(3, 128), wq, wo, up_weight, down_weight)
    dup, ddown, dwo, dwqt, dkvw, drw, dgain, dfg, out, ing = pl.pallas_call(
        kernel_f,
        out_shape=[S((D, FF), f32), S((FF, D), f32), S((3 * H, D), f32), S((3 * H, D), f32), S((D, 128), f32), S((E, D), f32),
                   S((1, D), f32), S((1, D), f32), S((T, D), bf16), S((T, D), bf16)],
        in_specs=[anywhere] * 6,
        out_specs=[anywhere] * 2 + [vmem] * 6 + [anywhere] * 2,
        scratch_shapes=[VM((8, 4, 512, 128), bf16), VM((768, 128), bf16), VM((768, 128), bf16), VM((SMALL, 128), bf16),
                        VM((D, FF), f32), VM((FF, D), f32), VM((2, T, D), bf16), pltpu.SemaphoreType.DMA((13,)),
                        pltpu.SemaphoreType.DMA((10,))],
        compiler_params=pltpu.CompilerParams(vmem_limit_bytes=62 << 20),
    )(shared.reshape(8, 4, 512, 128), dwo.reshape(768, 128), dwq.reshape(768, 128), small.reshape(SMALL, 128), out, ing)
    return (out, ing, dgain.reshape(D), dfg.reshape(D), dkvw, drw.T,
            jnp.swapaxes(dwqt.reshape(3, H, D), 1, 2), dwo.reshape(3, H, D), dup, ddown)


def solution(mesh):
    both = P(("dp", "expert"), None)
    ex = P("expert", None, None)
    return jax.shard_map(
        per_device, mesh=mesh,
        in_specs=(both, both, P(), P(), P(), P(), ex, ex, P(), P(), both, P(("dp", "expert"))),
        out_specs=(both, both, P(), P(), P(), P(), ex, ex, P(), P()),
        check_vma=False)
```

```python
import functools
import jax
import jax.numpy as jnp
from jax import lax
from jax.experimental import pallas as pl
from jax.experimental.pallas import tpu as pltpu
from jax.sharding import PartitionSpec as P

f32, bf16, i32 = jnp.float32, jnp.bfloat16, jnp.int32
T, D, H, J, E, FF, NB = 384, 512, 64, 8, 24, 2048, 8
EW = E * H
ROWS = J * T
SB = 2 * T
NSB = NB // 2
eps = 1e-06
NEG = -1e30
VM = pltpu.VMEM


def nn(a, b):
    return lax.dot_general(a, b, (((1,), (0,)), ((), ())), preferred_element_type=f32)


def nt(a, b):
    return lax.dot_general(a, b, (((1,), (1,)), ((), ())), preferred_element_type=f32)


def tn(a, b):
    return lax.dot_general(a, b, (((0,), (0,)), ((), ())), preferred_element_type=f32)


def lanes(rows):
    return lax.broadcasted_iota(i32, (rows, 128), 1)


def split3(v):
    a = v.astype(bf16).astype(f32)
    b = (v - a).astype(bf16).astype(f32)
    c = (v - a - b).astype(bf16).astype(f32)
    return a, b, c


MESH = pl.DeviceIdType.MESH
LINES = [(a, k) for a in "xyz" for k in (1, 2, 3)]
ALL_PEERS = [("c", 0)] + LINES


class Place:
    def __init__(self):
        dp, ex = lax.axis_index("dp"), lax.axis_index("expert")
        self.ex = ex
        self.at = {"x": dp // 4, "y": dp % 4, "z": ex // 2, "c": ex % 2}
        self.peers = {("c", 0): self.device(c=1 - self.at["c"])}
        for axis, k in LINES:
            self.peers[axis, k] = self.device(**{axis: (self.at[axis] + k) % 4})

    def device(self, **moved):
        at = {**self.at, **moved}
        return (at["x"] * 4 + at["y"], at["z"] * 2 + at["c"])


class Copies:
    def __init__(self, place, send, recv):
        self.place, self.send, self.recv, self.made, self.open = place, send, recv, [], set()

    def add(self, src, dst, peer):
        self.made.append((src, dst, peer))
        return len(self.made) - 1

    def get(self, i):
        src, dst, peer = self.made[i]
        return pltpu.make_async_remote_copy(src_ref=src(), dst_ref=dst(), send_sem=self.send.at[i], recv_sem=self.recv.at[i],
                                            device_id=self.place.peers[peer], device_id_type=MESH)

    def start(self, ids):
        self.open |= set(ids)
        for i in ids:
            self.get(i).start()

    def arrived(self, ids):
        for i in ids:
            self.get(i).wait_recv()

    def drain(self, keep=()):
        for i in sorted(self.open - set(keep)):
            self.get(i).wait_send()
        self.open &= set(keep)


class Scatter:
    def __init__(self, copies, big, r, ex, parts, groups, order, cut=False):
        self.cp, self.big, self.r, self.ex = copies, big, r, ex
        self.parts, self.groups, self.u0, self.u1 = parts, groups, parts[0][0], parts[-1][1]
        at = copies.place.at
        self.m = m = [at[a] for a in order]
        rng = lambda g: pl.ds(g[0], g[1] - g[0])
        us = rng((self.u0, self.u1))
        if cut:
            self.parts = parts * 4
            z = order.index("z")
            at_z = lambda q: (parts[0][0],) + (slice(None),) * z + (q,)
            self.part_ids = [copies.add(lambda q=q: big.at[(1,) + at_z(q)], lambda q=q: r[0].at[at_z(q)], ("c", 0)) for q in range(4)]
        else:
            self.part_ids = [copies.add(lambda g=g: big.at[1, rng(g)], lambda g=g: r[0].at[rng(g)], ("c", 0)) for g in parts]
        self.group_ids = [
            [copies.add(lambda g=g, k=k: big.at[0, rng(g), (m[0] + k) % 4], lambda g=g, k=k: r[1].at[rng(g), k - 1], (order[0], k))
             for k in (1, 2, 3)] for g in groups]
        self.ids2 = [copies.add(lambda k=k: big.at[0, us, m[0], (m[1] + k) % 4], lambda k=k: r[2].at[us, k - 1], (order[1], k))
                     for k in (1, 2, 3)]
        own = lambda: ex.at[us, m[2]]
        self.ids3 = [copies.add(own, own, (order[2], k)) for k in (1, 2, 3)]

    def start0(self, i):
        self.cp.start([self.part_ids[i]])

    def pass0(self, h):
        g = self.groups[h]
        self.cp.arrived([i for i, p in zip(self.part_ids, self.parts) if g[0] <= p[0] < g[1]])
        for u in range(*g):
            for a in range(4):
                v = self.big[0, u, a].astype(f32) + self.r[0][u, a].astype(f32)
                self.big[0, u, a] = v.astype(bf16)
        self.cp.start(self.group_ids[h])

    def add3(self, u, at, r):
        v = self.big[at].astype(f32)
        for k in range(3):
            v = v + r[u, k].astype(f32)
        return v.astype(bf16)

    def pass1(self):
        for h, g in enumerate(self.groups):
            self.cp.arrived(self.group_ids[h])
            for u in range(*g):
                at = (0, u, self.m[0])
                self.big[at] = self.add3(u, at, self.r[1])
        self.cp.start(self.ids2)

    def pass2(self):
        self.cp.arrived(self.ids2)
        for u in range(self.u0, self.u1):
            self.ex[u, self.m[2]] = self.add3(u, (0, u, self.m[0], self.m[1]), self.r[2])
        self.cp.start(self.ids3)

    def pass3(self):
        self.cp.arrived(self.ids3)

    def result(self, u):
        e = [self.ex[u, i].astype(f32) for i in range(4)]
        return (e[0] + e[1] + e[2] + e[3]).astype(bf16)


class Spread:
    def __init__(self, copies, out, kept, kept_sem, u0, u1, order):
        self.cp, self.out, self.kept, self.kept_sem, self.u0, self.u1 = copies, out, kept, kept_sem, u0, u1
        at = copies.place.at
        self.c, self.m = at["c"], [at[a] for a in order]
        us = pl.ds(u0, u1 - u0)
        quarter = lambda: out.at[us, self.c, self.m[0], self.m[1]]
        self.ids2 = [copies.add(quarter, quarter, (order[1], k)) for k in (1, 2, 3)]
        self.ids1, self.ids0 = [], []
        for u in range(u0, u1):
            piece = lambda k=0, u=u: out.at[u, self.c, (self.m[0] - k + 4) % 4]
            self.ids1.append([copies.add(piece, piece, (order[0], k)) for k in (1, 2, 3)])
            self.ids0.append([copies.add(functools.partial(piece, k), functools.partial(piece, k), ("c", 0)) for k in range(4)])

    def begin(self, values):
        for u, v in zip(range(self.u0, self.u1), values):
            self.out[u, self.c, self.m[0], self.m[1]] = v
        self.cp.start(self.ids2)

    def pass2(self):
        self.cp.arrived(self.ids2)

    def send(self, i):
        if i < len(self.ids1):
            self.cp.start(self.ids1[i] + self.ids0[i][:1])

    def forward(self, i):
        if i < len(self.ids1):
            for k in (1, 2, 3):
                self.cp.arrived(self.ids1[i][k - 1 : k])
                self.cp.start(self.ids0[i][k : k + 1])

    def finish(self, i):
        if i < len(self.ids0):
            self.cp.arrived(self.ids0[i])
            self.keep(self.u0 + i).start()

    def keep(self, u):
        return pltpu.make_async_copy(self.out.at[u], self.kept.at[u], self.kept_sem.at[u])


class SpreadOwner:
    def __init__(self, copies, out, u, axis):
        self.cp, self.out, self.u, self.p = copies, out, u, copies.place.at[axis]
        ref = lambda: out.at[u, self.p]
        self.ids = [copies.add(ref, ref, (axis, k)) for k in (1, 2, 3)]

    def begin(self, value):
        self.out[self.u, self.p] = value
        self.cp.start(self.ids)

    def finish(self):
        self.cp.arrived(self.ids)


class SmallSum:
    def __init__(self, copies, src, half, r0, r1, by, bz, out):
        self.cp, self.src, self.half, self.r0, self.r1, self.by, self.bz, self.out = copies, src, half, r0, r1, by, bz, out
        at = copies.place.at
        self.c, self.x, self.y, self.z = at["c"], at["x"], at["y"], at["z"]
        own_half = lambda: out.at[self.c]
        own = lambda: out.at[self.c, self.x]
        self.ids = [
            [copies.add(lambda: src.at[1 - self.c], lambda: r0, ("c", 0))],
            [copies.add(lambda k=k: half.at[(self.x + k) % 4], lambda k=k: r1.at[k - 1], ("x", k)) for k in (1, 2, 3)],
            [copies.add(lambda: by.at[self.y], lambda: by.at[self.y], ("y", k)) for k in (1, 2, 3)],
            [copies.add(lambda: bz.at[self.z], lambda: bz.at[self.z], ("z", k)) for k in (1, 2, 3)],
            [copies.add(own, own, ("x", k)) for k in (1, 2, 3)],
            [copies.add(own_half, own_half, ("c", 0))],
        ]

    def step(self, i):
        if i:
            self.cp.arrived(self.ids[i - 1])
        if i == 1:
            for a in range(4):
                self.half[a] = (self.src[self.c, a].astype(f32) + self.r0[a].astype(f32)).astype(bf16)
        if i == 2:
            v = self.half[self.x].astype(f32)
            for k in range(3):
                v = v + self.r1[k].astype(f32)
            self.by[self.y] = v.astype(bf16)
        if i in (3, 4):
            b = self.by if i == 3 else self.bz
            v = (b[0].astype(f32) + b[1].astype(f32) + b[2].astype(f32) + b[3].astype(f32)).astype(bf16)
            if i == 3:
                self.bz[self.z] = v
            else:
                self.out[self.c, self.x] = v
        if i < 6:
            self.cp.start(self.ids[i])


UNITS = 11
UP_UNIT, DOWN_UNIT, WO_UNIT = [0, 4, 8, 2], [1, 5, 9, 6], [3, 7, 10]
SHARED = sorted(UP_UNIT + DOWN_UNIT)
OWNER_ORDERS = ["zxy", "xzy", "yzx"]
EARLY = [([(0, 2), (2, 3), (3, 4)], [(0, 2), (2, 4)], "zxy"), ([(4, 6), (6, 7)], [(4, 6), (6, 7)], "xyz"),
         ([(7, 8)], [(7, 8)], "xzy"), ([(8, 10), (10, 11)], [(8, 10), (10, 11)], "yzx")]
CHUNK_PARTS, WO_PARTS = [[(0, 0)], [(1, 0)], [(3, 0)], [(0, 1), (1, 1)]], [(0, 2), (2, 0), (3, 1)]
SPREADS = [(0, 3, "zxy"), (3, 6, "xyz"), (6, 8, "yzx")]


def plane_axes(order):
    return [a for a in order if a != "z"]


def expert_row(ex, piece, order):
    p, q = plane_axes(order)
    at = {p: piece // 4, q: piece % 4, "z": ex // 2}
    r = ex % 2
    for a in order:
        r = r * 4 + at[a]
    return r * 16


def store_expert(big, core, units, ex0, value):
    low = value.astype(bf16)
    for o in range(2):
        slot = (core + (ex0 + o) % 2) % 2
        for row in range(0, 768, 16):
            v, piece = row // 256, (row % 256) // 16
            ct, r = row // 192, row % 192
            base = expert_row(ex0 + o, piece, OWNER_ORDERS[v]) % 1024
            big[slot, units[v], base : base + 16, :] = low[o * 192 + r : o * 192 + r + 16, ct * 128 : (ct + 1) * 128]


KVR = T + 16


class Gather:
    def __init__(self, copies, out):
        self.cp, self.out = copies, out
        at, ex = copies.place.at, copies.place.ex
        own = lambda: out.at[ex]
        from_z = lambda k: out.at[((at["z"] - k + 4) % 4) * 2 + at["c"]]
        self.line = [copies.add(own, own, ("z", k)) for k in (1, 2, 3)]
        self.core = [copies.add(functools.partial(from_z, k), functools.partial(from_z, k), ("c", 0)) for k in (0, 1, 2, 3)]

    def start(self):
        self.cp.start(self.line)
        self.cp.start(self.core[:1])

    def forward(self):
        for k in range(3):
            self.cp.arrived(self.line[k : k + 1])
            self.cp.start(self.core[k + 1 : k + 2])

    def neighbour(self):
        self.cp.arrived(self.core[:1])

    def finish(self):
        self.cp.arrived(self.core[1:])


class WideGather(Gather):
    def __init__(self, copies, out):
        self.cp, self.out = copies, out
        at, ex = copies.place.at, copies.place.ex
        wide, rows = D // 2, 3 * H // 4
        block = lambda k: ((at["z"] - k + 4) % 4) * 2 + at["c"]

        def quarter(axis, b):
            column = wide + 128 * "xy".index(axis)
            return out.at[b, pl.ds(pl.multiple_of(at[axis] * rows, 16), rows), column : column + 128]

        def both(make, peer):
            return copies.add(make, make, peer)

        self.quarters = [[both(functools.partial(quarter, a, ex), ("z", k)) for a in "xy"] for k in (1, 2, 3)]
        self.line = [both(lambda: out.at[ex, :, 0:wide], ("z", k)) for k in (1, 2, 3)]
        self.relays = [[both(lambda a=a, k=k: quarter(a, block(k)), (a, d)) for a in "xy" for d in (1, 2, 3)] for k in (1, 2, 3)]
        self.core = [both(lambda k=k: out.at[block(k)], ("c", 0)) for k in range(4)]

    def start(self):
        for ids in self.quarters:
            self.cp.start(ids)
        super().start()

    def relay(self):
        for ids, on in zip(self.quarters, self.relays):
            self.cp.arrived(ids)
            self.cp.start(on)

    def forward(self):
        for k in range(3):
            self.cp.arrived(self.relays[k] + self.line[k : k + 1])
            self.cp.start(self.core[k + 1 : k + 2])


def segment_in_block(tail, pos):
    tail = tail.astype(f32)
    return (pos >= 16.0 * tail[0:1] + tail[1:2]).astype(i32) + (pos >= 16.0 * tail[2:3] + tail[3:4]).astype(i32)


def sub8(v):
    return v.reshape(8, 8, v.shape[-1])


def route_rows(rt_ref):
    return [jnp.broadcast_to(rt_ref[j : j + 1, :], (8, T)) for j in range(J)]


def visible(me, sb):
    key = lax.broadcasted_iota(i32, (T, SB), 1)
    tok = lax.broadcasted_iota(i32, (T, SB), 0)
    ok = key - tok <= (me - 2 * sb) * T
    return ok


def prepare_keys(kv_ref, b, kaug, vaug, vt):
    ln = lanes(T)
    bs = pl.ds(pl.multiple_of(b * T, T), T)
    kv = kv_ref[b, 0:T, :].astype(f32)
    seg = segment_in_block(kv_ref[b, T:KVR, :], lax.broadcasted_iota(i32, (T, 128), 0).astype(f32))
    feat = jnp.where((ln < H + 3) & (seg != ln - H), NEG, 0.0)
    feat = jnp.where((ln >= H + 3) & (ln < H + 6), 1.0, feat)
    kaug[bs, :] = jnp.where(ln < H, kv, feat).astype(bf16)
    one = jnp.where(ln < H + 3, 1.0, 0.0)
    vaug[bs, :] = jnp.where(ln < H, pltpu.roll(kv, H, 1), one).astype(bf16)
    ones = jnp.where(lax.broadcasted_iota(i32, (16, T), 0) == 0, 1.0, 0.0)
    vt[:, bs] = jnp.concatenate([jnp.transpose(kv)[H:], ones], axis=0).astype(bf16)


def project_queries(normed, wq_ref, qall):
    for c in range(4):
        w = wq_ref[2 * c : 2 * c + 2].reshape(2 * 3 * H, D)
        qall[c * 48 : (c + 1) * 48] = (nt(w, normed) * 0.125).reshape(48, 8, T)


def choose(routes, table, j):
    acc = table[0:8]
    for e in range(1, E):
        acc = jnp.where((routes[j] == e)[None], table[e * 8 : (e + 1) * 8], acc)
    return acc


def to_experts(routes, rows, out, experts=range(E)):
    for e in experts:
        acc = jnp.zeros((8, 8, T), f32)
        for j in range(J):
            acc = jnp.where((routes[j] == e)[None], rows[j], acc)
        out[e * H : (e + 1) * H, :] = acc.reshape(H, T).astype(bf16)


def pick_queries(rt_ref, table, qt):
    routes = route_rows(rt_ref)
    for j in range(J):
        qt[0:H, j * T : (j + 1) * T] = choose(routes, table, j).reshape(H, T).astype(bf16)


def mark_queries(kv_ref, me, qt):
    pos = lax.broadcasted_iota(i32, (H, T), 1).astype(f32)
    seg = segment_in_block(kv_ref[me, T:KVR, :][:, 0:1], pos)
    feat = jnp.where(lax.broadcasted_iota(i32, (H, T), 0) == seg, 1.0, 0.0).astype(bf16)
    for j in range(J):
        qt[H:, j * T : (j + 1) * T] = feat


def attend(me, qt, kaug, vt, att, macc, acc, others):
    last = me // 2
    macc[...] = jnp.full(macc.shape, NEG, f32)
    acc[...] = jnp.zeros(acc.shape, f32)

    def score(sb, g, masked):
        s = nn(kaug[pl.ds(pl.multiple_of(sb * SB, SB), SB), :], qt[:, g * SB : (g + 1) * SB])
        if masked:
            key = lax.broadcasted_iota(i32, (SB, T), 0)
            tok = lax.broadcasted_iota(i32, (SB, T), 1)
            ok = key - tok <= (me - 2 * sb) * T
            s = jnp.where(jnp.concatenate([ok, ok], axis=1), s, NEG)
        return s.reshape(SB // 8, 8, SB)

    def soften(s, g):
        gs = slice(g * SB, (g + 1) * SB)
        old = macc[:, gs]
        top = jnp.max(jnp.maximum(old, jnp.max(s, axis=0)), axis=0, keepdims=True)
        top = jnp.broadcast_to(top, (8, SB))
        macc[:, gs] = top
        return jnp.exp(s - top[None]).reshape(SB, SB).astype(bf16), jnp.exp(old - top)

    def weigh(sb, g, p, kept):
        gs = slice(g * SB, (g + 1) * SB)
        old = acc[:, gs].reshape(10, 8, SB) * kept[None]
        acc[:, gs] = old.reshape(80, SB) + nn(vt[:, pl.ds(pl.multiple_of(sb * SB, SB), SB)], p)

    def block(sb, masked):
        s = score(sb, 0, masked)
        held = None
        for g in range(J // 2):
            ahead = score(sb, g + 1, masked) if g + 1 < J // 2 else None
            new = soften(s, g)
            if g:
                weigh(sb, g - 1, *held)
            held, s = new, ahead
        weigh(sb, J // 2 - 1, *held)

    block(last, True)
    others()
    lax.fori_loop(0, last, lambda sb, c: (block(sb, False), c)[1], 0)
    for g in range(J // 2):
        gs = slice(g * SB, (g + 1) * SB)
        tot = acc[H : H + 1, gs]
        att[:, gs] = (acc[0:H, gs] / tot).astype(bf16)
        l1, l2, l3 = split3(-(macc[0:1, gs] + jnp.log(tot)))
        row = lax.broadcasted_iota(i32, (16, SB), 0)
        feat = qt[H : H + 16, gs].astype(f32)
        feat = jnp.where(row == 3, l1, jnp.where(row == 4, l2, jnp.where(row == 5, l3, feat)))
        qt[H : H + 16, gs] = feat.astype(bf16)


def gates_of(normed, rw_ref, rt_ref, gate_ref):
    logits = nt(rw_ref[...], normed)
    eid = lax.broadcasted_iota(i32, (E, T), 0)
    per = [jnp.sum(jnp.where(rt_ref[j : j + 1, :] == eid, logits, 0.0), axis=0, keepdims=True) for j in range(J)]
    v = jnp.concatenate(per, axis=0)
    e = jnp.exp(v - jnp.max(v, axis=0, keepdims=True))
    gate_ref[...] = e / jnp.sum(e, axis=0, keepdims=True)


SMALL = 640


def dma_sems(n):
    return [pltpu.SemaphoreType.DMA((n,)), pltpu.SemaphoreType.DMA((n,))]


def kernel_all(x_ref, cot_ref, gain_ref, fgain_ref, kvw_ref, rw_ref, rt_ref, seg_ref, wq_in, wo_in, up_hbm, down_hbm,
               out_ref, ing_ref, all_hbm, dwo_ref, dwq_ref, small_ref,
               shared, all_sem, up_ref, down_ref, wsem, normed_ref, gate_ref, kv_ref, wq_ref, wo_ref, att_ref, qt_ref, table, kaug, vaug, vt, macc, acc,
               rows, gat, gm_ref, gn_ref, drw_ref, dfg_ref, big, r0, r1, r2, ex,
               dat_ref, qa, da, dqacc, tot, gsend, grecv, lbig, l0, l1, l2, lex, ssrc, shalf, s0, s1, sy, sz, send, recv, ksend, krecv):
    place = Place()
    me, core = place.ex, place.at["c"]
    dp = lax.axis_index("dp")
    copies = Copies(place, send, recv)
    gq, gk, go = WideGather(copies, wq_ref), Gather(copies, kv_ref), Gather(copies, wo_ref)
    big7 = big.reshape(2, UNITS, 4, 4, 4, 16, 128)
    lbig7 = lbig.reshape(2, 3, 4, 4, 4, 16, 128)
    early = [Scatter(copies, big7, (r0, r1, r2), ex, parts, groups, o) for parts, groups, o in EARLY]
    late = [Scatter(copies, lbig7, (l0, l1, l2), lex, [(u, u + 1)], [(u, u + 1)], o, cut=True) for u, o in enumerate(OWNER_ORDERS)]
    spreads = [Spread(copies, shared, all_hbm, all_sem, u0, u1, o) for u0, u1, o in SPREADS]
    owned_o = [SpreadOwner(copies, dwo_ref, u, plane_axes(o)[0]) for u, o in enumerate(OWNER_ORDERS)]
    owned_q = [SpreadOwner(copies, dwq_ref, u, plane_axes(o)[0]) for u, o in enumerate(OWNER_ORDERS)]
    small = SmallSum(copies, ssrc, shalf, s0, s1, sy, sz, small_ref)

    bar = pltpu.get_barrier_semaphore()
    for p in ALL_PEERS:
        pl.semaphore_signal(bar, inc=1, device_id=place.peers[p], device_id_type=MESH)
    for k in range(1, NB):
        pl.semaphore_signal(bar, inc=1, device_id=(dp, (me + k) % NB), device_id_type=MESH)
    loads = [pltpu.make_async_copy(up_hbm, up_ref, wsem.at[0]), pltpu.make_async_copy(down_hbm, down_ref, wsem.at[1])]
    for cp in loads:
        cp.start()
    wq_ref[me] = wq_in[...]
    wo_ref[me] = wo_in[...]

    x = x_ref[...].astype(f32)
    inv = lax.rsqrt(jnp.mean(x * x, axis=-1, keepdims=True) + eps)
    normed = (x * inv * gain_ref[...]).astype(bf16)
    normed_ref[...] = normed
    kv_ref[me, 0:T, :] = nn(normed, kvw_ref[...]).astype(bf16)
    seg = seg_ref[...]
    row = lax.broadcasted_iota(i32, (16, 128), 0)
    tail = jnp.zeros((16, 128), f32)
    for s in range(2):
        n = jnp.sum(jnp.sum((seg <= s).astype(f32), axis=0, keepdims=True), axis=1, keepdims=True)
        n = jnp.broadcast_to(n, (16, 128))
        hi = jnp.floor(n * 0.0625)
        tail = jnp.where(row == 2 * s, hi, jnp.where(row == 2 * s + 1, n - 16.0 * hi, tail))
    kv_ref[me, T:KVR, :] = tail.astype(bf16)
    pl.semaphore_wait(bar, len(ALL_PEERS) + NB - 1)
    gq.start()
    gk.start()
    gates_of(normed, rw_ref, rt_ref, gate_ref)
    gq.relay()
    gq.forward()
    gq.neighbour()
    gq.finish()
    project_queries(normed, wq_ref, table)
    pick_queries(rt_ref, table, qt_ref)
    mark_queries(kv_ref, me, qt_ref)
    gk.forward()
    go.start()
    gk.neighbour()
    for i in range(2):
        prepare_keys(kv_ref, 2 * (me // 2) + i, kaug, vaug, vt)

    def others():
        gk.finish()
        lax.fori_loop(0, NB, lambda b, c: (prepare_keys(kv_ref, b, kaug, vaug, vt), c)[1], 0)

    attend(me, qt_ref, kaug, vt, att_ref, macc, acc, others)

    go.forward()
    routes = route_rows(rt_ref)
    for j in range(J):
        rows[j] = sub8(att_ref[:, j * T : (j + 1) * T].astype(f32) * gate_ref[j : j + 1, :])
    to_experts(routes, rows, gat)
    go.neighbour()
    go.finish()
    x = x_ref[...].astype(f32)
    wo_all = wo_ref[...].reshape(EW, D)
    mixed = x + tn(gat[...], wo_all)
    inv = lax.rsqrt(jnp.mean(mixed * mixed, axis=-1, keepdims=True) + eps)
    n = mixed * inv
    fgain = fgain_ref[...]
    second = (n * fgain).astype(bf16)
    second_t = jnp.transpose(n * fgain).astype(bf16)
    cot = cot_ref[...]
    for cp in loads:
        cp.wait()
    C = 512
    out = mixed
    gsec = jnp.zeros((T, D), f32)
    ahead = nn(second, up_ref[:, 0:C]), nt(cot, down_ref[0:C, :])
    for c in range(FF // C):
        cs = slice(c * C, (c + 1) * C)
        v, gact = ahead
        if c + 1 < FF // C:
            ns = slice((c + 1) * C, (c + 2) * C)
            ahead = nn(second, up_ref[:, ns]), nt(cot, down_ref[ns, :])
        v2 = v * v
        th = jnp.tanh(0.7978845608028654 * (v + 0.044715 * v * v2))
        a = (0.5 * v * (1.0 + th)).astype(bf16)
        dth = 0.5 * (1.0 + th) + 0.5 * v * (1.0 - th * th) * (0.7978845608028654 * (1.0 + 0.134145 * v2))
        gh = (gact * dth).astype(bf16)
        out = out + nn(a, down_ref[cs, :])
        gsec = gsec + nt(gh, up_ref[:, cs])
        gdown = tn(a, cot).astype(bf16)
        gup = nn(second_t, gh).astype(bf16)
        for t in range(4):
            ts = slice(t * 128, (t + 1) * 128)
            big[(core + t // 2) % 2, DOWN_UNIT[c], t % 2 * 512 : t % 2 * 512 + 512, :] = gdown[:, ts]
            big[(core + t // 2) % 2, UP_UNIT[c], t % 2 * 512 : t % 2 * 512 + 512, :] = gup[:, ts]
        for b, i in CHUNK_PARTS[c]:
            early[b].start0(i)
    for i in (0, 1, 3):
        early[i].pass0(0)
    out_ref[...] = out.astype(bf16)
    dfg_ref[...] = jnp.sum(gsec * n, axis=0, keepdims=True)
    hh = gsec * fgain
    gm = cot.astype(f32) + inv * (hh - n * jnp.mean(hh * n, axis=-1, keepdims=True))
    gm_ref[...] = gm
    gml = gm.astype(bf16)
    for c in range(4):
        store_expert(big, core, WO_UNIT, 2 * c, nn(gat[c * 384 : (c + 1) * 384, :], gml))
    for b, i in WO_PARTS:
        early[b].start0(i)
    for c in range(4):
        w = wo_ref[2 * c : 2 * c + 2].reshape(2 * 3 * H, D)
        table[c * 48 : (c + 1) * 48] = nt(w, gml).reshape(48, 8, T)
    dots = []
    row = lax.broadcasted_iota(i32, (H, T), 0)
    for j in range(J):
        js = slice(j * T, (j + 1) * T)
        g = choose(routes, table, j).reshape(H, T)
        gate = gate_ref[j : j + 1, :]
        dot = jnp.sum(g * att_ref[:, js].astype(f32), axis=0, keepdims=True)
        dots.append(dot)
        d1, d2, d3 = split3(-(dot * gate))
        dat_ref[0:H, js] = (g * gate).astype(bf16)
        dat_ref[H:, js] = jnp.where(row == 0, d1, jnp.where(row == 1, d2, jnp.where(row == 2, d3, 0.0))).astype(bf16)
    dots = jnp.concatenate(dots, axis=0)
    gates = gate_ref[...]
    chosen = gates * (dots - jnp.sum(gates * dots, axis=0, keepdims=True))
    eid = lax.broadcasted_iota(i32, (E, T), 0)
    gl = jnp.zeros((E, T), f32)
    for j in range(J):
        gl = jnp.where(rt_ref[j : j + 1, :] == eid, chosen[j : j + 1, :], gl)
    hi = gl.astype(bf16)
    lo = (gl - hi.astype(f32)).astype(bf16)
    rw = rw_ref[...]
    gn_ref[...] = tn(hi, rw) + tn(lo, rw)
    nm = normed_ref[...]
    drw_ref[...] = nn(hi, nm) + nn(lo, nm)

    for j in range(J):
        js = slice(j * T, (j + 1) * T)
        qa[js, :] = jnp.transpose(qt_ref[:, js].astype(f32)).astype(bf16)
        da[js, :] = jnp.transpose(dat_ref[:, js].astype(f32)).astype(bf16)
    dqacc[...] = jnp.zeros(dqacc.shape, f32)
    for i, h in ((0, 1), (1, 1), (2, 0), (3, 1)):
        early[i].pass0(h)
    last = me // 2

    def half_block(sb, half, masked):
        ks = pl.ds(pl.multiple_of(sb * SB, SB), SB)

        @pl.when(half == 0)
        def _():
            tot[...] = jnp.zeros(tot.shape, f32)

        for i in range(2):
            gs = pl.ds(pl.multiple_of((half * 2 + i) * SB, SB), SB)
            p = jnp.exp(nt(qa[gs, :], kaug[ks, :]))
            if masked:
                ok = visible(me, sb)
                p = jnp.where(jnp.concatenate([ok, ok], axis=0), p, 0.0)
            ds = (p * nt(da[gs, :], vaug[ks, :])).astype(bf16)
            kv = jnp.concatenate([kv_ref[2 * sb, 0:T, :], kv_ref[2 * sb + 1, 0:T, :]], axis=0)
            dqacc[gs, :] += nn(ds, kv)
            tot[0:H, :] += nn(qt_ref[0:H, gs], ds)
            tot[H:, :] += nn(dat_ref[0:H, gs], p.astype(bf16))

        @pl.when(half == 1)
        def _():
            low = jnp.transpose(tot[...]).astype(bf16)
            gsend[2 * sb] = low[0:T]
            gsend[2 * sb + 1] = low[T:]

    def to_owner(kb):
        return pltpu.make_async_remote_copy(src_ref=gsend.at[kb], dst_ref=grecv.at[me], send_sem=ksend.at[kb],
                                            recv_sem=krecv.at[me], device_id=(dp, kb), device_id_type=MESH)

    def from_device(b):
        return pltpu.make_async_remote_copy(src_ref=gsend.at[b], dst_ref=grecv.at[b], send_sem=ksend.at[b],
                                            recv_sem=krecv.at[b], device_id=(dp, b), device_id_type=MESH)

    def at_3():
        for s in early:
            s.pass1()

    def at_5():
        for s in early:
            s.pass2()

    def step(i, carry):
        sb, half = i // 2, i % 2

        @pl.when(sb < last)
        def _():
            half_block(sb, half, False)

            @pl.when(half == 1)
            def _():
                to_owner(2 * sb).start()
                to_owner(2 * sb + 1).start()

        pl.when(i == 3)(at_3)
        pl.when(i == 5)(at_5)

        return carry

    lax.fori_loop(0, 2 * (NSB - 1), step, 0)

    def last_step(half, carry):
        half_block(last, half, True)

        return carry

    lax.fori_loop(0, 2, last_step, 0)

    @pl.when(2 * last < me)
    def _():
        to_owner(2 * last).start()

    for s in early:
        s.pass3()
    for s, e, (u0, u1, _) in zip(spreads, (early[0], early[1], early[3]), SPREADS):
        s.begin([e.result(SHARED[u]) for u in range(u0, u1)])
    for s, e, u in zip(owned_o, (early[0], early[2], early[3]), WO_UNIT):
        s.begin(e.result(u))
    for j in range(J):
        js = slice(j * T, (j + 1) * T)
        rows[j] = sub8(jnp.transpose(dqacc[js, :])[0:H].astype(bf16).astype(f32) * 0.125)
    for c in range(4):
        to_experts(routes, rows, gat, range(6 * c, 6 * c + 6))
        store_expert(lbig, core, [0, 1, 2], 2 * c, nn(gat[c * 384 : (c + 1) * 384, :], nm))
        for s in late:
            s.start0(c)
    for s in spreads:
        s.pass2()
        s.send(0)
    dqacc[0:T, :] = gsend[me].astype(f32)
    for b in range(1, NB):
        @pl.when(b > me)
        def _(b=b):
            from_device(b).wait_recv()
            dqacc[0:T, :] += grecv[b].astype(f32)
    gkv = dqacc[0:T, :].astype(bf16)
    dkvw = tn(nm, gkv).astype(bf16)
    done = set(copies.open)
    for s in late:
        s.pass0(0)
    for s in spreads:
        s.send(1)
    gn = gn_ref[...] + tn(gat[...], wq_ref[...].reshape(EW, D)) + nt(gkv, kvw_ref[...])
    x = x_ref[...].astype(f32)
    inv = lax.rsqrt(jnp.mean(x * x, axis=-1, keepdims=True) + eps)
    n = x * inv
    dgain = jnp.sum(gn * n, axis=0, keepdims=True)
    drw = drw_ref[...]
    dfg = dfg_ref[...]
    parts = [dkvw.astype(f32)] + [drw[:, t * 128 : (t + 1) * 128] for t in range(4)]
    parts += [v[:, t * 128 : (t + 1) * 128] for v in (dgain, dfg) for t in range(4)] + [jnp.zeros((SMALL - 616, 128), f32)]
    ssrc[...] = jnp.concatenate(parts, axis=0).astype(bf16).reshape(2, 4, SMALL // 8, 128)
    small.step(0)
    copies.drain(copies.open - done)
    small.step(1)
    for s in late:
        s.pass1()
    small.step(2)
    for s in spreads:
        s.send(2)
        s.forward(0)
    hh = gn * gain_ref[...]
    ing_ref[...] = (gm_ref[...] + inv * (hh - n * jnp.mean(hh * n, axis=-1, keepdims=True))).astype(bf16)
    for s in late:
        s.pass2()
    small.step(3)
    for s in spreads:
        s.finish(0)
        s.forward(1)
    for s, t, u in zip(owned_q, late, range(3)):
        t.pass3()
        s.begin(t.result(u))
    small.step(4)
    for s in spreads:
        s.finish(1)
        s.forward(2)
    copies.drain([i for s in owned_q for i in s.ids] + small.ids[4])
    for s in owned_o + owned_q:
        s.finish()
    small.step(5)
    for s in spreads:
        s.finish(2)
    small.step(6)
    for s in spreads:
        for u in range(s.u0, s.u1):
            s.keep(u).wait()
    for b in range(NB - 1):
        @pl.when(b < me)
        def _(b=b):
            to_owner(b).wait_send()
    copies.drain()


SCRATCH = [
    VM((8, 2, 4, 4, 4, 16, 128), bf16), pltpu.SemaphoreType.DMA((8,)),
    VM((D, FF), bf16), VM((FF, D), bf16), pltpu.SemaphoreType.DMA((2,)), VM((T, D), bf16), VM((J, T), f32), VM((NB, KVR, 128), bf16),
    VM((NB, 3 * H, D), bf16), VM((NB, 3 * H, D), bf16), VM((H, ROWS), bf16), VM((128, ROWS), bf16), VM((EW // 8, 8, T), f32),
    VM((ROWS, 128), bf16), VM((ROWS, 128), bf16), VM((80, ROWS), bf16), VM((8, ROWS), f32), VM((80, ROWS), f32),
    VM((J, 8, 8, T), f32), VM((EW, T), bf16), VM((T, D), f32), VM((T, D), f32), VM((E, D), f32), VM((1, D), f32),
    VM((2, UNITS, 1024, 128), bf16), VM((UNITS, 4, 4, 4, 16, 128), bf16), VM((UNITS, 3, 4, 4, 16, 128), bf16),
    VM((UNITS, 3, 4, 16, 128), bf16), VM((UNITS, 4, 4, 16, 128), bf16),
    VM((128, ROWS), bf16), VM((ROWS, 128), bf16), VM((ROWS, 128), bf16), VM((ROWS, 128), f32), VM((128, SB), f32),
    VM((NB, T, 128), bf16), VM((NB, T, 128), bf16),
    VM((2, 3, 1024, 128), bf16), VM((3, 4, 4, 4, 16, 128), bf16), VM((3, 3, 4, 4, 16, 128), bf16), VM((3, 3, 4, 16, 128), bf16),
    VM((3, 4, 4, 16, 128), bf16),
    VM((2, 4, SMALL // 8, 128), bf16), VM((4, SMALL // 8, 128), bf16), VM((4, SMALL // 8, 128), bf16),
    VM((3, SMALL // 8, 128), bf16), VM((4, SMALL // 8, 128), bf16), VM((4, SMALL // 8, 128), bf16),
] + dma_sems(234) + dma_sems(NB)


def kernel_f(all_hbm, wo_hbm, dwq_hbm, small_hbm, out_in, ing_in,
             dup_hbm, ddown_hbm, dwo_ref, dwqt_ref, dkvw_ref, drw_ref, dgain_ref, dfg_ref, out_hbm, ing_hbm,
             units, wo_ref, dwq_ref, small_ref, up, down, held, in_sem, out_sem):
    order = [SHARED.index(u) for pair in zip(UP_UNIT, DOWN_UNIT) for u in pair]
    loads = [pltpu.make_async_copy(all_hbm.at[u], units.at[u], in_sem.at[i]) for i, u in enumerate(order)]
    loads += [pltpu.make_async_copy(src, dst, in_sem.at[8 + i])
              for i, (src, dst) in enumerate(((wo_hbm, wo_ref), (dwq_hbm, dwq_ref), (small_hbm, small_ref),
                                              (out_in, held.at[0]), (ing_in, held.at[1])))]
    for cp in loads:
        cp.start()
    stores = []
    for c in range(4):
        cs = slice(c * 512, (c + 1) * 512)
        u, d = order[2 * c : 2 * c + 2]
        loads[2 * c].wait()
        for t in range(4):
            up[:, c * 512 + t * 128 : c * 512 + (t + 1) * 128] = units[u, t].astype(f32)
        stores.append(pltpu.make_async_copy(up.at[:, cs], dup_hbm.at[:, cs], out_sem.at[2 * c]))
        stores[-1].start()
        loads[2 * c + 1].wait()
        for t in range(4):
            down[cs, t * 128 : (t + 1) * 128] = units[d, t].astype(f32)
        stores.append(pltpu.make_async_copy(down.at[cs], ddown_hbm.at[cs], out_sem.at[2 * c + 1]))
        stores[-1].start()
    for cp in loads[8:]:
        cp.wait()
    for i, dst in enumerate((out_hbm, ing_hbm)):
        stores.append(pltpu.make_async_copy(held.at[i], dst, out_sem.at[8 + i]))
        stores[-1].start()
    for t in range(4):
        ts = slice(t * 128, (t + 1) * 128)
        dwo_ref[:, ts] = wo_ref[t * 192 : (t + 1) * 192, :].astype(f32)
        dwqt_ref[:, ts] = dwq_ref[t * 192 : (t + 1) * 192, :].astype(f32)
    small = small_ref[512:SMALL, :].astype(f32)
    dkvw_ref[...] = small_ref[0:512, :].astype(f32)
    for t in range(4):
        ts = slice(t * 128, (t + 1) * 128)
        drw_ref[:, ts] = small[t * E : (t + 1) * E]
        dgain_ref[:, ts] = small[96 + t : 97 + t]
        dfg_ref[:, ts] = small[100 + t : 101 + t]
    for cp in stores:
        cp.wait()


def per_device(inputs, cotangent, norm_gain, ffn_gain, kv_weight, router_weight, query_weight, output_weight, up_weight,
               down_weight, routes, segment_ids):
    wq = jnp.swapaxes(query_weight, 1, 2).reshape(3 * H, D)
    wo = output_weight.reshape(3 * H, D)
    vmem, anywhere = pl.BlockSpec(memory_space=VM), pl.BlockSpec(memory_space=pl.ANY)
    S = jax.ShapeDtypeStruct
    out, ing, shared, dwo, dwq, small = pl.pallas_call(
        kernel_all,
        out_shape=[S((T, D), bf16), S((T, D), bf16), S((8, 2, 4, 4, 4, 16, 128), bf16), S((3, 4, 4, 16, 128), bf16),
                   S((3, 4, 4, 16, 128), bf16), S((2, 4, SMALL // 8, 128), bf16)],
        in_specs=[vmem] * 10 + [anywhere] * 2,
        out_specs=[vmem, vmem, anywhere, vmem, vmem, vmem],
        scratch_shapes=SCRATCH,
        compiler_params=pltpu.CompilerParams(vmem_limit_bytes=62 << 20, collective_id=1, has_side_effects=True),
        cost_estimate=pl.CostEstimate(flops=1 << 35, bytes_accessed=1 << 24, transcendentals=0),
    )(inputs, cotangent, norm_gain.reshape(1, D), ffn_gain.reshape(1, D), kv_weight, router_weight.T, routes.T,
      segment_ids.reshape(3, 128), wq, wo, up_weight, down_weight)
    dup, ddown, dwo, dwqt, dkvw, drw, dgain, dfg, out, ing = pl.pallas_call(
        kernel_f,
        out_shape=[S((D, FF), f32), S((FF, D), f32), S((3 * H, D), f32), S((3 * H, D), f32), S((D, 128), f32), S((E, D), f32),
                   S((1, D), f32), S((1, D), f32), S((T, D), bf16), S((T, D), bf16)],
        in_specs=[anywhere] * 6,
        out_specs=[anywhere] * 2 + [vmem] * 6 + [anywhere] * 2,
        scratch_shapes=[VM((8, 4, 512, 128), bf16), VM((768, 128), bf16), VM((768, 128), bf16), VM((SMALL, 128), bf16),
                        VM((D, FF), f32), VM((FF, D), f32), VM((2, T, D), bf16), pltpu.SemaphoreType.DMA((13,)),
                        pltpu.SemaphoreType.DMA((10,))],
        compiler_params=pltpu.CompilerParams(vmem_limit_bytes=62 << 20),
    )(shared.reshape(8, 4, 512, 128), dwo.reshape(768, 128), dwq.reshape(768, 128), small.reshape(SMALL, 128), out, ing)
    return (out, ing, dgain.reshape(D), dfg.reshape(D), dkvw, drw.T,
            jnp.swapaxes(dwqt.reshape(3, H, D), 1, 2), dwo.reshape(3, H, D), dup, ddown)


def solution(mesh):
    both = P(("dp", "expert"), None)
    ex = P("expert", None, None)
    return jax.shard_map(
        per_device, mesh=mesh,
        in_specs=(both, both, P(), P(), P(), P(), ex, ex, P(), P(), both, P(("dp", "expert"))),
        out_specs=(both, both, P(), P(), P(), P(), ex, ex, P(), P()),
        check_vma=False)
```

```python
import functools
import jax
import jax.numpy as jnp
from jax import lax
from jax.experimental import pallas as pl
from jax.experimental.pallas import tpu as pltpu
from jax.sharding import PartitionSpec as P

f32, bf16, i32 = jnp.float32, jnp.bfloat16, jnp.int32
T, D, H, J, E, FF, NB = 384, 512, 64, 8, 24, 2048, 8
EW = E * H
ROWS = J * T
SB = 2 * T
NSB = NB // 2
eps = 1e-06
NEG = -1e30
VM = pltpu.VMEM


def nn(a, b):
    return lax.dot_general(a, b, (((1,), (0,)), ((), ())), preferred_element_type=f32)


def nt(a, b):
    return lax.dot_general(a, b, (((1,), (1,)), ((), ())), preferred_element_type=f32)


def tn(a, b):
    return lax.dot_general(a, b, (((0,), (0,)), ((), ())), preferred_element_type=f32)


def lanes(rows):
    return lax.broadcasted_iota(i32, (rows, 128), 1)


def split3(v):
    a = v.astype(bf16).astype(f32)
    b = (v - a).astype(bf16).astype(f32)
    c = (v - a - b).astype(bf16).astype(f32)
    return a, b, c


MESH = pl.DeviceIdType.MESH
LINES = [(a, k) for a in "xyz" for k in (1, 2, 3)]
ALL_PEERS = [("c", 0)] + LINES


class Place:
    def __init__(self):
        dp, ex = lax.axis_index("dp"), lax.axis_index("expert")
        self.ex = ex
        self.at = {"x": dp // 4, "y": dp % 4, "z": ex // 2, "c": ex % 2}
        self.peers = {("c", 0): self.device(c=1 - self.at["c"])}
        for axis, k in LINES:
            self.peers[axis, k] = self.device(**{axis: (self.at[axis] + k) % 4})

    def device(self, **moved):
        at = {**self.at, **moved}
        return (at["x"] * 4 + at["y"], at["z"] * 2 + at["c"])


class Copies:
    def __init__(self, place, send, recv):
        self.place, self.send, self.recv, self.made, self.open = place, send, recv, [], set()

    def add(self, src, dst, peer):
        self.made.append((src, dst, peer))
        return len(self.made) - 1

    def get(self, i):
        src, dst, peer = self.made[i]
        return pltpu.make_async_remote_copy(src_ref=src(), dst_ref=dst(), send_sem=self.send.at[i], recv_sem=self.recv.at[i],
                                            device_id=self.place.peers[peer], device_id_type=MESH)

    def start(self, ids):
        self.open |= set(ids)
        for i in ids:
            self.get(i).start()

    def arrived(self, ids):
        for i in ids:
            self.get(i).wait_recv()

    def drain(self, keep=()):
        for i in sorted(self.open - set(keep)):
            self.get(i).wait_send()
        self.open &= set(keep)


class Scatter:
    def __init__(self, copies, big, r, ex, parts, groups, order, cut=False):
        self.cp, self.big, self.r, self.ex = copies, big, r, ex
        self.parts, self.groups, self.u0, self.u1 = parts, groups, parts[0][0], parts[-1][1]
        at = copies.place.at
        self.m = m = [at[a] for a in order]
        rng = lambda g: pl.ds(g[0], g[1] - g[0])
        us = rng((self.u0, self.u1))
        if cut:
            self.parts = parts * 4
            z = order.index("z")
            at_z = lambda q: (parts[0][0],) + (slice(None),) * z + (q,)
            self.part_ids = [copies.add(lambda q=q: big.at[(1,) + at_z(q)], lambda q=q: r[0].at[at_z(q)], ("c", 0)) for q in range(4)]
        else:
            self.part_ids = [copies.add(lambda g=g: big.at[1, rng(g)], lambda g=g: r[0].at[rng(g)], ("c", 0)) for g in parts]
        self.group_ids = [
            [copies.add(lambda g=g, k=k: big.at[0, rng(g), (m[0] + k) % 4], lambda g=g, k=k: r[1].at[rng(g), k - 1], (order[0], k))
             for k in (1, 2, 3)] for g in groups]
        self.ids2 = [copies.add(lambda k=k: big.at[0, us, m[0], (m[1] + k) % 4], lambda k=k: r[2].at[us, k - 1], (order[1], k))
                     for k in (1, 2, 3)]
        own = lambda: ex.at[us, m[2]]
        self.ids3 = [copies.add(own, own, (order[2], k)) for k in (1, 2, 3)]

    def start0(self, i):
        self.cp.start([self.part_ids[i]])

    def pass0(self, h):
        g = self.groups[h]
        self.cp.arrived([i for i, p in zip(self.part_ids, self.parts) if g[0] <= p[0] < g[1]])
        for u in range(*g):
            for a in range(4):
                v = self.big[0, u, a].astype(f32) + self.r[0][u, a].astype(f32)
                self.big[0, u, a] = v.astype(bf16)
        self.cp.start(self.group_ids[h])

    def add3(self, u, at, r):
        v = self.big[at].astype(f32)
        for k in range(3):
            v = v + r[u, k].astype(f32)
        return v.astype(bf16)

    def pass1(self):
        for h, g in enumerate(self.groups):
            self.cp.arrived(self.group_ids[h])
            for u in range(*g):
                at = (0, u, self.m[0])
                self.big[at] = self.add3(u, at, self.r[1])
        self.cp.start(self.ids2)

    def pass2(self):
        self.cp.arrived(self.ids2)
        for u in range(self.u0, self.u1):
            self.ex[u, self.m[2]] = self.add3(u, (0, u, self.m[0], self.m[1]), self.r[2])
        self.cp.start(self.ids3)

    def pass3(self):
        self.cp.arrived(self.ids3)

    def result(self, u):
        e = [self.ex[u, i].astype(f32) for i in range(4)]
        return (e[0] + e[1] + e[2] + e[3]).astype(bf16)


class Spread:
    def __init__(self, copies, out, kept, kept_sem, u0, u1, order):
        self.cp, self.out, self.kept, self.kept_sem, self.u0, self.u1 = copies, out, kept, kept_sem, u0, u1
        at = copies.place.at
        self.c, self.m = at["c"], [at[a] for a in order]
        us = pl.ds(u0, u1 - u0)
        quarter = lambda: out.at[us, self.c, self.m[0], self.m[1]]
        self.ids2 = [copies.add(quarter, quarter, (order[1], k)) for k in (1, 2, 3)]
        self.ids1, self.ids0 = [], []
        for u in range(u0, u1):
            piece = lambda k=0, u=u: out.at[u, self.c, (self.m[0] - k + 4) % 4]
            self.ids1.append([copies.add(piece, piece, (order[0], k)) for k in (1, 2, 3)])
            self.ids0.append([copies.add(functools.partial(piece, k), functools.partial(piece, k), ("c", 0)) for k in range(4)])

    def begin(self, values):
        for u, v in zip(range(self.u0, self.u1), values):
            self.out[u, self.c, self.m[0], self.m[1]] = v
        self.cp.start(self.ids2)

    def pass2(self):
        self.cp.arrived(self.ids2)

    def send(self, i):
        if i < len(self.ids1):
            self.cp.start(self.ids1[i] + self.ids0[i][:1])

    def forward(self, i):
        if i < len(self.ids1):
            for k in (1, 2, 3):
                self.cp.arrived(self.ids1[i][k - 1 : k])
                self.cp.start(self.ids0[i][k : k + 1])

    def finish(self, i):
        if i < len(self.ids0):
            self.cp.arrived(self.ids0[i])
            self.keep(self.u0 + i).start()

    def keep(self, u):
        return pltpu.make_async_copy(self.out.at[u], self.kept.at[u], self.kept_sem.at[u])


class SpreadOwner:
    def __init__(self, copies, out, u, axis):
        self.cp, self.out, self.u, self.p = copies, out, u, copies.place.at[axis]
        ref = lambda: out.at[u, self.p]
        self.ids = [copies.add(ref, ref, (axis, k)) for k in (1, 2, 3)]

    def begin(self, value):
        self.out[self.u, self.p] = value
        self.cp.start(self.ids)

    def finish(self):
        self.cp.arrived(self.ids)


class SmallSum:
    def __init__(self, copies, src, half, r0, r1, by, bz, out):
        self.cp, self.src, self.half, self.r0, self.r1, self.by, self.bz, self.out = copies, src, half, r0, r1, by, bz, out
        at = copies.place.at
        self.c, self.x, self.y, self.z = at["c"], at["x"], at["y"], at["z"]
        own_half = lambda: out.at[self.c]
        own = lambda: out.at[self.c, self.x]
        self.ids = [
            [copies.add(lambda: src.at[1 - self.c], lambda: r0, ("c", 0))],
            [copies.add(lambda k=k: half.at[(self.x + k) % 4], lambda k=k: r1.at[k - 1], ("x", k)) for k in (1, 2, 3)],
            [copies.add(lambda: by.at[self.y], lambda: by.at[self.y], ("y", k)) for k in (1, 2, 3)],
            [copies.add(lambda: bz.at[self.z], lambda: bz.at[self.z], ("z", k)) for k in (1, 2, 3)],
            [copies.add(own, own, ("x", k)) for k in (1, 2, 3)],
            [copies.add(own_half, own_half, ("c", 0))],
        ]

    def step(self, i):
        if i:
            self.cp.arrived(self.ids[i - 1])
        if i == 1:
            for a in range(4):
                self.half[a] = (self.src[self.c, a].astype(f32) + self.r0[a].astype(f32)).astype(bf16)
        if i == 2:
            v = self.half[self.x].astype(f32)
            for k in range(3):
                v = v + self.r1[k].astype(f32)
            self.by[self.y] = v.astype(bf16)
        if i in (3, 4):
            b = self.by if i == 3 else self.bz
            v = (b[0].astype(f32) + b[1].astype(f32) + b[2].astype(f32) + b[3].astype(f32)).astype(bf16)
            if i == 3:
                self.bz[self.z] = v
            else:
                self.out[self.c, self.x] = v
        if i < 6:
            self.cp.start(self.ids[i])


UNITS = 11
UP_UNIT, DOWN_UNIT, WO_UNIT = [0, 4, 8, 2], [1, 5, 9, 6], [3, 7, 10]
SHARED = sorted(UP_UNIT + DOWN_UNIT)
OWNER_ORDERS = ["zxy", "xzy", "yzx"]
EARLY = [([(0, 2), (2, 3), (3, 4)], [(0, 2), (2, 4)], "zxy"), ([(4, 6), (6, 7)], [(4, 6), (6, 7)], "xyz"),
         ([(7, 8)], [(7, 8)], "xzy"), ([(8, 10), (10, 11)], [(8, 10), (10, 11)], "yzx")]
CHUNK_PARTS, WO_PARTS = [[(0, 0)], [(1, 0)], [(3, 0)], [(0, 1), (1, 1)]], [(0, 2), (2, 0), (3, 1)]
SPREADS = [(0, 3, "zxy"), (3, 6, "xyz"), (6, 8, "yzx")]


def plane_axes(order):
    return [a for a in order if a != "z"]


def expert_row(ex, piece, order):
    p, q = plane_axes(order)
    at = {p: piece // 4, q: piece % 4, "z": ex // 2}
    r = ex % 2
    for a in order:
        r = r * 4 + at[a]
    return r * 16


def store_expert(big, core, units, ex0, value):
    low = value.astype(bf16)
    for o in range(2):
        slot = (core + (ex0 + o) % 2) % 2
        for row in range(0, 768, 16):
            v, piece = row // 256, (row % 256) // 16
            ct, r = row // 192, row % 192
            base = expert_row(ex0 + o, piece, OWNER_ORDERS[v]) % 1024
            big[slot, units[v], base : base + 16, :] = low[o * 192 + r : o * 192 + r + 16, ct * 128 : (ct + 1) * 128]


KVR = T + 16


class Gather:
    def __init__(self, copies, out):
        self.cp, self.out = copies, out
        at, ex = copies.place.at, copies.place.ex
        own = lambda: out.at[ex]
        from_z = lambda k: out.at[((at["z"] - k + 4) % 4) * 2 + at["c"]]
        self.line = [copies.add(own, own, ("z", k)) for k in (1, 2, 3)]
        self.core = [copies.add(functools.partial(from_z, k), functools.partial(from_z, k), ("c", 0)) for k in (0, 1, 2, 3)]

    def start(self):
        self.cp.start(self.line)
        self.cp.start(self.core[:1])

    def forward(self):
        for k in range(3):
            self.cp.arrived(self.line[k : k + 1])
            self.cp.start(self.core[k + 1 : k + 2])

    def neighbour(self):
        self.cp.arrived(self.core[:1])

    def finish(self):
        self.cp.arrived(self.core[1:])


class WideGather(Gather):
    def __init__(self, copies, out):
        self.cp, self.out = copies, out
        at, ex = copies.place.at, copies.place.ex
        wide, rows = D // 2, 3 * H // 4
        block = lambda k: ((at["z"] - k + 4) % 4) * 2 + at["c"]

        def quarter(axis, b):
            column = wide + 128 * "xy".index(axis)
            return out.at[b, pl.ds(pl.multiple_of(at[axis] * rows, 16), rows), column : column + 128]

        def both(make, peer):
            return copies.add(make, make, peer)

        self.quarters = [[both(functools.partial(quarter, a, ex), ("z", k)) for a in "xy"] for k in (1, 2, 3)]
        self.line = [both(lambda: out.at[ex, :, 0:wide], ("z", k)) for k in (1, 2, 3)]
        self.relays = [[both(lambda a=a, k=k: quarter(a, block(k)), (a, d)) for a in "xy" for d in (1, 2, 3)] for k in (1, 2, 3)]
        self.core = [both(lambda k=k: out.at[block(k)], ("c", 0)) for k in range(4)]

    def start(self):
        for ids in self.quarters:
            self.cp.start(ids)
        super().start()

    def relay(self):
        for ids, on in zip(self.quarters, self.relays):
            self.cp.arrived(ids)
            self.cp.start(on)

    def forward(self):
        for k in range(3):
            self.cp.arrived(self.relays[k] + self.line[k : k + 1])
            self.cp.start(self.core[k + 1 : k + 2])


def segment_in_block(tail, pos):
    tail = tail.astype(f32)
    return (pos >= 16.0 * tail[0:1] + tail[1:2]).astype(i32) + (pos >= 16.0 * tail[2:3] + tail[3:4]).astype(i32)


def sub8(v):
    return v.reshape(8, 8, v.shape[-1])


def route_rows(rt_ref):
    return [jnp.broadcast_to(rt_ref[j : j + 1, :], (8, T)) for j in range(J)]


def visible(me, sb):
    key = lax.broadcasted_iota(i32, (T, SB), 1)
    tok = lax.broadcasted_iota(i32, (T, SB), 0)
    ok = key - tok <= (me - 2 * sb) * T
    return ok


def prepare_keys(kv_ref, b, kaug, vaug, vt):
    ln = lanes(T)
    bs = pl.ds(pl.multiple_of(b * T, T), T)
    kv = kv_ref[b, 0:T, :].astype(f32)
    seg = segment_in_block(kv_ref[b, T:KVR, :], lax.broadcasted_iota(i32, (T, 128), 0).astype(f32))
    feat = jnp.where((ln < H + 3) & (seg != ln - H), NEG, 0.0)
    feat = jnp.where((ln >= H + 3) & (ln < H + 6), 1.0, feat)
    kaug[bs, :] = jnp.where(ln < H, kv, feat).astype(bf16)
    one = jnp.where(ln < H + 3, 1.0, 0.0)
    vaug[bs, :] = jnp.where(ln < H, pltpu.roll(kv, H, 1), one).astype(bf16)
    ones = jnp.where(lax.broadcasted_iota(i32, (16, T), 0) == 0, 1.0, 0.0)
    vt[:, bs] = jnp.concatenate([jnp.transpose(kv)[H:], ones], axis=0).astype(bf16)


def project_queries(normed, wq_ref, qall):
    for c in range(4):
        w = wq_ref[2 * c : 2 * c + 2].reshape(2 * 3 * H, D)
        qall[c * 48 : (c + 1) * 48] = (nt(w, normed) * 0.125).reshape(48, 8, T)


def choose(routes, table, j):
    acc = table[0:8]
    for e in range(1, E):
        acc = jnp.where((routes[j] == e)[None], table[e * 8 : (e + 1) * 8], acc)
    return acc


def to_experts(routes, rows, out, experts=range(E)):
    for e in experts:
        acc = jnp.zeros((8, 8, T), f32)
        for j in range(J):
            acc = jnp.where((routes[j] == e)[None], rows[j], acc)
        out[e * H : (e + 1) * H, :] = acc.reshape(H, T).astype(bf16)


def pick_queries(rt_ref, table, qt):
    routes = route_rows(rt_ref)
    for j in range(J):
        qt[0:H, j * T : (j + 1) * T] = choose(routes, table, j).reshape(H, T).astype(bf16)


def mark_queries(kv_ref, me, qt):
    pos = lax.broadcasted_iota(i32, (H, T), 1).astype(f32)
    seg = segment_in_block(kv_ref[me, T:KVR, :][:, 0:1], pos)
    feat = jnp.where(lax.broadcasted_iota(i32, (H, T), 0) == seg, 1.0, 0.0).astype(bf16)
    for j in range(J):
        qt[H:, j * T : (j + 1) * T] = feat


def attend(me, qt, kaug, vt, att, macc, acc, others):
    last = me // 2
    macc[...] = jnp.full(macc.shape, NEG, f32)
    acc[...] = jnp.zeros(acc.shape, f32)

    def score(sb, g, masked):
        s = nn(kaug[pl.ds(pl.multiple_of(sb * SB, SB), SB), :], qt[:, g * SB : (g + 1) * SB])
        if masked:
            key = lax.broadcasted_iota(i32, (SB, T), 0)
            tok = lax.broadcasted_iota(i32, (SB, T), 1)
            ok = key - tok <= (me - 2 * sb) * T
            s = jnp.where(jnp.concatenate([ok, ok], axis=1), s, NEG)
        return s.reshape(SB // 8, 8, SB)

    def soften(s, g):
        gs = slice(g * SB, (g + 1) * SB)
        old = macc[:, gs]
        top = jnp.max(jnp.maximum(old, jnp.max(s, axis=0)), axis=0, keepdims=True)
        top = jnp.broadcast_to(top, (8, SB))
        macc[:, gs] = top
        return jnp.exp(s - top[None]).reshape(SB, SB).astype(bf16), jnp.exp(old - top)

    def weigh(sb, g, p, kept):
        gs = slice(g * SB, (g + 1) * SB)
        old = acc[:, gs].reshape(10, 8, SB) * kept[None]
        acc[:, gs] = old.reshape(80, SB) + nn(vt[:, pl.ds(pl.multiple_of(sb * SB, SB), SB)], p)

    def block(sb, masked):
        s = score(sb, 0, masked)
        held = None
        for g in range(J // 2):
            ahead = score(sb, g + 1, masked) if g + 1 < J // 2 else None
            new = soften(s, g)
            if g:
                weigh(sb, g - 1, *held)
            held, s = new, ahead
        weigh(sb, J // 2 - 1, *held)

    block(last, True)
    others()
    lax.fori_loop(0, last, lambda sb, c: (block(sb, False), c)[1], 0)
    for g in range(J // 2):
        gs = slice(g * SB, (g + 1) * SB)
        tot = acc[H : H + 1, gs]
        att[:, gs] = (acc[0:H, gs] / tot).astype(bf16)
        l1, l2, l3 = split3(-(macc[0:1, gs] + jnp.log(tot)))
        row = lax.broadcasted_iota(i32, (16, SB), 0)
        feat = qt[H : H + 16, gs].astype(f32)
        feat = jnp.where(row == 3, l1, jnp.where(row == 4, l2, jnp.where(row == 5, l3, feat)))
        qt[H : H + 16, gs] = feat.astype(bf16)


def gates_of(normed, rw_ref, rt_ref, gate_ref):
    logits = nt(rw_ref[...], normed)
    eid = lax.broadcasted_iota(i32, (E, T), 0)
    per = [jnp.sum(jnp.where(rt_ref[j : j + 1, :] == eid, logits, 0.0), axis=0, keepdims=True) for j in range(J)]
    v = jnp.concatenate(per, axis=0)
    e = jnp.exp(v - jnp.max(v, axis=0, keepdims=True))
    gate_ref[...] = e / jnp.sum(e, axis=0, keepdims=True)


SMALL = 640


def dma_sems(n):
    return [pltpu.SemaphoreType.DMA((n,)), pltpu.SemaphoreType.DMA((n,))]


def kernel_all(x_hbm, cot_hbm, gain_ref, fgain_ref, kvw_ref, rw_ref, rt_ref, seg_ref, wq_hbm, wo_hbm, up_hbm, down_hbm,
               out_ref, ing_ref, all_hbm, dwo_ref, dwq_ref, small_ref,
               x_ref, cot_ref, shared, all_sem, up_ref, down_ref, wsem, normed_ref, gate_ref, kv_ref, wq_ref, wo_ref, att_ref, qt_ref, table, kaug, vaug, vt, macc, acc,
               rows, gat, gm_ref, gn_ref, drw_ref, dfg_ref, big, r0, r1, r2, ex,
               dat_ref, qa, da, dqacc, tot, gsend, grecv, lbig, l0, l1, l2, lex, ssrc, shalf, s0, s1, sy, sz, send, recv, ksend, krecv):
    place = Place()
    me, core = place.ex, place.at["c"]
    dp = lax.axis_index("dp")
    copies = Copies(place, send, recv)
    gq, gk, go = WideGather(copies, wq_ref), Gather(copies, kv_ref), Gather(copies, wo_ref)
    big7 = big.reshape(2, UNITS, 4, 4, 4, 16, 128)
    lbig7 = lbig.reshape(2, 3, 4, 4, 4, 16, 128)
    early = [Scatter(copies, big7, (r0, r1, r2), ex, parts, groups, o) for parts, groups, o in EARLY]
    late = [Scatter(copies, lbig7, (l0, l1, l2), lex, [(u, u + 1)], [(u, u + 1)], o, cut=True) for u, o in enumerate(OWNER_ORDERS)]
    spreads = [Spread(copies, shared, all_hbm, all_sem, u0, u1, o) for u0, u1, o in SPREADS]
    owned_o = [SpreadOwner(copies, dwo_ref, u, plane_axes(o)[0]) for u, o in enumerate(OWNER_ORDERS)]
    owned_q = [SpreadOwner(copies, dwq_ref, u, plane_axes(o)[0]) for u, o in enumerate(OWNER_ORDERS)]
    small = SmallSum(copies, ssrc, shalf, s0, s1, sy, sz, small_ref)

    bar = pltpu.get_barrier_semaphore()
    for p in ALL_PEERS:
        pl.semaphore_signal(bar, inc=1, device_id=place.peers[p], device_id_type=MESH)
    for k in range(1, NB):
        pl.semaphore_signal(bar, inc=1, device_id=(dp, (me + k) % NB), device_id_type=MESH)
    load_x, load_wq, load_wo, *loads = [
        pltpu.make_async_copy(src, dst, wsem.at[i])
        for i, (src, dst) in enumerate(((x_hbm, x_ref), (wq_hbm, wq_ref.at[me]), (wo_hbm, wo_ref.at[me]), (cot_hbm, cot_ref),
                                        (up_hbm, up_ref), (down_hbm, down_ref)))]
    for cp in [load_x, load_wq, load_wo] + loads:
        cp.start()
    load_x.wait()

    x = x_ref[...].astype(f32)
    inv = lax.rsqrt(jnp.mean(x * x, axis=-1, keepdims=True) + eps)
    normed = (x * inv * gain_ref[...]).astype(bf16)
    normed_ref[...] = normed
    kv_ref[me, 0:T, :] = nn(normed, kvw_ref[...]).astype(bf16)
    seg = seg_ref[...]
    row = lax.broadcasted_iota(i32, (16, 128), 0)
    tail = jnp.zeros((16, 128), f32)
    for s in range(2):
        n = jnp.sum(jnp.sum((seg <= s).astype(f32), axis=0, keepdims=True), axis=1, keepdims=True)
        n = jnp.broadcast_to(n, (16, 128))
        hi = jnp.floor(n * 0.0625)
        tail = jnp.where(row == 2 * s, hi, jnp.where(row == 2 * s + 1, n - 16.0 * hi, tail))
    kv_ref[me, T:KVR, :] = tail.astype(bf16)
    load_wq.wait()
    pl.semaphore_wait(bar, len(ALL_PEERS) + NB - 1)
    gq.start()
    gk.start()
    gates_of(normed, rw_ref, rt_ref, gate_ref)
    gq.relay()
    gq.forward()
    gq.neighbour()
    gq.finish()
    project_queries(normed, wq_ref, table)
    pick_queries(rt_ref, table, qt_ref)
    mark_queries(kv_ref, me, qt_ref)
    gk.forward()
    load_wo.wait()
    go.start()
    gk.neighbour()
    for i in range(2):
        prepare_keys(kv_ref, 2 * (me // 2) + i, kaug, vaug, vt)

    def others():
        gk.finish()
        lax.fori_loop(0, NB, lambda b, c: (prepare_keys(kv_ref, b, kaug, vaug, vt), c)[1], 0)

    attend(me, qt_ref, kaug, vt, att_ref, macc, acc, others)

    go.forward()
    routes = route_rows(rt_ref)
    for j in range(J):
        rows[j] = sub8(att_ref[:, j * T : (j + 1) * T].astype(f32) * gate_ref[j : j + 1, :])
    to_experts(routes, rows, gat)
    go.neighbour()
    go.finish()
    x = x_ref[...].astype(f32)
    wo_all = wo_ref[...].reshape(EW, D)
    mixed = x + tn(gat[...], wo_all)
    inv = lax.rsqrt(jnp.mean(mixed * mixed, axis=-1, keepdims=True) + eps)
    n = mixed * inv
    fgain = fgain_ref[...]
    second = (n * fgain).astype(bf16)
    second_t = jnp.transpose(n * fgain).astype(bf16)
    for cp in loads:
        cp.wait()
    cot = cot_ref[...]
    C = 512
    out = mixed
    gsec = jnp.zeros((T, D), f32)
    ahead = nn(second, up_ref[:, 0:C]), nt(cot, down_ref[0:C, :])
    for c in range(FF // C):
        cs = slice(c * C, (c + 1) * C)
        v, gact = ahead
        if c + 1 < FF // C:
            ns = slice((c + 1) * C, (c + 2) * C)
            ahead = nn(second, up_ref[:, ns]), nt(cot, down_ref[ns, :])
        v2 = v * v
        th = jnp.tanh(0.7978845608028654 * (v + 0.044715 * v * v2))
        a = (0.5 * v * (1.0 + th)).astype(bf16)
        dth = 0.5 * (1.0 + th) + 0.5 * v * (1.0 - th * th) * (0.7978845608028654 * (1.0 + 0.134145 * v2))
        gh = (gact * dth).astype(bf16)
        out = out + nn(a, down_ref[cs, :])
        gsec = gsec + nt(gh, up_ref[:, cs])
        gdown = tn(a, cot).astype(bf16)
        gup = nn(second_t, gh).astype(bf16)
        for t in range(4):
            ts = slice(t * 128, (t + 1) * 128)
            big[(core + t // 2) % 2, DOWN_UNIT[c], t % 2 * 512 : t % 2 * 512 + 512, :] = gdown[:, ts]
            big[(core + t // 2) % 2, UP_UNIT[c], t % 2 * 512 : t % 2 * 512 + 512, :] = gup[:, ts]
        for b, i in CHUNK_PARTS[c]:
            early[b].start0(i)
    for i in (0, 1, 3):
        early[i].pass0(0)
    out_ref[...] = out.astype(bf16)
    dfg_ref[...] = jnp.sum(gsec * n, axis=0, keepdims=True)
    hh = gsec * fgain
    gm = cot.astype(f32) + inv * (hh - n * jnp.mean(hh * n, axis=-1, keepdims=True))
    gm_ref[...] = gm
    gml = gm.astype(bf16)
    for c in range(4):
        store_expert(big, core, WO_UNIT, 2 * c, nn(gat[c * 384 : (c + 1) * 384, :], gml))
    for b, i in WO_PARTS:
        early[b].start0(i)
    for c in range(4):
        w = wo_ref[2 * c : 2 * c + 2].reshape(2 * 3 * H, D)
        table[c * 48 : (c + 1) * 48] = nt(w, gml).reshape(48, 8, T)
    dots = []
    row = lax.broadcasted_iota(i32, (H, T), 0)
    for j in range(J):
        js = slice(j * T, (j + 1) * T)
        g = choose(routes, table, j).reshape(H, T)
        gate = gate_ref[j : j + 1, :]
        dot = jnp.sum(g * att_ref[:, js].astype(f32), axis=0, keepdims=True)
        dots.append(dot)
        d1, d2, d3 = split3(-(dot * gate))
        dat_ref[0:H, js] = (g * gate).astype(bf16)
        dat_ref[H:, js] = jnp.where(row == 0, d1, jnp.where(row == 1, d2, jnp.where(row == 2, d3, 0.0))).astype(bf16)
    dots = jnp.concatenate(dots, axis=0)
    gates = gate_ref[...]
    chosen = gates * (dots - jnp.sum(gates * dots, axis=0, keepdims=True))
    eid = lax.broadcasted_iota(i32, (E, T), 0)
    gl = jnp.zeros((E, T), f32)
    for j in range(J):
        gl = jnp.where(rt_ref[j : j + 1, :] == eid, chosen[j : j + 1, :], gl)
    hi = gl.astype(bf16)
    lo = (gl - hi.astype(f32)).astype(bf16)
    rw = rw_ref[...]
    gn_ref[...] = tn(hi, rw) + tn(lo, rw)
    nm = normed_ref[...]
    drw_ref[...] = nn(hi, nm) + nn(lo, nm)

    for j in range(J):
        js = slice(j * T, (j + 1) * T)
        qa[js, :] = jnp.transpose(qt_ref[:, js].astype(f32)).astype(bf16)
        da[js, :] = jnp.transpose(dat_ref[:, js].astype(f32)).astype(bf16)
    dqacc[...] = jnp.zeros(dqacc.shape, f32)
    for i, h in ((0, 1), (1, 1), (2, 0), (3, 1)):
        early[i].pass0(h)
    last = me // 2

    def block(sb, masked):
        ks = pl.ds(pl.multiple_of(sb * SB, SB), SB)
        kv = jnp.concatenate([kv_ref[2 * sb, 0:T, :], kv_ref[2 * sb + 1, 0:T, :]], axis=0)
        tot[...] = jnp.zeros(tot.shape, f32)
        for g in range(J // 2):
            gs = slice(g * SB, (g + 1) * SB)
            p = jnp.exp(nt(qa[gs, :], kaug[ks, :]))
            if masked:
                ok = visible(me, sb)
                p = jnp.where(jnp.concatenate([ok, ok], axis=0), p, 0.0)
            ds = (p * nt(da[gs, :], vaug[ks, :])).astype(bf16)
            dqacc[gs, :] += nn(ds, kv)
            tot[0:H, :] += nn(qt_ref[0:H, gs], ds)
            tot[H:, :] += nn(dat_ref[0:H, gs], p.astype(bf16))
        low = jnp.transpose(tot[...]).astype(bf16)
        gsend[2 * sb] = low[0:T]
        gsend[2 * sb + 1] = low[T:]

    def to_owner(kb):
        return pltpu.make_async_remote_copy(src_ref=gsend.at[kb], dst_ref=grecv.at[me], send_sem=ksend.at[kb],
                                            recv_sem=krecv.at[me], device_id=(dp, kb), device_id_type=MESH)

    def from_device(b):
        return pltpu.make_async_remote_copy(src_ref=gsend.at[b], dst_ref=grecv.at[b], send_sem=ksend.at[b],
                                            recv_sem=krecv.at[b], device_id=(dp, b), device_id_type=MESH)

    def at_1():
        for s in early:
            s.pass1()

    def at_2():
        for s in early:
            s.pass2()

    def step(sb, carry):
        @pl.when(sb < last)
        def _():
            block(sb, False)
            to_owner(2 * sb).start()
            to_owner(2 * sb + 1).start()

        pl.when(sb == 1)(at_1)
        pl.when(sb == 2)(at_2)
        return carry

    lax.fori_loop(0, NSB - 1, step, 0)
    block(last, True)

    @pl.when(2 * last < me)
    def _():
        to_owner(2 * last).start()

    for s in early:
        s.pass3()
    for s, e, (u0, u1, _) in zip(spreads, (early[0], early[1], early[3]), SPREADS):
        s.begin([e.result(SHARED[u]) for u in range(u0, u1)])
    for s, e, u in zip(owned_o, (early[0], early[2], early[3]), WO_UNIT):
        s.begin(e.result(u))
    for j in range(J):
        js = slice(j * T, (j + 1) * T)
        rows[j] = sub8(jnp.transpose(dqacc[js, :])[0:H].astype(bf16).astype(f32) * 0.125)
    for c in range(4):
        to_experts(routes, rows, gat, range(6 * c, 6 * c + 6))
        store_expert(lbig, core, [0, 1, 2], 2 * c, nn(gat[c * 384 : (c + 1) * 384, :], nm))
        for s in late:
            s.start0(c)
    for s in spreads:
        s.pass2()
        s.send(0)
    dqacc[0:T, :] = gsend[me].astype(f32)
    for b in range(1, NB):
        @pl.when(b > me)
        def _(b=b):
            from_device(b).wait_recv()
            dqacc[0:T, :] += grecv[b].astype(f32)
    gkv = dqacc[0:T, :].astype(bf16)
    dkvw = tn(nm, gkv).astype(bf16)
    done = set(copies.open)
    for s in late:
        s.pass0(0)
    for s in spreads:
        s.send(1)
    gn = gn_ref[...] + tn(gat[...], wq_ref[...].reshape(EW, D)) + nt(gkv, kvw_ref[...])
    x = x_ref[...].astype(f32)
    inv = lax.rsqrt(jnp.mean(x * x, axis=-1, keepdims=True) + eps)
    n = x * inv
    dgain = jnp.sum(gn * n, axis=0, keepdims=True)
    drw = drw_ref[...]
    dfg = dfg_ref[...]
    parts = [dkvw.astype(f32)] + [drw[:, t * 128 : (t + 1) * 128] for t in range(4)]
    parts += [v[:, t * 128 : (t + 1) * 128] for v in (dgain, dfg) for t in range(4)] + [jnp.zeros((SMALL - 616, 128), f32)]
    ssrc[...] = jnp.concatenate(parts, axis=0).astype(bf16).reshape(2, 4, SMALL // 8, 128)
    small.step(0)
    copies.drain(copies.open - done)
    small.step(1)
    for s in late:
        s.pass1()
    small.step(2)
    for s in spreads:
        s.send(2)
        s.forward(0)
    hh = gn * gain_ref[...]
    ing_ref[...] = (gm_ref[...] + inv * (hh - n * jnp.mean(hh * n, axis=-1, keepdims=True))).astype(bf16)
    for s in late:
        s.pass2()
    small.step(3)
    for s in spreads:
        s.finish(0)
        s.forward(1)
    for s, t, u in zip(owned_q, late, range(3)):
        t.pass3()
        s.begin(t.result(u))
    small.step(4)
    for s in spreads:
        s.finish(1)
        s.forward(2)
    copies.drain([i for s in owned_q for i in s.ids] + small.ids[4])
    for s in owned_o + owned_q:
        s.finish()
    small.step(5)
    for s in spreads:
        s.finish(2)
    small.step(6)
    for s in spreads:
        for u in range(s.u0, s.u1):
            s.keep(u).wait()
    for b in range(NB - 1):
        @pl.when(b < me)
        def _(b=b):
            to_owner(b).wait_send()
    copies.drain()


SCRATCH = [
    VM((T, D), bf16), VM((T, D), bf16),
    VM((8, 2, 4, 4, 4, 16, 128), bf16), pltpu.SemaphoreType.DMA((8,)),
    VM((D, FF), bf16), VM((FF, D), bf16), pltpu.SemaphoreType.DMA((6,)), VM((T, D), bf16), VM((J, T), f32), VM((NB, KVR, 128), bf16),
    VM((NB, 3 * H, D), bf16), VM((NB, 3 * H, D), bf16), VM((H, ROWS), bf16), VM((128, ROWS), bf16), VM((EW // 8, 8, T), f32),
    VM((ROWS, 128), bf16), VM((ROWS, 128), bf16), VM((80, ROWS), bf16), VM((8, ROWS), f32), VM((80, ROWS), f32),
    VM((J, 8, 8, T), f32), VM((EW, T), bf16), VM((T, D), f32), VM((T, D), f32), VM((E, D), f32), VM((1, D), f32),
    VM((2, UNITS, 1024, 128), bf16), VM((UNITS, 4, 4, 4, 16, 128), bf16), VM((UNITS, 3, 4, 4, 16, 128), bf16),
    VM((UNITS, 3, 4, 16, 128), bf16), VM((UNITS, 4, 4, 16, 128), bf16),
    VM((128, ROWS), bf16), VM((ROWS, 128), bf16), VM((ROWS, 128), bf16), VM((ROWS, 128), f32), VM((128, SB), f32),
    VM((NB, T, 128), bf16), VM((NB, T, 128), bf16),
    VM((2, 3, 1024, 128), bf16), VM((3, 4, 4, 4, 16, 128), bf16), VM((3, 3, 4, 4, 16, 128), bf16), VM((3, 3, 4, 16, 128), bf16),
    VM((3, 4, 4, 16, 128), bf16),
    VM((2, 4, SMALL // 8, 128), bf16), VM((4, SMALL // 8, 128), bf16), VM((4, SMALL // 8, 128), bf16),
    VM((3, SMALL // 8, 128), bf16), VM((4, SMALL // 8, 128), bf16), VM((4, SMALL // 8, 128), bf16),
] + dma_sems(234) + dma_sems(NB)


def kernel_f(all_hbm, wo_hbm, dwq_hbm, small_hbm, out_in, ing_in,
             dup_hbm, ddown_hbm, dwo_ref, dwqt_ref, dkvw_ref, drw_ref, dgain_ref, dfg_ref, out_hbm, ing_hbm,
             units, wo_ref, dwq_ref, small_ref, up, down, held, in_sem, out_sem):
    order = [SHARED.index(u) for pair in zip(UP_UNIT, DOWN_UNIT) for u in pair]
    loads = [pltpu.make_async_copy(all_hbm.at[u], units.at[u], in_sem.at[i]) for i, u in enumerate(order)]
    loads += [pltpu.make_async_copy(src, dst, in_sem.at[8 + i])
              for i, (src, dst) in enumerate(((wo_hbm, wo_ref), (dwq_hbm, dwq_ref), (small_hbm, small_ref),
                                              (out_in, held.at[0]), (ing_in, held.at[1])))]
    for cp in loads:
        cp.start()
    stores = []
    for c in range(4):
        cs = slice(c * 512, (c + 1) * 512)
        u, d = order[2 * c : 2 * c + 2]
        loads[2 * c].wait()
        for t in range(4):
            up[:, c * 512 + t * 128 : c * 512 + (t + 1) * 128] = units[u, t].astype(f32)
        stores.append(pltpu.make_async_copy(up.at[:, cs], dup_hbm.at[:, cs], out_sem.at[2 * c]))
        stores[-1].start()
        loads[2 * c + 1].wait()
        for t in range(4):
            down[cs, t * 128 : (t + 1) * 128] = units[d, t].astype(f32)
        stores.append(pltpu.make_async_copy(down.at[cs], ddown_hbm.at[cs], out_sem.at[2 * c + 1]))
        stores[-1].start()
    for cp in loads[8:]:
        cp.wait()
    for i, dst in enumerate((out_hbm, ing_hbm)):
        stores.append(pltpu.make_async_copy(held.at[i], dst, out_sem.at[8 + i]))
        stores[-1].start()
    for t in range(4):
        ts = slice(t * 128, (t + 1) * 128)
        dwo_ref[:, ts] = wo_ref[t * 192 : (t + 1) * 192, :].astype(f32)
        dwqt_ref[:, ts] = dwq_ref[t * 192 : (t + 1) * 192, :].astype(f32)
    small = small_ref[512:SMALL, :].astype(f32)
    dkvw_ref[...] = small_ref[0:512, :].astype(f32)
    for t in range(4):
        ts = slice(t * 128, (t + 1) * 128)
        drw_ref[:, ts] = small[t * E : (t + 1) * E]
        dgain_ref[:, ts] = small[96 + t : 97 + t]
        dfg_ref[:, ts] = small[100 + t : 101 + t]
    for cp in stores:
        cp.wait()


def per_device(inputs, cotangent, norm_gain, ffn_gain, kv_weight, router_weight, query_weight, output_weight, up_weight,
               down_weight, routes, segment_ids):
    wq = jnp.swapaxes(query_weight, 1, 2).reshape(3 * H, D)
    wo = output_weight.reshape(3 * H, D)
    vmem, anywhere = pl.BlockSpec(memory_space=VM), pl.BlockSpec(memory_space=pl.ANY)
    S = jax.ShapeDtypeStruct
    out, ing, shared, dwo, dwq, small = pl.pallas_call(
        kernel_all,
        out_shape=[S((T, D), bf16), S((T, D), bf16), S((8, 2, 4, 4, 4, 16, 128), bf16), S((3, 4, 4, 16, 128), bf16),
                   S((3, 4, 4, 16, 128), bf16), S((2, 4, SMALL // 8, 128), bf16)],
        in_specs=[anywhere] * 2 + [vmem] * 6 + [anywhere] * 4,
        out_specs=[vmem, vmem, anywhere, vmem, vmem, vmem],
        scratch_shapes=SCRATCH,
        compiler_params=pltpu.CompilerParams(vmem_limit_bytes=62 << 20, collective_id=1, has_side_effects=True),
        cost_estimate=pl.CostEstimate(flops=1 << 35, bytes_accessed=1 << 24, transcendentals=0),
    )(inputs, cotangent, norm_gain.reshape(1, D), ffn_gain.reshape(1, D), kv_weight, router_weight.T, routes.T,
      segment_ids.reshape(3, 128), wq, wo, up_weight, down_weight)
    dup, ddown, dwo, dwqt, dkvw, drw, dgain, dfg, out, ing = pl.pallas_call(
        kernel_f,
        out_shape=[S((D, FF), f32), S((FF, D), f32), S((3 * H, D), f32), S((3 * H, D), f32), S((D, 128), f32), S((E, D), f32),
                   S((1, D), f32), S((1, D), f32), S((T, D), bf16), S((T, D), bf16)],
        in_specs=[anywhere] * 6,
        out_specs=[anywhere] * 2 + [vmem] * 6 + [anywhere] * 2,
        scratch_shapes=[VM((8, 4, 512, 128), bf16), VM((768, 128), bf16), VM((768, 128), bf16), VM((SMALL, 128), bf16),
                        VM((D, FF), f32), VM((FF, D), f32), VM((2, T, D), bf16), pltpu.SemaphoreType.DMA((13,)),
                        pltpu.SemaphoreType.DMA((10,))],
        compiler_params=pltpu.CompilerParams(vmem_limit_bytes=62 << 20),
    )(shared.reshape(8, 4, 512, 128), dwo.reshape(768, 128), dwq.reshape(768, 128), small.reshape(SMALL, 128), out, ing)
    return (out, ing, dgain.reshape(D), dfg.reshape(D), dkvw, drw.T,
            jnp.swapaxes(dwqt.reshape(3, H, D), 1, 2), dwo.reshape(3, H, D), dup, ddown)


def solution(mesh):
    both = P(("dp", "expert"), None)
    ex = P("expert", None, None)
    return jax.shard_map(
        per_device, mesh=mesh,
        in_specs=(both, both, P(), P(), P(), P(), ex, ex, P(), P(), both, P(("dp", "expert"))),
        out_specs=(both, both, P(), P(), P(), P(), ex, ex, P(), P()),
        check_vma=False)
```

```python
import functools
import jax
import jax.numpy as jnp
from jax import lax
from jax.experimental import pallas as pl
from jax.experimental.pallas import tpu as pltpu
from jax.sharding import PartitionSpec as P

f32, bf16, i32 = jnp.float32, jnp.bfloat16, jnp.int32
T, D, H, J, E, FF, NB = 384, 512, 64, 8, 24, 2048, 8
EW = E * H
ROWS = J * T
SB = 2 * T
NSB = NB // 2
eps = 1e-06
NEG = -1e30
VM = pltpu.VMEM


def nn(a, b):
    return lax.dot_general(a, b, (((1,), (0,)), ((), ())), preferred_element_type=f32)


def nt(a, b):
    return lax.dot_general(a, b, (((1,), (1,)), ((), ())), preferred_element_type=f32)


def tn(a, b):
    return lax.dot_general(a, b, (((0,), (0,)), ((), ())), preferred_element_type=f32)


def lanes(rows):
    return lax.broadcasted_iota(i32, (rows, 128), 1)


def split3(v):
    a = v.astype(bf16).astype(f32)
    b = (v - a).astype(bf16).astype(f32)
    c = (v - a - b).astype(bf16).astype(f32)
    return a, b, c


MESH = pl.DeviceIdType.MESH
LINES = [(a, k) for a in "xyz" for k in (1, 2, 3)]
ALL_PEERS = [("c", 0)] + LINES


class Place:
    def __init__(self):
        dp, ex = lax.axis_index("dp"), lax.axis_index("expert")
        self.ex = ex
        self.at = {"x": dp // 4, "y": dp % 4, "z": ex // 2, "c": ex % 2}
        self.peers = {("c", 0): self.device(c=1 - self.at["c"])}
        for axis, k in LINES:
            self.peers[axis, k] = self.device(**{axis: (self.at[axis] + k) % 4})

    def device(self, **moved):
        at = {**self.at, **moved}
        return (at["x"] * 4 + at["y"], at["z"] * 2 + at["c"])


class Copies:
    def __init__(self, place, send, recv):
        self.place, self.send, self.recv, self.made, self.open = place, send, recv, [], set()

    def add(self, src, dst, peer):
        self.made.append((src, dst, peer))
        return len(self.made) - 1

    def get(self, i):
        src, dst, peer = self.made[i]
        return pltpu.make_async_remote_copy(src_ref=src(), dst_ref=dst(), send_sem=self.send.at[i], recv_sem=self.recv.at[i],
                                            device_id=self.place.peers[peer], device_id_type=MESH)

    def start(self, ids):
        self.open |= set(ids)
        for i in ids:
            self.get(i).start()

    def arrived(self, ids):
        for i in ids:
            self.get(i).wait_recv()

    def drain(self, keep=()):
        for i in sorted(self.open - set(keep)):
            self.get(i).wait_send()
        self.open &= set(keep)


class Scatter:
    def __init__(self, copies, big, r, ex, parts, groups, order, cut=False):
        self.cp, self.big, self.r, self.ex = copies, big, r, ex
        self.parts, self.groups, self.u0, self.u1 = parts, groups, parts[0][0], parts[-1][1]
        at = copies.place.at
        self.m = m = [at[a] for a in order]
        rng = lambda g: pl.ds(g[0], g[1] - g[0])
        us = rng((self.u0, self.u1))
        if cut:
            self.parts = parts * 4
            z = order.index("z")
            at_z = lambda q: (parts[0][0],) + (slice(None),) * z + (q,)
            self.part_ids = [copies.add(lambda q=q: big.at[(1,) + at_z(q)], lambda q=q: r[0].at[at_z(q)], ("c", 0)) for q in range(4)]
        else:
            self.part_ids = [copies.add(lambda g=g: big.at[1, rng(g)], lambda g=g: r[0].at[rng(g)], ("c", 0)) for g in parts]
        self.group_ids = [
            [copies.add(lambda g=g, k=k: big.at[0, rng(g), (m[0] + k) % 4], lambda g=g, k=k: r[1].at[rng(g), k - 1], (order[0], k))
             for k in (1, 2, 3)] for g in groups]
        self.ids2 = [copies.add(lambda k=k: big.at[0, us, m[0], (m[1] + k) % 4], lambda k=k: r[2].at[us, k - 1], (order[1], k))
                     for k in (1, 2, 3)]
        own = lambda: ex.at[us, m[2]]
        self.ids3 = [copies.add(own, own, (order[2], k)) for k in (1, 2, 3)]

    def start0(self, i):
        self.cp.start([self.part_ids[i]])

    def pass0(self, h):
        g = self.groups[h]
        self.cp.arrived([i for i, p in zip(self.part_ids, self.parts) if g[0] <= p[0] < g[1]])
        for u in range(*g):
            for a in range(4):
                v = self.big[0, u, a].astype(f32) + self.r[0][u, a].astype(f32)
                self.big[0, u, a] = v.astype(bf16)
        self.cp.start(self.group_ids[h])

    def add3(self, u, at, r):
        v = self.big[at].astype(f32)
        for k in range(3):
            v = v + r[u, k].astype(f32)
        return v.astype(bf16)

    def pass1(self):
        for h, g in enumerate(self.groups):
            self.cp.arrived(self.group_ids[h])
            for u in range(*g):
                at = (0, u, self.m[0])
                self.big[at] = self.add3(u, at, self.r[1])
        self.cp.start(self.ids2)

    def pass2(self):
        self.cp.arrived(self.ids2)
        for u in range(self.u0, self.u1):
            self.ex[u, self.m[2]] = self.add3(u, (0, u, self.m[0], self.m[1]), self.r[2])
        self.cp.start(self.ids3)

    def pass3(self):
        self.cp.arrived(self.ids3)

    def result(self, u):
        e = [self.ex[u, i].astype(f32) for i in range(4)]
        return (e[0] + e[1] + e[2] + e[3]).astype(bf16)


class Spread:
    def __init__(self, copies, out, kept, kept_sem, u0, u1, order):
        self.cp, self.out, self.kept, self.kept_sem, self.u0, self.u1 = copies, out, kept, kept_sem, u0, u1
        at = copies.place.at
        self.c, self.m = at["c"], [at[a] for a in order]
        us = pl.ds(u0, u1 - u0)
        quarter = lambda: out.at[us, self.c, self.m[0], self.m[1]]
        self.ids2 = [copies.add(quarter, quarter, (order[1], k)) for k in (1, 2, 3)]
        self.ids1, self.ids0 = [], []
        for u in range(u0, u1):
            piece = lambda k=0, u=u: out.at[u, self.c, (self.m[0] - k + 4) % 4]
            self.ids1.append([copies.add(piece, piece, (order[0], k)) for k in (1, 2, 3)])
            self.ids0.append([copies.add(functools.partial(piece, k), functools.partial(piece, k), ("c", 0)) for k in range(4)])

    def begin(self, values):
        for u, v in zip(range(self.u0, self.u1), values):
            self.out[u, self.c, self.m[0], self.m[1]] = v
        self.cp.start(self.ids2)

    def pass2(self):
        self.cp.arrived(self.ids2)

    def send(self, i):
        if i < len(self.ids1):
            self.cp.start(self.ids1[i] + self.ids0[i][:1])

    def forward(self, i):
        if i < len(self.ids1):
            for k in (1, 2, 3):
                self.cp.arrived(self.ids1[i][k - 1 : k])
                self.cp.start(self.ids0[i][k : k + 1])

    def finish(self, i):
        if i < len(self.ids0):
            self.cp.arrived(self.ids0[i])
            self.keep(self.u0 + i).start()

    def keep(self, u):
        return pltpu.make_async_copy(self.out.at[u], self.kept.at[u], self.kept_sem.at[u])


class SpreadOwner:
    def __init__(self, copies, out, u, axis):
        self.cp, self.out, self.u, self.p = copies, out, u, copies.place.at[axis]
        ref = lambda: out.at[u, self.p]
        self.ids = [copies.add(ref, ref, (axis, k)) for k in (1, 2, 3)]

    def begin(self, value):
        self.out[self.u, self.p] = value
        self.cp.start(self.ids)

    def finish(self):
        self.cp.arrived(self.ids)


class SmallSum:
    def __init__(self, copies, src, half, r0, r1, by, bz, out):
        self.cp, self.src, self.half, self.r0, self.r1, self.by, self.bz, self.out = copies, src, half, r0, r1, by, bz, out
        at = copies.place.at
        self.c, self.x, self.y, self.z = at["c"], at["x"], at["y"], at["z"]
        own_half = lambda: out.at[self.c]
        own = lambda: out.at[self.c, self.x]
        self.ids = [
            [copies.add(lambda: src.at[1 - self.c], lambda: r0, ("c", 0))],
            [copies.add(lambda k=k: half.at[(self.x + k) % 4], lambda k=k: r1.at[k - 1], ("x", k)) for k in (1, 2, 3)],
            [copies.add(lambda: by.at[self.y], lambda: by.at[self.y], ("y", k)) for k in (1, 2, 3)],
            [copies.add(lambda: bz.at[self.z], lambda: bz.at[self.z], ("z", k)) for k in (1, 2, 3)],
            [copies.add(own, own, ("x", k)) for k in (1, 2, 3)],
            [copies.add(own_half, own_half, ("c", 0))],
        ]

    def step(self, i):
        if i:
            self.cp.arrived(self.ids[i - 1])
        if i == 1:
            for a in range(4):
                self.half[a] = (self.src[self.c, a].astype(f32) + self.r0[a].astype(f32)).astype(bf16)
        if i == 2:
            v = self.half[self.x].astype(f32)
            for k in range(3):
                v = v + self.r1[k].astype(f32)
            self.by[self.y] = v.astype(bf16)
        if i in (3, 4):
            b = self.by if i == 3 else self.bz
            v = (b[0].astype(f32) + b[1].astype(f32) + b[2].astype(f32) + b[3].astype(f32)).astype(bf16)
            if i == 3:
                self.bz[self.z] = v
            else:
                self.out[self.c, self.x] = v
        if i < 6:
            self.cp.start(self.ids[i])


UNITS = 11
UP_UNIT, DOWN_UNIT, WO_UNIT = [0, 4, 8, 2], [1, 5, 9, 6], [3, 7, 10]
SHARED = sorted(UP_UNIT + DOWN_UNIT)
OWNER_ORDERS = ["zxy", "xzy", "yzx"]
EARLY = [([(0, 2), (2, 3), (3, 4)], [(0, 2), (2, 4)], "zxy"), ([(4, 6), (6, 7)], [(4, 6), (6, 7)], "xyz"),
         ([(7, 8)], [(7, 8)], "xzy"), ([(8, 10), (10, 11)], [(8, 10), (10, 11)], "yzx")]
CHUNK_PARTS, WO_PARTS = [[(0, 0)], [(1, 0)], [(3, 0)], [(0, 1), (1, 1)]], [(0, 2), (2, 0), (3, 1)]
SPREADS = [(0, 3, "zxy"), (3, 6, "xyz"), (6, 8, "yzx")]


def plane_axes(order):
    return [a for a in order if a != "z"]


def expert_row(ex, piece, order):
    p, q = plane_axes(order)
    at = {p: piece // 4, q: piece % 4, "z": ex // 2}
    r = ex % 2
    for a in order:
        r = r * 4 + at[a]
    return r * 16


def store_expert(big, core, units, ex0, value):
    low = value.astype(bf16)
    for o in range(2):
        slot = (core + (ex0 + o) % 2) % 2
        for row in range(0, 768, 16):
            v, piece = row // 256, (row % 256) // 16
            ct, r = row // 192, row % 192
            base = expert_row(ex0 + o, piece, OWNER_ORDERS[v]) % 1024
            big[slot, units[v], base : base + 16, :] = low[o * 192 + r : o * 192 + r + 16, ct * 128 : (ct + 1) * 128]


KVR = T + 16


class Gather:
    def __init__(self, copies, out):
        self.cp, self.out = copies, out
        at, ex = copies.place.at, copies.place.ex
        own = lambda: out.at[ex]
        from_z = lambda k: out.at[((at["z"] - k + 4) % 4) * 2 + at["c"]]
        self.line = [copies.add(own, own, ("z", k)) for k in (1, 2, 3)]
        self.core = [copies.add(functools.partial(from_z, k), functools.partial(from_z, k), ("c", 0)) for k in (0, 1, 2, 3)]

    def start(self):
        self.cp.start(self.line)
        self.cp.start(self.core[:1])

    def forward(self):
        for k in range(3):
            self.cp.arrived(self.line[k : k + 1])
            self.cp.start(self.core[k + 1 : k + 2])

    def neighbour(self):
        self.cp.arrived(self.core[:1])

    def finish(self):
        self.cp.arrived(self.core[1:])


class WideGather(Gather):
    def __init__(self, copies, out):
        self.cp, self.out = copies, out
        at, ex = copies.place.at, copies.place.ex
        wide, rows = D // 2, 3 * H // 4
        block = lambda k: ((at["z"] - k + 4) % 4) * 2 + at["c"]

        def quarter(axis, b):
            column = wide + 128 * "xy".index(axis)
            return out.at[b, pl.ds(pl.multiple_of(at[axis] * rows, 16), rows), column : column + 128]

        def both(make, peer):
            return copies.add(make, make, peer)

        self.quarters = [[both(functools.partial(quarter, a, ex), ("z", k)) for a in "xy"] for k in (1, 2, 3)]
        self.line = [both(lambda: out.at[ex, :, 0:wide], ("z", k)) for k in (1, 2, 3)]
        self.relays = [[both(lambda a=a, k=k: quarter(a, block(k)), (a, d)) for a in "xy" for d in (1, 2, 3)] for k in (1, 2, 3)]
        self.core = [both(lambda k=k: out.at[block(k)], ("c", 0)) for k in range(4)]

    def start(self):
        for ids in self.quarters:
            self.cp.start(ids)
        super().start()

    def relay(self):
        for ids, on in zip(self.quarters, self.relays):
            self.cp.arrived(ids)
            self.cp.start(on)

    def forward(self):
        for k in range(3):
            self.cp.arrived(self.relays[k] + self.line[k : k + 1])
            self.cp.start(self.core[k + 1 : k + 2])


def segment_in_block(tail, pos):
    tail = tail.astype(f32)
    return (pos >= 16.0 * tail[0:1] + tail[1:2]).astype(i32) + (pos >= 16.0 * tail[2:3] + tail[3:4]).astype(i32)


def sub8(v):
    return v.reshape(8, 8, v.shape[-1])


def route_rows(rt_ref):
    return [jnp.broadcast_to(rt_ref[j : j + 1, :], (8, T)) for j in range(J)]


def visible(me, sb):
    key = lax.broadcasted_iota(i32, (T, SB), 1)
    tok = lax.broadcasted_iota(i32, (T, SB), 0)
    ok = key - tok <= (me - 2 * sb) * T
    return ok


def prepare_keys(kv_ref, b, kaug, vaug, vt):
    ln = lanes(T)
    bs = pl.ds(pl.multiple_of(b * T, T), T)
    kv = kv_ref[b, 0:T, :].astype(f32)
    seg = segment_in_block(kv_ref[b, T:KVR, :], lax.broadcasted_iota(i32, (T, 128), 0).astype(f32))
    feat = jnp.where((ln < H + 3) & (seg != ln - H), NEG, 0.0)
    feat = jnp.where((ln >= H + 3) & (ln < H + 6), 1.0, feat)
    kaug[bs, :] = jnp.where(ln < H, kv, feat).astype(bf16)
    one = jnp.where(ln < H + 3, 1.0, 0.0)
    vaug[bs, :] = jnp.where(ln < H, pltpu.roll(kv, H, 1), one).astype(bf16)
    ones = jnp.where(lax.broadcasted_iota(i32, (16, T), 0) == 0, 1.0, 0.0)
    vt[:, bs] = jnp.concatenate([jnp.transpose(kv)[H:], ones], axis=0).astype(bf16)


def project_queries(normed, wq_ref, qall):
    for c in range(4):
        w = wq_ref[2 * c : 2 * c + 2].reshape(2 * 3 * H, D)
        qall[c * 48 : (c + 1) * 48] = (nt(w, normed) * 0.125).reshape(48, 8, T)


def choose(routes, table, j):
    acc = table[0:8]
    for e in range(1, E):
        acc = jnp.where((routes[j] == e)[None], table[e * 8 : (e + 1) * 8], acc)
    return acc


def to_experts(routes, rows, out, experts=range(E)):
    for e in experts:
        acc = jnp.zeros((8, 8, T), f32)
        for j in range(J):
            acc = jnp.where((routes[j] == e)[None], rows[j], acc)
        out[e * H : (e + 1) * H, :] = acc.reshape(H, T).astype(bf16)


def pick_queries(rt_ref, table, qt):
    routes = route_rows(rt_ref)
    for j in range(J):
        qt[0:H, j * T : (j + 1) * T] = choose(routes, table, j).reshape(H, T).astype(bf16)


def mark_queries(kv_ref, me, qt):
    pos = lax.broadcasted_iota(i32, (H, T), 1).astype(f32)
    seg = segment_in_block(kv_ref[me, T:KVR, :][:, 0:1], pos)
    feat = jnp.where(lax.broadcasted_iota(i32, (H, T), 0) == seg, 1.0, 0.0).astype(bf16)
    for j in range(J):
        qt[H:, j * T : (j + 1) * T] = feat


def attend(me, qt, kaug, vt, att, macc, acc, others):
    last = me // 2
    macc[...] = jnp.full(macc.shape, NEG, f32)
    acc[...] = jnp.zeros(acc.shape, f32)

    def score(sb, g, masked):
        s = nn(kaug[pl.ds(pl.multiple_of(sb * SB, SB), SB), :], qt[:, g * SB : (g + 1) * SB])
        if masked:
            key = lax.broadcasted_iota(i32, (SB, T), 0)
            tok = lax.broadcasted_iota(i32, (SB, T), 1)
            ok = key - tok <= (me - 2 * sb) * T
            s = jnp.where(jnp.concatenate([ok, ok], axis=1), s, NEG)
        return s.reshape(SB // 8, 8, SB)

    def soften(s, g):
        gs = slice(g * SB, (g + 1) * SB)
        old = macc[:, gs]
        top = jnp.max(jnp.maximum(old, jnp.max(s, axis=0)), axis=0, keepdims=True)
        top = jnp.broadcast_to(top, (8, SB))
        macc[:, gs] = top
        return jnp.exp(s - top[None]).reshape(SB, SB).astype(bf16), jnp.exp(old - top)

    def weigh(sb, g, p, kept):
        gs = slice(g * SB, (g + 1) * SB)
        old = acc[:, gs].reshape(10, 8, SB) * kept[None]
        acc[:, gs] = old.reshape(80, SB) + nn(vt[:, pl.ds(pl.multiple_of(sb * SB, SB), SB)], p)

    def block(sb, masked):
        s = score(sb, 0, masked)
        held = None
        for g in range(J // 2):
            ahead = score(sb, g + 1, masked) if g + 1 < J // 2 else None
            new = soften(s, g)
            if g:
                weigh(sb, g - 1, *held)
            held, s = new, ahead
        weigh(sb, J // 2 - 1, *held)

    block(last, True)
    others()
    lax.fori_loop(0, last, lambda sb, c: (block(sb, False), c)[1], 0)
    for g in range(J // 2):
        gs = slice(g * SB, (g + 1) * SB)
        tot = acc[H : H + 1, gs]
        att[:, gs] = (acc[0:H, gs] / tot).astype(bf16)
        l1, l2, l3 = split3(-(macc[0:1, gs] + jnp.log(tot)))
        row = lax.broadcasted_iota(i32, (16, SB), 0)
        feat = qt[H : H + 16, gs].astype(f32)
        feat = jnp.where(row == 3, l1, jnp.where(row == 4, l2, jnp.where(row == 5, l3, feat)))
        qt[H : H + 16, gs] = feat.astype(bf16)


def gates_of(normed, rw_ref, rt_ref, gate_ref):
    logits = nt(rw_ref[...], normed)
    eid = lax.broadcasted_iota(i32, (E, T), 0)
    per = [jnp.sum(jnp.where(rt_ref[j : j + 1, :] == eid, logits, 0.0), axis=0, keepdims=True) for j in range(J)]
    v = jnp.concatenate(per, axis=0)
    e = jnp.exp(v - jnp.max(v, axis=0, keepdims=True))
    gate_ref[...] = e / jnp.sum(e, axis=0, keepdims=True)


SMALL = 640


def dma_sems(n):
    return [pltpu.SemaphoreType.DMA((n,)), pltpu.SemaphoreType.DMA((n,))]


def kernel_all(x_hbm, cot_hbm, gain_ref, fgain_ref, kvw_ref, rw_ref, rt_ref, seg_ref, wq_hbm, wo_hbm, up_hbm, down_hbm,
               out_ref, ing_ref, all_hbm, dwo_ref, dwq_ref, small_ref,
               x_ref, cot_ref, shared, all_sem, up_ref, down_ref, wsem, normed_ref, gate_ref, kv_ref, wq_ref, wo_ref, att_ref, qt_ref, table, kaug, vaug, vt, macc, acc,
               rows, gat, gm_ref, gn_ref, drw_ref, dfg_ref, big, r0, r1, r2, ex,
               dat_ref, qa, da, dqacc, tot, gsend, grecv, lbig, l0, l1, l2, lex, ssrc, shalf, s0, s1, sy, sz, send, recv, ksend, krecv):
    place = Place()
    me, core = place.ex, place.at["c"]
    dp = lax.axis_index("dp")
    copies = Copies(place, send, recv)
    gq, gk, go = WideGather(copies, wq_ref), Gather(copies, kv_ref), Gather(copies, wo_ref)
    big7 = big.reshape(2, UNITS, 4, 4, 4, 16, 128)
    lbig7 = lbig.reshape(2, 3, 4, 4, 4, 16, 128)
    early = [Scatter(copies, big7, (r0, r1, r2), ex, parts, groups, o) for parts, groups, o in EARLY]
    late = [Scatter(copies, lbig7, (l0, l1, l2), lex, [(u, u + 1)], [(u, u + 1)], o, cut=True) for u, o in enumerate(OWNER_ORDERS)]
    spreads = [Spread(copies, shared, all_hbm, all_sem, u0, u1, o) for u0, u1, o in SPREADS]
    owned_o = [SpreadOwner(copies, dwo_ref, u, plane_axes(o)[0]) for u, o in enumerate(OWNER_ORDERS)]
    owned_q = [SpreadOwner(copies, dwq_ref, u, plane_axes(o)[0]) for u, o in enumerate(OWNER_ORDERS)]
    small = SmallSum(copies, ssrc, shalf, s0, s1, sy, sz, small_ref)

    bar = pltpu.get_barrier_semaphore()
    for p in ALL_PEERS:
        pl.semaphore_signal(bar, inc=1, device_id=place.peers[p], device_id_type=MESH)
    for k in range(1, NB):
        pl.semaphore_signal(bar, inc=1, device_id=(dp, (me + k) % NB), device_id_type=MESH)
    load_x, load_wq, load_wo, *loads = [
        pltpu.make_async_copy(src, dst, wsem.at[i])
        for i, (src, dst) in enumerate(((x_hbm, x_ref), (wq_hbm, wq_ref.at[me]), (wo_hbm, wo_ref.at[me]), (cot_hbm, cot_ref),
                                        (up_hbm, up_ref), (down_hbm, down_ref)))]
    for cp in [load_x, load_wq, load_wo] + loads:
        cp.start()
    load_x.wait()

    x = x_ref[...].astype(f32)
    inv = lax.rsqrt(jnp.mean(x * x, axis=-1, keepdims=True) + eps)
    normed = (x * inv * gain_ref[...]).astype(bf16)
    normed_ref[...] = normed
    kv_ref[me, 0:T, :] = nn(normed, kvw_ref[...]).astype(bf16)
    seg = seg_ref[...]
    row = lax.broadcasted_iota(i32, (16, 128), 0)
    tail = jnp.zeros((16, 128), f32)
    for s in range(2):
        n = jnp.sum(jnp.sum((seg <= s).astype(f32), axis=0, keepdims=True), axis=1, keepdims=True)
        n = jnp.broadcast_to(n, (16, 128))
        hi = jnp.floor(n * 0.0625)
        tail = jnp.where(row == 2 * s, hi, jnp.where(row == 2 * s + 1, n - 16.0 * hi, tail))
    kv_ref[me, T:KVR, :] = tail.astype(bf16)
    load_wq.wait()
    pl.semaphore_wait(bar, len(ALL_PEERS) + NB - 1)
    gq.start()
    gk.start()
    gates_of(normed, rw_ref, rt_ref, gate_ref)
    gq.relay()
    gq.forward()
    gq.neighbour()
    gq.finish()
    project_queries(normed, wq_ref, table)
    pick_queries(rt_ref, table, qt_ref)
    mark_queries(kv_ref, me, qt_ref)
    gk.forward()
    load_wo.wait()
    go.start()
    gk.neighbour()
    for i in range(2):
        prepare_keys(kv_ref, 2 * (me // 2) + i, kaug, vaug, vt)

    def others():
        gk.finish()
        lax.fori_loop(0, NB, lambda b, c: (prepare_keys(kv_ref, b, kaug, vaug, vt), c)[1], 0)

    attend(me, qt_ref, kaug, vt, att_ref, macc, acc, others)

    go.forward()
    routes = route_rows(rt_ref)
    for j in range(J):
        rows[j] = sub8(att_ref[:, j * T : (j + 1) * T].astype(f32) * gate_ref[j : j + 1, :])
    to_experts(routes, rows, gat)
    go.neighbour()
    go.finish()
    x = x_ref[...].astype(f32)
    wo_all = wo_ref[...].reshape(EW, D)
    mixed = x + tn(gat[...], wo_all)
    inv = lax.rsqrt(jnp.mean(mixed * mixed, axis=-1, keepdims=True) + eps)
    n = mixed * inv
    fgain = fgain_ref[...]
    second = (n * fgain).astype(bf16)
    second_t = jnp.transpose(n * fgain).astype(bf16)
    for cp in loads:
        cp.wait()
    cot = cot_ref[...]
    C = 512
    out = mixed
    gsec = jnp.zeros((T, D), f32)
    ahead = nn(second, up_ref[:, 0:C]), nt(cot, down_ref[0:C, :])
    for c in range(FF // C):
        cs = slice(c * C, (c + 1) * C)
        v, gact = ahead
        if c + 1 < FF // C:
            ns = slice((c + 1) * C, (c + 2) * C)
            ahead = nn(second, up_ref[:, ns]), nt(cot, down_ref[ns, :])
        v2 = v * v
        th = jnp.tanh(0.7978845608028654 * (v + 0.044715 * v * v2))
        a = (0.5 * v * (1.0 + th)).astype(bf16)
        dth = 0.5 * (1.0 + th) + 0.5 * v * (1.0 - th * th) * (0.7978845608028654 * (1.0 + 0.134145 * v2))
        gh = (gact * dth).astype(bf16)
        out = out + nn(a, down_ref[cs, :])
        gsec = gsec + nt(gh, up_ref[:, cs])
        gdown = tn(a, cot).astype(bf16)
        gup = nn(second_t, gh).astype(bf16)
        for t in range(4):
            ts = slice(t * 128, (t + 1) * 128)
            big[(core + t // 2) % 2, DOWN_UNIT[c], t % 2 * 512 : t % 2 * 512 + 512, :] = gdown[:, ts]
            big[(core + t // 2) % 2, UP_UNIT[c], t % 2 * 512 : t % 2 * 512 + 512, :] = gup[:, ts]
        for b, i in CHUNK_PARTS[c]:
            early[b].start0(i)
    for i in (0, 1, 3):
        early[i].pass0(0)
    out_ref[...] = out.astype(bf16)
    dfg_ref[...] = jnp.sum(gsec * n, axis=0, keepdims=True)
    hh = gsec * fgain
    gm = cot.astype(f32) + inv * (hh - n * jnp.mean(hh * n, axis=-1, keepdims=True))
    gm_ref[...] = gm
    gml = gm.astype(bf16)
    for c in range(4):
        store_expert(big, core, WO_UNIT, 2 * c, nn(gat[c * 384 : (c + 1) * 384, :], gml))
    for b, i in WO_PARTS:
        early[b].start0(i)
    for c in range(4):
        w = wo_ref[2 * c : 2 * c + 2].reshape(2 * 3 * H, D)
        table[c * 48 : (c + 1) * 48] = nt(w, gml).reshape(48, 8, T)
    dots = []
    row = lax.broadcasted_iota(i32, (H, T), 0)
    for j in range(J):
        js = slice(j * T, (j + 1) * T)
        g = choose(routes, table, j).reshape(H, T)
        gate = gate_ref[j : j + 1, :]
        dot = jnp.sum(g * att_ref[:, js].astype(f32), axis=0, keepdims=True)
        dots.append(dot)
        d1, d2, d3 = split3(-(dot * gate))
        dat_ref[0:H, js] = (g * gate).astype(bf16)
        dat_ref[H:, js] = jnp.where(row == 0, d1, jnp.where(row == 1, d2, jnp.where(row == 2, d3, 0.0))).astype(bf16)
    dots = jnp.concatenate(dots, axis=0)
    gates = gate_ref[...]
    chosen = gates * (dots - jnp.sum(gates * dots, axis=0, keepdims=True))
    eid = lax.broadcasted_iota(i32, (E, T), 0)
    gl = jnp.zeros((E, T), f32)
    for j in range(J):
        gl = jnp.where(rt_ref[j : j + 1, :] == eid, chosen[j : j + 1, :], gl)
    hi = gl.astype(bf16)
    lo = (gl - hi.astype(f32)).astype(bf16)
    rw = rw_ref[...]
    gn_ref[...] = tn(hi, rw) + tn(lo, rw)
    nm = normed_ref[...]
    drw_ref[...] = nn(hi, nm) + nn(lo, nm)

    for j in range(J):
        js = slice(j * T, (j + 1) * T)
        qa[js, :] = jnp.transpose(qt_ref[:, js].astype(f32)).astype(bf16)
        da[js, :] = jnp.transpose(dat_ref[:, js].astype(f32)).astype(bf16)
    dqacc[...] = jnp.zeros(dqacc.shape, f32)
    for i, h in ((0, 1), (1, 1), (2, 0), (3, 1)):
        early[i].pass0(h)
    last = me // 2

    def block(sb, masked):
        ks = pl.ds(pl.multiple_of(sb * SB, SB), SB)
        kv = jnp.concatenate([kv_ref[2 * sb, 0:T, :], kv_ref[2 * sb + 1, 0:T, :]], axis=0)
        tot[...] = jnp.zeros(tot.shape, f32)

        def two(i, carry):
            for g in range(2):
                gs = pl.ds(pl.multiple_of((2 * i + g) * SB, SB), SB)
                p = jnp.exp(nt(qa[gs, :], kaug[ks, :]))
                if masked:
                    ok = visible(me, sb)
                    p = jnp.where(jnp.concatenate([ok, ok], axis=0), p, 0.0)
                ds = (p * nt(da[gs, :], vaug[ks, :])).astype(bf16)
                dqacc[gs, :] += nn(ds, kv)
                tot[0:H, :] += nn(qt_ref[0:H, gs], ds)
                tot[H:, :] += nn(dat_ref[0:H, gs], p.astype(bf16))
            return carry

        lax.fori_loop(0, J // 4, two, 0)
        low = jnp.transpose(tot[...]).astype(bf16)
        gsend[2 * sb] = low[0:T]
        gsend[2 * sb + 1] = low[T:]

    def to_owner(kb):
        return pltpu.make_async_remote_copy(src_ref=gsend.at[kb], dst_ref=grecv.at[me], send_sem=ksend.at[kb],
                                            recv_sem=krecv.at[me], device_id=(dp, kb), device_id_type=MESH)

    def from_device(b):
        return pltpu.make_async_remote_copy(src_ref=gsend.at[b], dst_ref=grecv.at[b], send_sem=ksend.at[b],
                                            recv_sem=krecv.at[b], device_id=(dp, b), device_id_type=MESH)

    def at_1():
        for s in early:
            s.pass1()

    def at_2():
        for s in early:
            s.pass2()

    def step(sb, carry):
        @pl.when(sb < last)
        def _():
            block(sb, False)
            to_owner(2 * sb).start()
            to_owner(2 * sb + 1).start()

        pl.when(sb == 1)(at_1)
        pl.when(sb == 2)(at_2)
        return carry

    lax.fori_loop(0, NSB - 1, step, 0)
    block(last, True)

    @pl.when(2 * last < me)
    def _():
        to_owner(2 * last).start()

    for s in early:
        s.pass3()
    for s, e, (u0, u1, _) in zip(spreads, (early[0], early[1], early[3]), SPREADS):
        s.begin([e.result(SHARED[u]) for u in range(u0, u1)])
    for s, e, u in zip(owned_o, (early[0], early[2], early[3]), WO_UNIT):
        s.begin(e.result(u))
    for j in range(J):
        js = slice(j * T, (j + 1) * T)
        rows[j] = sub8(jnp.transpose(dqacc[js, :])[0:H].astype(bf16).astype(f32) * 0.125)
    for c in range(4):
        to_experts(routes, rows, gat, range(6 * c, 6 * c + 6))
        store_expert(lbig, core, [0, 1, 2], 2 * c, nn(gat[c * 384 : (c + 1) * 384, :], nm))
        for s in late:
            s.start0(c)
    for s in spreads:
        s.pass2()
        s.send(0)
    dqacc[0:T, :] = gsend[me].astype(f32)
    for b in range(1, NB):
        @pl.when(b > me)
        def _(b=b):
            from_device(b).wait_recv()
            dqacc[0:T, :] += grecv[b].astype(f32)
    gkv = dqacc[0:T, :].astype(bf16)
    dkvw = tn(nm, gkv).astype(bf16)
    done = set(copies.open)
    for s in late:
        s.pass0(0)
    for s in spreads:
        s.send(1)
    gn = gn_ref[...] + tn(gat[...], wq_ref[...].reshape(EW, D)) + nt(gkv, kvw_ref[...])
    x = x_ref[...].astype(f32)
    inv = lax.rsqrt(jnp.mean(x * x, axis=-1, keepdims=True) + eps)
    n = x * inv
    dgain = jnp.sum(gn * n, axis=0, keepdims=True)
    drw = drw_ref[...]
    dfg = dfg_ref[...]
    parts = [dkvw.astype(f32)] + [drw[:, t * 128 : (t + 1) * 128] for t in range(4)]
    parts += [v[:, t * 128 : (t + 1) * 128] for v in (dgain, dfg) for t in range(4)] + [jnp.zeros((SMALL - 616, 128), f32)]
    ssrc[...] = jnp.concatenate(parts, axis=0).astype(bf16).reshape(2, 4, SMALL // 8, 128)
    small.step(0)
    copies.drain(copies.open - done)
    small.step(1)
    for s in late:
        s.pass1()
    small.step(2)
    for s in spreads:
        s.send(2)
        s.forward(0)
    hh = gn * gain_ref[...]
    ing_ref[...] = (gm_ref[...] + inv * (hh - n * jnp.mean(hh * n, axis=-1, keepdims=True))).astype(bf16)
    for s in late:
        s.pass2()
    small.step(3)
    for s in spreads:
        s.finish(0)
        s.forward(1)
    for s, t, u in zip(owned_q, late, range(3)):
        t.pass3()
        s.begin(t.result(u))
    small.step(4)
    for s in spreads:
        s.finish(1)
        s.forward(2)
    copies.drain([i for s in owned_q for i in s.ids] + small.ids[4])
    for s in owned_o + owned_q:
        s.finish()
    small.step(5)
    for s in spreads:
        s.finish(2)
    small.step(6)
    for s in spreads:
        for u in range(s.u0, s.u1):
            s.keep(u).wait()
    for b in range(NB - 1):
        @pl.when(b < me)
        def _(b=b):
            to_owner(b).wait_send()
    copies.drain()


SCRATCH = [
    VM((T, D), bf16), VM((T, D), bf16),
    VM((8, 2, 4, 4, 4, 16, 128), bf16), pltpu.SemaphoreType.DMA((8,)),
    VM((D, FF), bf16), VM((FF, D), bf16), pltpu.SemaphoreType.DMA((6,)), VM((T, D), bf16), VM((J, T), f32), VM((NB, KVR, 128), bf16),
    VM((NB, 3 * H, D), bf16), VM((NB, 3 * H, D), bf16), VM((H, ROWS), bf16), VM((128, ROWS), bf16), VM((EW // 8, 8, T), f32),
    VM((ROWS, 128), bf16), VM((ROWS, 128), bf16), VM((80, ROWS), bf16), VM((8, ROWS), f32), VM((80, ROWS), f32),
    VM((J, 8, 8, T), f32), VM((EW, T), bf16), VM((T, D), f32), VM((T, D), f32), VM((E, D), f32), VM((1, D), f32),
    VM((2, UNITS, 1024, 128), bf16), VM((UNITS, 4, 4, 4, 16, 128), bf16), VM((UNITS, 3, 4, 4, 16, 128), bf16),
    VM((UNITS, 3, 4, 16, 128), bf16), VM((UNITS, 4, 4, 16, 128), bf16),
    VM((128, ROWS), bf16), VM((ROWS, 128), bf16), VM((ROWS, 128), bf16), VM((ROWS, 128), f32), VM((128, SB), f32),
    VM((NB, T, 128), bf16), VM((NB, T, 128), bf16),
    VM((2, 3, 1024, 128), bf16), VM((3, 4, 4, 4, 16, 128), bf16), VM((3, 3, 4, 4, 16, 128), bf16), VM((3, 3, 4, 16, 128), bf16),
    VM((3, 4, 4, 16, 128), bf16),
    VM((2, 4, SMALL // 8, 128), bf16), VM((4, SMALL // 8, 128), bf16), VM((4, SMALL // 8, 128), bf16),
    VM((3, SMALL // 8, 128), bf16), VM((4, SMALL // 8, 128), bf16), VM((4, SMALL // 8, 128), bf16),
] + dma_sems(234) + dma_sems(NB)


def kernel_f(all_hbm, wo_hbm, dwq_hbm, small_hbm, out_in, ing_in,
             dup_hbm, ddown_hbm, dwo_ref, dwqt_ref, dkvw_ref, drw_ref, dgain_ref, dfg_ref, out_hbm, ing_hbm,
             units, wo_ref, dwq_ref, small_ref, up, down, held, in_sem, out_sem):
    order = [SHARED.index(u) for pair in zip(UP_UNIT, DOWN_UNIT) for u in pair]
    loads = [pltpu.make_async_copy(all_hbm.at[u], units.at[u], in_sem.at[i]) for i, u in enumerate(order)]
    loads += [pltpu.make_async_copy(src, dst, in_sem.at[8 + i])
              for i, (src, dst) in enumerate(((wo_hbm, wo_ref), (dwq_hbm, dwq_ref), (small_hbm, small_ref),
                                              (out_in, held.at[0]), (ing_in, held.at[1])))]
    for cp in loads:
        cp.start()
    stores = []
    for c in range(4):
        cs = slice(c * 512, (c + 1) * 512)
        u, d = order[2 * c : 2 * c + 2]
        loads[2 * c].wait()
        for t in range(4):
            up[:, c * 512 + t * 128 : c * 512 + (t + 1) * 128] = units[u, t].astype(f32)
        stores.append(pltpu.make_async_copy(up.at[:, cs], dup_hbm.at[:, cs], out_sem.at[2 * c]))
        stores[-1].start()
        loads[2 * c + 1].wait()
        for t in range(4):
            down[cs, t * 128 : (t + 1) * 128] = units[d, t].astype(f32)
        stores.append(pltpu.make_async_copy(down.at[cs], ddown_hbm.at[cs], out_sem.at[2 * c + 1]))
        stores[-1].start()
    for cp in loads[8:]:
        cp.wait()
    for i, dst in enumerate((out_hbm, ing_hbm)):
        stores.append(pltpu.make_async_copy(held.at[i], dst, out_sem.at[8 + i]))
        stores[-1].start()
    for t in range(4):
        ts = slice(t * 128, (t + 1) * 128)
        dwo_ref[:, ts] = wo_ref[t * 192 : (t + 1) * 192, :].astype(f32)
        dwqt_ref[:, ts] = dwq_ref[t * 192 : (t + 1) * 192, :].astype(f32)
    small = small_ref[512:SMALL, :].astype(f32)
    dkvw_ref[...] = small_ref[0:512, :].astype(f32)
    for t in range(4):
        ts = slice(t * 128, (t + 1) * 128)
        drw_ref[:, ts] = small[t * E : (t + 1) * E]
        dgain_ref[:, ts] = small[96 + t : 97 + t]
        dfg_ref[:, ts] = small[100 + t : 101 + t]
    for cp in stores:
        cp.wait()


def per_device(inputs, cotangent, norm_gain, ffn_gain, kv_weight, router_weight, query_weight, output_weight, up_weight,
               down_weight, routes, segment_ids):
    wq = jnp.swapaxes(query_weight, 1, 2).reshape(3 * H, D)
    wo = output_weight.reshape(3 * H, D)
    vmem, anywhere = pl.BlockSpec(memory_space=VM), pl.BlockSpec(memory_space=pl.ANY)
    S = jax.ShapeDtypeStruct
    out, ing, shared, dwo, dwq, small = pl.pallas_call(
        kernel_all,
        out_shape=[S((T, D), bf16), S((T, D), bf16), S((8, 2, 4, 4, 4, 16, 128), bf16), S((3, 4, 4, 16, 128), bf16),
                   S((3, 4, 4, 16, 128), bf16), S((2, 4, SMALL // 8, 128), bf16)],
        in_specs=[anywhere] * 2 + [vmem] * 6 + [anywhere] * 4,
        out_specs=[vmem, vmem, anywhere, vmem, vmem, vmem],
        scratch_shapes=SCRATCH,
        compiler_params=pltpu.CompilerParams(vmem_limit_bytes=62 << 20, collective_id=1, has_side_effects=True),
        cost_estimate=pl.CostEstimate(flops=1 << 35, bytes_accessed=1 << 24, transcendentals=0),
    )(inputs, cotangent, norm_gain.reshape(1, D), ffn_gain.reshape(1, D), kv_weight, router_weight.T, routes.T,
      segment_ids.reshape(3, 128), wq, wo, up_weight, down_weight)
    dup, ddown, dwo, dwqt, dkvw, drw, dgain, dfg, out, ing = pl.pallas_call(
        kernel_f,
        out_shape=[S((D, FF), f32), S((FF, D), f32), S((3 * H, D), f32), S((3 * H, D), f32), S((D, 128), f32), S((E, D), f32),
                   S((1, D), f32), S((1, D), f32), S((T, D), bf16), S((T, D), bf16)],
        in_specs=[anywhere] * 6,
        out_specs=[anywhere] * 2 + [vmem] * 6 + [anywhere] * 2,
        scratch_shapes=[VM((8, 4, 512, 128), bf16), VM((768, 128), bf16), VM((768, 128), bf16), VM((SMALL, 128), bf16),
                        VM((D, FF), f32), VM((FF, D), f32), VM((2, T, D), bf16), pltpu.SemaphoreType.DMA((13,)),
                        pltpu.SemaphoreType.DMA((10,))],
        compiler_params=pltpu.CompilerParams(vmem_limit_bytes=62 << 20),
    )(shared.reshape(8, 4, 512, 128), dwo.reshape(768, 128), dwq.reshape(768, 128), small.reshape(SMALL, 128), out, ing)
    return (out, ing, dgain.reshape(D), dfg.reshape(D), dkvw, drw.T,
            jnp.swapaxes(dwqt.reshape(3, H, D), 1, 2), dwo.reshape(3, H, D), dup, ddown)


def solution(mesh):
    both = P(("dp", "expert"), None)
    ex = P("expert", None, None)
    return jax.shard_map(
        per_device, mesh=mesh,
        in_specs=(both, both, P(), P(), P(), P(), ex, ex, P(), P(), both, P(("dp", "expert"))),
        out_specs=(both, both, P(), P(), P(), P(), ex, ex, P(), P()),
        check_vma=False)
```
